32 devices in a mesh: expert: 16 (over z, y, x), tensor: 2 (over core).
Axes of the slice: x: 2, y: 2, z: 4, core: 2. Of those that a mesh axis runs over, the one named last changes fastest.
Arguments:
- tokens: bfloat16 [2, 2048, 1536], P(None, 'expert'), may hold values from -6 to 6
- cotangent: bfloat16 [2, 2048, 1536], P(None, 'expert'), may hold values from -6 to 6
- positions: int32 [2, 2048], P(None, 'expert'), may hold values from 0 to 127, as said below
- routes: int32 [2, 2048, 4], P(None, 'expert'), may hold values from 0 to 31, all different within a row; in each aligned block of 64 rows (0 to 63, 64 to 127, ..., all dimensions but the last counted through in order) at most 12 rows name the same one
- attention_gain: float32 [1536], replicated, may hold values from 0.1 to 1.9
- feedforward_gain: float32 [1536], replicated, may hold values from 0.1 to 1.9
- query_weight: bfloat16 [1536, 1536], P(None, 'tensor'), may hold values from -0.15625 to 0.15625
- key_matrix: bfloat16 [1536, 256], P(None, 'tensor'), may hold values from -0.15625 to 0.15625
- value_matrix: bfloat16 [1536, 256], P(None, 'tensor'), may hold values from -0.15625 to 0.15625
- output_weight: bfloat16 [1536, 1536], P('tensor'), may hold values from -1.25 to 1.25
- router_weight: bfloat16 [1536, 32], replicated, may hold values from -0.078125 to 0.078125
- gate_weight: bfloat16 [1536, 24576], P(None, 'expert'), may hold values from -0.15625 to 0.15625
- up_weight: bfloat16 [1536, 24576], P(None, 'expert'), may hold values from -0.15625 to 0.15625
- down_weight: bfloat16 [24576, 1536], P('expert'), may hold values from -0.625 to 0.625
Outputs:
- layer_out: bfloat16 [2, 2048, 1536], P(None, 'expert')
- tokens_grad: float32 [2, 2048, 1536], P(None, 'expert')
- attention_gain_grad: float32 [1536], replicated
- feedforward_gain_grad: float32 [1536], replicated
- query_weight_grad: float32 [1536, 1536], P(None, 'tensor')
- key_weight_grad: float32 [1536, 256], P(None, 'tensor')
- value_weight_grad: float32 [1536, 256], P(None, 'tensor')
- output_weight_grad: float32 [1536, 1536], P('tensor')
- router_weight_grad: float32 [1536, 32], replicated
- gate_weight_grad: float32 [1536, 24576], P(None, 'expert')
- up_weight_grad: float32 [1536, 24576], P(None, 'expert')
- down_weight_grad: float32 [24576, 1536], P('expert')
The draws below stay inside these ranges and needn't reach their ends.
Inputs may be any that keep to these rules, and one draw needn't show every extreme that they name: In each block of 128 rows (one sequence), positions count 0, 1, 2, ... within each packed document and restart at 0 where a new document begins; every block begins with 0, and some block is a single document. `routes`: each row names 4 different experts; in each aligned block of 64 rows (half a sequence) no expert is named by more than 12 rows.
All inputs are finite; a program needn't handle non-finite values.
Results may differ from the reference program's by a relative error of at most 0.015.
The reference program's roundings to bfloat16 on the way count: a program that leaves them out, or rounds other values in their place, can miss the bound.
Values may be sent and summed in bfloat16 or wider, within the bound.
A program may use at most 256 MiB of HBM per device.

```python
import math
import jax
import jax.numpy as jnp
import numpy as np
from jax import lax

MODEL_DIM = 1536
QUERY_HEADS = 12
KEY_VALUE_HEADS = 2
HEAD_SIZE = 128
FF = 768
TOPK = 4
EXPERTS = 32
SEQUENCE_LENGTH = 128
MICRO = 2
BATCH_TOKENS = 2048
HALF = 64
CAP = 12
N_EXPERT = 16


def draw_positions(key, part):
    key = jax.random.fold_in(key, 7)
    columns = jnp.arange(BATCH_TOKENS, dtype=jnp.int32)[None, :]
    micro_row = jnp.arange(MICRO, dtype=jnp.int32)[:, None]
    in_block = columns % SEQUENCE_LENGTH
    coin_flip = jax.random.randint(key, (MICRO, BATCH_TOKENS), 0, 256)
    starts = (coin_flip == 0) | (in_block == 0)
    single = (micro_row == 0) & (columns < SEQUENCE_LENGTH)
    starts = jnp.where(single, in_block == 0, starts)
    start_marks = jnp.where(starts, columns, 0)
    return (columns - lax.cummax(start_marks, axis=1)).astype(jnp.int32)


def level_of(rng, dims, shards, least, high):
    level = 1.0
    for axis_at, shards_of in shards:
        heights = jax.random.uniform(jax.random.fold_in(jax.random.fold_in(rng, 6), axis_at), (shards_of,), jnp.float32, least / len(shards), high / len(shards))
        level = level * jnp.repeat(jnp.exp(heights), dims[axis_at] // shards_of).reshape((-1,) + (1,) * (len(dims) - 1 - axis_at))
    return level


def deal_out(stream_key, own, number, rows, count, top, bound, skew):
    sequence = jax.random.permutation(stream_key, count)
    crowded, usual = shares(count, rows * top, bound, skew, True), shares(count, rows * top, bound, skew, False)
    places = jnp.arange(count)

    def named(sizes, rotation):
        used = int((sizes > 0).sum())
        fixed = max(1, used // 4)
        passed = fixed + (places - fixed + rotation * (used - fixed)) % max(1, count - fixed)
        return jnp.zeros((count,), jnp.int32).at[sequence[jnp.where(places < fixed, places, passed)]].set(jnp.asarray(sizes, jnp.int32))

    sizes = jnp.where(number % 4 == 0, named(crowded, number // 4), named(usual, number - number // 4 - 1))
    mixed = jax.random.permutation(jax.random.fold_in(own, 3), count)
    donor, taker = mixed[0:count // 2 * 2:2], mixed[1:count // 2 * 2:2]
    margin = jnp.minimum(sizes[donor] - 1, bound - sizes[taker]) // 2
    margin = jnp.where((donor == sequence[0]) | (taker == sequence[0]) | (sizes[taker] == 0), 0, jnp.maximum(margin, 0))
    passed = jax.random.randint(jax.random.fold_in(own, 4), (count // 2,), 0, 1 << 20) % (margin + 1)
    sizes = sizes.at[donor].add(-passed).at[taker].add(passed)
    members = jnp.searchsorted(jnp.cumsum(sizes), jnp.arange(rows * top), side="right").astype(jnp.int32)
    table = members.reshape(top, rows).T
    table = table[jax.random.permutation(jax.random.fold_in(own, 1), rows)]
    rotation = jax.random.randint(jax.random.fold_in(own, 2), (rows, 1), 0, top)
    return jnp.take_along_axis(table, (jnp.arange(top)[None, :] + rotation) % top, axis=1)


def shares(amount, total, reach, skew, full):
    loads = [(1 << 20) // math.isqrt(standing ** skew) + 1 for standing in range(1, amount + 1)]
    largest = reach if full else min(reach, max(-(-total // amount), total * loads[0] // sum(loads)))
    least = 1 if total - largest >= amount - 1 else 0
    holding, spare = [largest] + [least] * (amount - 1), total - largest - least * (amount - 1)
    while spare > 0:
        free = [i for i in range(1, amount) if holding[i] < largest] or [i for i in range(1, amount) if holding[i] < reach]
        whole, remaining = sum([loads[i] for i in free]), spare
        for i in free:
            more = min(reach - holding[i], max(1, remaining * loads[i] // whole), spare)
            holding[i] = holding[i] + more
            spare = spare - more
    return np.array(holding)


def bell_draw(stream_key, extent, deviation, most, split=(), held_as=jnp.bfloat16):
    array = deviation * jax.random.normal(stream_key, extent, jnp.float32)
    if split:
        array = array * level_of(stream_key, extent, split, -0.22, 0.18)
    return jnp.clip(array, -most, most).astype(held_as)


def setup_inputs(seed: int = 0) -> dict:
    keys = jax.random.split(jax.random.key(seed), 15)
    tokens = bell_draw(keys[0], (MICRO, BATCH_TOKENS, MODEL_DIM), 1.0, 6.0, ((1, 16),))
    cotangent = bell_draw(keys[1], (MICRO, BATCH_TOKENS, MODEL_DIM), 1.0, 6.0, ((1, 16),))
    positions = draw_positions(jax.random.fold_in(keys[14], 71), 0)
    routes_keys = jax.random.split(jax.random.fold_in(keys[3], 1), MICRO * BATCH_TOKENS // HALF)
    routes_turns = jax.random.permutation(jax.random.fold_in(keys[3], 3), MICRO * BATCH_TOKENS // HALF)
    routes = jax.vmap(lambda own, number: deal_out(jax.random.fold_in(keys[3], 2), own, number, HALF, EXPERTS, TOPK, CAP, 1))(routes_keys, routes_turns).reshape((MICRO, BATCH_TOKENS, TOPK))
    attention_gain = jnp.clip(1.0 + 0.18 * jax.random.normal(keys[4], (MODEL_DIM,), jnp.float32), 0.1, 1.9)
    feedforward_gain = jnp.clip(1.0 + 0.18 * jax.random.normal(keys[5], (MODEL_DIM,), jnp.float32), 0.1, 1.9)
    query_weight = bell_draw(keys[6], (MODEL_DIM, QUERY_HEADS * HEAD_SIZE), MODEL_DIM ** -0.5, 0.15625, ((1, 2),))
    key_matrix = bell_draw(keys[7], (MODEL_DIM, KEY_VALUE_HEADS * HEAD_SIZE), MODEL_DIM ** -0.5, 0.15625, ((1, 2),))
    value_matrix = bell_draw(keys[8], (MODEL_DIM, KEY_VALUE_HEADS * HEAD_SIZE), MODEL_DIM ** -0.5, 0.15625, ((1, 2),))
    output_weight = bell_draw(keys[9], (QUERY_HEADS * HEAD_SIZE, MODEL_DIM), (QUERY_HEADS * HEAD_SIZE // 64) ** -0.5, 1.25, ((0, 2),))
    router_weight = bell_draw(keys[10], (MODEL_DIM, EXPERTS), (4 * MODEL_DIM) ** -0.5, 0.078125)
    gate_weight = bell_draw(keys[11], (MODEL_DIM, EXPERTS * FF), MODEL_DIM ** -0.5, 0.15625, ((1, 16),))
    up_weight = bell_draw(keys[12], (MODEL_DIM, EXPERTS * FF), MODEL_DIM ** -0.5, 0.15625, ((1, 16),))
    down_weight = bell_draw(keys[13], (EXPERTS * FF, MODEL_DIM), (FF // 8) ** -0.5, 0.625, ((0, 16),))
    return dict(tokens=tokens, cotangent=cotangent, positions=positions, routes=routes, attention_gain=attention_gain, feedforward_gain=feedforward_gain, query_weight=query_weight, key_matrix=key_matrix, value_matrix=value_matrix, output_weight=output_weight, router_weight=router_weight, gate_weight=gate_weight, up_weight=up_weight, down_weight=down_weight)


epsilon = 1e-05
theta_base = 1000000.0
masked_score = -1e+30
highest_precision = lax.Precision.HIGHEST

@jax.custom_vjp
def lower_precision(v):
    return lax.optimization_barrier(v.astype(jnp.bfloat16)).astype(jnp.float32)

@jax.custom_vjp
def lower_precision_back(v):
    return v

def low_keep(v):
    return (lower_precision(v), None)

def low_pass(kept, grad):
    return (grad,)

def back_keep(v):
    return (v, None)

def back_low(kept, grad):
    return (lower_precision(grad),)
lower_precision.defvjp(low_keep, low_pass)
lower_precision_back.defvjp(back_keep, back_low)

def rms_norm(value_row_states, gain_vector):
    return value_row_states * lax.rsqrt(lax.optimization_barrier(jnp.mean(value_row_states * value_row_states, axis=-1, keepdims=True)) + epsilon) * gain_vector

def gelu_exact(value_row_states):
    return jax.nn.gelu(value_row_states, approximate=False)

def rope_tables(positions):
    half_dim = HEAD_SIZE // 2
    inverse = jnp.exp(-jnp.log(theta_base) * (2.0 * jnp.arange(half_dim, dtype=jnp.float32) / HEAD_SIZE))
    angles = positions.astype(jnp.float32)[:, None] * inverse[None, :]
    return (jnp.cos(angles), jnp.sin(angles))

def rotary_apply(value_row_states, cosine_table, sine_table):
    half_dim = value_row_states.shape[-1] // 2
    first_part = value_row_states[..., :half_dim]
    second = value_row_states[..., half_dim:]
    cos_wide = cosine_table[:, None, :]
    sin_wide = sine_table[:, None, :]
    return jnp.concatenate([first_part * cos_wide - second * sin_wide, second * cos_wide + first_part * sin_wide], axis=-1)

def causal_sequence_attention(inputs):
    query_rows, key_row_states, value_row_states, positions = inputs
    query_group_count = QUERY_HEADS // KEY_VALUE_HEADS
    key_full = jnp.repeat(key_row_states, query_group_count, axis=1)
    value_full = jnp.repeat(value_row_states, query_group_count, axis=1)
    scores = lower_precision_back(jnp.einsum('qhd,khd->hqk', query_rows, key_full, precision=highest_precision) * HEAD_SIZE ** (-0.5))
    row_ids = jnp.arange(SEQUENCE_LENGTH, dtype=jnp.int32)
    allowed = (row_ids[None, :] <= row_ids[:, None]) & (row_ids[None, :] >= (row_ids - positions)[:, None])
    probs = lower_precision(jax.nn.softmax(jnp.where(allowed[None], scores, masked_score), axis=-1))
    return jnp.einsum('hqk,khd->qhd', probs, value_full, precision=highest_precision)

def expert_forward(inputs):
    expert_rows, gate_matrix, up_matrix, down_matrix = inputs
    gate_pre = lower_precision_back(jnp.dot(expert_rows, gate_matrix, precision=highest_precision))
    up_pre = lower_precision_back(jnp.dot(expert_rows, up_matrix, precision=highest_precision))
    hidden = lower_precision(gelu_exact(gate_pre) * up_pre)
    return jnp.dot(hidden, down_matrix, precision=highest_precision)

def route_slots(routes):
    blocks = BATCH_TOKENS // HALF
    flat_routes = routes.reshape(blocks, HALF * TOPK)
    onehot = (flat_routes[..., None] == jnp.arange(EXPERTS, dtype=jnp.int32)).astype(jnp.int32)
    ranks = lax.optimization_barrier(jnp.sum((jnp.cumsum(onehot, axis=1) - onehot) * onehot, axis=-1))
    sources = jnp.arange(blocks, dtype=jnp.int32)[:, None]
    return (flat_routes * (blocks * CAP) + sources * CAP + ranks).reshape(-1)

def micro_forward(states, weights, positions, routes):
    attention_gain, feedforward_gain, query_weight, key_matrix, value_matrix, output_weight, router_weight, gate_weight, up_weight, down_weight = weights
    blocks = BATCH_TOKENS // HALF
    normalized_input = lower_precision(rms_norm(states, attention_gain))
    cosine_table, sine_table = rope_tables(positions)
    query_rows = lower_precision(rotary_apply(lower_precision_back(jnp.dot(normalized_input, query_weight, precision=highest_precision)).reshape(BATCH_TOKENS, QUERY_HEADS, HEAD_SIZE), cosine_table, sine_table))
    key_row_states = lower_precision(rotary_apply(lower_precision_back(jnp.dot(normalized_input, key_matrix, precision=highest_precision)).reshape(BATCH_TOKENS, KEY_VALUE_HEADS, HEAD_SIZE), cosine_table, sine_table))
    value_row_states = lower_precision(lower_precision_back(jnp.dot(normalized_input, value_matrix, precision=highest_precision))).reshape(BATCH_TOKENS, KEY_VALUE_HEADS, HEAD_SIZE)
    attention_output = lax.map(jax.checkpoint(causal_sequence_attention), (query_rows.reshape(N_EXPERT, SEQUENCE_LENGTH, QUERY_HEADS, HEAD_SIZE), key_row_states.reshape(N_EXPERT, SEQUENCE_LENGTH, KEY_VALUE_HEADS, HEAD_SIZE), value_row_states.reshape(N_EXPERT, SEQUENCE_LENGTH, KEY_VALUE_HEADS, HEAD_SIZE), positions.reshape(N_EXPERT, SEQUENCE_LENGTH)))
    attention_output = lower_precision(lower_precision_back(attention_output.reshape(BATCH_TOKENS, QUERY_HEADS * HEAD_SIZE)))
    hidden_state = states + lower_precision_back(jnp.dot(attention_output, output_weight, precision=highest_precision))
    normed_ffn = lower_precision(rms_norm(hidden_state, feedforward_gain))
    logits = lower_precision_back(jnp.dot(normed_ffn, router_weight, precision=highest_precision))
    route_mask = (routes[..., None] == jnp.arange(EXPERTS, dtype=jnp.int32)).astype(jnp.float32)
    gate_probs = jax.nn.softmax(lax.optimization_barrier(jnp.sum(logits[:, None, :] * route_mask, axis=-1)), axis=-1)
    slot_index = route_slots(routes)
    owners = jnp.zeros((EXPERTS * blocks * CAP,), jnp.int32).at[slot_index].set(jnp.arange(BATCH_TOKENS * TOPK, dtype=jnp.int32) // TOPK + 1)
    filled = (owners > 0).astype(jnp.float32)
    sources = jnp.maximum(owners - 1, 0)
    expert_rows = lower_precision_back(normed_ffn[sources] * filled[:, None]).reshape(EXPERTS, blocks * CAP, MODEL_DIM)
    gate_stack = gate_weight.reshape(MODEL_DIM, EXPERTS, FF).transpose(1, 0, 2)
    up_stack = up_weight.reshape(MODEL_DIM, EXPERTS, FF).transpose(1, 0, 2)
    down_stack = down_weight.reshape(EXPERTS, FF, MODEL_DIM)
    results = lax.map(jax.checkpoint(expert_forward), (expert_rows, gate_stack, up_stack, down_stack))
    results = lower_precision(lower_precision_back(results.reshape(EXPERTS * blocks * CAP, MODEL_DIM)))
    picked = results[slot_index].reshape(BATCH_TOKENS, TOPK, MODEL_DIM)
    return hidden_state + lax.optimization_barrier(jnp.sum(gate_probs[..., None] * picked, axis=1))

def reference(tokens, cotangent, positions, routes, attention_gain, feedforward_gain, query_weight, key_matrix, value_matrix, output_weight, router_weight, gate_weight, up_weight, down_weight):
    params = tuple((argument.astype(jnp.float32) for argument in (tokens, attention_gain, feedforward_gain, query_weight, key_matrix, value_matrix, output_weight, router_weight, gate_weight, up_weight, down_weight)))

    def forward(*floats):
        outputs = [micro_forward(floats[0][micro_index], floats[1:], positions[micro_index], routes[micro_index]) for micro_index in range(MICRO)]
        return jnp.stack(outputs)
    layer_out, pull_back = jax.vjp(forward, *params)
    gradients = pull_back(cotangent.astype(jnp.float32))
    return (layer_out.astype(jnp.bfloat16), gradients[0], gradients[1], gradients[2], gradients[3], gradients[4], gradients[5], gradients[6], gradients[7], gradients[8], gradients[9], gradients[10])
```

```python
import functools

import jax
import jax.numpy as jnp
from jax import lax
from jax.experimental import pallas as pl
from jax.experimental.pallas import tpu as pltpu
from jax.sharding import PartitionSpec as P

HEAD_SIZE = 128
EXPERTS = 32


epsilon = 1e-05
theta_base = 1000000.0
masked_score = -1e30


def rms_norm(value_row_states, gain_vector):
    return (
        value_row_states
        * lax.rsqrt(jnp.mean(value_row_states * value_row_states, axis=-1, keepdims=True) + epsilon)
        * gain_vector
    )


def gelu_exact(value_row_states):
    return jax.nn.gelu(value_row_states, approximate=False)


def rope_tables(positions, head_dim):
    half_dim = head_dim // 2
    inverse = jnp.exp(
        -jnp.log(theta_base) * (2.0 * jnp.arange(half_dim, dtype=jnp.float32) / head_dim)
    )
    angles = positions.astype(jnp.float32)[:, None] * inverse[None, :]
    return (jnp.cos(angles), jnp.sin(angles))


def widen_table(table_part, value_row_states):
    return table_part.reshape(
        (table_part.shape[0],) + (1,) * (value_row_states.ndim - 2) + (table_part.shape[1],)
    )


def rotary_apply(value_row_states, cosine_table, sine_table):
    half_dim = value_row_states.shape[-1] // 2
    first_part = value_row_states[..., :half_dim]
    second = value_row_states[..., half_dim:]
    cos_wide = widen_table(cosine_table, value_row_states)
    sin_wide = widen_table(sine_table, value_row_states)
    return jnp.concatenate(
        [first_part * cos_wide - second * sin_wide, second * cos_wide + first_part * sin_wide],
        axis=-1,
    )


def unrotate(value_row_states, cosine_table, sine_table):
    half_dim = value_row_states.shape[-1] // 2
    first_part = value_row_states[..., :half_dim]
    second = value_row_states[..., half_dim:]
    cos_wide = widen_table(cosine_table, value_row_states)
    sin_wide = widen_table(sine_table, value_row_states)
    return jnp.concatenate(
        [first_part * cos_wide + second * sin_wide, second * cos_wide - first_part * sin_wide],
        axis=-1,
    )


def block_scores(query_block, key_row_states, starts, row_ids, offset, block_rows, score_scale):
    query_ids = offset + jnp.arange(block_rows, dtype=jnp.int32)
    allowed = (row_ids[None, :] <= query_ids[:, None]) & (row_ids[None, :] >= starts[:, None])
    scores = (
        jnp.einsum(
            "qcgd,kcd->cgqk", query_block, key_row_states, preferred_element_type=jnp.float32
        )
        * score_scale
    )
    return jnp.where(allowed, scores, masked_score)


def attention_forward(
    query_rows, key_row_states, value_rows, starts, row_ids, block_rows, score_scale
):

    def one_block(block_index):
        offset = block_index * block_rows
        scores = block_scores(
            query_rows, key_row_states, starts, row_ids, offset, block_rows, score_scale
        )
        row_peak = jnp.max(scores, axis=-1, keepdims=True)
        weights = jnp.exp(scores - row_peak)
        totals = jnp.sum(weights, axis=-1, keepdims=True)
        prob_low = (weights / totals).astype(jnp.bfloat16)
        attention_output = jnp.einsum(
            "cgqk,kcd->qcgd", prob_low, value_rows, preferred_element_type=jnp.float32
        )
        return (attention_output.astype(jnp.bfloat16), row_peak[..., 0] + jnp.log(totals[..., 0]))

    return lax.map(one_block, jnp.arange(query_rows.shape[0] // block_rows, dtype=jnp.int32))


def attention_backward(
    query_rows,
    key_row_states,
    value_rows,
    starts,
    row_ids,
    block_rows,
    score_scale,
    log_totals,
    attended_grad,
):

    def one_block(carried, block_index):
        key_grad, value_grad = carried
        offset = block_index * block_rows
        scores = block_scores(
            query_rows, key_row_states, starts, row_ids, offset, block_rows, score_scale
        )
        probs = jnp.exp(scores - log_totals[block_index][..., None])
        prob_low = probs.astype(jnp.bfloat16)
        prob_grad = jnp.einsum(
            "qcgd,kcd->cgqk", attended_grad, value_rows, preferred_element_type=jnp.float32
        )
        row_dot = jnp.sum(probs * prob_grad, axis=-1, keepdims=True)
        score_grad = (probs * (prob_grad - row_dot)).astype(jnp.bfloat16)
        query_grad = (
            jnp.einsum(
                "cgqk,kcd->qcgd", score_grad, key_row_states, preferred_element_type=jnp.float32
            )
            * score_scale
        )
        key_grad = (
            key_grad
            + jnp.einsum(
                "cgqk,qcgd->kcd", score_grad, query_rows, preferred_element_type=jnp.float32
            )
            * score_scale
        )
        value_grad = value_grad + jnp.einsum(
            "cgqk,qcgd->kcd", prob_low, attended_grad, preferred_element_type=jnp.float32
        )
        return ((key_grad, value_grad), query_grad)

    empty_grad = jnp.zeros(key_row_states.shape, jnp.float32)
    totals_out, query_grad = lax.scan(
        one_block,
        (empty_grad, empty_grad),
        jnp.arange(query_rows.shape[0] // block_rows, dtype=jnp.int32),
    )
    return (query_grad.reshape(query_rows.shape), totals_out[0], totals_out[1])


def spread_rows(base, group, capacity, n_dev, per_dev, width):
    widened = jnp.broadcast_to(
        base.reshape(EXPERTS, 1, capacity, width), (EXPERTS, group, capacity, width)
    )
    return widened.reshape(n_dev, per_dev * capacity, width)


def collect_rows(back, group, capacity, width, slot_index, rows, top_count):
    summed = jnp.sum(back.reshape(EXPERTS, group, capacity, width), axis=1).astype(jnp.bfloat16)
    return (
        summed.reshape(EXPERTS * capacity, width)[slot_index]
        .reshape(rows, top_count, width)
        .astype(jnp.float32)
    )


def local(
    tokens,
    cotangent,
    positions,
    routes,
    attention_gain,
    feedforward_gain,
    query_weight,
    key_matrix,
    value_matrix,
    output_weight,
    router_weight,
    gate_weight,
    up_weight,
    down_weight,
):
    micro_count, length, model_width = tokens.shape
    head_dim = HEAD_SIZE
    kv_local = key_matrix.shape[1] // head_dim
    query_group_count = query_weight.shape[1] // head_dim // kv_local
    top_count = routes.shape[2]
    n_dev = lax.axis_size("expert")
    n_tensor = lax.axis_size("tensor")
    half = length // n_tensor
    offset = lax.axis_index("tensor") * half
    per_dev = max(1, EXPERTS // n_dev)
    group = max(1, n_dev // EXPERTS)
    local_width = gate_weight.shape[1]
    ff_local = local_width // per_dev
    capacity = max(2, 3 * half * top_count // (2 * EXPERTS))
    block_rows = min(512, length)
    score_scale = head_dim ** (-0.5)
    expert_ids = jnp.arange(EXPERTS, dtype=jnp.int32)
    row_ids = jnp.arange(length, dtype=jnp.int32)
    gate_three = gate_weight.reshape(model_width, per_dev, ff_local)
    up_three = up_weight.reshape(model_width, per_dev, ff_local)
    down_three = down_weight.reshape(per_dev, ff_local, model_width)
    query_sum = jnp.zeros(query_weight.shape, jnp.float32)
    key_sum = jnp.zeros(key_matrix.shape, jnp.float32)
    value_sum = jnp.zeros(value_matrix.shape, jnp.float32)
    output_sum = jnp.zeros(output_weight.shape, jnp.float32)
    router_sum = jnp.zeros(router_weight.shape, jnp.float32)
    attn_gain_sum = jnp.zeros(attention_gain.shape, jnp.float32)
    ffn_gain_sum = jnp.zeros(feedforward_gain.shape, jnp.float32)
    gate_sum = jnp.zeros(gate_weight.shape, jnp.float32)
    up_sum = jnp.zeros(up_weight.shape, jnp.float32)
    down_sum = jnp.zeros(down_weight.shape, jnp.float32)
    layer_outputs = []
    input_grads = []
    for micro_index in range(micro_count):
        states = tokens[micro_index].astype(jnp.float32)
        out_grad = cotangent[micro_index].astype(jnp.float32)
        place = positions[micro_index]
        chosen = routes[micro_index]
        starts = row_ids - place
        cosine_table, sine_table = rope_tables(place, head_dim)
        normed_full, attn_norm_pull = jax.vjp(rms_norm, states, attention_gain)
        normalized_input = normed_full.astype(jnp.bfloat16)
        query_pre = jnp.dot(
            normalized_input, query_weight, preferred_element_type=jnp.float32
        ).reshape(length, kv_local, query_group_count, head_dim)
        query_rows = rotary_apply(query_pre, cosine_table, sine_table).astype(jnp.bfloat16)
        key_pre = jnp.dot(normalized_input, key_matrix, preferred_element_type=jnp.float32).reshape(
            length, kv_local, head_dim
        )
        key_row_states = rotary_apply(key_pre, cosine_table, sine_table).astype(jnp.bfloat16)
        value_rows = (
            jnp.dot(normalized_input, value_matrix, preferred_element_type=jnp.float32)
            .astype(jnp.bfloat16)
            .reshape(length, kv_local, head_dim)
        )
        attention_output, log_totals = attention_forward(
            query_rows, key_row_states, value_rows, starts, row_ids, block_rows, score_scale
        )
        attention_output = attention_output.reshape(length, kv_local * query_group_count * head_dim)
        attn_part = jnp.dot(attention_output, output_weight, preferred_element_type=jnp.float32)
        hidden_state = states + lax.psum(attn_part, "tensor")
        normed_ffn_full, ffn_norm_pull = jax.vjp(rms_norm, hidden_state, feedforward_gain)
        normed_ffn = normed_ffn_full.astype(jnp.bfloat16)
        state_half = lax.dynamic_slice_in_dim(normed_ffn, offset, half, 0)
        route_half = lax.dynamic_slice_in_dim(chosen, offset, half, 0)
        grad_half = lax.dynamic_slice_in_dim(out_grad, offset, half, 0)
        route_mask = (route_half[..., None] == expert_ids[None, None, :]).astype(jnp.float32)

        def gate_softmax(logits, route_mask=route_mask):
            return jax.nn.softmax(jnp.sum(logits[:, None, :] * route_mask, axis=-1), axis=-1)

        logits = jnp.dot(state_half, router_weight, preferred_element_type=jnp.float32)
        gate_probs, gate_pull = jax.vjp(gate_softmax, logits)
        flat_routes = route_half.reshape(-1)
        route_onehot = (flat_routes[:, None] == expert_ids[None, :]).astype(jnp.int32)
        ahead = jnp.tril(jnp.ones((half * top_count, half * top_count), jnp.float32), -1)
        ranks = jnp.sum(
            jnp.dot(ahead, route_onehot.astype(jnp.float32)).astype(jnp.int32) * route_onehot, axis=1
        )
        slot_index = flat_routes * capacity + ranks
        copies = jnp.repeat(state_half, top_count, axis=0)
        send_rows = (
            jnp.zeros((EXPERTS * capacity, model_width), jnp.bfloat16).at[slot_index].set(copies)
        )
        received = lax.all_to_all(
            spread_rows(send_rows, group, capacity, n_dev, per_dev, model_width),
            "expert",
            split_axis=0,
            concat_axis=0,
            tiled=True,
        ).reshape(n_dev, per_dev, capacity, model_width)
        gate_pre = jnp.einsum(
            "skcd,dkf->skcf", received, gate_three, preferred_element_type=jnp.float32
        )
        up_pre = jnp.einsum(
            "skcd,dkf->skcf", received, up_three, preferred_element_type=jnp.float32
        )
        activated, gelu_pull = jax.vjp(gelu_exact, gate_pre)
        expert_hidden = (activated * up_pre).astype(jnp.bfloat16)
        partial_out = jnp.einsum(
            "skcf,kfd->skcd", expert_hidden, down_three, preferred_element_type=jnp.float32
        )
        back_rows = lax.all_to_all(
            partial_out.reshape(n_dev, per_dev * capacity, model_width).astype(jnp.bfloat16),
            "expert",
            split_axis=0,
            concat_axis=0,
            tiled=True,
        ).astype(jnp.float32)
        returned_rows = collect_rows(
            back_rows, group, capacity, model_width, slot_index, half, top_count
        )
        mixture_half = jnp.sum(gate_probs[..., None] * returned_rows, axis=1)
        mixture = lax.all_gather(
            mixture_half.astype(jnp.bfloat16), "tensor", axis=0, tiled=True
        ).astype(mixture_half.dtype)
        layer_outputs.append((hidden_state + mixture).astype(jnp.bfloat16))
        gate_grad = jnp.sum(grad_half[:, None, :] * returned_rows, axis=-1)
        row_grad = (
            (gate_probs[..., None] * grad_half[:, None, :])
            .astype(jnp.bfloat16)
            .reshape(-1, model_width)
        )
        send_grad = (
            jnp.zeros((EXPERTS * capacity, model_width), jnp.bfloat16).at[slot_index].set(row_grad)
        )
        grad_received = lax.all_to_all(
            spread_rows(send_grad, group, capacity, n_dev, per_dev, model_width),
            "expert",
            split_axis=0,
            concat_axis=0,
            tiled=True,
        ).reshape(n_dev, per_dev, capacity, model_width)
        hidden_grad = jnp.einsum(
            "skcd,kfd->skcf", grad_received, down_three, preferred_element_type=jnp.float32
        )
        down_part = jnp.einsum(
            "skcf,skcd->kfd", expert_hidden, grad_received, preferred_element_type=jnp.float32
        ).reshape(down_weight.shape)
        gate_pre_grad = gelu_pull(hidden_grad * up_pre)[0].astype(jnp.bfloat16)
        up_pre_grad = (hidden_grad * activated).astype(jnp.bfloat16)
        gate_part = jnp.einsum(
            "skcd,skcf->dkf", received, gate_pre_grad, preferred_element_type=jnp.float32
        ).reshape(gate_weight.shape)
        up_part = jnp.einsum(
            "skcd,skcf->dkf", received, up_pre_grad, preferred_element_type=jnp.float32
        ).reshape(up_weight.shape)
        input_part = jnp.einsum(
            "skcf,dkf->skcd", gate_pre_grad, gate_three, preferred_element_type=jnp.float32
        )
        input_part = input_part + jnp.einsum(
            "skcf,dkf->skcd", up_pre_grad, up_three, preferred_element_type=jnp.float32
        )
        input_back = lax.all_to_all(
            input_part.reshape(n_dev, per_dev * capacity, model_width).astype(jnp.bfloat16),
            "expert",
            split_axis=0,
            concat_axis=0,
            tiled=True,
        ).astype(jnp.float32)
        route_input = collect_rows(
            input_back, group, capacity, model_width, slot_index, half, top_count
        )
        logit_grad = gate_pull(gate_grad)[0].astype(jnp.bfloat16)
        router_part = jnp.dot(state_half.T, logit_grad, preferred_element_type=jnp.float32)
        ffn_half_grad = jnp.sum(route_input, axis=1) + jnp.dot(
            logit_grad, router_weight.T, preferred_element_type=jnp.float32
        )
        gate_sum = gate_sum + gate_part
        up_sum = up_sum + up_part
        down_sum = down_sum + down_part
        router_sum = router_sum + router_part
        normed_ffn_grad = lax.all_gather(ffn_half_grad, "tensor", axis=0, tiled=True)
        state_norm_grad, ffn_gain_grad = ffn_norm_pull(normed_ffn_grad)
        state_grad = out_grad + state_norm_grad
        ffn_gain_sum = ffn_gain_sum + ffn_gain_grad
        attention_grad = state_grad.astype(jnp.bfloat16)
        output_sum = output_sum + jnp.dot(
            attention_output.T, attention_grad, preferred_element_type=jnp.float32
        )
        attended_grad = (
            jnp.dot(attention_grad, output_weight.T, preferred_element_type=jnp.float32)
            .astype(jnp.bfloat16)
            .reshape(length, kv_local, query_group_count, head_dim)
        )
        query_grad, key_grad, value_grad = attention_backward(
            query_rows,
            key_row_states,
            value_rows,
            starts,
            row_ids,
            block_rows,
            score_scale,
            log_totals,
            attended_grad,
        )
        query_grad = (
            unrotate(query_grad, cosine_table, sine_table).astype(jnp.bfloat16).reshape(length, -1)
        )
        key_grad = (
            unrotate(key_grad, cosine_table, sine_table).astype(jnp.bfloat16).reshape(length, -1)
        )
        value_grad = value_grad.astype(jnp.bfloat16).reshape(length, -1)
        query_sum = query_sum + jnp.dot(
            normalized_input.T, query_grad, preferred_element_type=jnp.float32
        )
        key_sum = key_sum + jnp.dot(
            normalized_input.T, key_grad, preferred_element_type=jnp.float32
        )
        value_sum = value_sum + jnp.dot(
            normalized_input.T, value_grad, preferred_element_type=jnp.float32
        )
        normed_part = jnp.dot(query_grad, query_weight.T, preferred_element_type=jnp.float32)
        normed_part = normed_part + jnp.dot(
            key_grad, key_matrix.T, preferred_element_type=jnp.float32
        )
        normed_part = normed_part + jnp.dot(
            value_grad, value_matrix.T, preferred_element_type=jnp.float32
        )
        normed_grad = lax.psum(normed_part, "tensor")
        state_in_grad, attn_gain_grad = attn_norm_pull(normed_grad)
        attn_gain_sum = attn_gain_sum + attn_gain_grad
        input_grads.append(state_grad + state_in_grad)
    gate_sum, up_sum, down_sum, router_sum = lax.psum(
        (gate_sum, up_sum, down_sum, router_sum), "tensor"
    )
    reduced = lax.psum(
        (query_sum, key_sum, value_sum, output_sum, router_sum, attn_gain_sum, ffn_gain_sum),
        "expert",
    )
    return (
        jnp.stack(layer_outputs),
        jnp.stack(input_grads),
        reduced[5],
        reduced[6],
        reduced[0],
        reduced[1],
        reduced[2],
        reduced[3],
        reduced[4],
        gate_sum,
        up_sum,
        down_sum,
    )


MESH = pl.DeviceIdType.MESH
ANY = pl.ANY
VMEM_LIMIT = 60 * 2**20


def mm(a, b):
    return lax.dot_general(a, b, (((1,), (0,)), ((), ())), preferred_element_type=jnp.float32)


def mm_nt(a, b):
    return lax.dot_general(a, b, (((1,), (1,)), ((), ())), preferred_element_type=jnp.float32)


def mm_tn(a, b):
    return lax.dot_general(a, b, (((0,), (0,)), ((), ())), preferred_element_type=jnp.float32)


def remote(src, dst, send_sem, recv_sem, device):
    return pltpu.make_async_remote_copy(
        src_ref=src,
        dst_ref=dst,
        send_sem=send_sem,
        recv_sem=recv_sem,
        device_id=device,
        device_id_type=MESH,
    )


def tiles(count, body):
    def step(i, carry):
        body(i)
        return carry

    lax.fori_loop(0, count, step, 0)


def cols(i, width):
    return pl.ds(pl.multiple_of(i * width, width), width)


def moe_kernel(
    x_ref, g_ref, rt_ref, wg_hbm, wu_hbm, wd_hbm,
    mix_ref, dx_ref, rx_ref, rh_ref, rg_ref, ru_ref, re_ref,
    xz, gz, rz, xs, gs, xr, gr, eg, hid, gpg, upg, ys, ds_, yr, dr, zy, zd, yz, dz,
    onehot, prob, gg, wg, wu, wd,
    r_s, r_r, za_s, za_r, xa_s, xa_r, xb_s, xb_r, zb_s, zb_r, pair_s, pair_r, w_sem, own_sem,
):
    e = lax.axis_index("expert")
    c = lax.axis_index("tensor")
    z = e // 4
    o = lax.rem(e, 4) * 2 + c
    micro = x_ref.shape[0]
    half = x_ref.shape[1] // 2
    width = g_ref.shape[2]
    ff = wg.shape[1]
    col = 4 * half
    rows = xs.shape[1]
    blk = rows // 8
    cap = blk // 4
    me = 2 * e + c
    tw = 256
    nt = width // tw

    def z_dev(k):
        return (lax.rem(z + k, 4) * 4 + lax.rem(e, 4), c)

    def z_back(k):
        return (lax.rem(z + 4 - k, 4) * 4 + lax.rem(e, 4), c)

    def p_dev(d):
        t = lax.rem(o + d, 8)
        return (z * 4 + t // 2, lax.rem(t, 2))

    def p_back(d):
        t = lax.rem(o + 8 - d, 8)
        return (z * 4 + t // 2, lax.rem(t, 2))

    barrier = pltpu.get_barrier_semaphore()
    for k in range(1, 4):
        pl.semaphore_signal(barrier, inc=1, device_id=z_dev(k), device_id_type=MESH)
    for d in range(1, 8):
        pl.semaphore_signal(barrier, inc=1, device_id=p_dev(d), device_id_type=MESH)
    loads = [
        pltpu.make_async_copy(wg_hbm.at[:, cols(c, ff)], wg, w_sem.at[0]),
        pltpu.make_async_copy(wu_hbm.at[:, cols(c, ff)], wu, w_sem.at[1]),
        pltpu.make_async_copy(wd_hbm.at[cols(c, ff), :], wd, w_sem.at[2]),
    ]
    for cp in loads:
        cp.start()
    pl.semaphore_wait(barrier, 10)

    mine = pl.ds(pl.multiple_of(c * half, half), half)
    sent = []
    got_r = []
    for k in range(1, 4):
        cp = remote(rt_ref, rz.at[k], r_s.at[k], r_r.at[k], z_dev(k))
        cp.start()
        sent.append(cp)
        got_r.append(cp)
    got_z = {}

    def z_send(m):
        for a, (src, dst) in enumerate(((g_ref, gz), (x_ref, xz))):
            for k in range(1, 4):
                i = (m * 2 + a) * 4 + k
                cp = remote(
                    src.at[m, mine, :], dst.at[m, pl.ds(k * half, half), :],
                    za_s.at[i], za_r.at[i], z_dev(k),
                )
                cp.start()
                sent.append(cp)
                got_z[(m, a, k)] = cp

    z_send(0)
    for m in range(micro):
        xz[m, 0:half, :] = x_ref[m, mine, :]
        gz[m, 0:half, :] = g_ref[m, mine, :]
    rz[0] = rt_ref[...]
    for cp in got_r:
        cp.wait_recv()

    lanes = micro * half
    up = lax.broadcasted_iota(jnp.int32, (lanes, lanes), 0)
    across = lax.broadcasted_iota(jnp.int32, (lanes, lanes), 1)
    before = ((up < across) & (up // half == across // half)).astype(jnp.bfloat16)
    expert = 8 * z + lax.rem(o + lax.broadcasted_iota(jnp.int32, (8, lanes), 0), 8)
    place_row = lax.broadcasted_iota(jnp.int32, (lanes, col), 0)
    place_col = lax.broadcasted_iota(jnp.int32, (lanes, col), 1)
    slots = [jnp.zeros((8, col), jnp.float32) for _ in range(micro)]
    for k in range(4):
        named = rz[k]
        hit = named[0:1, :] == expert
        for j in range(1, rt_ref.shape[0] // 2):
            hit = hit | (named[j : j + 1, :] == expert)
        mask = jnp.where(hit, 1.0, 0.0)
        rank = mm(mask.astype(jnp.bfloat16), before)
        slot = (mask * (rank + (cap * k + 1))).astype(jnp.bfloat16)
        for m in range(micro):
            at = place_col - k * half
            put = (at >= 0) & (at < half) & (place_row == at + m * half)
            slots[m] = slots[m] + mm(slot, put.astype(jnp.bfloat16))
    number = lax.broadcasted_iota(jnp.int32, (blk, col), 0) + 1
    for m in range(micro):
        for d in range(8):
            row = slots[m][d : d + 1, :].astype(jnp.int32)
            onehot[m, d * blk : (d + 1) * blk, :] = jnp.where(row == number, 1.0, 0.0).astype(
                jnp.bfloat16
            )

    got_p = {}

    def pack(m):
        for a, (src, out, dst) in enumerate(((gz, gs, gr), (xz, xs, xr))):
            for k in range(1, 4):
                got_z[(m, a, k)].wait_recv()

            def body(i, src=src, out=out):
                at = cols(i, tw)
                out[m, :, at] = mm(onehot[m], src[m, :, at]).astype(jnp.bfloat16)

            tiles(nt, body)
            if a == 1:
                out[m, :, width:] = mm(onehot[m], src[m, :, width:]).astype(jnp.bfloat16)
            dst[m, 0:blk, :] = out[m, 0:blk, :]
            for d in range(1, 8):
                i = (m * 2 + a) * 8 + d
                at = pl.ds(d * blk, blk)
                cp = remote(
                    out.at[m, at, :], dst.at[m, at, :], xa_s.at[i], xa_r.at[i], p_dev(d)
                )
                cp.start()
                sent.append(cp)
                got_p[(m, a, d)] = cp

    for m in range(1, micro):
        z_send(m)
    for m in range(micro):
        pack(m)
    for cp in loads:
        cp.wait()

    got_b = {}
    lane = lax.broadcasted_iota(jnp.int32, (1, 128), 1)

    def to_pair(m):
        for i, (src, dst) in enumerate(
            ((xr, rx_ref), (hid, rh_ref), (gpg, rg_ref), (upg, ru_ref), (eg, re_ref))
        ):
            src_at = src.at[m, :, 0:width] if i == 0 else src.at[m]
            n = m * 8 + i
            cp = remote(src_at, dst.at[c, m], pair_s.at[n], pair_r.at[n], (e, 1 - c))
            cp.start()
            sent.append(cp)
            got_b[("pair", m, i)] = cp
            cp = pltpu.make_async_copy(src_at, dst.at[c, m], own_sem.at[n])
            cp.start()
            loads.append(cp)

    loads.clear()

    def run(m):
        for a in range(2):
            for d in range(1, 8):
                got_p[(m, a, d)].wait_recv()
        tail = xr[m, :, width:].astype(jnp.float32)
        pick = (lane == me) | (lane == me + 32)
        prob[...] = jnp.broadcast_to(
            jnp.sum(jnp.where(pick, tail, 0.0), axis=1, keepdims=True), (rows, 128)
        )
        gg[...] = jnp.zeros_like(gg)

        def weigh(i):
            at = cols(i, tw)
            eg[m, :, at] = (prob[:, 0:1] * gr[m, :, at].astype(jnp.float32)).astype(jnp.bfloat16)

        tiles(nt, weigh)

        def inner(i):
            at = cols(i, tw)
            xrow = xr[m, :, 0:width]
            gate = mm(xrow, wg[:, at])
            upv = mm(xrow, wu[:, at])
            back = mm_nt(eg[m], wd[at, :])
            cdf = 0.5 * (1.0 + lax.erf(gate * 0.7071067811865476))
            act = gate * cdf
            slope = cdf + gate * (jnp.exp(gate * gate * -0.5) * 0.3989422804014327)
            hid[m, :, at] = (act * upv).astype(jnp.bfloat16)
            gpg[m, :, at] = (back * upv * slope).astype(jnp.bfloat16)
            upg[m, :, at] = (back * act).astype(jnp.bfloat16)

        tiles(ff // tw, inner)

        def outer(i):
            at = cols(i, tw)
            low = mm(hid[m], wd[:, at]).astype(jnp.bfloat16).astype(jnp.float32)
            gg[...] += jnp.broadcast_to(
                jnp.sum(low * gr[m, :, at].astype(jnp.float32), axis=1, keepdims=True),
                (rows, 128),
            )
            ys[m, :, at] = (prob[:, 0:1] * low).astype(jnp.bfloat16)

        tiles(nt, outer)

        def inputs(i):
            at = cols(i, tw)
            ds_[m, :, at] = (mm_nt(gpg[m], wg[at, :]) + mm_nt(upg[m], wu[at, :])).astype(
                jnp.bfloat16
            )

        tiles(nt, inputs)
        total = gg[...]
        high = total.astype(jnp.bfloat16).astype(jnp.float32)
        ds_[m, :, width:] = jnp.where(
            lane == me, high, jnp.where(lane == me + 32, total - high, 0.0)
        ).astype(jnp.bfloat16)
        for a, (src, dst) in enumerate(((ds_, dr), (ys, yr))):
            dst[m, 0:blk, :] = src[m, 0:blk, :]
            for d in range(1, 8):
                i = (m * 2 + a) * 8 + d
                at = pl.ds(d * blk, blk)
                cp = remote(
                    src.at[m, at, :], dst.at[m, at, :], xb_s.at[i], xb_r.at[i], p_back(d)
                )
                cp.start()
                sent.append(cp)
                got_b[(m, a, d)] = cp
        to_pair(m)

    for m in range(micro):
        run(m)

    got_c = {}

    def gather(m, a):
        src, out, dst = ((dr, zd, dz), (yr, zy, yz))[a]
        for d in range(1, 8):
            got_b[(m, a, d)].wait_recv()

        def body(i):
            at = cols(i, tw)
            out[m, :, at] = mm_tn(onehot[m], src[m, :, at]).astype(jnp.bfloat16)

        tiles(nt, body)
        if a == 0:
            out[m, :, width:] = mm_tn(onehot[m], src[m, :, width:]).astype(jnp.bfloat16)
        for k in range(1, 4):
            i = (m * 2 + a) * 4 + k
            at = pl.ds(k * half, half)
            cp = remote(out.at[m, at, :], dst.at[m, at, :], zb_s.at[i], zb_r.at[i], z_back(k))
            cp.start()
            sent.append(cp)
            got_c[(m, a, k)] = cp

    def finish(m, a):
        own, other, out = ((zd, dz, dx_ref), (zy, yz, mix_ref))[a]
        for k in range(1, 4):
            got_c[(m, a, k)].wait_recv()
        total = own[m, 0:half, :].astype(jnp.float32)
        for k in range(1, 4):
            total = total + other[m, k * half : (k + 1) * half, :].astype(jnp.float32)
        out[m, mine, :] = total.astype(out.dtype)
        n = m * 8 + 5 + a
        cp = remote(
            out.at[m, mine, :], out.at[m, mine, :], pair_s.at[n], pair_r.at[n], (e, 1 - c)
        )
        cp.start()
        sent.append(cp)
        got_c[("pair", m, a)] = cp

    order = [(m, a) for a in range(2) for m in range(micro)]
    for i, (m, a) in enumerate(order):
        gather(m, a)
        if i >= 1:
            finish(*order[i - 1])
    finish(*order[-1])
    for m in range(micro):
        for i in range(5):
            got_b[("pair", m, i)].wait_recv()
        for a in range(2):
            got_c[("pair", m, a)].wait_recv()
    for cp in loads:
        cp.wait()
    for cp in sent:
        cp.wait_send()


def moe_call(xrows, grows, routes_t, gate_weight, up_weight, down_weight):
    micro, length, wide = xrows.shape
    width = grows.shape[2]
    half = length // 2
    ff = gate_weight.shape[1] // 2
    cap = 3 * half * 4 // (2 * EXPERTS)
    rows = 8 * 4 * cap
    bf = jnp.bfloat16
    f32 = jnp.float32
    vmem = pl.BlockSpec(memory_space=pltpu.VMEM)
    hbm = pl.BlockSpec(memory_space=ANY)

    def buf(*shape, dtype=bf):
        return pltpu.VMEM(shape, dtype)

    sem = pltpu.SemaphoreType.DMA
    col = 4 * half
    return pl.pallas_call(
        moe_kernel,
        out_shape=(
            jax.ShapeDtypeStruct((micro, length, width), bf),
            jax.ShapeDtypeStruct((micro, length, wide), f32),
            jax.ShapeDtypeStruct((2, micro, rows, width), bf),
            jax.ShapeDtypeStruct((2, micro, rows, ff), bf),
            jax.ShapeDtypeStruct((2, micro, rows, ff), bf),
            jax.ShapeDtypeStruct((2, micro, rows, ff), bf),
            jax.ShapeDtypeStruct((2, micro, rows, width), bf),
        ),
        in_specs=[vmem, vmem, vmem, hbm, hbm, hbm],
        out_specs=(vmem, vmem, hbm, hbm, hbm, hbm, hbm),
        scratch_shapes=[
            buf(micro, col, wide), buf(micro, col, width), buf(4, 8, micro * half, dtype=jnp.int32),
            buf(micro, rows, wide), buf(micro, rows, width), buf(micro, rows, wide), buf(micro, rows, width),
            buf(micro, rows, width), buf(micro, rows, ff), buf(micro, rows, ff), buf(micro, rows, ff),
            buf(micro, rows, width), buf(micro, rows, wide), buf(micro, rows, width), buf(micro, rows, wide),
            buf(micro, col, width), buf(micro, col, wide), buf(micro, col, width), buf(micro, col, wide),
            buf(micro, rows, col), buf(rows, 128, dtype=f32), buf(rows, 128, dtype=f32),
            buf(width, ff), buf(width, ff), buf(ff, width),
            sem((4,)), sem((4,)), sem((8 * micro,)), sem((8 * micro,)), sem((16 * micro,)), sem((16 * micro,)),
            sem((16 * micro,)), sem((16 * micro,)), sem((8 * micro,)), sem((8 * micro,)), sem((8 * micro,)),
            sem((8 * micro,)), sem((3,)), sem((8 * micro,)),
        ],
        compiler_params=pltpu.CompilerParams(
            collective_id=1, has_side_effects=True, vmem_limit_bytes=VMEM_LIMIT
        ),
        cost_estimate=pl.CostEstimate(
            flops=2 * 6 * micro * rows * width * ff, bytes_accessed=40 * 2**20, transcendentals=0
        ),
        name="moe_rows",
    )(xrows, grows, routes_t, gate_weight, up_weight, down_weight)


def grads_kernel(x_ref, h_ref, g_ref, u_ref, e_ref, gate_out, up_out, down_out):
    gate_out[...] = mm_tn(x_ref[0], g_ref[0])
    up_out[...] = mm_tn(x_ref[0], u_ref[0])
    down_out[...] = mm_tn(h_ref[0], e_ref[0])


def grads_call(rx, rh, rg, ru, re):
    _, micro, rows, width = rx.shape
    ff = rh.shape[3]
    n = micro * rows
    tw = 256
    per = ff // tw
    f32 = jnp.float32
    wide = pl.BlockSpec((1, n, width), lambda i: (i // per, 0, 0))
    thin = pl.BlockSpec((1, n, tw), lambda i: (i // per, 0, i % per))
    return pl.pallas_call(
        grads_kernel,
        grid=(2 * per,),
        in_specs=[wide, thin, thin, thin, wide],
        out_specs=(
            pl.BlockSpec((width, tw), lambda i: (0, i)),
            pl.BlockSpec((width, tw), lambda i: (0, i)),
            pl.BlockSpec((tw, width), lambda i: (i, 0)),
        ),
        out_shape=(
            jax.ShapeDtypeStruct((width, 2 * ff), f32),
            jax.ShapeDtypeStruct((width, 2 * ff), f32),
            jax.ShapeDtypeStruct((2 * ff, width), f32),
        ),
        compiler_params=pltpu.CompilerParams(vmem_limit_bytes=VMEM_LIMIT),
        cost_estimate=pl.CostEstimate(
            flops=2 * 6 * n * width * ff, bytes_accessed=45 * 2**20, transcendentals=0
        ),
        name="expert_grads",
    )(
        rx.reshape(2, n, width), rh.reshape(2, n, ff), rg.reshape(2, n, ff),
        ru.reshape(2, n, ff), re.reshape(2, n, width),
    )


def reduce_kernel(
    n_ref, d_ref, a_ref, g_ref, s_ref, oa, ob, os,
    fn, fd, fa, fg, fs, pa, pb, za, zb, zs,
    f_s, f_r, y_s, y_r, z_s, z_r, p_s, p_r,
):
    e = lax.axis_index("expert")
    c = lax.axis_index("tensor")
    z = e // 4
    q = lax.rem(e, 4)
    qx = lax.rem(q, 2)
    qy = q // 2
    rows = n_ref.shape[0]
    wn = n_ref.shape[1] // 2
    wd = d_ref.shape[1] // 2
    wa = a_ref.shape[1] // 2
    wg = g_ref.shape[1] // 2
    ws = s_ref.shape[1] // 4
    hs = s_ref.shape[0] // 4
    ha = wn // 4
    hb = wa // 4

    def flip(bit, by):
        return lax.rem(bit + by, 2)

    def p_dev(d):
        return (z * 4 + flip(qy, d // 2) * 2 + flip(qx, d % 2), c)

    def z_dev(k):
        return (lax.rem(z + k, 4) * 4 + q, c)

    def part(i, size):
        return pl.ds(pl.multiple_of(i * size, size), size)

    barrier = pltpu.get_barrier_semaphore()
    for k in range(1, 4):
        pl.semaphore_signal(barrier, inc=1, device_id=z_dev(k), device_id_type=MESH)
        pl.semaphore_signal(barrier, inc=1, device_id=p_dev(k), device_id_type=MESH)
    pl.semaphore_wait(barrier, 6)

    sent = []
    got = []
    for d in (3, 1, 2):
        r = flip(qx, d % 2)
        s = flip(qy, d // 2)
        at = pl.ds(d * rows, rows)
        for i, (src, dst) in enumerate(
            (
                (n_ref.at[:, part(r, wn)], fn.at[at, :]),
                (d_ref.at[:, part(s, wd)], fd.at[at, :]),
                (a_ref.at[:, part(r, wa)], fa.at[at, :]),
                (g_ref.at[:, part(s, wg)], fg.at[at, :]),
                (s_ref.at[part(s * 2 + r, hs), :], fs.at[d]),
            )
        ):
            cp = remote(src, dst, f_s.at[d * 5 + i], f_r.at[d * 5 + i], p_dev(d))
            cp.start()
            sent.append(cp)
            got.append(cp)
    fn[0:rows, :] = n_ref[:, part(qx, wn)]
    fd[0:rows, :] = d_ref[:, part(qy, wd)]
    fa[0:rows, :] = a_ref[:, part(qx, wa)]
    fg[0:rows, :] = g_ref[:, part(qy, wg)]
    total = s_ref[part(q, hs), :].astype(jnp.float32)
    for cp in got:
        cp.wait_recv()
    for d in range(1, 4):
        total = total + fs[d].astype(jnp.float32)
    fs[0] = total.astype(jnp.bfloat16)
    tw = 256

    def one(i):
        at = cols(i, tw)
        pa[:, at] = mm_tn(fn[...], fd[:, at]).astype(jnp.bfloat16)

    tiles(wd // tw, one)

    def two(i):
        at = cols(i, tw)
        pb[:, at] = mm_tn(fa[...], fg[:, at]).astype(jnp.bfloat16)

    tiles(wg // tw, two)

    got = []
    for k in (2, 1, 3):
        t = lax.rem(z + k, 4)
        for i, (src, dst) in enumerate(
            (
                (pa.at[part(t, ha), :], za.at[k]),
                (pb.at[part(t, hb), :], zb.at[k]),
                (fs.at[0, :, part(t, ws)], zs.at[k]),
            )
        ):
            cp = remote(src, dst, y_s.at[k * 3 + i], y_r.at[k * 3 + i], z_dev(k))
            cp.start()
            sent.append(cp)
            got.append(cp)
    for cp in got:
        cp.wait_recv()

    def spots(px, py, t):
        return (
            oa.at[part(px * 4 + t, ha), part(py, wd)],
            ob.at[part(px * 4 + t, hb), part(py, wg)],
            os.at[part(py * 2 + px, hs), part(t, ws)],
        )

    def store(ref, first, others):
        acc = first.astype(jnp.float32)
        for k in range(1, 4):
            acc = acc + others[k].astype(jnp.float32)
        ref[...] = acc.astype(jnp.bfloat16)

    mine = spots(qx, qy, z)
    store(mine[0], pa[part(z, ha), :], za)
    store(mine[1], pb[part(z, hb), :], zb)
    store(mine[2], fs[0, :, part(z, ws)], zs)

    got_z = {}
    got_p = {}

    def send(ref, i, k, d, j):
        n = ((k * 3) + i) * 4 + j
        cp = remote(ref, ref, p_s.at[n], p_r.at[n], p_dev(d))
        cp.start()
        sent.append(cp)
        got_p[(k, i, j)] = cp

    for k in (2, 1, 3):
        for i in range(3):
            cp = remote(mine[i], mine[i], z_s.at[k * 3 + i], z_r.at[k * 3 + i], z_dev(k))
            cp.start()
            sent.append(cp)
            got_z[(k, i)] = cp

    def own(k):
        here = spots(qx, qy, lax.rem(z + 4 - k, 4))
        if k:
            for i in range(3):
                got_z[(k, i)].wait_recv()
        for i in range(3):
            send(here[i], i, k, 1, 1)
            send(here[i], i, k, 2, 2)

    def forward(k):
        t = lax.rem(z + 4 - k, 4)
        beside = spots(flip(qx, 1), qy, t)
        above = spots(qx, flip(qy, 1), t)
        got_p[(k, 0, 1)].wait_recv()
        send(beside[0], 0, k, 2, 3)
        got_p[(k, 2, 1)].wait_recv()
        send(beside[2], 2, k, 2, 3)
        got_p[(k, 1, 2)].wait_recv()
        send(above[1], 1, k, 1, 3)

    turns = (0, 1, 3, 2)
    for n, k in enumerate(turns):
        own(k)
        if n:
            forward(turns[n - 1])
    forward(turns[-1])
    for k in range(4):
        for i in range(3):
            first = 2 if i in (0, 2) else 1
            got_p[(k, i, first)].wait_recv()
            got_p[(k, i, 3)].wait_recv()
    for cp in sent:
        cp.wait_send()


def reduce_call(normed, dqkv, attended, agrad, small):
    bf = jnp.bfloat16
    rows = normed.shape[0]
    wn, wd = normed.shape[1], dqkv.shape[1]
    wa, wg = attended.shape[1], agrad.shape[1]
    vmem = pl.BlockSpec(memory_space=pltpu.VMEM)

    def buf(*shape):
        return pltpu.VMEM(shape, bf)

    sem = pltpu.SemaphoreType.DMA
    hs, ws = small.shape[0] // 4, small.shape[1] // 4
    return pl.pallas_call(
        reduce_kernel,
        out_shape=(
            jax.ShapeDtypeStruct((wn, wd), bf),
            jax.ShapeDtypeStruct((wa, wg), bf),
            jax.ShapeDtypeStruct(small.shape, bf),
        ),
        in_specs=[vmem] * 5,
        out_specs=(vmem,) * 3,
        scratch_shapes=[
            buf(4 * rows, wn // 2), buf(4 * rows, wd // 2), buf(4 * rows, wa // 2), buf(4 * rows, wg // 2),
            buf(4, hs, small.shape[1]),
            buf(wn // 2, wd // 2), buf(wa // 2, wg // 2),
            buf(4, wn // 8, wd // 2), buf(4, wa // 8, wg // 2), buf(4, hs, ws),
            sem((20,)), sem((20,)), sem((12,)), sem((12,)), sem((12,)), sem((12,)), sem((48,)), sem((48,)),
        ],
        compiler_params=pltpu.CompilerParams(
            collective_id=2, has_side_effects=True, vmem_limit_bytes=VMEM_LIMIT
        ),
        cost_estimate=pl.CostEstimate(
            flops=2 * rows * 4 * (wn * wd + wa * wg) // 4, bytes_accessed=10 * 2**20, transcendentals=0
        ),
        name="reduce_grads",
    )(normed, dqkv, attended, agrad, small)


def suits(mesh):
    return mesh.shape["expert"] == 16 and mesh.shape["tensor"] == 2


def local_fast(
    tokens, cotangent, positions, routes, attention_gain, feedforward_gain, query_weight, key_matrix,
    value_matrix, output_weight, router_weight, gate_weight, up_weight, down_weight,
):
    micro_count, length, model_width = tokens.shape
    head_dim = HEAD_SIZE
    kv_local = key_matrix.shape[1] // head_dim
    query_group_count = query_weight.shape[1] // head_dim // kv_local
    half = length // 2
    c = lax.axis_index("tensor")
    f32 = jnp.float32
    bf = jnp.bfloat16
    score_scale = head_dim ** (-0.5)
    row_ids = jnp.arange(length, dtype=jnp.int32)
    expert_ids = jnp.arange(EXPERTS, dtype=jnp.int32)

    kept = []
    for m in range(micro_count):
        states = tokens[m].astype(f32)
        place = positions[m]
        tables = rope_tables(place, head_dim)
        normed_full, attn_pull = jax.vjp(rms_norm, states, attention_gain)
        normed = normed_full.astype(bf)
        query_pre = jnp.dot(normed, query_weight, preferred_element_type=f32).reshape(
            length, kv_local, query_group_count, head_dim
        )
        q = rotary_apply(query_pre, *tables).astype(bf)
        key_pre = jnp.dot(normed, key_matrix, preferred_element_type=f32).reshape(
            length, kv_local, head_dim
        )
        k = rotary_apply(key_pre, *tables).astype(bf)
        v = (
            jnp.dot(normed, value_matrix, preferred_element_type=f32)
            .astype(bf)
            .reshape(length, kv_local, head_dim)
        )
        att, log_totals = attention_forward(
            q, k, v, row_ids - place, row_ids, length, score_scale
        )
        att = att.reshape(length, -1)
        part = jnp.dot(att, output_weight, preferred_element_type=f32)
        kept.append((states, place, tables, normed, attn_pull, q, k, v, att, log_totals, part))
    parts = lax.psum(jnp.stack([t[-1] for t in kept]), "tensor")
    hidden = jnp.stack([t[0] for t in kept]) + parts
    ffn_full, ffn_pull = jax.vjp(rms_norm, hidden, feedforward_gain)
    normed_ffn = ffn_full.astype(bf)
    logits = jnp.dot(normed_ffn, router_weight, preferred_element_type=f32)
    mask = jnp.any(routes[..., None] == expert_ids, axis=2)
    top = jnp.max(jnp.where(mask, logits, -jnp.inf), axis=-1, keepdims=True)
    weight = jnp.where(mask, jnp.exp(logits - top), 0.0)
    probs = weight / jnp.sum(weight, axis=-1, keepdims=True)
    high = lax.reduce_precision(probs, 8, 7)
    xrows = jnp.concatenate(
        [
            normed_ffn, high.astype(bf), (probs - high).astype(bf),
            jnp.zeros((micro_count, length, 128 - 2 * EXPERTS), bf),
        ],
        axis=-1,
    )
    mine = lax.dynamic_slice_in_dim(routes, c * half, half, 1)
    routes_t = mine.transpose(2, 0, 1).reshape(routes.shape[2], micro_count * half)
    routes_t = jnp.concatenate([routes_t, jnp.full_like(routes_t, -1)], axis=0)
    mix, dx, rx, rh, rg, ru, re = moe_call(
        xrows, cotangent, routes_t, gate_weight, up_weight, down_weight
    )
    layer_out = (hidden + mix.astype(f32)).astype(bf)
    gate_sum, up_sum, down_sum = grads_call(rx, rh, rg, ru, re)
    gate_grad = dx[..., model_width : model_width + EXPERTS] + dx[
        ..., model_width + EXPERTS : model_width + 2 * EXPERTS
    ]
    logit_grad = probs * (gate_grad - jnp.sum(probs * gate_grad, axis=-1, keepdims=True))
    logit_grad = logit_grad.astype(bf)
    normed_ffn_grad = dx[..., :model_width] + jnp.dot(
        logit_grad, router_weight.T, preferred_element_type=f32
    )
    state_norm_grad, ffn_gain_grad = ffn_pull(normed_ffn_grad)
    state_grad = cotangent.astype(f32) + state_norm_grad
    agrad = state_grad.astype(bf)
    router_t = jnp.einsum(
        "mtx,mtd->xd", logit_grad, normed_ffn, preferred_element_type=f32
    )
    back = []
    for m in range(micro_count):
        states, place, tables, normed, attn_pull, q, k, v, att, log_totals, part = kept[m]
        attended_grad = (
            jnp.dot(agrad[m], output_weight.T, preferred_element_type=f32)
            .astype(bf)
            .reshape(length, kv_local, query_group_count, head_dim)
        )
        dq, dk, dv = attention_backward(
            q, k, v, row_ids - place, row_ids, length, score_scale, log_totals, attended_grad
        )
        dq = unrotate(dq, *tables).astype(bf).reshape(length, -1)
        dk = unrotate(dk, *tables).astype(bf).reshape(length, -1)
        dv = dv.astype(bf).reshape(length, -1)
        part = jnp.dot(dq, query_weight.T, preferred_element_type=f32)
        part = part + jnp.dot(dk, key_matrix.T, preferred_element_type=f32)
        part = part + jnp.dot(dv, value_matrix.T, preferred_element_type=f32)
        back.append((jnp.concatenate([dq, dk, dv], axis=1), part))
    normed_grad = lax.psum(jnp.stack([t[1] for t in back]), "tensor")
    input_grads = []
    attn_gain_grad = jnp.zeros_like(attention_gain)
    for m in range(micro_count):
        grad, gain = kept[m][4](normed_grad[m])
        input_grads.append(state_grad[m] + grad)
        attn_gain_grad = attn_gain_grad + gain
    small = jnp.concatenate(
        [
            router_t, ffn_gain_grad[None], attn_gain_grad[None],
            jnp.zeros((64 - EXPERTS - 2, model_width), f32),
        ],
        axis=0,
    ).astype(bf)
    rows = micro_count * length
    oa, ob, os = reduce_call(
        jnp.stack([t[3] for t in kept]).reshape(rows, -1),
        jnp.stack([t[0] for t in back]).reshape(rows, -1),
        jnp.stack([t[8] for t in kept]).reshape(rows, -1),
        agrad.reshape(rows, -1),
        small,
    )
    wq = query_weight.shape[1]
    os = os.astype(f32)
    return (
        layer_out,
        jnp.stack(input_grads),
        os[EXPERTS + 1],
        os[EXPERTS],
        oa[:, :wq].astype(f32),
        oa[:, wq : wq + head_dim].astype(f32),
        oa[:, wq + head_dim :].astype(f32),
        ob.astype(f32),
        os[:EXPERTS].T,
        gate_sum,
        up_sum,
        down_sum,
    )


def solution(mesh):
    in_specs = (
        P(None, "expert", None),
        P(None, "expert", None),
        P(None, "expert"),
        P(None, "expert", None),
        P(),
        P(),
        P(None, "tensor"),
        P(None, "tensor"),
        P(None, "tensor"),
        P("tensor", None),
        P(),
        P(None, "expert"),
        P(None, "expert"),
        P("expert", None),
    )
    out_specs = (
        P(None, "expert", None),
        P(None, "expert", None),
        P(),
        P(),
        P(None, "tensor"),
        P(None, "tensor"),
        P(None, "tensor"),
        P("tensor", None),
        P(),
        P(None, "expert"),
        P(None, "expert"),
        P("expert", None),
    )
    body = local_fast if suits(mesh) else local
    return jax.shard_map(body, mesh=mesh, in_specs=in_specs, out_specs=out_specs, check_vma=False)
```

```python
import functools

import jax
import jax.numpy as jnp
from jax import lax
from jax.experimental import pallas as pl
from jax.experimental.pallas import tpu as pltpu
from jax.sharding import PartitionSpec as P

HEAD_SIZE = 128
EXPERTS = 32


epsilon = 1e-05
theta_base = 1000000.0
masked_score = -1e30


def rms_norm(value_row_states, gain_vector):
    return (
        value_row_states
        * lax.rsqrt(jnp.mean(value_row_states * value_row_states, axis=-1, keepdims=True) + epsilon)
        * gain_vector
    )


def gelu_exact(value_row_states):
    return jax.nn.gelu(value_row_states, approximate=False)


def rope_tables(positions, head_dim):
    half_dim = head_dim // 2
    inverse = jnp.exp(
        -jnp.log(theta_base) * (2.0 * jnp.arange(half_dim, dtype=jnp.float32) / head_dim)
    )
    angles = positions.astype(jnp.float32)[:, None] * inverse[None, :]
    return (jnp.cos(angles), jnp.sin(angles))


def widen_table(table_part, value_row_states):
    return table_part.reshape(
        (table_part.shape[0],) + (1,) * (value_row_states.ndim - 2) + (table_part.shape[1],)
    )


def rotary_apply(value_row_states, cosine_table, sine_table):
    half_dim = value_row_states.shape[-1] // 2
    first_part = value_row_states[..., :half_dim]
    second = value_row_states[..., half_dim:]
    cos_wide = widen_table(cosine_table, value_row_states)
    sin_wide = widen_table(sine_table, value_row_states)
    return jnp.concatenate(
        [first_part * cos_wide - second * sin_wide, second * cos_wide + first_part * sin_wide],
        axis=-1,
    )


def unrotate(value_row_states, cosine_table, sine_table):
    half_dim = value_row_states.shape[-1] // 2
    first_part = value_row_states[..., :half_dim]
    second = value_row_states[..., half_dim:]
    cos_wide = widen_table(cosine_table, value_row_states)
    sin_wide = widen_table(sine_table, value_row_states)
    return jnp.concatenate(
        [first_part * cos_wide + second * sin_wide, second * cos_wide - first_part * sin_wide],
        axis=-1,
    )


def block_scores(query_block, key_row_states, starts, row_ids, offset, block_rows, score_scale):
    query_ids = offset + jnp.arange(block_rows, dtype=jnp.int32)
    allowed = (row_ids[None, :] <= query_ids[:, None]) & (row_ids[None, :] >= starts[:, None])
    scores = (
        jnp.einsum(
            "qcgd,kcd->cgqk", query_block, key_row_states, preferred_element_type=jnp.float32
        )
        * score_scale
    )
    return jnp.where(allowed, scores, masked_score)


def attention_forward(
    query_rows, key_row_states, value_rows, starts, row_ids, block_rows, score_scale
):

    def one_block(block_index):
        offset = block_index * block_rows
        scores = block_scores(
            query_rows, key_row_states, starts, row_ids, offset, block_rows, score_scale
        )
        row_peak = jnp.max(scores, axis=-1, keepdims=True)
        weights = jnp.exp(scores - row_peak)
        totals = jnp.sum(weights, axis=-1, keepdims=True)
        prob_low = (weights / totals).astype(jnp.bfloat16)
        attention_output = jnp.einsum(
            "cgqk,kcd->qcgd", prob_low, value_rows, preferred_element_type=jnp.float32
        )
        return (attention_output.astype(jnp.bfloat16), row_peak[..., 0] + jnp.log(totals[..., 0]))

    return lax.map(one_block, jnp.arange(query_rows.shape[0] // block_rows, dtype=jnp.int32))


def attention_backward(
    query_rows,
    key_row_states,
    value_rows,
    starts,
    row_ids,
    block_rows,
    score_scale,
    log_totals,
    attended_grad,
):

    def one_block(carried, block_index):
        key_grad, value_grad = carried
        offset = block_index * block_rows
        scores = block_scores(
            query_rows, key_row_states, starts, row_ids, offset, block_rows, score_scale
        )
        probs = jnp.exp(scores - log_totals[block_index][..., None])
        prob_low = probs.astype(jnp.bfloat16)
        prob_grad = jnp.einsum(
            "qcgd,kcd->cgqk", attended_grad, value_rows, preferred_element_type=jnp.float32
        )
        row_dot = jnp.sum(probs * prob_grad, axis=-1, keepdims=True)
        score_grad = (probs * (prob_grad - row_dot)).astype(jnp.bfloat16)
        query_grad = (
            jnp.einsum(
                "cgqk,kcd->qcgd", score_grad, key_row_states, preferred_element_type=jnp.float32
            )
            * score_scale
        )
        key_grad = (
            key_grad
            + jnp.einsum(
                "cgqk,qcgd->kcd", score_grad, query_rows, preferred_element_type=jnp.float32
            )
            * score_scale
        )
        value_grad = value_grad + jnp.einsum(
            "cgqk,qcgd->kcd", prob_low, attended_grad, preferred_element_type=jnp.float32
        )
        return ((key_grad, value_grad), query_grad)

    empty_grad = jnp.zeros(key_row_states.shape, jnp.float32)
    totals_out, query_grad = lax.scan(
        one_block,
        (empty_grad, empty_grad),
        jnp.arange(query_rows.shape[0] // block_rows, dtype=jnp.int32),
    )
    return (query_grad.reshape(query_rows.shape), totals_out[0], totals_out[1])


def spread_rows(base, group, capacity, n_dev, per_dev, width):
    widened = jnp.broadcast_to(
        base.reshape(EXPERTS, 1, capacity, width), (EXPERTS, group, capacity, width)
    )
    return widened.reshape(n_dev, per_dev * capacity, width)


def collect_rows(back, group, capacity, width, slot_index, rows, top_count):
    summed = jnp.sum(back.reshape(EXPERTS, group, capacity, width), axis=1).astype(jnp.bfloat16)
    return (
        summed.reshape(EXPERTS * capacity, width)[slot_index]
        .reshape(rows, top_count, width)
        .astype(jnp.float32)
    )


def local(
    tokens,
    cotangent,
    positions,
    routes,
    attention_gain,
    feedforward_gain,
    query_weight,
    key_matrix,
    value_matrix,
    output_weight,
    router_weight,
    gate_weight,
    up_weight,
    down_weight,
):
    micro_count, length, model_width = tokens.shape
    head_dim = HEAD_SIZE
    kv_local = key_matrix.shape[1] // head_dim
    query_group_count = query_weight.shape[1] // head_dim // kv_local
    top_count = routes.shape[2]
    n_dev = lax.axis_size("expert")
    n_tensor = lax.axis_size("tensor")
    half = length // n_tensor
    offset = lax.axis_index("tensor") * half
    per_dev = max(1, EXPERTS // n_dev)
    group = max(1, n_dev // EXPERTS)
    local_width = gate_weight.shape[1]
    ff_local = local_width // per_dev
    capacity = max(2, 3 * half * top_count // (2 * EXPERTS))
    block_rows = min(512, length)
    score_scale = head_dim ** (-0.5)
    expert_ids = jnp.arange(EXPERTS, dtype=jnp.int32)
    row_ids = jnp.arange(length, dtype=jnp.int32)
    gate_three = gate_weight.reshape(model_width, per_dev, ff_local)
    up_three = up_weight.reshape(model_width, per_dev, ff_local)
    down_three = down_weight.reshape(per_dev, ff_local, model_width)
    query_sum = jnp.zeros(query_weight.shape, jnp.float32)
    key_sum = jnp.zeros(key_matrix.shape, jnp.float32)
    value_sum = jnp.zeros(value_matrix.shape, jnp.float32)
    output_sum = jnp.zeros(output_weight.shape, jnp.float32)
    router_sum = jnp.zeros(router_weight.shape, jnp.float32)
    attn_gain_sum = jnp.zeros(attention_gain.shape, jnp.float32)
    ffn_gain_sum = jnp.zeros(feedforward_gain.shape, jnp.float32)
    gate_sum = jnp.zeros(gate_weight.shape, jnp.float32)
    up_sum = jnp.zeros(up_weight.shape, jnp.float32)
    down_sum = jnp.zeros(down_weight.shape, jnp.float32)
    layer_outputs = []
    input_grads = []
    for micro_index in range(micro_count):
        states = tokens[micro_index].astype(jnp.float32)
        out_grad = cotangent[micro_index].astype(jnp.float32)
        place = positions[micro_index]
        chosen = routes[micro_index]
        starts = row_ids - place
        cosine_table, sine_table = rope_tables(place, head_dim)
        normed_full, attn_norm_pull = jax.vjp(rms_norm, states, attention_gain)
        normalized_input = normed_full.astype(jnp.bfloat16)
        query_pre = jnp.dot(
            normalized_input, query_weight, preferred_element_type=jnp.float32
        ).reshape(length, kv_local, query_group_count, head_dim)
        query_rows = rotary_apply(query_pre, cosine_table, sine_table).astype(jnp.bfloat16)
        key_pre = jnp.dot(normalized_input, key_matrix, preferred_element_type=jnp.float32).reshape(
            length, kv_local, head_dim
        )
        key_row_states = rotary_apply(key_pre, cosine_table, sine_table).astype(jnp.bfloat16)
        value_rows = (
            jnp.dot(normalized_input, value_matrix, preferred_element_type=jnp.float32)
            .astype(jnp.bfloat16)
            .reshape(length, kv_local, head_dim)
        )
        attention_output, log_totals = attention_forward(
            query_rows, key_row_states, value_rows, starts, row_ids, block_rows, score_scale
        )
        attention_output = attention_output.reshape(length, kv_local * query_group_count * head_dim)
        attn_part = jnp.dot(attention_output, output_weight, preferred_element_type=jnp.float32)
        hidden_state = states + lax.psum(attn_part, "tensor")
        normed_ffn_full, ffn_norm_pull = jax.vjp(rms_norm, hidden_state, feedforward_gain)
        normed_ffn = normed_ffn_full.astype(jnp.bfloat16)
        state_half = lax.dynamic_slice_in_dim(normed_ffn, offset, half, 0)
        route_half = lax.dynamic_slice_in_dim(chosen, offset, half, 0)
        grad_half = lax.dynamic_slice_in_dim(out_grad, offset, half, 0)
        route_mask = (route_half[..., None] == expert_ids[None, None, :]).astype(jnp.float32)

        def gate_softmax(logits, route_mask=route_mask):
            return jax.nn.softmax(jnp.sum(logits[:, None, :] * route_mask, axis=-1), axis=-1)

        logits = jnp.dot(state_half, router_weight, preferred_element_type=jnp.float32)
        gate_probs, gate_pull = jax.vjp(gate_softmax, logits)
        flat_routes = route_half.reshape(-1)
        route_onehot = (flat_routes[:, None] == expert_ids[None, :]).astype(jnp.int32)
        ahead = jnp.tril(jnp.ones((half * top_count, half * top_count), jnp.float32), -1)
        ranks = jnp.sum(
            jnp.dot(ahead, route_onehot.astype(jnp.float32)).astype(jnp.int32) * route_onehot, axis=1
        )
        slot_index = flat_routes * capacity + ranks
        copies = jnp.repeat(state_half, top_count, axis=0)
        send_rows = (
            jnp.zeros((EXPERTS * capacity, model_width), jnp.bfloat16).at[slot_index].set(copies)
        )
        received = lax.all_to_all(
            spread_rows(send_rows, group, capacity, n_dev, per_dev, model_width),
            "expert",
            split_axis=0,
            concat_axis=0,
            tiled=True,
        ).reshape(n_dev, per_dev, capacity, model_width)
        gate_pre = jnp.einsum(
            "skcd,dkf->skcf", received, gate_three, preferred_element_type=jnp.float32
        )
        up_pre = jnp.einsum(
            "skcd,dkf->skcf", received, up_three, preferred_element_type=jnp.float32
        )
        activated, gelu_pull = jax.vjp(gelu_exact, gate_pre)
        expert_hidden = (activated * up_pre).astype(jnp.bfloat16)
        partial_out = jnp.einsum(
            "skcf,kfd->skcd", expert_hidden, down_three, preferred_element_type=jnp.float32
        )
        back_rows = lax.all_to_all(
            partial_out.reshape(n_dev, per_dev * capacity, model_width).astype(jnp.bfloat16),
            "expert",
            split_axis=0,
            concat_axis=0,
            tiled=True,
        ).astype(jnp.float32)
        returned_rows = collect_rows(
            back_rows, group, capacity, model_width, slot_index, half, top_count
        )
        mixture_half = jnp.sum(gate_probs[..., None] * returned_rows, axis=1)
        mixture = lax.all_gather(
            mixture_half.astype(jnp.bfloat16), "tensor", axis=0, tiled=True
        ).astype(mixture_half.dtype)
        layer_outputs.append((hidden_state + mixture).astype(jnp.bfloat16))
        gate_grad = jnp.sum(grad_half[:, None, :] * returned_rows, axis=-1)
        row_grad = (
            (gate_probs[..., None] * grad_half[:, None, :])
            .astype(jnp.bfloat16)
            .reshape(-1, model_width)
        )
        send_grad = (
            jnp.zeros((EXPERTS * capacity, model_width), jnp.bfloat16).at[slot_index].set(row_grad)
        )
        grad_received = lax.all_to_all(
            spread_rows(send_grad, group, capacity, n_dev, per_dev, model_width),
            "expert",
            split_axis=0,
            concat_axis=0,
            tiled=True,
        ).reshape(n_dev, per_dev, capacity, model_width)
        hidden_grad = jnp.einsum(
            "skcd,kfd->skcf", grad_received, down_three, preferred_element_type=jnp.float32
        )
        down_part = jnp.einsum(
            "skcf,skcd->kfd", expert_hidden, grad_received, preferred_element_type=jnp.float32
        ).reshape(down_weight.shape)
        gate_pre_grad = gelu_pull(hidden_grad * up_pre)[0].astype(jnp.bfloat16)
        up_pre_grad = (hidden_grad * activated).astype(jnp.bfloat16)
        gate_part = jnp.einsum(
            "skcd,skcf->dkf", received, gate_pre_grad, preferred_element_type=jnp.float32
        ).reshape(gate_weight.shape)
        up_part = jnp.einsum(
            "skcd,skcf->dkf", received, up_pre_grad, preferred_element_type=jnp.float32
        ).reshape(up_weight.shape)
        input_part = jnp.einsum(
            "skcf,dkf->skcd", gate_pre_grad, gate_three, preferred_element_type=jnp.float32
        )
        input_part = input_part + jnp.einsum(
            "skcf,dkf->skcd", up_pre_grad, up_three, preferred_element_type=jnp.float32
        )
        input_back = lax.all_to_all(
            input_part.reshape(n_dev, per_dev * capacity, model_width).astype(jnp.bfloat16),
            "expert",
            split_axis=0,
            concat_axis=0,
            tiled=True,
        ).astype(jnp.float32)
        route_input = collect_rows(
            input_back, group, capacity, model_width, slot_index, half, top_count
        )
        logit_grad = gate_pull(gate_grad)[0].astype(jnp.bfloat16)
        router_part = jnp.dot(state_half.T, logit_grad, preferred_element_type=jnp.float32)
        ffn_half_grad = jnp.sum(route_input, axis=1) + jnp.dot(
            logit_grad, router_weight.T, preferred_element_type=jnp.float32
        )
        gate_sum = gate_sum + gate_part
        up_sum = up_sum + up_part
        down_sum = down_sum + down_part
        router_sum = router_sum + router_part
        normed_ffn_grad = lax.all_gather(ffn_half_grad, "tensor", axis=0, tiled=True)
        state_norm_grad, ffn_gain_grad = ffn_norm_pull(normed_ffn_grad)
        state_grad = out_grad + state_norm_grad
        ffn_gain_sum = ffn_gain_sum + ffn_gain_grad
        attention_grad = state_grad.astype(jnp.bfloat16)
        output_sum = output_sum + jnp.dot(
            attention_output.T, attention_grad, preferred_element_type=jnp.float32
        )
        attended_grad = (
            jnp.dot(attention_grad, output_weight.T, preferred_element_type=jnp.float32)
            .astype(jnp.bfloat16)
            .reshape(length, kv_local, query_group_count, head_dim)
        )
        query_grad, key_grad, value_grad = attention_backward(
            query_rows,
            key_row_states,
            value_rows,
            starts,
            row_ids,
            block_rows,
            score_scale,
            log_totals,
            attended_grad,
        )
        query_grad = (
            unrotate(query_grad, cosine_table, sine_table).astype(jnp.bfloat16).reshape(length, -1)
        )
        key_grad = (
            unrotate(key_grad, cosine_table, sine_table).astype(jnp.bfloat16).reshape(length, -1)
        )
        value_grad = value_grad.astype(jnp.bfloat16).reshape(length, -1)
        query_sum = query_sum + jnp.dot(
            normalized_input.T, query_grad, preferred_element_type=jnp.float32
        )
        key_sum = key_sum + jnp.dot(
            normalized_input.T, key_grad, preferred_element_type=jnp.float32
        )
        value_sum = value_sum + jnp.dot(
            normalized_input.T, value_grad, preferred_element_type=jnp.float32
        )
        normed_part = jnp.dot(query_grad, query_weight.T, preferred_element_type=jnp.float32)
        normed_part = normed_part + jnp.dot(
            key_grad, key_matrix.T, preferred_element_type=jnp.float32
        )
        normed_part = normed_part + jnp.dot(
            value_grad, value_matrix.T, preferred_element_type=jnp.float32
        )
        normed_grad = lax.psum(normed_part, "tensor")
        state_in_grad, attn_gain_grad = attn_norm_pull(normed_grad)
        attn_gain_sum = attn_gain_sum + attn_gain_grad
        input_grads.append(state_grad + state_in_grad)
    gate_sum, up_sum, down_sum, router_sum = lax.psum(
        (gate_sum, up_sum, down_sum, router_sum), "tensor"
    )
    reduced = lax.psum(
        (query_sum, key_sum, value_sum, output_sum, router_sum, attn_gain_sum, ffn_gain_sum),
        "expert",
    )
    return (
        jnp.stack(layer_outputs),
        jnp.stack(input_grads),
        reduced[5],
        reduced[6],
        reduced[0],
        reduced[1],
        reduced[2],
        reduced[3],
        reduced[4],
        gate_sum,
        up_sum,
        down_sum,
    )


MESH = pl.DeviceIdType.MESH
ANY = pl.ANY
VMEM_LIMIT = 60 * 2**20


def mm(a, b):
    return lax.dot_general(a, b, (((1,), (0,)), ((), ())), preferred_element_type=jnp.float32)


def mm_nt(a, b):
    return lax.dot_general(a, b, (((1,), (1,)), ((), ())), preferred_element_type=jnp.float32)


def mm_tn(a, b):
    return lax.dot_general(a, b, (((0,), (0,)), ((), ())), preferred_element_type=jnp.float32)


def remote(src, dst, send_sem, recv_sem, device):
    return pltpu.make_async_remote_copy(
        src_ref=src,
        dst_ref=dst,
        send_sem=send_sem,
        recv_sem=recv_sem,
        device_id=device,
        device_id_type=MESH,
    )


def tiles(count, body):
    def step(i, carry):
        body(i)
        return carry

    lax.fori_loop(0, count, step, 0)


def cols(i, width):
    return pl.ds(pl.multiple_of(i * width, width), width)


def front_kernel(
    tok_ref, g_ref, pos_ref, routes_ref, rt_ref, gain_a, gain_f, wq_ref, wk_ref, wv_ref, wo_ref, router_ref,
    wg_hbm, wu_hbm, wd_hbm,
    lay_ref, dx_ref, nrm_ref, att_ref, q_ref, k_ref, v_ref, pr_ref, tab_ref, hs_ref, x_ref,
    rx_ref, rh_ref, rg_ref, ru_ref, re_ref,
    xz, gz, rz, xs, gs, xr, gr, eg, hid, gpg, upg, yr, dr, yz, dz, own_part, other_part,
    onehot, prob, gg, wg, wu, wd,
    r_s, r_r, za_s, za_r, xa_s, xa_r, xb_s, xb_r, zb_s, zb_r, pair_s, pair_r, part_s, part_r, w_sem, own_sem,
):
    ys, ds_, zy, zd = gs, xs, gz, xz
    e = lax.axis_index("expert")
    c = lax.axis_index("tensor")
    z = e // 4
    o = lax.rem(e, 4) * 2 + c
    micro, length, width = tok_ref.shape
    half = length // 2
    f32 = jnp.float32
    bf = jnp.bfloat16
    ff = wg.shape[1]
    col = 4 * half
    rows = xs.shape[1]
    blk = rows // 8
    cap = blk // 4
    me = 2 * e + c
    tw = 256
    nt = width // tw

    def z_dev(k):
        return (lax.rem(z + k, 4) * 4 + lax.rem(e, 4), c)

    def z_back(k):
        return (lax.rem(z + 4 - k, 4) * 4 + lax.rem(e, 4), c)

    def p_dev(d):
        t = lax.rem(o + d, 8)
        return (z * 4 + t // 2, lax.rem(t, 2))

    def p_back(d):
        t = lax.rem(o + 8 - d, 8)
        return (z * 4 + t // 2, lax.rem(t, 2))

    barrier = pltpu.get_barrier_semaphore()
    for k in range(1, 4):
        pl.semaphore_signal(barrier, inc=1, device_id=z_dev(k), device_id_type=MESH)
    for d in range(1, 8):
        pl.semaphore_signal(barrier, inc=1, device_id=p_dev(d), device_id_type=MESH)
    loads = [
        pltpu.make_async_copy(wg_hbm.at[:, cols(c, ff)], wg, w_sem.at[0]),
        pltpu.make_async_copy(wu_hbm.at[:, cols(c, ff)], wu, w_sem.at[1]),
        pltpu.make_async_copy(wd_hbm.at[cols(c, ff), :], wd, w_sem.at[2]),
    ]
    for cp in loads:
        cp.start()
    pl.semaphore_wait(barrier, 10)

    mine = pl.ds(pl.multiple_of(c * half, half), half)
    sent = []
    got_r = []
    for k in range(1, 4):
        cp = remote(rt_ref, rz.at[k], r_s.at[k], r_r.at[k], z_dev(k))
        cp.start()
        sent.append(cp)
        got_r.append(cp)
    got_z = {}

    def z_send(m, a):
        src, dst = ((g_ref, gz), (x_ref, xz))[a]
        for k in range(1, 4):
            i = (m * 2 + a) * 4 + k
            cp = remote(
                src.at[m, mine, :], dst.at[m, pl.ds(k * half, half), :],
                za_s.at[i], za_r.at[i], z_dev(k),
            )
            cp.start()
            sent.append(cp)
            got_z[(m, a, k)] = cp
        dst[m, 0:half, :] = src[m, mine, :]

    for m in range(micro):
        z_send(m, 0)
    rz[0] = rt_ref[...]

    head = HEAD_SIZE
    heads = wq_ref.shape[1] // head
    lane = lax.broadcasted_iota(jnp.int32, (1, 128), 1)
    row = lax.broadcasted_iota(jnp.int32, (length, length), 0)
    column = lax.broadcasted_iota(jnp.int32, (length, length), 1)
    turn = jnp.exp(
        (-2.0 / head * jnp.log(jnp.float32(theta_base))) * lax.rem(lane, head // 2).astype(f32)
    )
    allowed = []
    for m in range(micro):
        states = tok_ref[m].astype(f32)
        scale = lax.rsqrt(jnp.mean(states * states, axis=1, keepdims=True) + epsilon)
        nrm_ref[m] = (states * scale * gain_a[...]).astype(bf)
        place = pos_ref[m : m + 1, :].astype(f32)
        place = jnp.sum(jnp.where(row == column, place, 0.0), axis=1, keepdims=True)
        angle = place * turn
        tab_ref[m, 0] = jnp.cos(angle)
        tab_ref[m, 1] = jnp.where(lane < head // 2, -1.0, 1.0) * jnp.sin(angle)
        allowed.append((column <= row) & (column >= row - place.astype(jnp.int32)))

    def rope(u, m):
        return u * tab_ref[m, 0] + pltpu.roll(u, head // 2, 1) * tab_ref[m, 1]

    everything = nrm_ref[...].reshape(micro * length, width)

    def project(i):
        both = mm(everything, wq_ref[:, cols(i, tw)])
        for m in range(micro):
            for j in range(tw // head):
                at = pl.ds(pl.multiple_of((i * (tw // head) + j) * length, length), length)
                u = both[m * length : (m + 1) * length, j * head : (j + 1) * head]
                q_ref[m, at, :] = rope(u, m).astype(bf)

    tiles(wq_ref.shape[1] // tw, project)
    key_pre = mm(everything, wk_ref[...])
    value_pre = mm(everything, wv_ref[...])
    for m in range(micro):
        at = slice(m * length, (m + 1) * length)
        k_ref[m] = rope(key_pre[at], m).astype(bf)
        v_ref[m] = value_pre[at].astype(bf)
    for m in range(micro):
        score = mm_nt(q_ref[m], k_ref[m]).reshape(heads, length, length) * (head**-0.5)
        score = jnp.where(allowed[m][None], score, masked_score)
        weight = jnp.exp(score - jnp.max(score, axis=-1, keepdims=True))
        weight = weight / jnp.sum(weight, axis=-1, keepdims=True)
        weight = weight.reshape(heads * length, length)
        pr_ref[m] = weight
        out = mm(weight.astype(bf), v_ref[m]).astype(bf)
        for h in range(heads):
            att_ref[m, :, h * head : (h + 1) * head] = out[h * length : (h + 1) * length]
    att_all = att_ref[...].reshape(micro * length, heads * head)
    got_part = []
    for j in range(3):

        def outward(i, j=j):
            at = cols(i + j * (nt // 3), tw)
            own_part[:, at] = mm(att_all, wo_ref[:, at])

        tiles(nt // 3, outward)
        at = pl.ds(j * (width // 3), width // 3)
        cp = remote(
            own_part.at[:, at], other_part.at[:, at], part_s.at[j], part_r.at[j], (e, 1 - c)
        )
        cp.start()
        sent.append(cp)
        got_part.append(cp)

    for cp in got_r:
        cp.wait_recv()

    lanes = micro * half
    up = lax.broadcasted_iota(jnp.int32, (lanes, lanes), 0)
    across = lax.broadcasted_iota(jnp.int32, (lanes, lanes), 1)
    before = ((up < across) & (up // half == across // half)).astype(jnp.bfloat16)
    expert = 8 * z + lax.rem(o + lax.broadcasted_iota(jnp.int32, (8, lanes), 0), 8)
    place_row = lax.broadcasted_iota(jnp.int32, (lanes, col), 0)
    place_col = lax.broadcasted_iota(jnp.int32, (lanes, col), 1)
    slots = [jnp.zeros((8, col), jnp.float32) for _ in range(micro)]
    for k in range(4):
        named = rz[k]
        hit = named[0:1, :] == expert
        for j in range(1, rt_ref.shape[0] // 2):
            hit = hit | (named[j : j + 1, :] == expert)
        mask = jnp.where(hit, 1.0, 0.0)
        rank = mm(mask.astype(jnp.bfloat16), before)
        slot = (mask * (rank + (cap * k + 1))).astype(jnp.bfloat16)
        for m in range(micro):
            at = place_col - k * half
            put = (at >= 0) & (at < half) & (place_row == at + m * half)
            slots[m] = slots[m] + mm(slot, put.astype(jnp.bfloat16))
    number = lax.broadcasted_iota(jnp.int32, (blk, col), 0) + 1
    for m in range(micro):
        for d in range(8):
            row = slots[m][d : d + 1, :].astype(jnp.int32)
            onehot[m, d * blk : (d + 1) * blk, :] = jnp.where(row == number, 1.0, 0.0).astype(
                jnp.bfloat16
            )

    got_p = {}

    def pack(m, a):
        src, out, dst = ((gz, gs, gr), (xz, xs, xr))[a]
        for k in range(1, 4):
            got_z[(m, a, k)].wait_recv()

        def body(i):
            at = cols(i, tw)
            out[m, :, at] = mm(onehot[m], src[m, :, at]).astype(bf)

        tiles(nt, body)
        if a == 1:
            out[m, :, width:] = mm(onehot[m], src[m, :, width:]).astype(bf)
        dst[m, 0:blk, :] = out[m, 0:blk, :]
        for d in range(1, 8):
            i = (m * 2 + a) * 8 + d
            at = pl.ds(d * blk, blk)
            cp = remote(out.at[m, at, :], dst.at[m, at, :], xa_s.at[i], xa_r.at[i], p_dev(d))
            cp.start()
            sent_p.setdefault((m, a), []).append(cp)
            got_p[(m, a, d)] = cp

    sent_p = {}
    wide = lax.broadcasted_iota(jnp.int32, (EXPERTS, 128), 1)
    double = (lax.rem(wide, EXPERTS) == lax.broadcasted_iota(jnp.int32, (EXPERTS, 128), 0)) & (
        wide < 2 * EXPERTS
    )
    router = mm(router_ref[...], jnp.where(double, 1.0, 0.0).astype(bf)).astype(bf)
    for cp in got_part:
        cp.wait_recv()
    for m in range(micro):
        at = slice(m * length, (m + 1) * length)
        state = tok_ref[m].astype(f32) + (own_part[at, :] + other_part[at, :])
        hs_ref[m] = state
        scale = lax.rsqrt(jnp.mean(state * state, axis=1, keepdims=True) + epsilon)
        low = (state * scale * gain_f[...]).astype(bf)
        x_ref[m, :, 0:width] = low
        logits = mm(low, router)
        names = lax.rem(lane, EXPERTS)
        hit = routes_ref[m, :, 0:1] == names
        for j in range(1, routes_ref.shape[2]):
            hit = hit | (routes_ref[m, :, j : j + 1] == names)
        hit = hit & (lane < 2 * EXPERTS)
        best = jnp.max(jnp.where(hit, logits, masked_score), axis=1, keepdims=True)
        weight = jnp.where(hit, jnp.exp(logits - best), 0.0)
        first = jnp.sum(jnp.where(lane < EXPERTS, weight, 0.0), axis=1, keepdims=True)
        weight = weight / first
        top = weight.astype(bf).astype(f32)
        x_ref[m, :, width:] = jnp.where(lane < EXPERTS, top, weight - top).astype(bf)
        z_send(m, 1)
    for a in range(2):
        for m in range(micro):
            pack(m, a)
    for cp in loads:
        cp.wait()

    got_b = {}
    def to_pair(m):
        for i, (src, dst) in enumerate(
            ((xr, rx_ref), (hid, rh_ref), (gpg, rg_ref), (upg, ru_ref), (eg, re_ref))
        ):
            src_at = src.at[m, :, 0:width] if i == 0 else src.at[m]
            n = m * 8 + i
            cp = remote(src_at, dst.at[c, m], pair_s.at[n], pair_r.at[n], (e, 1 - c))
            cp.start()
            sent.append(cp)
            got_b[("pair", m, i)] = cp
            cp = pltpu.make_async_copy(src_at, dst.at[c, m], own_sem.at[n])
            cp.start()
            loads.append(cp)

    loads.clear()

    def run(m):
        for a in range(2):
            for d in range(1, 8):
                got_p[(m, a, d)].wait_recv()
            for cp in sent_p[(m, a)]:
                cp.wait_send()
        tail = xr[m, :, width:].astype(jnp.float32)
        pick = (lane == me) | (lane == me + 32)
        prob[...] = jnp.broadcast_to(
            jnp.sum(jnp.where(pick, tail, 0.0), axis=1, keepdims=True), (rows, 128)
        )
        gg[...] = jnp.zeros_like(gg)

        def weigh(i):
            at = cols(i, tw)
            eg[m, :, at] = (prob[:, 0:1] * gr[m, :, at].astype(jnp.float32)).astype(jnp.bfloat16)

        tiles(nt, weigh)

        def inner(i):
            at = cols(i, tw)
            xrow = xr[m, :, 0:width]
            gate = mm(xrow, wg[:, at])
            upv = mm(xrow, wu[:, at])
            back = mm_nt(eg[m], wd[at, :])
            cdf = 0.5 * (1.0 + lax.erf(gate * 0.7071067811865476))
            act = gate * cdf
            slope = cdf + gate * (jnp.exp(gate * gate * -0.5) * 0.3989422804014327)
            hid[m, :, at] = (act * upv).astype(jnp.bfloat16)
            gpg[m, :, at] = (back * upv * slope).astype(jnp.bfloat16)
            upg[m, :, at] = (back * act).astype(jnp.bfloat16)

        tiles(ff // tw, inner)

        def outer(i):
            at = cols(i, tw)
            low = mm(hid[m], wd[:, at]).astype(jnp.bfloat16).astype(jnp.float32)
            gg[...] += jnp.broadcast_to(
                jnp.sum(low * gr[m, :, at].astype(jnp.float32), axis=1, keepdims=True),
                (rows, 128),
            )
            ys[m, :, at] = (prob[:, 0:1] * low).astype(jnp.bfloat16)

        tiles(nt, outer)

        def inputs(i):
            at = cols(i, tw)
            ds_[m, :, at] = (mm_nt(gpg[m], wg[at, :]) + mm_nt(upg[m], wu[at, :])).astype(
                jnp.bfloat16
            )

        tiles(nt, inputs)
        total = gg[...]
        high = total.astype(jnp.bfloat16).astype(jnp.float32)
        ds_[m, :, width:] = jnp.where(
            lane == me, high, jnp.where(lane == me + 32, total - high, 0.0)
        ).astype(jnp.bfloat16)
        for a, (src, dst) in enumerate(((ds_, dr), (ys, yr))):
            dst[m, 0:blk, :] = src[m, 0:blk, :]
            for d in range(1, 8):
                i = (m * 2 + a) * 8 + d
                at = pl.ds(d * blk, blk)
                cp = remote(
                    src.at[m, at, :], dst.at[m, at, :], xb_s.at[i], xb_r.at[i], p_back(d)
                )
                cp.start()
                sent.append(cp)
                got_b[(m, a, d)] = cp
        to_pair(m)

    for m in range(micro):
        run(m)

    got_c = {}

    def gather(m, a):
        src, out, dst = ((dr, zd, dz), (yr, zy, yz))[a]
        for d in range(1, 8):
            got_b[(m, a, d)].wait_recv()

        def body(i):
            at = cols(i, tw)
            out[m, :, at] = mm_tn(onehot[m], src[m, :, at]).astype(jnp.bfloat16)

        tiles(nt, body)
        if a == 0:
            out[m, :, width:] = mm_tn(onehot[m], src[m, :, width:]).astype(jnp.bfloat16)
        for k in range(1, 4):
            i = (m * 2 + a) * 4 + k
            at = pl.ds(k * half, half)
            cp = remote(out.at[m, at, :], dst.at[m, at, :], zb_s.at[i], zb_r.at[i], z_back(k))
            cp.start()
            sent.append(cp)
            got_c[(m, a, k)] = cp

    def finish(m, a):
        own, other, out = ((zd, dz, dx_ref), (zy, yz, lay_ref))[a]
        for k in range(1, 4):
            got_c[(m, a, k)].wait_recv()
        total = own[m, 0:half, :].astype(jnp.float32)
        for k in range(1, 4):
            total = total + other[m, k * half : (k + 1) * half, :].astype(jnp.float32)
        if a == 1:
            total = hs_ref[m, mine, :] + total
        out[m, mine, :] = total.astype(out.dtype)
        n = m * 8 + 5 + a
        cp = remote(
            out.at[m, mine, :], out.at[m, mine, :], pair_s.at[n], pair_r.at[n], (e, 1 - c)
        )
        cp.start()
        sent.append(cp)
        got_c[("pair", m, a)] = cp

    order = [(m, a) for a in range(2) for m in range(micro)]
    for i, (m, a) in enumerate(order):
        gather(m, a)
        if i >= 1:
            finish(*order[i - 1])
    finish(*order[-1])
    for m in range(micro):
        for i in range(5):
            got_b[("pair", m, i)].wait_recv()
        for a in range(2):
            got_c[("pair", m, a)].wait_recv()
    for cp in loads:
        cp.wait()
    for cp in sent:
        cp.wait_send()


def front_call(
    tokens, cotangent, positions, routes, routes_t, gain_a, gain_f, wq, wk, wv, wo, router, gate_weight,
    up_weight, down_weight,
):
    micro, length, width = tokens.shape
    wide = width + 128
    half = length // 2
    ff = gate_weight.shape[1] // 2
    cap = 3 * half * routes.shape[2] // (2 * EXPERTS)
    rows = 8 * 4 * cap
    bf = jnp.bfloat16
    f32 = jnp.float32
    vmem = pl.BlockSpec(memory_space=pltpu.VMEM)
    hbm = pl.BlockSpec(memory_space=ANY)
    heads = wq.shape[1] // HEAD_SIZE

    def buf(*shape, dtype=bf):
        return pltpu.VMEM(shape, dtype)

    def out(*shape, dtype=bf):
        return jax.ShapeDtypeStruct(shape, dtype)

    sem = pltpu.SemaphoreType.DMA
    col = 4 * half
    return pl.pallas_call(
        front_kernel,
        out_shape=(
            out(micro, length, width),
            out(micro, length, wide, dtype=f32),
            out(micro, length, width),
            out(micro, length, wq.shape[1]),
            out(micro, heads * length, HEAD_SIZE),
            out(micro, length, HEAD_SIZE),
            out(micro, length, HEAD_SIZE),
            out(micro, heads * length, length, dtype=f32),
            out(micro, 2, length, HEAD_SIZE, dtype=f32),
            out(micro, length, width, dtype=f32),
            out(micro, length, wide),
            out(2, micro, rows, width),
            out(2, micro, rows, ff),
            out(2, micro, rows, ff),
            out(2, micro, rows, ff),
            out(2, micro, rows, width),
        ),
        in_specs=[vmem] * 12 + [hbm] * 3,
        out_specs=(vmem,) * 11 + (hbm,) * 5,
        scratch_shapes=[
            buf(micro, col, wide), buf(micro, col, width), buf(4, 8, micro * half, dtype=jnp.int32),
            buf(micro, rows, wide), buf(micro, rows, width), buf(micro, rows, wide), buf(micro, rows, width),
            buf(micro, rows, width), buf(micro, rows, ff), buf(micro, rows, ff), buf(micro, rows, ff),
            buf(micro, rows, width), buf(micro, rows, wide), buf(micro, col, width), buf(micro, col, wide),
            buf(micro * length, width, dtype=f32), buf(micro * length, width, dtype=f32),
            buf(micro, rows, col), buf(rows, 128, dtype=f32), buf(rows, 128, dtype=f32),
            buf(width, ff), buf(width, ff), buf(ff, width),
            sem((4,)), sem((4,)), sem((8 * micro,)), sem((8 * micro,)), sem((16 * micro,)), sem((16 * micro,)),
            sem((16 * micro,)), sem((16 * micro,)), sem((8 * micro,)), sem((8 * micro,)), sem((8 * micro,)),
            sem((8 * micro,)), sem((3,)), sem((3,)), sem((3,)), sem((8 * micro,)),
        ],
        compiler_params=pltpu.CompilerParams(
            collective_id=1, has_side_effects=True, vmem_limit_bytes=VMEM_LIMIT
        ),
        cost_estimate=pl.CostEstimate(
            flops=2 * 6 * micro * rows * width * ff, bytes_accessed=40 * 2**20, transcendentals=0
        ),
        name="front",
    )(
        tokens, cotangent, positions, routes, routes_t, gain_a, gain_f, wq, wk, wv, wo, router, gate_weight,
        up_weight, down_weight,
    )


def grads_kernel(x_ref, h_ref, g_ref, u_ref, e_ref, gate_out, up_out, down_out):
    gate_out[...] = mm_tn(x_ref[0], g_ref[0])
    up_out[...] = mm_tn(x_ref[0], u_ref[0])
    down_out[...] = mm_tn(h_ref[0], e_ref[0])


def grads_call(rx, rh, rg, ru, re):
    _, micro, rows, width = rx.shape
    ff = rh.shape[3]
    n = micro * rows
    tw = 256
    per = ff // tw
    f32 = jnp.float32
    wide = pl.BlockSpec((1, n, width), lambda i: (i // per, 0, 0))
    thin = pl.BlockSpec((1, n, tw), lambda i: (i // per, 0, i % per))
    return pl.pallas_call(
        grads_kernel,
        grid=(2 * per,),
        in_specs=[wide, thin, thin, thin, wide],
        out_specs=(
            pl.BlockSpec((width, tw), lambda i: (0, i)),
            pl.BlockSpec((width, tw), lambda i: (0, i)),
            pl.BlockSpec((tw, width), lambda i: (i, 0)),
        ),
        out_shape=(
            jax.ShapeDtypeStruct((width, 2 * ff), f32),
            jax.ShapeDtypeStruct((width, 2 * ff), f32),
            jax.ShapeDtypeStruct((2 * ff, width), f32),
        ),
        compiler_params=pltpu.CompilerParams(vmem_limit_bytes=VMEM_LIMIT),
        cost_estimate=pl.CostEstimate(
            flops=2 * 6 * n * width * ff, bytes_accessed=45 * 2**20, transcendentals=0
        ),
        name="expert_grads",
    )(
        rx.reshape(2, n, width), rh.reshape(2, n, ff), rg.reshape(2, n, ff),
        ru.reshape(2, n, ff), re.reshape(2, n, width),
    )


def back_kernel(
    tok_ref, g_ref, gain_a, gain_f, wq_ref, wk_ref, wv_ref, wo_ref, router_ref,
    dx_ref, nrm_ref, att_ref, q_ref, k_ref, v_ref, pr_ref, tab_ref, hs_ref, x_ref,
    tg_ref, oa, ob, os,
    d_ref, a_ref, s_ref, sg, ag, own_part, other_part,
    fn, fd, fa, fg, fs, pa, pb, za, zb, zs,
    f_s, f_r, y_s, y_r, z_s, z_r, p_s, p_r, part_s, part_r,
):
    micro, length, width = tok_ref.shape
    f32 = jnp.float32
    bf = jnp.bfloat16
    head = HEAD_SIZE
    heads = wq_ref.shape[1] // head
    wq = wq_ref.shape[1]
    tw = 256
    nt = width // tw
    n_ref = nrm_ref
    e = lax.axis_index("expert")
    c = lax.axis_index("tensor")
    z = e // 4
    q = lax.rem(e, 4)
    qx = lax.rem(q, 2)
    qy = q // 2
    rows = micro * length
    wn = n_ref.shape[1] // 2
    wd = d_ref.shape[1] // 2
    wa = att_ref.shape[1] // 2
    wg = a_ref.shape[1] // 2
    ws = s_ref.shape[1] // 4
    hs = s_ref.shape[0] // 4
    ha = wn // 4
    hb = wa // 4

    def flip(bit, by):
        return lax.rem(bit + by, 2)

    def p_dev(d):
        return (z * 4 + flip(qy, d // 2) * 2 + flip(qx, d % 2), c)

    def z_dev(k):
        return (lax.rem(z + k, 4) * 4 + q, c)

    def part(i, size):
        return pl.ds(pl.multiple_of(i * size, size), size)

    barrier = pltpu.get_barrier_semaphore()
    for k in range(1, 4):
        pl.semaphore_signal(barrier, inc=1, device_id=z_dev(k), device_id_type=MESH)
        pl.semaphore_signal(barrier, inc=1, device_id=p_dev(k), device_id_type=MESH)
    pl.semaphore_signal(barrier, inc=1, device_id=(e, 1 - c), device_id_type=MESH)
    pl.semaphore_wait(barrier, 7)

    sent = []
    got = []

    def factor(i, src, dst):
        for d in (3, 1, 2):
            r = flip(qx, d % 2)
            s = flip(qy, d // 2)
            at = pl.ds(d * rows, rows)
            if i == 0 or i == 2:
                view = src.at[:, part(r, src.shape[1] // 2)]
            elif i == 1 or i == 3:
                view = src.at[:, part(s, src.shape[1] // 2)]
            else:
                view = src.at[part(s * 2 + r, hs), :]
            to = fs.at[d] if i == 4 else dst.at[at, :]
            cp = remote(view, to, f_s.at[d * 5 + i], f_r.at[d * 5 + i], p_dev(d))
            cp.start()
            sent.append(cp)
            got.append(cp)

    factor(0, n_ref, fn)
    factor(2, att_ref, fa)

    lane = lax.broadcasted_iota(jnp.int32, (1, 128), 1)
    gain_row = jnp.zeros((1, width), f32)
    s_ref[...] = jnp.zeros_like(s_ref)
    router_row = jnp.zeros((128, width), f32)
    for m in range(micro):
        here = slice(m * length, (m + 1) * length)
        tail = dx_ref[m, :, width:]
        grad = tail + pltpu.roll(tail, 128 - EXPERTS, 1)
        tail = x_ref[m, :, width:].astype(f32)
        prob = jnp.where(lane < EXPERTS, tail + pltpu.roll(tail, 128 - EXPERTS, 1), 0.0)
        shared = jnp.sum(prob * grad, axis=1, keepdims=True)
        low = (prob * (grad - shared)).astype(bf)
        router_row = router_row + mm_tn(low, x_ref[m, :, 0:width])
        full = dx_ref[m, :, 0:width] + mm_nt(low[:, 0:EXPERTS], router_ref[...])
        state = hs_ref[m]
        scale = lax.rsqrt(jnp.mean(state * state, axis=1, keepdims=True) + epsilon)
        u = full * gain_f[...]
        common = jnp.mean(u * state, axis=1, keepdims=True) * (scale * scale * scale)
        total = g_ref[m].astype(f32) + (scale * u - state * common)
        sg[m] = total
        a_ref[here, :] = total.astype(bf)
        gain_row = gain_row + jnp.sum(full * state * scale, axis=0, keepdims=True)
    s_ref[0:EXPERTS, :] = router_row[0:EXPERTS].astype(bf)
    factor(3, a_ref, fg)

    def inward(i):
        at = cols(i, tw)
        both = mm_nt(a_ref[...], wo_ref[at, :]).astype(bf)
        for m in range(micro):
            for j in range(tw // head):
                to = pl.ds(pl.multiple_of((i * (tw // head) + j) * length, length), length)
                ag[m, to, :] = both[m * length : (m + 1) * length, j * head : (j + 1) * head]

    tiles(wq // tw, inward)

    def unrope(u, m):
        return u * tab_ref[m, 0] - pltpu.roll(u, head // 2, 1) * tab_ref[m, 1]

    for m in range(micro):
        here = slice(m * length, (m + 1) * length)
        prob = pr_ref[m]
        back = mm_nt(ag[m], v_ref[m])
        shared = jnp.sum(prob * back, axis=1, keepdims=True)
        low = (prob * (back - shared)).astype(bf)
        dq = mm(low, k_ref[m]) * (head**-0.5)
        for h in range(heads):
            u = unrope(dq[h * length : (h + 1) * length], m)
            d_ref[here, h * head : (h + 1) * head] = u.astype(bf)
        dk = mm_tn(low, q_ref[m]) * (head**-0.5)
        d_ref[here, wq : wq + head] = unrope(dk, m).astype(bf)
        d_ref[here, wq + head : wq + 2 * head] = mm_tn(prob.astype(bf), ag[m]).astype(bf)
    factor(1, d_ref, fd)
    got_part = []
    for j in range(3):

        def outward(i, j=j):
            at = cols(i + j * (nt // 3), tw)
            own_part[:, at] = (
                mm_nt(d_ref[:, 0:wq], wq_ref[at, :])
                + mm_nt(d_ref[:, wq : wq + head], wk_ref[at, :])
                + mm_nt(d_ref[:, wq + head :], wv_ref[at, :])
            )

        tiles(nt // 3, outward)
        at = pl.ds(j * (width // 3), width // 3)
        cp = remote(
            own_part.at[:, at], other_part.at[:, at], part_s.at[j], part_r.at[j], (e, 1 - c)
        )
        cp.start()
        sent.append(cp)
        got_part.append(cp)
    fn[0:rows, :] = n_ref[:, part(qx, wn)]
    fd[0:rows, :] = d_ref[:, part(qy, wd)]
    fa[0:rows, :] = att_ref[:, part(qx, wa)]
    fg[0:rows, :] = a_ref[:, part(qy, wg)]
    for cp in got_part:
        cp.wait_recv()
    last_row = jnp.zeros((1, width), f32)
    for m in range(micro):
        here = slice(m * length, (m + 1) * length)
        full = own_part[here, :] + other_part[here, :]
        state = tok_ref[m].astype(f32)
        scale = lax.rsqrt(jnp.mean(state * state, axis=1, keepdims=True) + epsilon)
        u = full * gain_a[...]
        common = jnp.mean(u * state, axis=1, keepdims=True) * (scale * scale * scale)
        tg_ref[m] = sg[m] + (scale * u - state * common)
        last_row = last_row + jnp.sum(full * state * scale, axis=0, keepdims=True)
    index = lax.broadcasted_iota(jnp.int32, (hs, 1), 0)
    s_ref[2 * hs : 3 * hs, :] = jnp.where(
        index == 0, gain_row, jnp.where(index == 1, last_row, 0.0)
    ).astype(bf)
    factor(4, s_ref, fs)
    total = s_ref[part(q, hs), :].astype(jnp.float32)
    for cp in got:
        cp.wait_recv()
    for d in range(1, 4):
        total = total + fs[d].astype(jnp.float32)
    fs[0] = total.astype(jnp.bfloat16)

    def one(i):
        at = cols(i, tw)
        pa[:, at] = mm_tn(fn[...], fd[:, at]).astype(jnp.bfloat16)

    tiles(wd // tw, one)

    def two(i):
        at = cols(i, tw)
        pb[:, at] = mm_tn(fa[...], fg[:, at]).astype(jnp.bfloat16)

    tiles(wg // tw, two)

    got = []
    for k in (2, 1, 3):
        t = lax.rem(z + k, 4)
        for i, (src, dst) in enumerate(
            (
                (pa.at[part(t, ha), :], za.at[k]),
                (pb.at[part(t, hb), :], zb.at[k]),
                (fs.at[0, :, part(t, ws)], zs.at[k]),
            )
        ):
            cp = remote(src, dst, y_s.at[k * 3 + i], y_r.at[k * 3 + i], z_dev(k))
            cp.start()
            sent.append(cp)
            got.append(cp)
    for cp in got:
        cp.wait_recv()

    def spots(px, py, t):
        return (
            oa.at[part(px * 4 + t, ha), part(py, wd)],
            ob.at[part(px * 4 + t, hb), part(py, wg)],
            os.at[part(py * 2 + px, hs), part(t, ws)],
        )

    def store(ref, first, others):
        acc = first.astype(jnp.float32)
        for k in range(1, 4):
            acc = acc + others[k].astype(jnp.float32)
        ref[...] = acc.astype(jnp.bfloat16)

    mine = spots(qx, qy, z)
    store(mine[0], pa[part(z, ha), :], za)
    store(mine[1], pb[part(z, hb), :], zb)
    store(mine[2], fs[0, :, part(z, ws)], zs)

    got_z = {}
    got_p = {}

    def send(ref, i, k, d, j):
        n = ((k * 3) + i) * 4 + j
        cp = remote(ref, ref, p_s.at[n], p_r.at[n], p_dev(d))
        cp.start()
        sent.append(cp)
        got_p[(k, i, j)] = cp

    for k in (2, 1, 3):
        for i in range(3):
            cp = remote(mine[i], mine[i], z_s.at[k * 3 + i], z_r.at[k * 3 + i], z_dev(k))
            cp.start()
            sent.append(cp)
            got_z[(k, i)] = cp

    def own(k):
        here = spots(qx, qy, lax.rem(z + 4 - k, 4))
        if k:
            for i in range(3):
                got_z[(k, i)].wait_recv()
        for i in range(3):
            send(here[i], i, k, 1, 1)
            send(here[i], i, k, 2, 2)

    def forward(k):
        t = lax.rem(z + 4 - k, 4)
        beside = spots(flip(qx, 1), qy, t)
        above = spots(qx, flip(qy, 1), t)
        got_p[(k, 0, 1)].wait_recv()
        send(beside[0], 0, k, 2, 3)
        got_p[(k, 2, 1)].wait_recv()
        send(beside[2], 2, k, 2, 3)
        got_p[(k, 1, 2)].wait_recv()
        send(above[1], 1, k, 1, 3)

    turns = (0, 1, 3, 2)
    for n, k in enumerate(turns):
        own(k)
        if n:
            forward(turns[n - 1])
    forward(turns[-1])
    for k in range(4):
        for i in range(3):
            first = 2 if i in (0, 2) else 1
            got_p[(k, i, first)].wait_recv()
            got_p[(k, i, 3)].wait_recv()
    for cp in sent:
        cp.wait_send()


def back_call(
    tokens, cotangent, gain_a, gain_f, wq, wk, wv, wo, router, dx, nrm, att, q, k, v, pr, tab, hs, xrows
):
    bf = jnp.bfloat16
    f32 = jnp.float32
    micro, length, width = tokens.shape
    rows = micro * length
    wd = wq.shape[1] + wk.shape[1] + wv.shape[1]
    wa = wq.shape[1]
    heads = wa // HEAD_SIZE
    vmem = pl.BlockSpec(memory_space=pltpu.VMEM)

    def buf(*shape, dtype=bf):
        return pltpu.VMEM(shape, dtype)

    sem = pltpu.SemaphoreType.DMA
    small = (64, width)
    hsm, wsm = 16, width // 4
    return pl.pallas_call(
        back_kernel,
        out_shape=(
            jax.ShapeDtypeStruct((micro, length, width), f32),
            jax.ShapeDtypeStruct((width, wd), bf),
            jax.ShapeDtypeStruct((wa, width), bf),
            jax.ShapeDtypeStruct(small, bf),
        ),
        in_specs=[vmem] * 19,
        out_specs=(vmem,) * 4,
        scratch_shapes=[
            buf(rows, wd), buf(rows, width), buf(*small), buf(micro, length, width, dtype=f32),
            buf(micro, heads * length, HEAD_SIZE), buf(rows, width, dtype=f32), buf(rows, width, dtype=f32),
            buf(4 * rows, width // 2), buf(4 * rows, wd // 2), buf(4 * rows, wa // 2), buf(4 * rows, width // 2),
            buf(4, hsm, width),
            buf(width // 2, wd // 2), buf(wa // 2, width // 2),
            buf(4, width // 8, wd // 2), buf(4, wa // 8, width // 2), buf(4, hsm, wsm),
            sem((20,)), sem((20,)), sem((12,)), sem((12,)), sem((12,)), sem((12,)), sem((48,)), sem((48,)),
            sem((3,)), sem((3,)),
        ],
        compiler_params=pltpu.CompilerParams(
            collective_id=2, has_side_effects=True, vmem_limit_bytes=VMEM_LIMIT
        ),
        cost_estimate=pl.CostEstimate(
            flops=2 * rows * 4 * (width * wd + wa * width) // 4, bytes_accessed=20 * 2**20, transcendentals=0
        ),
        name="back",
    )(
        tokens, cotangent, gain_a, gain_f, wq, wk, wv, wo, router,
        dx, nrm.reshape(rows, width), att.reshape(rows, wa), q, k, v, pr, tab, hs, xrows,
    )


def suits(mesh):
    return mesh.shape["expert"] == 16 and mesh.shape["tensor"] == 2


def local_fast(
    tokens, cotangent, positions, routes, attention_gain, feedforward_gain, query_weight, key_matrix,
    value_matrix, output_weight, router_weight, gate_weight, up_weight, down_weight,
):
    micro_count, length, model_width = tokens.shape
    half = length // 2
    c = lax.axis_index("tensor")
    f32 = jnp.float32
    mine = lax.dynamic_slice_in_dim(routes, c * half, half, 1)
    routes_t = mine.transpose(2, 0, 1).reshape(routes.shape[2], micro_count * half)
    routes_t = jnp.concatenate([routes_t, jnp.full_like(routes_t, -1)], axis=0)
    gain_a = attention_gain[None]
    gain_f = feedforward_gain[None]
    layer_out, dx, nrm, att, q, k, v, pr, tab, hs, xrows, rx, rh, rg, ru, re = front_call(
        tokens, cotangent, positions, routes, routes_t, gain_a, gain_f, query_weight, key_matrix,
        value_matrix, output_weight, router_weight, gate_weight, up_weight, down_weight,
    )
    tokens_grad, oa, ob, os = back_call(
        tokens, cotangent, gain_a, gain_f, query_weight, key_matrix, value_matrix, output_weight,
        router_weight, dx, nrm, att, q, k, v, pr, tab, hs, xrows,
    )
    gate_sum, up_sum, down_sum = grads_call(rx, rh, rg, ru, re)
    wq = query_weight.shape[1]
    wk = wq + key_matrix.shape[1]
    os = os.astype(f32)
    return (
        layer_out,
        tokens_grad,
        os[EXPERTS + 1],
        os[EXPERTS],
        oa[:, :wq].astype(f32),
        oa[:, wq:wk].astype(f32),
        oa[:, wk:].astype(f32),
        ob.astype(f32),
        os[:EXPERTS].T,
        gate_sum,
        up_sum,
        down_sum,
    )


def solution(mesh):
    in_specs = (
        P(None, "expert", None),
        P(None, "expert", None),
        P(None, "expert"),
        P(None, "expert", None),
        P(),
        P(),
        P(None, "tensor"),
        P(None, "tensor"),
        P(None, "tensor"),
        P("tensor", None),
        P(),
        P(None, "expert"),
        P(None, "expert"),
        P("expert", None),
    )
    out_specs = (
        P(None, "expert", None),
        P(None, "expert", None),
        P(),
        P(),
        P(None, "tensor"),
        P(None, "tensor"),
        P(None, "tensor"),
        P("tensor", None),
        P(),
        P(None, "expert"),
        P(None, "expert"),
        P("expert", None),
    )
    body = local_fast if suits(mesh) else local
    return jax.shard_map(body, mesh=mesh, in_specs=in_specs, out_specs=out_specs, check_vma=False)
```

```python
import functools

import jax
import jax.numpy as jnp
from jax import lax
from jax.experimental import pallas as pl
from jax.experimental.pallas import tpu as pltpu
from jax.sharding import PartitionSpec as P

HEAD_SIZE = 128
EXPERTS = 32


epsilon = 1e-05
theta_base = 1000000.0
masked_score = -1e30


def rms_norm(value_row_states, gain_vector):
    return (
        value_row_states
        * lax.rsqrt(jnp.mean(value_row_states * value_row_states, axis=-1, keepdims=True) + epsilon)
        * gain_vector
    )


def gelu_exact(value_row_states):
    return jax.nn.gelu(value_row_states, approximate=False)


def rope_tables(positions, head_dim):
    half_dim = head_dim // 2
    inverse = jnp.exp(
        -jnp.log(theta_base) * (2.0 * jnp.arange(half_dim, dtype=jnp.float32) / head_dim)
    )
    angles = positions.astype(jnp.float32)[:, None] * inverse[None, :]
    return (jnp.cos(angles), jnp.sin(angles))


def widen_table(table_part, value_row_states):
    return table_part.reshape(
        (table_part.shape[0],) + (1,) * (value_row_states.ndim - 2) + (table_part.shape[1],)
    )


def rotary_apply(value_row_states, cosine_table, sine_table):
    half_dim = value_row_states.shape[-1] // 2
    first_part = value_row_states[..., :half_dim]
    second = value_row_states[..., half_dim:]
    cos_wide = widen_table(cosine_table, value_row_states)
    sin_wide = widen_table(sine_table, value_row_states)
    return jnp.concatenate(
        [first_part * cos_wide - second * sin_wide, second * cos_wide + first_part * sin_wide],
        axis=-1,
    )


def unrotate(value_row_states, cosine_table, sine_table):
    half_dim = value_row_states.shape[-1] // 2
    first_part = value_row_states[..., :half_dim]
    second = value_row_states[..., half_dim:]
    cos_wide = widen_table(cosine_table, value_row_states)
    sin_wide = widen_table(sine_table, value_row_states)
    return jnp.concatenate(
        [first_part * cos_wide + second * sin_wide, second * cos_wide - first_part * sin_wide],
        axis=-1,
    )


def block_scores(query_block, key_row_states, starts, row_ids, offset, block_rows, score_scale):
    query_ids = offset + jnp.arange(block_rows, dtype=jnp.int32)
    allowed = (row_ids[None, :] <= query_ids[:, None]) & (row_ids[None, :] >= starts[:, None])
    scores = (
        jnp.einsum(
            "qcgd,kcd->cgqk", query_block, key_row_states, preferred_element_type=jnp.float32
        )
        * score_scale
    )
    return jnp.where(allowed, scores, masked_score)


def attention_forward(
    query_rows, key_row_states, value_rows, starts, row_ids, block_rows, score_scale
):

    def one_block(block_index):
        offset = block_index * block_rows
        scores = block_scores(
            query_rows, key_row_states, starts, row_ids, offset, block_rows, score_scale
        )
        row_peak = jnp.max(scores, axis=-1, keepdims=True)
        weights = jnp.exp(scores - row_peak)
        totals = jnp.sum(weights, axis=-1, keepdims=True)
        prob_low = (weights / totals).astype(jnp.bfloat16)
        attention_output = jnp.einsum(
            "cgqk,kcd->qcgd", prob_low, value_rows, preferred_element_type=jnp.float32
        )
        return (attention_output.astype(jnp.bfloat16), row_peak[..., 0] + jnp.log(totals[..., 0]))

    return lax.map(one_block, jnp.arange(query_rows.shape[0] // block_rows, dtype=jnp.int32))


def attention_backward(
    query_rows,
    key_row_states,
    value_rows,
    starts,
    row_ids,
    block_rows,
    score_scale,
    log_totals,
    attended_grad,
):

    def one_block(carried, block_index):
        key_grad, value_grad = carried
        offset = block_index * block_rows
        scores = block_scores(
            query_rows, key_row_states, starts, row_ids, offset, block_rows, score_scale
        )
        probs = jnp.exp(scores - log_totals[block_index][..., None])
        prob_low = probs.astype(jnp.bfloat16)
        prob_grad = jnp.einsum(
            "qcgd,kcd->cgqk", attended_grad, value_rows, preferred_element_type=jnp.float32
        )
        row_dot = jnp.sum(probs * prob_grad, axis=-1, keepdims=True)
        score_grad = (probs * (prob_grad - row_dot)).astype(jnp.bfloat16)
        query_grad = (
            jnp.einsum(
                "cgqk,kcd->qcgd", score_grad, key_row_states, preferred_element_type=jnp.float32
            )
            * score_scale
        )
        key_grad = (
            key_grad
            + jnp.einsum(
                "cgqk,qcgd->kcd", score_grad, query_rows, preferred_element_type=jnp.float32
            )
            * score_scale
        )
        value_grad = value_grad + jnp.einsum(
            "cgqk,qcgd->kcd", prob_low, attended_grad, preferred_element_type=jnp.float32
        )
        return ((key_grad, value_grad), query_grad)

    empty_grad = jnp.zeros(key_row_states.shape, jnp.float32)
    totals_out, query_grad = lax.scan(
        one_block,
        (empty_grad, empty_grad),
        jnp.arange(query_rows.shape[0] // block_rows, dtype=jnp.int32),
    )
    return (query_grad.reshape(query_rows.shape), totals_out[0], totals_out[1])


def spread_rows(base, group, capacity, n_dev, per_dev, width):
    widened = jnp.broadcast_to(
        base.reshape(EXPERTS, 1, capacity, width), (EXPERTS, group, capacity, width)
    )
    return widened.reshape(n_dev, per_dev * capacity, width)


def collect_rows(back, group, capacity, width, slot_index, rows, top_count):
    summed = jnp.sum(back.reshape(EXPERTS, group, capacity, width), axis=1).astype(jnp.bfloat16)
    return (
        summed.reshape(EXPERTS * capacity, width)[slot_index]
        .reshape(rows, top_count, width)
        .astype(jnp.float32)
    )


def local(
    tokens,
    cotangent,
    positions,
    routes,
    attention_gain,
    feedforward_gain,
    query_weight,
    key_matrix,
    value_matrix,
    output_weight,
    router_weight,
    gate_weight,
    up_weight,
    down_weight,
):
    micro_count, length, model_width = tokens.shape
    head_dim = HEAD_SIZE
    kv_local = key_matrix.shape[1] // head_dim
    query_group_count = query_weight.shape[1] // head_dim // kv_local
    top_count = routes.shape[2]
    n_dev = lax.axis_size("expert")
    n_tensor = lax.axis_size("tensor")
    half = length // n_tensor
    offset = lax.axis_index("tensor") * half
    per_dev = max(1, EXPERTS // n_dev)
    group = max(1, n_dev // EXPERTS)
    local_width = gate_weight.shape[1]
    ff_local = local_width // per_dev
    capacity = max(2, 3 * half * top_count // (2 * EXPERTS))
    block_rows = min(512, length)
    score_scale = head_dim ** (-0.5)
    expert_ids = jnp.arange(EXPERTS, dtype=jnp.int32)
    row_ids = jnp.arange(length, dtype=jnp.int32)
    gate_three = gate_weight.reshape(model_width, per_dev, ff_local)
    up_three = up_weight.reshape(model_width, per_dev, ff_local)
    down_three = down_weight.reshape(per_dev, ff_local, model_width)
    query_sum = jnp.zeros(query_weight.shape, jnp.float32)
    key_sum = jnp.zeros(key_matrix.shape, jnp.float32)
    value_sum = jnp.zeros(value_matrix.shape, jnp.float32)
    output_sum = jnp.zeros(output_weight.shape, jnp.float32)
    router_sum = jnp.zeros(router_weight.shape, jnp.float32)
    attn_gain_sum = jnp.zeros(attention_gain.shape, jnp.float32)
    ffn_gain_sum = jnp.zeros(feedforward_gain.shape, jnp.float32)
    gate_sum = jnp.zeros(gate_weight.shape, jnp.float32)
    up_sum = jnp.zeros(up_weight.shape, jnp.float32)
    down_sum = jnp.zeros(down_weight.shape, jnp.float32)
    layer_outputs = []
    input_grads = []
    for micro_index in range(micro_count):
        states = tokens[micro_index].astype(jnp.float32)
        out_grad = cotangent[micro_index].astype(jnp.float32)
        place = positions[micro_index]
        chosen = routes[micro_index]
        starts = row_ids - place
        cosine_table, sine_table = rope_tables(place, head_dim)
        normed_full, attn_norm_pull = jax.vjp(rms_norm, states, attention_gain)
        normalized_input = normed_full.astype(jnp.bfloat16)
        query_pre = jnp.dot(
            normalized_input, query_weight, preferred_element_type=jnp.float32
        ).reshape(length, kv_local, query_group_count, head_dim)
        query_rows = rotary_apply(query_pre, cosine_table, sine_table).astype(jnp.bfloat16)
        key_pre = jnp.dot(normalized_input, key_matrix, preferred_element_type=jnp.float32).reshape(
            length, kv_local, head_dim
        )
        key_row_states = rotary_apply(key_pre, cosine_table, sine_table).astype(jnp.bfloat16)
        value_rows = (
            jnp.dot(normalized_input, value_matrix, preferred_element_type=jnp.float32)
            .astype(jnp.bfloat16)
            .reshape(length, kv_local, head_dim)
        )
        attention_output, log_totals = attention_forward(
            query_rows, key_row_states, value_rows, starts, row_ids, block_rows, score_scale
        )
        attention_output = attention_output.reshape(length, kv_local * query_group_count * head_dim)
        attn_part = jnp.dot(attention_output, output_weight, preferred_element_type=jnp.float32)
        hidden_state = states + lax.psum(attn_part, "tensor")
        normed_ffn_full, ffn_norm_pull = jax.vjp(rms_norm, hidden_state, feedforward_gain)
        normed_ffn = normed_ffn_full.astype(jnp.bfloat16)
        state_half = lax.dynamic_slice_in_dim(normed_ffn, offset, half, 0)
        route_half = lax.dynamic_slice_in_dim(chosen, offset, half, 0)
        grad_half = lax.dynamic_slice_in_dim(out_grad, offset, half, 0)
        route_mask = (route_half[..., None] == expert_ids[None, None, :]).astype(jnp.float32)

        def gate_softmax(logits, route_mask=route_mask):
            return jax.nn.softmax(jnp.sum(logits[:, None, :] * route_mask, axis=-1), axis=-1)

        logits = jnp.dot(state_half, router_weight, preferred_element_type=jnp.float32)
        gate_probs, gate_pull = jax.vjp(gate_softmax, logits)
        flat_routes = route_half.reshape(-1)
        route_onehot = (flat_routes[:, None] == expert_ids[None, :]).astype(jnp.int32)
        ahead = jnp.tril(jnp.ones((half * top_count, half * top_count), jnp.float32), -1)
        ranks = jnp.sum(
            jnp.dot(ahead, route_onehot.astype(jnp.float32)).astype(jnp.int32) * route_onehot, axis=1
        )
        slot_index = flat_routes * capacity + ranks
        copies = jnp.repeat(state_half, top_count, axis=0)
        send_rows = (
            jnp.zeros((EXPERTS * capacity, model_width), jnp.bfloat16).at[slot_index].set(copies)
        )
        received = lax.all_to_all(
            spread_rows(send_rows, group, capacity, n_dev, per_dev, model_width),
            "expert",
            split_axis=0,
            concat_axis=0,
            tiled=True,
        ).reshape(n_dev, per_dev, capacity, model_width)
        gate_pre = jnp.einsum(
            "skcd,dkf->skcf", received, gate_three, preferred_element_type=jnp.float32
        )
        up_pre = jnp.einsum(
            "skcd,dkf->skcf", received, up_three, preferred_element_type=jnp.float32
        )
        activated, gelu_pull = jax.vjp(gelu_exact, gate_pre)
        expert_hidden = (activated * up_pre).astype(jnp.bfloat16)
        partial_out = jnp.einsum(
            "skcf,kfd->skcd", expert_hidden, down_three, preferred_element_type=jnp.float32
        )
        back_rows = lax.all_to_all(
            partial_out.reshape(n_dev, per_dev * capacity, model_width).astype(jnp.bfloat16),
            "expert",
            split_axis=0,
            concat_axis=0,
            tiled=True,
        ).astype(jnp.float32)
        returned_rows = collect_rows(
            back_rows, group, capacity, model_width, slot_index, half, top_count
        )
        mixture_half = jnp.sum(gate_probs[..., None] * returned_rows, axis=1)
        mixture = lax.all_gather(
            mixture_half.astype(jnp.bfloat16), "tensor", axis=0, tiled=True
        ).astype(mixture_half.dtype)
        layer_outputs.append((hidden_state + mixture).astype(jnp.bfloat16))
        gate_grad = jnp.sum(grad_half[:, None, :] * returned_rows, axis=-1)
        row_grad = (
            (gate_probs[..., None] * grad_half[:, None, :])
            .astype(jnp.bfloat16)
            .reshape(-1, model_width)
        )
        send_grad = (
            jnp.zeros((EXPERTS * capacity, model_width), jnp.bfloat16).at[slot_index].set(row_grad)
        )
        grad_received = lax.all_to_all(
            spread_rows(send_grad, group, capacity, n_dev, per_dev, model_width),
            "expert",
            split_axis=0,
            concat_axis=0,
            tiled=True,
        ).reshape(n_dev, per_dev, capacity, model_width)
        hidden_grad = jnp.einsum(
            "skcd,kfd->skcf", grad_received, down_three, preferred_element_type=jnp.float32
        )
        down_part = jnp.einsum(
            "skcf,skcd->kfd", expert_hidden, grad_received, preferred_element_type=jnp.float32
        ).reshape(down_weight.shape)
        gate_pre_grad = gelu_pull(hidden_grad * up_pre)[0].astype(jnp.bfloat16)
        up_pre_grad = (hidden_grad * activated).astype(jnp.bfloat16)
        gate_part = jnp.einsum(
            "skcd,skcf->dkf", received, gate_pre_grad, preferred_element_type=jnp.float32
        ).reshape(gate_weight.shape)
        up_part = jnp.einsum(
            "skcd,skcf->dkf", received, up_pre_grad, preferred_element_type=jnp.float32
        ).reshape(up_weight.shape)
        input_part = jnp.einsum(
            "skcf,dkf->skcd", gate_pre_grad, gate_three, preferred_element_type=jnp.float32
        )
        input_part = input_part + jnp.einsum(
            "skcf,dkf->skcd", up_pre_grad, up_three, preferred_element_type=jnp.float32
        )
        input_back = lax.all_to_all(
            input_part.reshape(n_dev, per_dev * capacity, model_width).astype(jnp.bfloat16),
            "expert",
            split_axis=0,
            concat_axis=0,
            tiled=True,
        ).astype(jnp.float32)
        route_input = collect_rows(
            input_back, group, capacity, model_width, slot_index, half, top_count
        )
        logit_grad = gate_pull(gate_grad)[0].astype(jnp.bfloat16)
        router_part = jnp.dot(state_half.T, logit_grad, preferred_element_type=jnp.float32)
        ffn_half_grad = jnp.sum(route_input, axis=1) + jnp.dot(
            logit_grad, router_weight.T, preferred_element_type=jnp.float32
        )
        gate_sum = gate_sum + gate_part
        up_sum = up_sum + up_part
        down_sum = down_sum + down_part
        router_sum = router_sum + router_part
        normed_ffn_grad = lax.all_gather(ffn_half_grad, "tensor", axis=0, tiled=True)
        state_norm_grad, ffn_gain_grad = ffn_norm_pull(normed_ffn_grad)
        state_grad = out_grad + state_norm_grad
        ffn_gain_sum = ffn_gain_sum + ffn_gain_grad
        attention_grad = state_grad.astype(jnp.bfloat16)
        output_sum = output_sum + jnp.dot(
            attention_output.T, attention_grad, preferred_element_type=jnp.float32
        )
        attended_grad = (
            jnp.dot(attention_grad, output_weight.T, preferred_element_type=jnp.float32)
            .astype(jnp.bfloat16)
            .reshape(length, kv_local, query_group_count, head_dim)
        )
        query_grad, key_grad, value_grad = attention_backward(
            query_rows,
            key_row_states,
            value_rows,
            starts,
            row_ids,
            block_rows,
            score_scale,
            log_totals,
            attended_grad,
        )
        query_grad = (
            unrotate(query_grad, cosine_table, sine_table).astype(jnp.bfloat16).reshape(length, -1)
        )
        key_grad = (
            unrotate(key_grad, cosine_table, sine_table).astype(jnp.bfloat16).reshape(length, -1)
        )
        value_grad = value_grad.astype(jnp.bfloat16).reshape(length, -1)
        query_sum = query_sum + jnp.dot(
            normalized_input.T, query_grad, preferred_element_type=jnp.float32
        )
        key_sum = key_sum + jnp.dot(
            normalized_input.T, key_grad, preferred_element_type=jnp.float32
        )
        value_sum = value_sum + jnp.dot(
            normalized_input.T, value_grad, preferred_element_type=jnp.float32
        )
        normed_part = jnp.dot(query_grad, query_weight.T, preferred_element_type=jnp.float32)
        normed_part = normed_part + jnp.dot(
            key_grad, key_matrix.T, preferred_element_type=jnp.float32
        )
        normed_part = normed_part + jnp.dot(
            value_grad, value_matrix.T, preferred_element_type=jnp.float32
        )
        normed_grad = lax.psum(normed_part, "tensor")
        state_in_grad, attn_gain_grad = attn_norm_pull(normed_grad)
        attn_gain_sum = attn_gain_sum + attn_gain_grad
        input_grads.append(state_grad + state_in_grad)
    gate_sum, up_sum, down_sum, router_sum = lax.psum(
        (gate_sum, up_sum, down_sum, router_sum), "tensor"
    )
    reduced = lax.psum(
        (query_sum, key_sum, value_sum, output_sum, router_sum, attn_gain_sum, ffn_gain_sum),
        "expert",
    )
    return (
        jnp.stack(layer_outputs),
        jnp.stack(input_grads),
        reduced[5],
        reduced[6],
        reduced[0],
        reduced[1],
        reduced[2],
        reduced[3],
        reduced[4],
        gate_sum,
        up_sum,
        down_sum,
    )


MESH = pl.DeviceIdType.MESH
ANY = pl.ANY
VMEM_LIMIT = 60 * 2**20


def mm(a, b):
    return lax.dot_general(a, b, (((1,), (0,)), ((), ())), preferred_element_type=jnp.float32)


def mm_nt(a, b):
    return lax.dot_general(a, b, (((1,), (1,)), ((), ())), preferred_element_type=jnp.float32)


def mm_tn(a, b):
    return lax.dot_general(a, b, (((0,), (0,)), ((), ())), preferred_element_type=jnp.float32)


def remote(src, dst, send_sem, recv_sem, device):
    return pltpu.make_async_remote_copy(
        src_ref=src,
        dst_ref=dst,
        send_sem=send_sem,
        recv_sem=recv_sem,
        device_id=device,
        device_id_type=MESH,
    )


def tiles(count, body):
    def step(i, carry):
        body(i)
        return carry

    lax.fori_loop(0, count, step, 0)


def cols(i, width):
    return pl.ds(pl.multiple_of(i * width, width), width)


def front_kernel(
    tok_ref, g_ref, pos_ref, routes_ref, gain_a, gain_f, wq_ref, wk_ref, wv_ref, wo_ref, router_ref,
    wg_hbm, wu_hbm, wd_hbm,
    lay_ref, dx_ref, nrm_ref, att_ref, q_ref, k_ref, v_ref, pr_ref, tab_ref, hs_ref, x_ref,
    rx_ref, rh_ref, rg_ref, ru_ref, re_ref,
    xz, gz, rz, xs, gs, xr, gr, eg, hid, gpg, upg, yr, dr, yz, dz, own_part, other_part, rel,
    onehot, prob, gg, wg, wu, wd,
    r_s, r_r, za_s, za_r, xa_s, xa_r, xb_s, xb_r, zb_s, zb_r, pair_s, pair_r, part_s, part_r, fw_s, fw_r, rel_s, rel_r, w_sem, own_sem,
):
    ys, ds_, zy, zd = gs, xs, gz, xz
    e = lax.axis_index("expert")
    c = lax.axis_index("tensor")
    z = e // 4
    o = lax.rem(e, 4) * 2 + c
    micro, length, width = tok_ref.shape
    half = length // 2
    f32 = jnp.float32
    bf = jnp.bfloat16
    ff = wg.shape[1]
    col = 4 * half
    rows = xs.shape[1]
    blk = rows // 8
    cap = blk // 4
    me = 2 * e + c
    tw = 256
    nt = width // tw

    def z_dev(k):
        return (lax.rem(z + k, 4) * 4 + lax.rem(e, 4), c)

    def z_back(k):
        return (lax.rem(z + 4 - k, 4) * 4 + lax.rem(e, 4), c)

    def p_dev(d):
        t = lax.rem(o + d, 8)
        return (z * 4 + t // 2, lax.rem(t, 2))

    def p_back(d):
        t = lax.rem(o + 8 - d, 8)
        return (z * 4 + t // 2, lax.rem(t, 2))

    inner = (z == 1) | (z == 2)
    edge = (z == 0) | (z == 3)
    not_first = z != 0
    not_last = z != 3
    beside = jnp.where((z == 0) | (z == 3), jnp.where(z == 0, 1, 2), jnp.where(z == 1, 0, 3))
    beside_dev = (beside * 4 + lax.rem(e, 4), c)
    far_slot = jnp.where(z == 1, 1, 3)
    far_back = jnp.where(z == 0, 1, 3)

    @pl.when(z == 3)
    def _():
        for m in range(micro):
            yz[m, half : 2 * half, :] = jnp.zeros((half, width), bf)
            dz[m, half : 2 * half, :] = jnp.zeros((half, width + 128), bf)

    @pl.when(z == 0)
    def _():
        for m in range(micro):
            yz[m, 3 * half : 4 * half, :] = jnp.zeros((half, width), bf)
            dz[m, 3 * half : 4 * half, :] = jnp.zeros((half, width + 128), bf)

    barrier = pltpu.get_barrier_semaphore()
    for k in range(1, 4):
        pl.semaphore_signal(barrier, inc=1, device_id=z_dev(k), device_id_type=MESH)
    for d in range(1, 8):
        pl.semaphore_signal(barrier, inc=1, device_id=p_dev(d), device_id_type=MESH)
    loads = [
        pltpu.make_async_copy(wg_hbm.at[:, cols(c, ff)], wg, w_sem.at[0]),
        pltpu.make_async_copy(wu_hbm.at[:, cols(c, ff)], wu, w_sem.at[1]),
        pltpu.make_async_copy(wd_hbm.at[cols(c, ff), :], wd, w_sem.at[2]),
    ]
    for cp in loads:
        cp.start()
    pl.semaphore_wait(barrier, 10)

    mine = pl.ds(pl.multiple_of(c * half, half), half)
    sent = []
    got_r = []
    for k in range(1, 4):
        cp = remote(routes_ref, rz.at[k], r_s.at[k], r_r.at[k], z_dev(k))
        cp.start()
        sent.append(cp)
        got_r.append(cp)
    got_z = {}

    sent_if = []
    got_f = {}

    def start_if(cond, cp):
        pl.when(cond)(cp.start)
        sent_if.append((cond, cp))

    def z_send(m, a):
        src, dst = ((g_ref, gz), (x_ref, xz))[a]
        for k in (2, 1, 3):
            i = (m * 2 + a) * 4 + k
            cp = remote(
                src.at[m, mine, :], dst.at[m, pl.ds(k * half, half), :],
                za_s.at[i], za_r.at[i], z_dev(k),
            )
            if k == 2:
                cp.start()
                sent.append(cp)
            else:
                start_if(not_last if k == 1 else not_first, cp)
            got_z[(m, a, k)] = cp
        dst[m, 0:half, :] = src[m, mine, :]

    def z_forward(m, a):
        dst = (gz, xz)[a]
        i = (m * 2 + a) * 4
        got_z[(m, a, 2)].wait_recv()
        cp = remote(
            dst.at[m, pl.ds(2 * half, half), :],
            dst.at[m, pl.ds(pl.multiple_of(far_slot * half, half), half), :],
            fw_s.at[m * 2 + a], za_r.at[i + far_slot], beside_dev,
        )
        pl.when(inner)(cp.start)
        got_f[(m, a)] = cp

    for m in range(micro):
        z_send(m, 0)
    rz[0] = routes_ref[...]

    head = HEAD_SIZE
    heads = wq_ref.shape[1] // head
    lane = lax.broadcasted_iota(jnp.int32, (1, 128), 1)
    row = lax.broadcasted_iota(jnp.int32, (length, length), 0)
    column = lax.broadcasted_iota(jnp.int32, (length, length), 1)
    turn = jnp.exp(
        (-2.0 / head * jnp.log(jnp.float32(theta_base))) * lax.rem(lane, head // 2).astype(f32)
    )
    allowed = []
    for m in range(micro):
        states = tok_ref[m].astype(f32)
        scale = lax.rsqrt(jnp.mean(states * states, axis=1, keepdims=True) + epsilon)
        nrm_ref[m] = (states * scale * gain_a[...].reshape(1, width)).astype(bf)
        place = pos_ref[m : m + 1, :].astype(f32)
        place = jnp.sum(jnp.where(row == column, place, 0.0), axis=1, keepdims=True)
        angle = place * turn
        tab_ref[m, 0] = jnp.cos(angle)
        tab_ref[m, 1] = jnp.where(lane < head // 2, -1.0, 1.0) * jnp.sin(angle)
        allowed.append((column <= row) & (column >= row - place.astype(jnp.int32)))

    def rope(u, m):
        return u * tab_ref[m, 0] + pltpu.roll(u, head // 2, 1) * tab_ref[m, 1]

    everything = nrm_ref[...].reshape(micro * length, width)

    def project(i):
        both = mm(everything, wq_ref[:, cols(i, tw)])
        for m in range(micro):
            for j in range(tw // head):
                at = pl.ds(pl.multiple_of((i * (tw // head) + j) * length, length), length)
                u = both[m * length : (m + 1) * length, j * head : (j + 1) * head]
                q_ref[m, at, :] = rope(u, m).astype(bf)

    tiles(wq_ref.shape[1] // tw, project)
    z_forward(0, 0)
    key_pre = mm(everything, wk_ref[...])
    value_pre = mm(everything, wv_ref[...])
    for m in range(micro):
        at = slice(m * length, (m + 1) * length)
        k_ref[m] = rope(key_pre[at], m).astype(bf)
        v_ref[m] = value_pre[at].astype(bf)
    for m in range(micro):
        score = mm_nt(q_ref[m], k_ref[m]).reshape(heads, length, length) * (head**-0.5)
        score = jnp.where(allowed[m][None], score, masked_score)
        weight = jnp.exp(score - jnp.max(score, axis=-1, keepdims=True))
        weight = weight / jnp.sum(weight, axis=-1, keepdims=True)
        weight = weight.reshape(heads * length, length)
        pr_ref[m] = weight
        out = mm(weight.astype(bf), v_ref[m]).astype(bf)
        for h in range(heads):
            att_ref[m, :, h * head : (h + 1) * head] = out[h * length : (h + 1) * length]
    att_all = att_ref[...].reshape(micro * length, heads * head)
    got_part = []
    for j in range(3):

        def outward(i, j=j):
            at = cols(i + j * (nt // 3), tw)
            own_part[:, at] = mm(att_all, wo_ref[:, at])

        tiles(nt // 3, outward)
        at = pl.ds(j * (width // 3), width // 3)
        cp = remote(
            own_part.at[:, at], other_part.at[:, at], part_s.at[j], part_r.at[j], (e, 1 - c)
        )
        cp.start()
        sent.append(cp)
        got_part.append(cp)

    z_forward(1, 0)
    for cp in got_r:
        cp.wait_recv()

    before = ((row < column) & (row // half == column // half)).astype(bf)
    expert = 8 * z + lax.rem(o + lax.broadcasted_iota(jnp.int32, (8, length), 0), 8)
    place_row = lax.broadcasted_iota(jnp.int32, (length, col), 0)
    place_col = lax.broadcasted_iota(jnp.int32, (length, col), 1)
    slots = [jnp.zeros((8, col), f32) for _ in range(micro)]
    for k in range(4):
        at = place_col - k * half
        put = ((at >= 0) & (at < half) & (place_row == at + c * half)).astype(bf)
        for m in range(micro):
            named = rz[k, m]
            hit = named[0:1, :] == expert
            for j in range(1, routes_ref.shape[1]):
                hit = hit | (named[j : j + 1, :] == expert)
            mask = jnp.where(hit, 1.0, 0.0)
            rank = mm(mask.astype(bf), before)
            slots[m] = slots[m] + mm((mask * (rank + (cap * k + 1))).astype(bf), put)
    number = lax.broadcasted_iota(jnp.int32, (blk, col), 0) + 1
    for m in range(micro):
        for d in range(8):
            spot = slots[m][d : d + 1, :].astype(jnp.int32)
            onehot[m, d * blk : (d + 1) * blk, :] = jnp.where(spot == number, 1.0, 0.0).astype(
                jnp.bfloat16
            )

    got_p = {}

    def pack(m, a):
        src, out, dst = ((gz, gs, gr), (xz, xs, xr))[a]
        for k in (1, 3):
            got_z[(m, a, k)].wait_recv()

        def body(i):
            at = cols(i, tw)
            out[m, :, at] = mm(onehot[m], src[m, :, at]).astype(bf)

        tiles(nt, body)
        if a == 1:
            out[m, :, width:] = mm(onehot[m], src[m, :, width:]).astype(bf)
        dst[m, 0:blk, :] = out[m, 0:blk, :]
        for d in range(1, 8):
            i = (m * 2 + a) * 8 + d
            at = pl.ds(d * blk, blk)
            cp = remote(out.at[m, at, :], dst.at[m, at, :], xa_s.at[i], xa_r.at[i], p_dev(d))
            cp.start()
            sent_p.setdefault((m, a), []).append(cp)
            got_p[(m, a, d)] = cp

    sent_p = {}
    tall = lax.broadcasted_iota(jnp.int32, (128, EXPERTS), 0)
    double = (lax.rem(tall, EXPERTS) == lax.broadcasted_iota(jnp.int32, (128, EXPERTS), 1)) & (
        tall < 2 * EXPERTS
    )
    router = mm(jnp.where(double, 1.0, 0.0).astype(bf), router_ref[...]).astype(bf)
    for cp in got_part:
        cp.wait_recv()
    for m in range(micro):
        at = slice(m * length, (m + 1) * length)
        state = tok_ref[m].astype(f32) + (own_part[at, :] + other_part[at, :])
        hs_ref[m] = state
        scale = lax.rsqrt(jnp.mean(state * state, axis=1, keepdims=True) + epsilon)
        low = (state * scale * gain_f[...].reshape(1, width)).astype(bf)
        x_ref[m, :, 0:width] = low
        logits = mm_nt(low, router)
        names = lax.rem(lane, EXPERTS)
        hit = lane < 0
        for j in range(routes_ref.shape[1]):
            named = routes_ref[m, j : j + 1, :].astype(f32)
            named = jnp.sum(jnp.where(row == column, named, 0.0), axis=1, keepdims=True)
            hit = hit | (named.astype(jnp.int32) == names)
        hit = hit & (lane < 2 * EXPERTS)
        best = jnp.max(jnp.where(hit, logits, masked_score), axis=1, keepdims=True)
        weight = jnp.where(hit, jnp.exp(logits - best), 0.0)
        first = jnp.sum(jnp.where(lane < EXPERTS, weight, 0.0), axis=1, keepdims=True)
        weight = weight / first
        top = weight.astype(bf).astype(f32)
        x_ref[m, :, width:] = jnp.where(lane < EXPERTS, top, weight - top).astype(bf)
        z_send(m, 1)
    for m in range(micro):
        pack(m, 0)
    for m in range(micro):
        z_forward(m, 1)
        pack(m, 1)
    for cp in loads:
        cp.wait()

    got_b = {}
    def to_pair(m):
        for i, (src, dst) in enumerate(
            ((xr, rx_ref), (hid, rh_ref), (gpg, rg_ref), (upg, ru_ref), (eg, re_ref))
        ):
            src_at = src.at[m, :, 0:width] if i == 0 else src.at[m]
            n = m * 8 + i
            cp = remote(src_at, dst.at[c, m], pair_s.at[n], pair_r.at[n], (e, 1 - c))
            cp.start()
            sent.append(cp)
            got_b[("pair", m, i)] = cp
            cp = pltpu.make_async_copy(src_at, dst.at[c, m], own_sem.at[n])
            cp.start()
            loads.append(cp)

    loads.clear()

    def send_back(m, a):
        src, dst = ((ds_, dr), (ys, yr))[a]
        dst[m, 0:blk, :] = src[m, 0:blk, :]
        for d in range(1, 8):
            i = (m * 2 + a) * 8 + d
            at = pl.ds(d * blk, blk)
            cp = remote(src.at[m, at, :], dst.at[m, at, :], xb_s.at[i], xb_r.at[i], p_back(d))
            cp.start()
            sent.append(cp)
            got_b[(m, a, d)] = cp

    def run(m):
        for a in range(2):
            for d in range(1, 8):
                got_p[(m, a, d)].wait_recv()
            for cp in sent_p[(m, a)]:
                cp.wait_send()
        tail = xr[m, :, width:].astype(jnp.float32)
        pick = (lane == me) | (lane == me + 32)
        prob[...] = jnp.broadcast_to(
            jnp.sum(jnp.where(pick, tail, 0.0), axis=1, keepdims=True), (rows, 128)
        )
        gg[...] = jnp.zeros_like(gg)

        def weigh(i):
            at = cols(i, tw)
            eg[m, :, at] = (prob[:, 0:1] * gr[m, :, at].astype(jnp.float32)).astype(jnp.bfloat16)

        tiles(nt, weigh)

        def inner(i):
            at = cols(i, tw)
            xrow = xr[m, :, 0:width]
            gate = mm(xrow, wg[:, at])
            upv = mm(xrow, wu[:, at])
            back = mm_nt(eg[m], wd[at, :])
            cdf = 0.5 * (1.0 + lax.erf(gate * 0.7071067811865476))
            act = gate * cdf
            slope = cdf + gate * (jnp.exp(gate * gate * -0.5) * 0.3989422804014327)
            hid[m, :, at] = (act * upv).astype(jnp.bfloat16)
            gpg[m, :, at] = (back * upv * slope).astype(jnp.bfloat16)
            upg[m, :, at] = (back * act).astype(jnp.bfloat16)

        tiles(ff // tw, inner)

        def outer(i):
            at = cols(i, tw)
            low = mm(hid[m], wd[:, at]).astype(jnp.bfloat16).astype(jnp.float32)
            gg[...] += jnp.broadcast_to(
                jnp.sum(low * gr[m, :, at].astype(jnp.float32), axis=1, keepdims=True),
                (rows, 128),
            )
            ys[m, :, at] = (prob[:, 0:1] * low).astype(jnp.bfloat16)

        tiles(nt, outer)

        def inputs(i):
            at = cols(i, tw)
            ds_[m, :, at] = (mm_nt(gpg[m], wg[at, :]) + mm_nt(upg[m], wu[at, :])).astype(
                jnp.bfloat16
            )

        tiles(nt, inputs)
        total = gg[...]
        high = total.astype(jnp.bfloat16).astype(jnp.float32)
        ds_[m, :, width:] = jnp.where(
            lane == me, high, jnp.where(lane == me + 32, total - high, 0.0)
        ).astype(jnp.bfloat16)
        send_back(m, 0)
        to_pair(m)

    for m in range(micro):
        run(m)
    for m in range(micro):
        send_back(m, 1)

    got_c = {}

    def gather(m, a):
        src, out, dst = ((dr, zd, dz), (yr, zy, yz))[a]
        for d in range(1, 8):
            got_b[(m, a, d)].wait_recv()
        pl.when(inner)(got_f[(m, 1 - a)].wait_send)

        def body(i):
            at = cols(i, tw)
            out[m, :, at] = mm_tn(onehot[m], src[m, :, at]).astype(bf)

        tiles(nt, body)
        if a == 0:
            out[m, :, width:] = mm_tn(onehot[m], src[m, :, width:]).astype(bf)
        part = rel.at[m, a] if a == 0 else rel.at[m, a, :, 0:width]
        far = pl.ds(pl.multiple_of(far_back * half, half), half)
        relay = remote(out.at[m, far, :], part, rel_s.at[m * 2 + a], rel_r.at[m * 2 + a], beside_dev)
        start_if(edge, relay)
        for k in (1, 3, 2):
            i = (m * 2 + a) * 4 + k
            at = pl.ds(k * half, half)
            cp = remote(out.at[m, at, :], dst.at[m, at, :], zb_s.at[i], zb_r.at[i], z_back(k))
            got_c[(m, a, k)] = cp
            if k == 2:

                @pl.when(inner)
                def _():
                    relay.wait_recv()
                    wide = out.shape[2]
                    out[m, 2 * half : 3 * half, :] = (
                        out[m, 2 * half : 3 * half, :].astype(f32)
                        + rel[m, a, :, 0:wide].astype(f32)
                    ).astype(bf)

                cp.start()
                sent.append(cp)
            else:
                start_if(not_first if k == 1 else not_last, cp)

    def finish(m, a):
        own, other, out = ((zd, dz, dx_ref), (zy, yz, lay_ref))[a]
        pl.when(not_last)(got_c[(m, a, 1)].wait_recv)
        pl.when(not_first)(got_c[(m, a, 3)].wait_recv)
        got_c[(m, a, 2)].wait_recv()
        total = own[m, 0:half, :].astype(jnp.float32)
        for k in range(1, 4):
            total = total + other[m, k * half : (k + 1) * half, :].astype(jnp.float32)
        if a == 1:
            total = hs_ref[m, mine, :] + total
        out[m, mine, :] = total.astype(out.dtype)
        n = m * 8 + 5 + a
        cp = remote(
            out.at[m, mine, :], out.at[m, mine, :], pair_s.at[n], pair_r.at[n], (e, 1 - c)
        )
        cp.start()
        sent.append(cp)
        got_c[("pair", m, a)] = cp

    order = [(m, a) for a in range(2) for m in range(micro)]
    for i, (m, a) in enumerate(order):
        gather(m, a)
        if i >= 1:
            finish(*order[i - 1])
    finish(*order[-1])
    for m in range(micro):
        for i in range(5):
            got_b[("pair", m, i)].wait_recv()
        for a in range(2):
            got_c[("pair", m, a)].wait_recv()
    for cp in loads:
        cp.wait()
    for cp in sent:
        cp.wait_send()
    for cond, cp in sent_if:
        pl.when(cond)(cp.wait_send)


def front_call(
    tokens, cotangent, positions, routes, gain_a, gain_f, wq, wk, wv, wo, router, gate_weight,
    up_weight, down_weight,
):
    micro, length, width = tokens.shape
    wide = width + 128
    half = length // 2
    ff = gate_weight.shape[1] // 2
    cap = 3 * half * routes.shape[1] // (2 * EXPERTS)
    rows = 8 * 4 * cap
    bf = jnp.bfloat16
    f32 = jnp.float32
    vmem = pl.BlockSpec(memory_space=pltpu.VMEM)
    hbm = pl.BlockSpec(memory_space=ANY)
    heads = wq.shape[1] // HEAD_SIZE

    def buf(*shape, dtype=bf):
        return pltpu.VMEM(shape, dtype)

    def out(*shape, dtype=bf):
        return jax.ShapeDtypeStruct(shape, dtype)

    sem = pltpu.SemaphoreType.DMA
    col = 4 * half
    return pl.pallas_call(
        front_kernel,
        out_shape=(
            out(micro, length, width),
            out(micro, length, wide, dtype=f32),
            out(micro, length, width),
            out(micro, length, wq.shape[1]),
            out(micro, heads * length, HEAD_SIZE),
            out(micro, length, HEAD_SIZE),
            out(micro, length, HEAD_SIZE),
            out(micro, heads * length, length, dtype=f32),
            out(micro, 2, length, HEAD_SIZE, dtype=f32),
            out(micro, length, width, dtype=f32),
            out(micro, length, wide),
            out(2, micro, rows, width),
            out(2, micro, rows, ff),
            out(2, micro, rows, ff),
            out(2, micro, rows, ff),
            out(2, micro, rows, width),
        ),
        in_specs=[vmem] * 11 + [hbm] * 3,
        out_specs=(vmem,) * 11 + (hbm,) * 5,
        scratch_shapes=[
            buf(micro, col, wide), buf(micro, col, width), pltpu.VMEM((4, *routes.shape), jnp.int32),
            buf(micro, rows, wide), buf(micro, rows, width), buf(micro, rows, wide), buf(micro, rows, width),
            buf(micro, rows, width), buf(micro, rows, ff), buf(micro, rows, ff), buf(micro, rows, ff),
            buf(micro, rows, width), buf(micro, rows, wide), buf(micro, col, width), buf(micro, col, wide),
            buf(micro * length, width, dtype=f32), buf(micro * length, width, dtype=f32),
            buf(micro, 2, half, wide), buf(micro, rows, col), buf(rows, 128, dtype=f32), buf(rows, 128, dtype=f32),
            buf(width, ff), buf(width, ff), buf(ff, width),
            sem((4,)), sem((4,)), sem((8 * micro,)), sem((8 * micro,)), sem((16 * micro,)), sem((16 * micro,)),
            sem((16 * micro,)), sem((16 * micro,)), sem((8 * micro,)), sem((8 * micro,)), sem((8 * micro,)),
            sem((8 * micro,)), sem((3,)), sem((3,)), sem((2 * micro,)), sem((2 * micro,)), sem((2 * micro,)),
            sem((2 * micro,)), sem((3,)), sem((8 * micro,)),
        ],
        compiler_params=pltpu.CompilerParams(
            collective_id=1, has_side_effects=True, vmem_limit_bytes=VMEM_LIMIT
        ),
        cost_estimate=pl.CostEstimate(
            flops=2 * 6 * micro * rows * width * ff, bytes_accessed=40 * 2**20, transcendentals=0
        ),
        name="front",
    )(
        tokens, cotangent, positions, routes, gain_a, gain_f, wq, wk, wv, wo, router, gate_weight,
        up_weight, down_weight,
    )


def grads_kernel(x_ref, h_ref, g_ref, u_ref, e_ref, gate_out, up_out, down_out):
    gate_out[...] = mm_tn(x_ref[0], g_ref[0])
    up_out[...] = mm_tn(x_ref[0], u_ref[0])
    down_out[...] = mm_tn(h_ref[0], e_ref[0])


def grads_call(rx, rh, rg, ru, re):
    _, micro, rows, width = rx.shape
    ff = rh.shape[3]
    n = micro * rows
    tw = 256
    per = ff // tw
    f32 = jnp.float32
    wide = pl.BlockSpec((1, n, width), lambda i: (i // per, 0, 0))
    thin = pl.BlockSpec((1, n, tw), lambda i: (i // per, 0, i % per))
    return pl.pallas_call(
        grads_kernel,
        grid=(2 * per,),
        in_specs=[wide, thin, thin, thin, wide],
        out_specs=(
            pl.BlockSpec((width, tw), lambda i: (0, i)),
            pl.BlockSpec((width, tw), lambda i: (0, i)),
            pl.BlockSpec((tw, width), lambda i: (i, 0)),
        ),
        out_shape=(
            jax.ShapeDtypeStruct((width, 2 * ff), f32),
            jax.ShapeDtypeStruct((width, 2 * ff), f32),
            jax.ShapeDtypeStruct((2 * ff, width), f32),
        ),
        compiler_params=pltpu.CompilerParams(vmem_limit_bytes=VMEM_LIMIT),
        cost_estimate=pl.CostEstimate(
            flops=2 * 6 * n * width * ff, bytes_accessed=45 * 2**20, transcendentals=0
        ),
        name="expert_grads",
    )(
        rx.reshape(2, n, width), rh.reshape(2, n, ff), rg.reshape(2, n, ff),
        ru.reshape(2, n, ff), re.reshape(2, n, width),
    )


def back_kernel(
    tok_ref, g_ref, gain_a, gain_f, wq_ref, wk_ref, wv_ref, wo_ref, router_ref,
    dx_ref, nrm_ref, att_ref, q_ref, k_ref, v_ref, pr_ref, tab_ref, hs_ref, x_ref,
    tg_ref, oa, ob, os,
    d_ref, a_ref, s_ref, sg, ag, own_part, other_part,
    fn, fd, fa, fg, fs, pa, pb, za, zb, zs, ra, rb,
    f_s, f_r, w_s, w_r, c_s, c_r, y_s, y_r, l_s, l_r, z_s, z_r, h_s, h_r, p_s, p_r, part_s, part_r,
):
    micro, length, width = tok_ref.shape
    f32 = jnp.float32
    bf = jnp.bfloat16
    head = HEAD_SIZE
    heads = wq_ref.shape[1] // head
    wq = wq_ref.shape[1]
    tw = 256
    nt = width // tw
    n_ref = nrm_ref
    e = lax.axis_index("expert")
    c = lax.axis_index("tensor")
    z = e // 4
    q = lax.rem(e, 4)
    qx = lax.rem(q, 2)
    qy = q // 2
    rows = micro * length
    wn = n_ref.shape[1] // 2
    wd = d_ref.shape[1] // 2
    wa = att_ref.shape[1] // 2
    per = length
    wg = a_ref.shape[1] // 2
    ws = s_ref.shape[1] // 4
    hs = s_ref.shape[0] // 4
    ha = wn // 4
    hb = wa // 4

    def flip(bit, by):
        return lax.rem(bit + by, 2)

    def p_dev(d):
        return (z * 4 + flip(qy, d // 2) * 2 + flip(qx, d % 2), c)

    def z_dev(k):
        return (lax.rem(z + k, 4) * 4 + q, c)

    def part(i, size):
        return pl.ds(pl.multiple_of(i * size, size), size)

    inner = (z == 1) | (z == 2)
    edge = (z == 0) | (z == 3)
    not_first = z != 0
    not_last = z != 3
    beside = jnp.where(edge, jnp.where(z == 0, 1, 2), jnp.where(z == 1, 0, 3))
    beside_dev = (beside * 4 + q, c)
    twin = (e, 1 - c)
    sent_if = []

    def start_if(cond, cp):
        pl.when(cond)(cp.start)
        sent_if.append((cond, cp))

    def clear(slot):
        za[slot] = jnp.zeros((ha, wd), bf)
        zb[slot] = jnp.zeros((hb, wg), bf)

    pl.when(z == 0)(lambda: clear(1))
    pl.when(z == 3)(lambda: clear(3))

    barrier = pltpu.get_barrier_semaphore()
    for k in range(1, 4):
        pl.semaphore_signal(barrier, inc=1, device_id=z_dev(k), device_id_type=MESH)
        pl.semaphore_signal(barrier, inc=1, device_id=p_dev(k), device_id_type=MESH)
    pl.semaphore_signal(barrier, inc=1, device_id=(e, 1 - c), device_id_type=MESH)
    pl.semaphore_wait(barrier, 7)

    sent = []
    got_f = {}
    bits = {0: 0, 3: 0, 1: 1, 2: 1}

    def piece(src, i, d):
        bit = flip(qx, d % 2) if bits[i] == 0 else flip(qy, d // 2)
        return part(bit, src.shape[1] // 2)

    def mine(d):
        return pl.ds(pl.multiple_of(d * rows + c * per, per), per)

    def factor(i, src, dst):
        for d in (1, 2):
            if bits[i] == 0:
                view = src.at[pl.ds(pl.multiple_of(c * per, per), per), piece(src, i, d)]
                to = dst.at[mine(d), :]
            else:
                view = src.at[:, piece(src, i, d)]
                to = dst.at[pl.ds(d * rows, rows), :]
            cp = remote(view, to, f_s.at[d * 4 + i], f_r.at[d * 4 + i], p_dev(d))
            cp.start()
            sent.append(cp)
            got_f[(i, d)] = cp

    def to_twin(i, d, dst):
        cp = remote(dst.at[mine(d), :], dst.at[mine(d), :], w_s.at[d * 4 + i], w_r.at[d * 4 + i], twin)
        cp.start()
        sent.append(cp)
        got_f[("twin", i, d)] = cp

    def relay(i, dst):
        via, over = (1, 2) if bits[i] == 0 else (2, 1)
        got_f[(i, via)].wait_recv()
        if bits[i] == 0:
            src, to = dst.at[mine(via), :], dst.at[mine(3), :]
        else:
            src, to = dst.at[pl.ds(via * rows, rows), :], dst.at[pl.ds(3 * rows, rows), :]
        cp = remote(src, to, f_s.at[12 + i], f_r.at[12 + i], p_dev(over))
        cp.start()
        sent.append(cp)
        got_f[(i, 3)] = cp
        if bits[i] == 0:
            to_twin(i, via, dst)
            got_f[(i, over)].wait_recv()
            to_twin(i, over, dst)

    def arrive(i, dst):
        if bits[i]:
            got_f[(i, 1)].wait_recv()
            got_f[(i, 3)].wait_recv()
        else:
            got_f[(i, 3)].wait_recv()
            to_twin(i, 3, dst)
            for d in (1, 2, 3):
                got_f[("twin", i, d)].wait_recv()

    factor(2, att_ref, fa)

    lane = lax.broadcasted_iota(jnp.int32, (1, 128), 1)
    gain_row = jnp.zeros((1, width), f32)
    s_ref[...] = jnp.zeros_like(s_ref)
    router_row = jnp.zeros((128, width), f32)
    for m in range(micro):
        here = slice(m * length, (m + 1) * length)
        tail = dx_ref[m, :, width:]
        grad = tail + pltpu.roll(tail, 128 - EXPERTS, 1)
        tail = x_ref[m, :, width:].astype(f32)
        prob = jnp.where(lane < EXPERTS, tail + pltpu.roll(tail, 128 - EXPERTS, 1), 0.0)
        shared = jnp.sum(prob * grad, axis=1, keepdims=True)
        low = (prob * (grad - shared)).astype(bf)
        router_row = router_row + mm_tn(low, x_ref[m, :, 0:width])
        full = dx_ref[m, :, 0:width] + mm(low[:, 0:EXPERTS], router_ref[...])
        state = hs_ref[m]
        scale = lax.rsqrt(jnp.mean(state * state, axis=1, keepdims=True) + epsilon)
        u = full * gain_f[...].reshape(1, width)
        common = jnp.mean(u * state, axis=1, keepdims=True) * (scale * scale * scale)
        total = g_ref[m].astype(f32) + (scale * u - state * common)
        sg[m] = total
        a_ref[here, :] = total.astype(bf)
        gain_row = gain_row + jnp.sum(full * state * scale, axis=0, keepdims=True)
    s_ref[0:EXPERTS, :] = router_row[0:EXPERTS].astype(bf)
    factor(3, a_ref, fg)
    factor(0, n_ref, fn)
    relay(2, fa)

    def inward(i):
        at = cols(i, tw)
        both = mm_nt(a_ref[...], wo_ref[at, :]).astype(bf)
        for m in range(micro):
            for j in range(tw // head):
                to = pl.ds(pl.multiple_of((i * (tw // head) + j) * length, length), length)
                ag[m, to, :] = both[m * length : (m + 1) * length, j * head : (j + 1) * head]

    tiles(wq // tw, inward)
    relay(3, fg)

    def unrope(u, m):
        return u * tab_ref[m, 0] - pltpu.roll(u, head // 2, 1) * tab_ref[m, 1]

    for m in range(micro):
        here = slice(m * length, (m + 1) * length)
        prob = pr_ref[m]
        back = mm_nt(ag[m], v_ref[m])
        shared = jnp.sum(prob * back, axis=1, keepdims=True)
        low = (prob * (back - shared)).astype(bf)
        dq = mm(low, k_ref[m]) * (head**-0.5)
        for h in range(heads):
            u = unrope(dq[h * length : (h + 1) * length], m)
            d_ref[here, h * head : (h + 1) * head] = u.astype(bf)
        dk = mm_tn(low, q_ref[m]) * (head**-0.5)
        d_ref[here, wq : wq + head] = unrope(dk, m).astype(bf)
        d_ref[here, wq + head : wq + 2 * head] = mm_tn(prob.astype(bf), ag[m]).astype(bf)
    factor(1, d_ref, fd)
    relay(0, fn)
    got_part = []
    for j in range(3):

        def outward(i, j=j):
            at = cols(i + j * (nt // 3), tw)
            own_part[:, at] = (
                mm_nt(d_ref[:, 0:wq], wq_ref[at, :])
                + mm_nt(d_ref[:, wq : wq + head], wk_ref[at, :])
                + mm_nt(d_ref[:, wq + head :], wv_ref[at, :])
            )

        tiles(nt // 3, outward)
        at = pl.ds(j * (width // 3), width // 3)
        cp = remote(
            own_part.at[:, at], other_part.at[:, at], part_s.at[j], part_r.at[j], (e, 1 - c)
        )
        cp.start()
        sent.append(cp)
        got_part.append(cp)
    fn[0:rows, :] = n_ref[:, part(qx, wn)]
    fd[0:rows, :] = d_ref[:, part(qy, wd)]
    fa[0:rows, :] = att_ref[:, part(qy, wa)]
    fg[0:rows, :] = a_ref[:, part(qx, wg)]
    arrive(2, fa)
    arrive(3, fg)

    def two(i):
        at = cols(i, tw)
        pb[:, at] = mm_tn(fa[...], fg[:, at]).astype(bf)

    tiles(wg // tw, two)
    got_y = {}

    def spread(i):
        src, dst, size, rest = ((pa, za, ha, ra), (pb, zb, hb, rb))[i]
        far = lax.rem(z + jnp.where(z == 0, 3, 1), 4)
        cp = remote(src.at[part(far, size), :], rest, l_s.at[i], l_r.at[i], beside_dev)
        start_if(edge, cp)
        got_y[("far", i)] = cp
        for k in (1, 3):
            cp = remote(
                src.at[part(lax.rem(z + k, 4), size), :], dst.at[k],
                y_s.at[k * 3 + i], y_r.at[k * 3 + i], z_dev(k),
            )
            start_if(not_last if k == 1 else not_first, cp)
            got_y[(i, k)] = cp

    def spread_rest(i):
        src, dst, size, rest = ((pa, za, ha, ra), (pb, zb, hb, rb))[i]
        across = part(lax.rem(z + 2, 4), size)

        @pl.when(inner)
        def _():
            got_y[("far", i)].wait_recv()
            src[across, :] = (src[across, :].astype(f32) + rest[...].astype(f32)).astype(bf)

        cp = remote(src.at[across, :], dst.at[2], y_s.at[6 + i], y_r.at[6 + i], z_dev(2))
        cp.start()
        sent.append(cp)
        got_y[(i, 2)] = cp

    spread(1)
    relay(1, fd)
    for cp in got_part:
        cp.wait_recv()
    last_row = jnp.zeros((1, width), f32)
    for m in range(micro):
        here = slice(m * length, (m + 1) * length)
        full = own_part[here, :] + other_part[here, :]
        state = tok_ref[m].astype(f32)
        scale = lax.rsqrt(jnp.mean(state * state, axis=1, keepdims=True) + epsilon)
        u = full * gain_a[...].reshape(1, width)
        common = jnp.mean(u * state, axis=1, keepdims=True) * (scale * scale * scale)
        tg_ref[m] = sg[m] + (scale * u - state * common)
        last_row = last_row + jnp.sum(full * state * scale, axis=0, keepdims=True)
    index = lax.broadcasted_iota(jnp.int32, (hs, 1), 0)
    s_ref[2 * hs : 3 * hs, :] = jnp.where(
        index == 0, gain_row, jnp.where(index == 1, last_row, 0.0)
    ).astype(bf)
    got_s = []
    for d in (3, 1, 2):
        to = flip(qy, d // 2) * 2 + flip(qx, d % 2)
        cp = remote(s_ref.at[part(to, hs), :], fs.at[d], c_s.at[d], c_r.at[d], p_dev(d))
        cp.start()
        sent.append(cp)
        got_s.append(cp)
    spread_rest(1)
    arrive(0, fn)
    arrive(1, fd)

    def one(i):
        at = cols(i, tw)
        pa[:, at] = mm_tn(fn[...], fd[:, at]).astype(bf)

    tiles(wd // tw, one)
    spread(0)
    total = s_ref[part(q, hs), :].astype(jnp.float32)
    for cp in got_s:
        cp.wait_recv()
    for d in range(1, 4):
        total = total + fs[d].astype(jnp.float32)
    fs[0] = total.astype(jnp.bfloat16)
    for k in (2, 1, 3):
        cp = remote(
            fs.at[0, :, part(lax.rem(z + k, 4), ws)], zs.at[k],
            y_s.at[k * 3 + 2], y_r.at[k * 3 + 2], z_dev(k),
        )
        cp.start()
        sent.append(cp)
        got_y[(2, k)] = cp
    spread_rest(0)

    def spots(px, py, t):
        return (
            oa.at[part(px * 4 + t, ha), part(py, wd)],
            ob.at[part(py * 4 + t, hb), part(px, wg)],
            os.at[part(py * 2 + px, hs), part(t, ws)],
        )

    home = spots(qx, qy, z)

    def total_of(i):
        first, others = (
            (pa[part(z, ha), :], za), (pb[part(z, hb), :], zb), (fs[0, :, part(z, ws)], zs),
        )[i]
        if i < 2:
            pl.when(not_first)(got_y[(i, 1)].wait_recv)
            pl.when(not_last)(got_y[(i, 3)].wait_recv)
        else:
            got_y[(i, 1)].wait_recv()
            got_y[(i, 3)].wait_recv()
        got_y[(i, 2)].wait_recv()
        acc = first.astype(f32)
        for k in range(1, 4):
            acc = acc + others[k].astype(f32)
        home[i][...] = acc.astype(bf)
        for k in (2, 1, 3):
            cp = remote(home[i], home[i], z_s.at[k * 3 + i], z_r.at[k * 3 + i], z_dev(k))
            if k == 2:
                cp.start()
                sent.append(cp)
            else:
                start_if(not_last if k == 1 else not_first, cp)

    turns = (
        0,
        jnp.where(inner, 2, jnp.where(z == 0, 3, 1)),
        jnp.where(inner, 1, 2),
        jnp.where(inner, 3, jnp.where(z == 0, 1, 3)),
    )
    got_p = {}

    def send(ref, i, n, d, j):
        at = ((n * 3) + i) * 4 + j
        cp = remote(ref, ref, p_s.at[at], p_r.at[at], p_dev(d))
        cp.start()
        sent.append(cp)
        got_p[(n, i, j)] = cp

    def own(n, i):
        k = turns[n]
        here = spots(qx, qy, lax.rem(z + 4 - k, 4))[i]
        if n:
            cp = remote(here, here, z_s.at[k * 3 + i], z_r.at[k * 3 + i], beside_dev)
            cp.wait_recv()
        if n == 1:
            to = jnp.where(z == 1, 1, 3)
            cp = remote(here, here, h_s.at[i], z_r.at[to * 3 + i], beside_dev)
            start_if(inner, cp)
        send(here, i, n, 1, 1)
        send(here, i, n, 2, 2)

    def forward(n, i):
        t = lax.rem(z + 4 - turns[n], 4)
        if i == 1:
            got_p[(n, i, 2)].wait_recv()
            send(spots(qx, flip(qy, 1), t)[i], i, n, 1, 3)
        else:
            got_p[(n, i, 1)].wait_recv()
            send(spots(flip(qx, 1), qy, t)[i], i, n, 2, 3)

    total_of(1)
    own(0, 1)
    total_of(0)
    own(0, 0)
    total_of(2)
    own(0, 2)
    own(1, 1)
    forward(0, 1)
    own(1, 0)
    forward(0, 0)
    forward(0, 2)
    own(1, 2)
    for n in (2, 3):
        for i in (1, 0, 2):
            own(n, i)
            forward(n - 1, i)
    for i in (1, 0, 2):
        forward(3, i)
    for n in range(4):
        for i in range(3):
            first = 1 if i == 1 else 2
            got_p[(n, i, first)].wait_recv()
            got_p[(n, i, 3)].wait_recv()
    for cp in sent:
        cp.wait_send()
    for cond, cp in sent_if:
        pl.when(cond)(cp.wait_send)


def back_call(
    tokens, cotangent, gain_a, gain_f, wq, wk, wv, wo, router, dx, nrm, att, q, k, v, pr, tab, hs, xrows
):
    bf = jnp.bfloat16
    f32 = jnp.float32
    micro, length, width = tokens.shape
    rows = micro * length
    wd = wq.shape[1] + wk.shape[1] + wv.shape[1]
    wa = wq.shape[1]
    heads = wa // HEAD_SIZE
    vmem = pl.BlockSpec(memory_space=pltpu.VMEM)

    def buf(*shape, dtype=bf):
        return pltpu.VMEM(shape, dtype)

    sem = pltpu.SemaphoreType.DMA
    small = (64, width)
    hsm, wsm = 16, width // 4
    return pl.pallas_call(
        back_kernel,
        out_shape=(
            jax.ShapeDtypeStruct((micro, length, width), f32),
            jax.ShapeDtypeStruct((width, wd), bf),
            jax.ShapeDtypeStruct((wa, width), bf),
            jax.ShapeDtypeStruct(small, bf),
        ),
        in_specs=[vmem] * 19,
        out_specs=(vmem,) * 4,
        scratch_shapes=[
            buf(rows, wd), buf(rows, width), buf(*small), buf(micro, length, width, dtype=f32),
            buf(micro, heads * length, HEAD_SIZE), buf(rows, width, dtype=f32), buf(rows, width, dtype=f32),
            buf(4 * rows, width // 2), buf(4 * rows, wd // 2), buf(4 * rows, wa // 2), buf(4 * rows, width // 2),
            buf(4, hsm, width),
            buf(width // 2, wd // 2), buf(wa // 2, width // 2),
            buf(4, width // 8, wd // 2), buf(4, wa // 8, width // 2), buf(4, hsm, wsm),
            buf(width // 8, wd // 2), buf(wa // 8, width // 2),
            sem((16,)), sem((16,)), sem((16,)), sem((16,)), sem((4,)), sem((4,)), sem((12,)), sem((12,)),
            sem((2,)), sem((2,)), sem((12,)), sem((12,)), sem((3,)), sem((3,)), sem((48,)), sem((48,)),
            sem((3,)), sem((3,)),
        ],
        compiler_params=pltpu.CompilerParams(
            collective_id=2, has_side_effects=True, vmem_limit_bytes=VMEM_LIMIT
        ),
        cost_estimate=pl.CostEstimate(
            flops=2 * rows * 4 * (width * wd + wa * width) // 4, bytes_accessed=20 * 2**20, transcendentals=0
        ),
        name="back",
    )(
        tokens, cotangent, gain_a, gain_f, wq, wk, wv, wo, router,
        dx, nrm.reshape(rows, width), att.reshape(rows, wa), q, k, v, pr, tab, hs, xrows,
    )


def suits(mesh):
    return mesh.shape["expert"] == 16 and mesh.shape["tensor"] == 2


def local_fast(
    tokens, cotangent, positions, routes, attention_gain, feedforward_gain, query_weight, key_matrix,
    value_matrix, output_weight, router_weight, gate_weight, up_weight, down_weight,
):
    micro_count, length, model_width = tokens.shape
    f32 = jnp.float32
    gain_a, gain_f = attention_gain, feedforward_gain
    router_t = router_weight.T
    layer_out, dx, nrm, att, q, k, v, pr, tab, hs, xrows, rx, rh, rg, ru, re = front_call(
        tokens, cotangent, positions, routes.transpose(0, 2, 1), gain_a, gain_f, query_weight, key_matrix,
        value_matrix, output_weight, router_t, gate_weight, up_weight, down_weight,
    )
    tokens_grad, oa, ob, os = back_call(
        tokens, cotangent, gain_a, gain_f, query_weight, key_matrix, value_matrix, output_weight,
        router_t, dx, nrm, att, q, k, v, pr, tab, hs, xrows,
    )
    gate_sum, up_sum, down_sum = grads_call(rx, rh, rg, ru, re)
    wq = query_weight.shape[1]
    wk = wq + key_matrix.shape[1]
    os = os.astype(f32)
    return (
        layer_out,
        tokens_grad,
        os[EXPERTS + 1],
        os[EXPERTS],
        oa[:, :wq].astype(f32),
        oa[:, wq:wk].astype(f32),
        oa[:, wk:].astype(f32),
        ob.astype(f32),
        os[:EXPERTS].T,
        gate_sum,
        up_sum,
        down_sum,
    )


def solution(mesh):
    in_specs = (
        P(None, "expert", None),
        P(None, "expert", None),
        P(None, "expert"),
        P(None, "expert", None),
        P(),
        P(),
        P(None, "tensor"),
        P(None, "tensor"),
        P(None, "tensor"),
        P("tensor", None),
        P(),
        P(None, "expert"),
        P(None, "expert"),
        P("expert", None),
    )
    out_specs = (
        P(None, "expert", None),
        P(None, "expert", None),
        P(),
        P(),
        P(None, "tensor"),
        P(None, "tensor"),
        P(None, "tensor"),
        P("tensor", None),
        P(),
        P(None, "expert"),
        P(None, "expert"),
        P("expert", None),
    )
    body = local_fast if suits(mesh) else local
    return jax.shard_map(body, mesh=mesh, in_specs=in_specs, out_specs=out_specs, check_vma=False)
```

```python
import functools

import jax
import jax.numpy as jnp
from jax import lax
from jax.experimental import pallas as pl
from jax.experimental.pallas import tpu as pltpu
from jax.sharding import PartitionSpec as P

HEAD_SIZE = 128
EXPERTS = 32


epsilon = 1e-05
theta_base = 1000000.0
masked_score = -1e30


def rms_norm(value_row_states, gain_vector):
    return (
        value_row_states
        * lax.rsqrt(jnp.mean(value_row_states * value_row_states, axis=-1, keepdims=True) + epsilon)
        * gain_vector
    )


def gelu_exact(value_row_states):
    return jax.nn.gelu(value_row_states, approximate=False)


def rope_tables(positions, head_dim):
    half_dim = head_dim // 2
    inverse = jnp.exp(
        -jnp.log(theta_base) * (2.0 * jnp.arange(half_dim, dtype=jnp.float32) / head_dim)
    )
    angles = positions.astype(jnp.float32)[:, None] * inverse[None, :]
    return (jnp.cos(angles), jnp.sin(angles))


def widen_table(table_part, value_row_states):
    return table_part.reshape(
        (table_part.shape[0],) + (1,) * (value_row_states.ndim - 2) + (table_part.shape[1],)
    )


def rotary_apply(value_row_states, cosine_table, sine_table):
    half_dim = value_row_states.shape[-1] // 2
    first_part = value_row_states[..., :half_dim]
    second = value_row_states[..., half_dim:]
    cos_wide = widen_table(cosine_table, value_row_states)
    sin_wide = widen_table(sine_table, value_row_states)
    return jnp.concatenate(
        [first_part * cos_wide - second * sin_wide, second * cos_wide + first_part * sin_wide],
        axis=-1,
    )


def unrotate(value_row_states, cosine_table, sine_table):
    half_dim = value_row_states.shape[-1] // 2
    first_part = value_row_states[..., :half_dim]
    second = value_row_states[..., half_dim:]
    cos_wide = widen_table(cosine_table, value_row_states)
    sin_wide = widen_table(sine_table, value_row_states)
    return jnp.concatenate(
        [first_part * cos_wide + second * sin_wide, second * cos_wide - first_part * sin_wide],
        axis=-1,
    )


def block_scores(query_block, key_row_states, starts, row_ids, offset, block_rows, score_scale):
    query_ids = offset + jnp.arange(block_rows, dtype=jnp.int32)
    allowed = (row_ids[None, :] <= query_ids[:, None]) & (row_ids[None, :] >= starts[:, None])
    scores = (
        jnp.einsum(
            "qcgd,kcd->cgqk", query_block, key_row_states, preferred_element_type=jnp.float32
        )
        * score_scale
    )
    return jnp.where(allowed, scores, masked_score)


def attention_forward(
    query_rows, key_row_states, value_rows, starts, row_ids, block_rows, score_scale
):

    def one_block(block_index):
        offset = block_index * block_rows
        scores = block_scores(
            query_rows, key_row_states, starts, row_ids, offset, block_rows, score_scale
        )
        row_peak = jnp.max(scores, axis=-1, keepdims=True)
        weights = jnp.exp(scores - row_peak)
        totals = jnp.sum(weights, axis=-1, keepdims=True)
        prob_low = (weights / totals).astype(jnp.bfloat16)
        attention_output = jnp.einsum(
            "cgqk,kcd->qcgd", prob_low, value_rows, preferred_element_type=jnp.float32
        )
        return (attention_output.astype(jnp.bfloat16), row_peak[..., 0] + jnp.log(totals[..., 0]))

    return lax.map(one_block, jnp.arange(query_rows.shape[0] // block_rows, dtype=jnp.int32))


def attention_backward(
    query_rows,
    key_row_states,
    value_rows,
    starts,
    row_ids,
    block_rows,
    score_scale,
    log_totals,
    attended_grad,
):

    def one_block(carried, block_index):
        key_grad, value_grad = carried
        offset = block_index * block_rows
        scores = block_scores(
            query_rows, key_row_states, starts, row_ids, offset, block_rows, score_scale
        )
        probs = jnp.exp(scores - log_totals[block_index][..., None])
        prob_low = probs.astype(jnp.bfloat16)
        prob_grad = jnp.einsum(
            "qcgd,kcd->cgqk", attended_grad, value_rows, preferred_element_type=jnp.float32
        )
        row_dot = jnp.sum(probs * prob_grad, axis=-1, keepdims=True)
        score_grad = (probs * (prob_grad - row_dot)).astype(jnp.bfloat16)
        query_grad = (
            jnp.einsum(
                "cgqk,kcd->qcgd", score_grad, key_row_states, preferred_element_type=jnp.float32
            )
            * score_scale
        )
        key_grad = (
            key_grad
            + jnp.einsum(
                "cgqk,qcgd->kcd", score_grad, query_rows, preferred_element_type=jnp.float32
            )
            * score_scale
        )
        value_grad = value_grad + jnp.einsum(
            "cgqk,qcgd->kcd", prob_low, attended_grad, preferred_element_type=jnp.float32
        )
        return ((key_grad, value_grad), query_grad)

    empty_grad = jnp.zeros(key_row_states.shape, jnp.float32)
    totals_out, query_grad = lax.scan(
        one_block,
        (empty_grad, empty_grad),
        jnp.arange(query_rows.shape[0] // block_rows, dtype=jnp.int32),
    )
    return (query_grad.reshape(query_rows.shape), totals_out[0], totals_out[1])


def spread_rows(base, group, capacity, n_dev, per_dev, width):
    widened = jnp.broadcast_to(
        base.reshape(EXPERTS, 1, capacity, width), (EXPERTS, group, capacity, width)
    )
    return widened.reshape(n_dev, per_dev * capacity, width)


def collect_rows(back, group, capacity, width, slot_index, rows, top_count):
    summed = jnp.sum(back.reshape(EXPERTS, group, capacity, width), axis=1).astype(jnp.bfloat16)
    return (
        summed.reshape(EXPERTS * capacity, width)[slot_index]
        .reshape(rows, top_count, width)
        .astype(jnp.float32)
    )


def local(
    tokens,
    cotangent,
    positions,
    routes,
    attention_gain,
    feedforward_gain,
    query_weight,
    key_matrix,
    value_matrix,
    output_weight,
    router_weight,
    gate_weight,
    up_weight,
    down_weight,
):
    micro_count, length, model_width = tokens.shape
    head_dim = HEAD_SIZE
    kv_local = key_matrix.shape[1] // head_dim
    query_group_count = query_weight.shape[1] // head_dim // kv_local
    top_count = routes.shape[2]
    n_dev = lax.axis_size("expert")
    n_tensor = lax.axis_size("tensor")
    half = length // n_tensor
    offset = lax.axis_index("tensor") * half
    per_dev = max(1, EXPERTS // n_dev)
    group = max(1, n_dev // EXPERTS)
    local_width = gate_weight.shape[1]
    ff_local = local_width // per_dev
    capacity = max(2, 3 * half * top_count // (2 * EXPERTS))
    block_rows = min(512, length)
    score_scale = head_dim ** (-0.5)
    expert_ids = jnp.arange(EXPERTS, dtype=jnp.int32)
    row_ids = jnp.arange(length, dtype=jnp.int32)
    gate_three = gate_weight.reshape(model_width, per_dev, ff_local)
    up_three = up_weight.reshape(model_width, per_dev, ff_local)
    down_three = down_weight.reshape(per_dev, ff_local, model_width)
    query_sum = jnp.zeros(query_weight.shape, jnp.float32)
    key_sum = jnp.zeros(key_matrix.shape, jnp.float32)
    value_sum = jnp.zeros(value_matrix.shape, jnp.float32)
    output_sum = jnp.zeros(output_weight.shape, jnp.float32)
    router_sum = jnp.zeros(router_weight.shape, jnp.float32)
    attn_gain_sum = jnp.zeros(attention_gain.shape, jnp.float32)
    ffn_gain_sum = jnp.zeros(feedforward_gain.shape, jnp.float32)
    gate_sum = jnp.zeros(gate_weight.shape, jnp.float32)
    up_sum = jnp.zeros(up_weight.shape, jnp.float32)
    down_sum = jnp.zeros(down_weight.shape, jnp.float32)
    layer_outputs = []
    input_grads = []
    for micro_index in range(micro_count):
        states = tokens[micro_index].astype(jnp.float32)
        out_grad = cotangent[micro_index].astype(jnp.float32)
        place = positions[micro_index]
        chosen = routes[micro_index]
        starts = row_ids - place
        cosine_table, sine_table = rope_tables(place, head_dim)
        normed_full, attn_norm_pull = jax.vjp(rms_norm, states, attention_gain)
        normalized_input = normed_full.astype(jnp.bfloat16)
        query_pre = jnp.dot(
            normalized_input, query_weight, preferred_element_type=jnp.float32
        ).reshape(length, kv_local, query_group_count, head_dim)
        query_rows = rotary_apply(query_pre, cosine_table, sine_table).astype(jnp.bfloat16)
        key_pre = jnp.dot(normalized_input, key_matrix, preferred_element_type=jnp.float32).reshape(
            length, kv_local, head_dim
        )
        key_row_states = rotary_apply(key_pre, cosine_table, sine_table).astype(jnp.bfloat16)
        value_rows = (
            jnp.dot(normalized_input, value_matrix, preferred_element_type=jnp.float32)
            .astype(jnp.bfloat16)
            .reshape(length, kv_local, head_dim)
        )
        attention_output, log_totals = attention_forward(
            query_rows, key_row_states, value_rows, starts, row_ids, block_rows, score_scale
        )
        attention_output = attention_output.reshape(length, kv_local * query_group_count * head_dim)
        attn_part = jnp.dot(attention_output, output_weight, preferred_element_type=jnp.float32)
        hidden_state = states + lax.psum(attn_part, "tensor")
        normed_ffn_full, ffn_norm_pull = jax.vjp(rms_norm, hidden_state, feedforward_gain)
        normed_ffn = normed_ffn_full.astype(jnp.bfloat16)
        state_half = lax.dynamic_slice_in_dim(normed_ffn, offset, half, 0)
        route_half = lax.dynamic_slice_in_dim(chosen, offset, half, 0)
        grad_half = lax.dynamic_slice_in_dim(out_grad, offset, half, 0)
        route_mask = (route_half[..., None] == expert_ids[None, None, :]).astype(jnp.float32)

        def gate_softmax(logits, route_mask=route_mask):
            return jax.nn.softmax(jnp.sum(logits[:, None, :] * route_mask, axis=-1), axis=-1)

        logits = jnp.dot(state_half, router_weight, preferred_element_type=jnp.float32)
        gate_probs, gate_pull = jax.vjp(gate_softmax, logits)
        flat_routes = route_half.reshape(-1)
        route_onehot = (flat_routes[:, None] == expert_ids[None, :]).astype(jnp.int32)
        ahead = jnp.tril(jnp.ones((half * top_count, half * top_count), jnp.float32), -1)
        ranks = jnp.sum(
            jnp.dot(ahead, route_onehot.astype(jnp.float32)).astype(jnp.int32) * route_onehot, axis=1
        )
        slot_index = flat_routes * capacity + ranks
        copies = jnp.repeat(state_half, top_count, axis=0)
        send_rows = (
            jnp.zeros((EXPERTS * capacity, model_width), jnp.bfloat16).at[slot_index].set(copies)
        )
        received = lax.all_to_all(
            spread_rows(send_rows, group, capacity, n_dev, per_dev, model_width),
            "expert",
            split_axis=0,
            concat_axis=0,
            tiled=True,
        ).reshape(n_dev, per_dev, capacity, model_width)
        gate_pre = jnp.einsum(
            "skcd,dkf->skcf", received, gate_three, preferred_element_type=jnp.float32
        )
        up_pre = jnp.einsum(
            "skcd,dkf->skcf", received, up_three, preferred_element_type=jnp.float32
        )
        activated, gelu_pull = jax.vjp(gelu_exact, gate_pre)
        expert_hidden = (activated * up_pre).astype(jnp.bfloat16)
        partial_out = jnp.einsum(
            "skcf,kfd->skcd", expert_hidden, down_three, preferred_element_type=jnp.float32
        )
        back_rows = lax.all_to_all(
            partial_out.reshape(n_dev, per_dev * capacity, model_width).astype(jnp.bfloat16),
            "expert",
            split_axis=0,
            concat_axis=0,
            tiled=True,
        ).astype(jnp.float32)
        returned_rows = collect_rows(
            back_rows, group, capacity, model_width, slot_index, half, top_count
        )
        mixture_half = jnp.sum(gate_probs[..., None] * returned_rows, axis=1)
        mixture = lax.all_gather(
            mixture_half.astype(jnp.bfloat16), "tensor", axis=0, tiled=True
        ).astype(mixture_half.dtype)
        layer_outputs.append((hidden_state + mixture).astype(jnp.bfloat16))
        gate_grad = jnp.sum(grad_half[:, None, :] * returned_rows, axis=-1)
        row_grad = (
            (gate_probs[..., None] * grad_half[:, None, :])
            .astype(jnp.bfloat16)
            .reshape(-1, model_width)
        )
        send_grad = (
            jnp.zeros((EXPERTS * capacity, model_width), jnp.bfloat16).at[slot_index].set(row_grad)
        )
        grad_received = lax.all_to_all(
            spread_rows(send_grad, group, capacity, n_dev, per_dev, model_width),
            "expert",
            split_axis=0,
            concat_axis=0,
            tiled=True,
        ).reshape(n_dev, per_dev, capacity, model_width)
        hidden_grad = jnp.einsum(
            "skcd,kfd->skcf", grad_received, down_three, preferred_element_type=jnp.float32
        )
        down_part = jnp.einsum(
            "skcf,skcd->kfd", expert_hidden, grad_received, preferred_element_type=jnp.float32
        ).reshape(down_weight.shape)
        gate_pre_grad = gelu_pull(hidden_grad * up_pre)[0].astype(jnp.bfloat16)
        up_pre_grad = (hidden_grad * activated).astype(jnp.bfloat16)
        gate_part = jnp.einsum(
            "skcd,skcf->dkf", received, gate_pre_grad, preferred_element_type=jnp.float32
        ).reshape(gate_weight.shape)
        up_part = jnp.einsum(
            "skcd,skcf->dkf", received, up_pre_grad, preferred_element_type=jnp.float32
        ).reshape(up_weight.shape)
        input_part = jnp.einsum(
            "skcf,dkf->skcd", gate_pre_grad, gate_three, preferred_element_type=jnp.float32
        )
        input_part = input_part + jnp.einsum(
            "skcf,dkf->skcd", up_pre_grad, up_three, preferred_element_type=jnp.float32
        )
        input_back = lax.all_to_all(
            input_part.reshape(n_dev, per_dev * capacity, model_width).astype(jnp.bfloat16),
            "expert",
            split_axis=0,
            concat_axis=0,
            tiled=True,
        ).astype(jnp.float32)
        route_input = collect_rows(
            input_back, group, capacity, model_width, slot_index, half, top_count
        )
        logit_grad = gate_pull(gate_grad)[0].astype(jnp.bfloat16)
        router_part = jnp.dot(state_half.T, logit_grad, preferred_element_type=jnp.float32)
        ffn_half_grad = jnp.sum(route_input, axis=1) + jnp.dot(
            logit_grad, router_weight.T, preferred_element_type=jnp.float32
        )
        gate_sum = gate_sum + gate_part
        up_sum = up_sum + up_part
        down_sum = down_sum + down_part
        router_sum = router_sum + router_part
        normed_ffn_grad = lax.all_gather(ffn_half_grad, "tensor", axis=0, tiled=True)
        state_norm_grad, ffn_gain_grad = ffn_norm_pull(normed_ffn_grad)
        state_grad = out_grad + state_norm_grad
        ffn_gain_sum = ffn_gain_sum + ffn_gain_grad
        attention_grad = state_grad.astype(jnp.bfloat16)
        output_sum = output_sum + jnp.dot(
            attention_output.T, attention_grad, preferred_element_type=jnp.float32
        )
        attended_grad = (
            jnp.dot(attention_grad, output_weight.T, preferred_element_type=jnp.float32)
            .astype(jnp.bfloat16)
            .reshape(length, kv_local, query_group_count, head_dim)
        )
        query_grad, key_grad, value_grad = attention_backward(
            query_rows,
            key_row_states,
            value_rows,
            starts,
            row_ids,
            block_rows,
            score_scale,
            log_totals,
            attended_grad,
        )
        query_grad = (
            unrotate(query_grad, cosine_table, sine_table).astype(jnp.bfloat16).reshape(length, -1)
        )
        key_grad = (
            unrotate(key_grad, cosine_table, sine_table).astype(jnp.bfloat16).reshape(length, -1)
        )
        value_grad = value_grad.astype(jnp.bfloat16).reshape(length, -1)
        query_sum = query_sum + jnp.dot(
            normalized_input.T, query_grad, preferred_element_type=jnp.float32
        )
        key_sum = key_sum + jnp.dot(
            normalized_input.T, key_grad, preferred_element_type=jnp.float32
        )
        value_sum = value_sum + jnp.dot(
            normalized_input.T, value_grad, preferred_element_type=jnp.float32
        )
        normed_part = jnp.dot(query_grad, query_weight.T, preferred_element_type=jnp.float32)
        normed_part = normed_part + jnp.dot(
            key_grad, key_matrix.T, preferred_element_type=jnp.float32
        )
        normed_part = normed_part + jnp.dot(
            value_grad, value_matrix.T, preferred_element_type=jnp.float32
        )
        normed_grad = lax.psum(normed_part, "tensor")
        state_in_grad, attn_gain_grad = attn_norm_pull(normed_grad)
        attn_gain_sum = attn_gain_sum + attn_gain_grad
        input_grads.append(state_grad + state_in_grad)
    gate_sum, up_sum, down_sum, router_sum = lax.psum(
        (gate_sum, up_sum, down_sum, router_sum), "tensor"
    )
    reduced = lax.psum(
        (query_sum, key_sum, value_sum, output_sum, router_sum, attn_gain_sum, ffn_gain_sum),
        "expert",
    )
    return (
        jnp.stack(layer_outputs),
        jnp.stack(input_grads),
        reduced[5],
        reduced[6],
        reduced[0],
        reduced[1],
        reduced[2],
        reduced[3],
        reduced[4],
        gate_sum,
        up_sum,
        down_sum,
    )


MESH = pl.DeviceIdType.MESH
ANY = pl.ANY
VMEM_LIMIT = 60 * 2**20


def mm(a, b):
    return lax.dot_general(a, b, (((1,), (0,)), ((), ())), preferred_element_type=jnp.float32)


def mm_nt(a, b):
    return lax.dot_general(a, b, (((1,), (1,)), ((), ())), preferred_element_type=jnp.float32)


def mm_tn(a, b):
    return lax.dot_general(a, b, (((0,), (0,)), ((), ())), preferred_element_type=jnp.float32)


def remote(src, dst, send_sem, recv_sem, device):
    return pltpu.make_async_remote_copy(
        src_ref=src,
        dst_ref=dst,
        send_sem=send_sem,
        recv_sem=recv_sem,
        device_id=device,
        device_id_type=MESH,
    )


def tiles(count, body):
    def step(i, carry):
        body(i)
        return carry

    lax.fori_loop(0, count, step, 0)


def cols(i, width):
    return pl.ds(pl.multiple_of(i * width, width), width)


def front_kernel(
    tok_hbm, g_hbm, wq_hbm, wk_hbm, wv_hbm, wo_hbm, wg_hbm, wu_hbm, wd_hbm,
    pos_ref, routes_ref, gain_a, gain_f, router_ref,
    dx_ref, nrm_hbm, att_hbm, q_hbm, k_hbm, v_hbm, pr_hbm, tab_hbm, hs_hbm, x_hbm, y0_hbm, y1_hbm, hot_hbm,
    fn, fa, rx_ref, rh_ref, rg_ref, ru_ref, re_ref,
    tok_ref, wq_ref, wk_ref, wv_ref, wo_ref, nrm_ref, att_ref, q_ref, k_ref, v_ref, pr_ref, tab_ref, hs_ref, x_ref,
    xz, gz, rz, xs, gs, xr, gr, eg, hid, gpg, upg, y0r, dr, dz, own_part, other_part, rel,
    onehot, prob, gg, wg, wu, wd,
    r_s, r_r, za_s, za_r, xa_s, xa_r, xb_s, xb_r, zb_s, zb_r, pair_s, pair_r, part_s, part_r, fw_s, rel_s, rel_r,
    f_s, f_r, w_s, w_r, in_sem, out_sem, own_sem,
):
    ys, ds_, zd = gs, xs, xz
    e = lax.axis_index("expert")
    c = lax.axis_index("tensor")
    z = e // 4
    o = lax.rem(e, 4) * 2 + c
    micro, length, width = tok_ref.shape
    half = length // 2
    f32 = jnp.float32
    bf = jnp.bfloat16
    ff = wg.shape[1]
    col = 4 * half
    rows = xs.shape[1]
    blk = rows // 8
    cap = blk // 4
    me = 2 * e + c
    tw = 256
    nt = width // tw

    def z_dev(k):
        return (lax.rem(z + k, 4) * 4 + lax.rem(e, 4), c)

    def z_back(k):
        return (lax.rem(z + 4 - k, 4) * 4 + lax.rem(e, 4), c)

    def p_dev(d):
        t = lax.rem(o + d, 8)
        return (z * 4 + t // 2, lax.rem(t, 2))

    def p_back(d):
        t = lax.rem(o + 8 - d, 8)
        return (z * 4 + t // 2, lax.rem(t, 2))

    inner = (z == 1) | (z == 2)
    edge = (z == 0) | (z == 3)
    not_first = z != 0
    not_last = z != 3
    beside = jnp.where((z == 0) | (z == 3), jnp.where(z == 0, 1, 2), jnp.where(z == 1, 0, 3))
    beside_dev = (beside * 4 + lax.rem(e, 4), c)
    far_slot = jnp.where(z == 1, 1, 3)
    far_back = jnp.where(z == 0, 1, 3)

    @pl.when(z == 3)
    def _():
        for m in range(micro):
            dz[m, half : 2 * half, :] = jnp.zeros((half, width + 128), bf)

    @pl.when(z == 0)
    def _():
        for m in range(micro):
            dz[m, 3 * half : 4 * half, :] = jnp.zeros((half, width + 128), bf)

    barrier = pltpu.get_barrier_semaphore()
    for k in range(1, 4):
        pl.semaphore_signal(barrier, inc=1, device_id=z_dev(k), device_id_type=MESH)
    for d in range(1, 8):
        pl.semaphore_signal(barrier, inc=1, device_id=p_dev(d), device_id_type=MESH)
    loads = {}
    for i, (name, src, dst) in enumerate(
        (
            ("tok", tok_hbm, tok_ref), ("wq", wq_hbm, wq_ref), ("wk", wk_hbm, wk_ref), ("wv", wv_hbm, wv_ref),
            ("wo", wo_hbm, wo_ref), ("wg", wg_hbm.at[:, cols(c, ff)], wg), ("wu", wu_hbm.at[:, cols(c, ff)], wu),
            ("wd", wd_hbm.at[cols(c, ff), :], wd),
        )
    ):
        loads[name] = pltpu.make_async_copy(src, dst, in_sem.at[i])
        loads[name].start()
    saves = []

    def save(src, dst):
        cp = pltpu.make_async_copy(src, dst, out_sem.at[len(saves)])
        cp.start()
        saves.append(cp)

    pl.semaphore_wait(barrier, 10)

    mine = pl.ds(pl.multiple_of(c * half, half), half)
    sent = []
    got_r = []
    for k in range(1, 4):
        cp = remote(routes_ref, rz.at[k], r_s.at[k], r_r.at[k], z_dev(k))
        cp.start()
        sent.append(cp)
        got_r.append(cp)
    got_z = {}

    sent_if = []
    away = {}
    got_f = {}

    def start_if(cond, cp):
        pl.when(cond)(cp.start)
        sent_if.append((cond, cp))

    cut = width // 2
    parts = (((0, width),), ((0, cut), (cut, width + 128 - cut)))

    def sem_of(m, a, j, k, per):
        return ((m * 2 + a) * 2 + j) * per + k

    def z_send(m, a):
        src, dst = ((g_hbm, gz), (x_ref, xz))[a]
        for j, (left, size) in enumerate(parts[a]):
            wide = pl.ds(left, size)
            for k in (2, 1, 3):
                i = sem_of(m, a, j, k, 4)
                cp = remote(
                    src.at[m, mine, wide], dst.at[m, pl.ds(k * half, half), wide],
                    za_s.at[i], za_r.at[i], z_dev(k),
                )
                cond = {1: not_last, 2: True, 3: not_first}[k]
                if k == 2:
                    cp.start()
                else:
                    pl.when(cond)(cp.start)
                got_z[(m, a, j, k)] = cp
                away.setdefault((m, a), []).append((cond, cp))
        if a == 1:
            dst[m, 0:half, :] = src[m, mine, :]
        else:
            cp = pltpu.make_async_copy(src.at[m, mine, :], dst.at[m, 0:half, :], in_sem.at[8 + m])
            cp.start()
            loads[("g", m)] = cp

    def z_sent(m, a):
        for cond, cp in away.pop((m, a)):
            if cond is True:
                cp.wait_send()
            else:
                pl.when(cond)(cp.wait_send)

    def z_forward(m, a):
        dst = (gz, xz)[a]
        for j, (left, size) in enumerate(parts[a]):
            wide = pl.ds(left, size)
            got_z[(m, a, j, 2)].wait_recv()
            cp = remote(
                dst.at[m, pl.ds(2 * half, half), wide],
                dst.at[m, pl.ds(pl.multiple_of(far_slot * half, half), half), wide],
                fw_s.at[sem_of(m, a, j, 0, 1)], za_r.at[sem_of(m, a, j, 0, 4) + far_slot], beside_dev,
            )
            pl.when(inner)(cp.start)
            got_f[(m, a, j)] = cp

    z_send(0, 0)
    rz[0] = routes_ref[...]

    qx = lax.rem(e, 2)
    qy = lax.rem(e, 4) // 2
    every = micro * length
    twin = (e, 1 - c)
    got_a = {}

    def f_dev(d):
        return (z * 4 + lax.rem(qy + d // 2, 2) * 2 + lax.rem(qx + d % 2, 2), c)

    def block(d):
        return pl.ds(pl.multiple_of(d * every + c * length, length), length)

    def factor(i, dst):
        for d in (1, 2):
            if i == 0:
                size = width // 2
                view = nrm_ref.at[c, :, cols(lax.rem(qx + d % 2, 2), size)]
                to = dst.at[block(d), :]
                copies = [(view, to)]
            else:
                size = att_ref.shape[2] // 2
                at = cols(lax.rem(qy + d // 2, 2), size)
                copies = [
                    (att_ref.at[m, :, at], dst.at[pl.ds(d * every + m * length, length), :])
                    for m in range(micro)
                ]
            for m, (view, to) in enumerate(copies):
                n = (d * 2 + i // 2) * 2 + m
                cp = remote(view, to, f_s.at[n], f_r.at[n], f_dev(d))
                cp.start()
                sent.append(cp)
                got_a[(i, d, m)] = cp

    def to_twin(d):
        got_a[(0, d, 0)].wait_recv()
        cp = remote(fn.at[block(d), :], fn.at[block(d), :], w_s.at[d], w_r.at[d], twin)
        cp.start()
        sent.append(cp)
        got_a[("twin", d)] = cp

    def pass_on():
        to_twin(1)
        to_twin(2)
        cp = remote(fn.at[block(1), :], fn.at[block(3), :], f_s.at[12], f_r.at[12], f_dev(2))
        cp.start()
        sent.append(cp)
        got_a[(0, 3, 0)] = cp
        for m in range(micro):
            got_a[(2, 2, m)].wait_recv()
        cp = remote(
            fa.at[pl.ds(2 * every, every), :], fa.at[pl.ds(3 * every, every), :], f_s.at[13], f_r.at[13], f_dev(1)
        )
        cp.start()
        sent.append(cp)
        got_a[(2, 3, 0)] = cp

    head = HEAD_SIZE
    heads = wq_ref.shape[1] // head
    lane = lax.broadcasted_iota(jnp.int32, (1, 128), 1)
    row = lax.broadcasted_iota(jnp.int32, (length, length), 0)
    column = lax.broadcasted_iota(jnp.int32, (length, length), 1)
    turn = jnp.exp(
        (-2.0 / head * jnp.log(jnp.float32(theta_base))) * lax.rem(lane, head // 2).astype(f32)
    )
    allowed = []
    loads["tok"].wait()
    for m in range(micro):
        states = tok_ref[m].astype(f32)
        scale = lax.rsqrt(jnp.mean(states * states, axis=1, keepdims=True) + epsilon)
        nrm_ref[m] = (states * scale * gain_a[...].reshape(1, width)).astype(bf)
        place = pos_ref[m : m + 1, :].astype(f32)
        place = jnp.sum(jnp.where(row == column, place, 0.0), axis=1, keepdims=True)
        angle = place * turn
        tab_ref[m, 0] = jnp.cos(angle)
        tab_ref[m, 1] = jnp.where(lane < head // 2, -1.0, 1.0) * jnp.sin(angle)
        allowed.append((column <= row) & (column >= row - place.astype(jnp.int32)))

    def rope(u, m):
        return u * tab_ref[m, 0] + pltpu.roll(u, head // 2, 1) * tab_ref[m, 1]

    factor(0, fn)
    save(nrm_ref, nrm_hbm)
    save(tab_ref, tab_hbm)
    everything = nrm_ref[...].reshape(micro * length, width)

    def project(i):
        both = mm(everything, wq_ref[:, cols(i, tw)])
        for m in range(micro):
            for j in range(tw // head):
                at = pl.ds(pl.multiple_of((i * (tw // head) + j) * length, length), length)
                u = both[m * length : (m + 1) * length, j * head : (j + 1) * head]
                q_ref[m, at, :] = rope(u, m).astype(bf)

    for name in ("wq", "wk", "wv"):
        loads[name].wait()
    tiles(wq_ref.shape[1] // tw, project)
    key_pre = mm(everything, wk_ref[...])
    value_pre = mm(everything, wv_ref[...])
    for m in range(micro):
        at = slice(m * length, (m + 1) * length)
        k_ref[m] = rope(key_pre[at], m).astype(bf)
        v_ref[m] = value_pre[at].astype(bf)
    for m in range(micro):
        score = mm_nt(q_ref[m], k_ref[m]).reshape(heads, length, length) * (head**-0.5)
        score = jnp.where(allowed[m][None], score, masked_score)
        weight = jnp.exp(score - jnp.max(score, axis=-1, keepdims=True))
        weight = weight / jnp.sum(weight, axis=-1, keepdims=True)
        weight = weight.reshape(heads * length, length)
        pr_ref[m] = weight
        out = mm(weight.astype(bf), v_ref[m]).astype(bf)
        for h in range(heads):
            att_ref[m, :, h * head : (h + 1) * head] = out[h * length : (h + 1) * length]
    for src, dst in ((q_ref, q_hbm), (k_ref, k_hbm), (v_ref, v_hbm), (pr_ref, pr_hbm), (att_ref, att_hbm)):
        save(src, dst)
    factor(2, fa)
    z_forward(0, 0)
    z_sent(0, 0)
    for m in range(1, micro):
        z_send(m, 0)
    loads["wo"].wait()
    att_all = att_ref[...].reshape(micro * length, heads * head)
    got_part = []
    for j in range(3):

        def outward(i, j=j):
            at = cols(i + j * (nt // 3), tw)
            own_part[:, at] = mm(att_all, wo_ref[:, at])

        tiles(nt // 3, outward)
        at = pl.ds(j * (width // 3), width // 3)
        cp = remote(
            own_part.at[:, at], other_part.at[:, at], part_s.at[j], part_r.at[j], (e, 1 - c)
        )
        cp.start()
        sent.append(cp)
        got_part.append(cp)

    for cp in got_r:
        cp.wait_recv()

    before = ((row < column) & (row // half == column // half)).astype(bf)
    expert = 8 * z + lax.rem(o + lax.broadcasted_iota(jnp.int32, (8, length), 0), 8)
    place_row = lax.broadcasted_iota(jnp.int32, (length, col), 0)
    place_col = lax.broadcasted_iota(jnp.int32, (length, col), 1)
    slots = [jnp.zeros((8, col), f32) for _ in range(micro)]
    for k in range(4):
        at = place_col - k * half
        put = ((at >= 0) & (at < half) & (place_row == at + c * half)).astype(bf)
        for m in range(micro):
            named = rz[k, m]
            hit = named[0:1, :] == expert
            for j in range(1, routes_ref.shape[1]):
                hit = hit | (named[j : j + 1, :] == expert)
            mask = jnp.where(hit, 1.0, 0.0)
            rank = mm(mask.astype(bf), before)
            slots[m] = slots[m] + mm((mask * (rank + (cap * k + 1))).astype(bf), put)
    number = lax.broadcasted_iota(jnp.int32, (blk, col), 0) + 1
    for m in range(micro):
        for d in range(8):
            spot = slots[m][d : d + 1, :].astype(jnp.int32)
            onehot[m, d * blk : (d + 1) * blk, :] = jnp.where(spot == number, 1.0, 0.0).astype(
                jnp.bfloat16
            )

    got_p = {}

    def pack(m, a):
        src, out, dst = ((gz, gs, gr), (xz, xs, xr))[a]
        if a == 0:
            loads[("g", m)].wait()
        for j, (left, size) in enumerate(parts[a]):
            for k in (1, 3):
                got_z[(m, a, j, k)].wait_recv()

            def body(i, left=left):
                at = cols(i + left // tw, tw)
                out[m, :, at] = mm(onehot[m], src[m, :, at]).astype(bf)

            tiles(size // tw, body)
            if (left + size) % tw:
                out[m, :, width:] = mm(onehot[m], src[m, :, width:]).astype(bf)
            wide = slice(left, left + size)
            dst[m, 0:blk, wide] = out[m, 0:blk, wide]
            wide = pl.ds(left, size)
            for d in range(1, 8):
                i = sem_of(m, a, j, d, 8)
                at = pl.ds(d * blk, blk)
                cp = remote(
                    out.at[m, at, wide], dst.at[m, at, wide], xa_s.at[i], xa_r.at[i], p_dev(d)
                )
                cp.start()
                sent_p.setdefault((m, a), []).append(cp)
                got_p[(m, a, j, d)] = cp

    sent_p = {}
    pack(0, 0)
    tall = lax.broadcasted_iota(jnp.int32, (128, EXPERTS), 0)
    double = (lax.rem(tall, EXPERTS) == lax.broadcasted_iota(jnp.int32, (128, EXPERTS), 1)) & (
        tall < 2 * EXPERTS
    )
    router = mm(jnp.where(double, 1.0, 0.0).astype(bf), router_ref[...]).astype(bf)
    for cp in got_part:
        cp.wait_recv()
    for m in range(micro):
        at = slice(m * length, (m + 1) * length)
        state = tok_ref[m].astype(f32) + (own_part[at, :] + other_part[at, :])
        hs_ref[m] = state
        save(hs_ref.at[m], hs_hbm.at[m])
        scale = lax.rsqrt(jnp.mean(state * state, axis=1, keepdims=True) + epsilon)
        low = (state * scale * gain_f[...].reshape(1, width)).astype(bf)
        x_ref[m, :, 0:width] = low
        logits = mm_nt(low, router)
        names = lax.rem(lane, EXPERTS)
        hit = lane < 0
        for j in range(routes_ref.shape[1]):
            named = routes_ref[m, j : j + 1, :].astype(f32)
            named = jnp.sum(jnp.where(row == column, named, 0.0), axis=1, keepdims=True)
            hit = hit | (named.astype(jnp.int32) == names)
        hit = hit & (lane < 2 * EXPERTS)
        best = jnp.max(jnp.where(hit, logits, masked_score), axis=1, keepdims=True)
        weight = jnp.where(hit, jnp.exp(logits - best), 0.0)
        first = jnp.sum(jnp.where(lane < EXPERTS, weight, 0.0), axis=1, keepdims=True)
        weight = weight / first
        top = weight.astype(bf).astype(f32)
        x_ref[m, :, width:] = jnp.where(lane < EXPERTS, top, weight - top).astype(bf)
        if m == 0:
            z_send(m, 1)
        save(x_ref.at[m], x_hbm.at[m])
    for m in range(1, micro):
        z_forward(m, 0)
        pack(m, 0)
    pass_on()
    z_forward(0, 1)
    z_sent(0, 1)
    for m in range(1, micro):
        z_send(m, 1)
    pack(0, 1)
    for m in range(1, micro):
        z_forward(m, 1)
        pack(m, 1)
    for name in ("wg", "wu", "wd"):
        loads[name].wait()
    save(onehot.at[1], hot_hbm)

    got_b = {}
    def to_pair(m):
        for i, (src, dst) in enumerate(
            ((xr, rx_ref), (hid, rh_ref), (gpg, rg_ref), (upg, ru_ref), (eg, re_ref))
        ):
            src_at = src.at[m, :, 0:width] if i == 0 else src.at[m]
            n = m * 8 + i
            cp = remote(src_at, dst.at[c, m], pair_s.at[n], pair_r.at[n], (e, 1 - c))
            cp.start()
            sent.append(cp)
            got_b[("pair", m, i)] = cp
            cp = pltpu.make_async_copy(src_at, dst.at[c, m], own_sem.at[n])
            cp.start()
            saves.append(cp)

    def send_back(m, a, j):
        src, dst = ((ds_.at[m], dr.at[m]), (ys.at[m], y0r))[a]
        left, size = parts[1 - a][j]
        wide = slice(left, left + size)
        dst[0:blk, wide] = src[0:blk, wide]
        wide = pl.ds(left, size)
        for d in range(1, 8):
            i = sem_of(m, a, j, d, 8)
            at = pl.ds(d * blk, blk)
            cp = remote(src.at[at, wide], dst.at[at, wide], xb_s.at[i], xb_r.at[i], p_back(d))
            cp.start()
            sent.append(cp)
            got_b[(m, a, j, d)] = cp

    def run(m):
        for a in range(2):
            for j in range(len(parts[a])):
                for d in range(1, 8):
                    got_p[(m, a, j, d)].wait_recv()
            for cp in sent_p[(m, a)]:
                cp.wait_send()
        tail = xr[m, :, width:].astype(jnp.float32)
        pick = (lane == me) | (lane == me + 32)
        prob[...] = jnp.broadcast_to(
            jnp.sum(jnp.where(pick, tail, 0.0), axis=1, keepdims=True), (rows, 128)
        )
        gg[...] = jnp.zeros_like(gg)

        def weigh(i):
            at = cols(i, tw)
            eg[m, :, at] = (prob[:, 0:1] * gr[m, :, at].astype(jnp.float32)).astype(jnp.bfloat16)

        tiles(nt, weigh)

        def inner(i):
            at = cols(i, tw)
            xrow = xr[m, :, 0:width]
            gate = mm(xrow, wg[:, at])
            upv = mm(xrow, wu[:, at])
            back = mm_nt(eg[m], wd[at, :])
            cdf = 0.5 * (1.0 + lax.erf(gate * 0.7071067811865476))
            act = gate * cdf
            slope = cdf + gate * (jnp.exp(gate * gate * -0.5) * 0.3989422804014327)
            hid[m, :, at] = (act * upv).astype(jnp.bfloat16)
            gpg[m, :, at] = (back * upv * slope).astype(jnp.bfloat16)
            upg[m, :, at] = (back * act).astype(jnp.bfloat16)

        tiles(ff // tw, inner)

        def outer(i):
            at = cols(i, tw)
            low = mm(hid[m], wd[:, at]).astype(jnp.bfloat16).astype(jnp.float32)
            gg[...] += jnp.broadcast_to(
                jnp.sum(low * gr[m, :, at].astype(jnp.float32), axis=1, keepdims=True),
                (rows, 128),
            )
            ys[m, :, at] = (prob[:, 0:1] * low).astype(jnp.bfloat16)

        tiles(nt, outer)

        def inputs(i):
            at = cols(i, tw)
            ds_[m, :, at] = (mm_nt(gpg[m], wg[at, :]) + mm_nt(upg[m], wu[at, :])).astype(
                jnp.bfloat16
            )

        tiles(cut // tw, inputs)
        send_back(m, 0, 0)
        tiles((width - cut) // tw, lambda i: inputs(i + cut // tw))
        total = gg[...]
        high = total.astype(jnp.bfloat16).astype(jnp.float32)
        ds_[m, :, width:] = jnp.where(
            lane == me, high, jnp.where(lane == me + 32, total - high, 0.0)
        ).astype(jnp.bfloat16)
        send_back(m, 0, 1)
        to_pair(m)

    for m in range(micro):
        run(m)
    send_back(0, 1, 0)
    save(ys.at[1], y1_hbm)

    got_c = {}

    def gather(m, j):
        left, size = parts[1][j]
        for d in range(1, 8):
            got_b[(m, 0, j, d)].wait_recv()
        pl.when(inner)(got_f[(m, 1, j)].wait_send)

        def body(i):
            at = cols(i + left // tw, tw)
            zd[m, :, at] = mm_tn(onehot[m], dr[m, :, at]).astype(bf)

        tiles(size // tw, body)
        if j == 1:
            zd[m, :, width:] = mm_tn(onehot[m], dr[m, :, width:]).astype(bf)
        wide = pl.ds(left, size)
        far = pl.ds(pl.multiple_of(far_back * half, half), half)
        relay = remote(
            zd.at[m, far, wide], rel.at[m, :, wide], rel_s.at[m * 2 + j], rel_r.at[m * 2 + j], beside_dev
        )
        start_if(edge, relay)
        for k in (1, 3, 2):
            i = (m * 2 + j) * 4 + k
            at = pl.ds(k * half, half)
            cp = remote(zd.at[m, at, wide], dz.at[m, at, wide], zb_s.at[i], zb_r.at[i], z_back(k))
            got_c[(m, j, k)] = cp
            if k == 2:

                @pl.when(inner)
                def _():
                    relay.wait_recv()
                    here = slice(left, left + size)
                    zd[m, 2 * half : 3 * half, here] = (
                        zd[m, 2 * half : 3 * half, here].astype(f32) + rel[m, :, here].astype(f32)
                    ).astype(bf)

                cp.start()
                sent.append(cp)
            else:
                start_if(not_first if k == 1 else not_last, cp)

    def finish(m, j):
        left, size = parts[1][j]
        here = slice(left, left + size)
        pl.when(not_last)(got_c[(m, j, 1)].wait_recv)
        pl.when(not_first)(got_c[(m, j, 3)].wait_recv)
        got_c[(m, j, 2)].wait_recv()
        total = zd[m, 0:half, here].astype(f32)
        for k in range(1, 4):
            total = total + dz[m, k * half : (k + 1) * half, here].astype(f32)
        dx_ref[m, mine, here] = total
        n = m * 8 + 5 + j
        wide = pl.ds(left, size)
        cp = remote(
            dx_ref.at[m, mine, wide], dx_ref.at[m, mine, wide], pair_s.at[n], pair_r.at[n], (e, 1 - c)
        )
        cp.start()
        sent.append(cp)
        got_c[("pair", m, j)] = cp

    order = [(m, j) for m in range(micro) for j in range(2)]
    for i, (m, j) in enumerate(order):
        gather(m, j)
        if i >= 1:
            finish(*order[i - 1])
    for d in range(1, 8):
        got_b[(0, 1, 0, d)].wait_recv()
    pl.when(inner)(got_f[(0, 0, 0)].wait_send)

    def outputs(i):
        at = cols(i, tw)
        gz[0, :, at] = mm_tn(onehot[0], y0r[:, at]).astype(bf)

    tiles(nt, outputs)
    save(gz.at[0], y0_hbm)
    pl.when(inner)(got_f[(1, 0, 0)].wait_send)
    finish(*order[-1])
    to_twin(3)
    got_a[(2, 3, 0)].wait_recv()
    for m in range(micro):
        got_a[(2, 1, m)].wait_recv()
    for d in range(1, 4):
        got_a[("twin", d)].wait_recv()
    for m in range(micro):
        for i in range(5):
            got_b[("pair", m, i)].wait_recv()
        for j in range(2):
            got_c[("pair", m, j)].wait_recv()
    for at in list(away):
        z_sent(*at)
    for cp in saves:
        cp.wait()
    for cp in sent:
        cp.wait_send()
    for cond, cp in sent_if:
        pl.when(cond)(cp.wait_send)


def front_call(
    tokens, cotangent, positions, routes, gain_a, gain_f, wq, wk, wv, wo, router, gate_weight,
    up_weight, down_weight,
):
    micro, length, width = tokens.shape
    wide = width + 128
    half = length // 2
    ff = gate_weight.shape[1] // 2
    cap = 3 * half * routes.shape[1] // (2 * EXPERTS)
    rows = 8 * 4 * cap
    bf = jnp.bfloat16
    f32 = jnp.float32
    vmem = pl.BlockSpec(memory_space=pltpu.VMEM)
    hbm = pl.BlockSpec(memory_space=ANY)
    heads = wq.shape[1] // HEAD_SIZE

    def buf(*shape, dtype=bf):
        return pltpu.VMEM(shape, dtype)

    def out(*shape, dtype=bf):
        return jax.ShapeDtypeStruct(shape, dtype)

    sem = pltpu.SemaphoreType.DMA
    col = 4 * half
    hw = wq.shape[1]
    return pl.pallas_call(
        front_kernel,
        out_shape=(
            out(micro, length, wide, dtype=f32),
            out(micro, length, width),
            out(micro, length, hw),
            out(micro, heads * length, HEAD_SIZE),
            out(micro, length, HEAD_SIZE),
            out(micro, length, HEAD_SIZE),
            out(micro, heads * length, length, dtype=f32),
            out(micro, 2, length, HEAD_SIZE, dtype=f32),
            out(micro, length, width, dtype=f32),
            out(micro, length, wide),
            out(col, width),
            out(rows, width),
            out(rows, col),
            out(4 * micro * length, width // 2),
            out(4 * micro * length, hw // 2),
            out(2, micro, rows, width),
            out(2, micro, rows, ff),
            out(2, micro, rows, ff),
            out(2, micro, rows, ff),
            out(2, micro, rows, width),
        ),
        in_specs=[hbm] * 9 + [vmem] * 5,
        out_specs=(vmem,) + (hbm,) * 19,
        scratch_shapes=[
            buf(micro, length, width), buf(width, hw), buf(width, HEAD_SIZE), buf(width, HEAD_SIZE), buf(hw, width),
            buf(micro, length, width), buf(micro, length, hw), buf(micro, heads * length, HEAD_SIZE),
            buf(micro, length, HEAD_SIZE), buf(micro, length, HEAD_SIZE),
            buf(micro, heads * length, length, dtype=f32), buf(micro, 2, length, HEAD_SIZE, dtype=f32),
            buf(micro, length, width, dtype=f32), buf(micro, length, wide),
            buf(micro, col, wide), buf(micro, col, width), pltpu.VMEM((4, *routes.shape), jnp.int32),
            buf(micro, rows, wide), buf(micro, rows, width), buf(micro, rows, wide), buf(micro, rows, width),
            buf(micro, rows, width), buf(micro, rows, ff), buf(micro, rows, ff), buf(micro, rows, ff),
            buf(rows, width), buf(micro, rows, wide), buf(micro, col, wide),
            buf(micro * length, width, dtype=f32), buf(micro * length, width, dtype=f32),
            buf(micro, half, wide), buf(micro, rows, col), buf(rows, 128, dtype=f32), buf(rows, 128, dtype=f32),
            buf(width, ff), buf(width, ff), buf(ff, width),
            sem((4,)), sem((4,)), sem((16 * micro,)), sem((16 * micro,)), sem((32 * micro,)), sem((32 * micro,)),
            sem((32 * micro,)), sem((32 * micro,)), sem((8 * micro,)), sem((8 * micro,)), sem((8 * micro,)),
            sem((8 * micro,)), sem((3,)), sem((3,)), sem((4 * micro,)), sem((2 * micro,)), sem((2 * micro,)),
            sem((14,)), sem((14,)), sem((4,)), sem((4,)), sem((8 + micro,)), sem((16 + 5 * micro,)), sem((8 * micro,)),
        ],
        compiler_params=pltpu.CompilerParams(
            collective_id=1, has_side_effects=True, vmem_limit_bytes=VMEM_LIMIT
        ),
        cost_estimate=pl.CostEstimate(
            flops=2 * 6 * micro * rows * width * ff, bytes_accessed=40 * 2**20, transcendentals=0
        ),
        name="front",
    )(
        tokens, cotangent, wq, wk, wv, wo, gate_weight, up_weight, down_weight,
        positions, routes, gain_a, gain_f, router,
    )


def back_kernel(
    tok_hbm, g_hbm, wq_hbm, wk_hbm, wv_hbm, wo_hbm,
    dx_hbm, nrm_hbm, att_hbm, q_hbm, k_hbm, v_hbm, pr_hbm, tab_hbm, hs_hbm, x_hbm, y0_hbm, y1_hbm, hot_hbm,
    fn_hbm, fa_hbm, gain_a, gain_f, router_ref,
    lay_ref, tg_hbm, oa, ob_hbm, os,
    tok_ref, g_ref, wq_ref, wk_ref, wv_ref, wo_ref, dx_ref, q_ref, k_ref, v_ref, pr_ref, tab_ref, hs_ref, x_ref,
    hot, y1r, zy, yz, rel, tg_ref, ob,
    d_ref, a_ref, s_ref, sg, ag, own_part, other_part,
    fn, fd, fa, fg, fs, pa, pb, za, zb, zs, ra, rb,
    f_s, f_r, w_s, w_r, c_s, c_r, y_s, y_r, l_s, l_r, z_s, z_r, h_s, h_r, p_s, p_r, part_s, part_r,
    yp_s, yp_r, yz_s, yz_r, rel_s, rel_r, pair_s, pair_r, in_sem, out_sem,
):
    micro, length, width = tok_ref.shape
    half = length // 2
    f32 = jnp.float32
    bf = jnp.bfloat16
    head = HEAD_SIZE
    heads = wq_ref.shape[1] // head
    wq = wq_ref.shape[1]
    tw = 256
    nt = width // tw
    e = lax.axis_index("expert")
    c = lax.axis_index("tensor")
    z = e // 4
    q = lax.rem(e, 4)
    qx = lax.rem(q, 2)
    qy = q // 2
    rows = micro * length
    wn = fn.shape[1]
    wd = d_ref.shape[1] // 2
    wa = fa.shape[1]
    per = length
    wg = a_ref.shape[1] // 2
    ws = s_ref.shape[1] // 4
    hs = s_ref.shape[0] // 4
    ha = wn // 4
    hb = wa // 4

    def flip(bit, by):
        return lax.rem(bit + by, 2)

    def p_dev(d):
        return (z * 4 + flip(qy, d // 2) * 2 + flip(qx, d % 2), c)

    def z_dev(k):
        return (lax.rem(z + k, 4) * 4 + q, c)

    def part(i, size):
        return pl.ds(pl.multiple_of(i * size, size), size)

    inner = (z == 1) | (z == 2)
    edge = (z == 0) | (z == 3)
    not_first = z != 0
    not_last = z != 3
    beside = jnp.where(edge, jnp.where(z == 0, 1, 2), jnp.where(z == 1, 0, 3))
    beside_dev = (beside * 4 + q, c)
    twin = (e, 1 - c)
    sent_if = []

    def start_if(cond, cp):
        pl.when(cond)(cp.start)
        sent_if.append((cond, cp))

    o = q * 2 + c
    blk = y1r.shape[0] // 8
    own_rows = pl.ds(pl.multiple_of(c * half, half), half)

    def any_dev(n):
        t = lax.rem(o + n, 8)
        return (z * 4 + t // 2, lax.rem(t, 2))

    def any_back(n):
        t = lax.rem(o + 8 - n, 8)
        return (z * 4 + t // 2, lax.rem(t, 2))

    def fill(m, slot):
        yz[m, slot * half : (slot + 1) * half, :] = jnp.zeros((half, width), bf)

    def clear(slot):
        za[slot] = jnp.zeros((ha, wd), bf)
        zb[slot] = jnp.zeros((hb, wg), bf)

    pl.when(z == 0)(lambda: clear(1))
    pl.when(z == 3)(lambda: clear(3))

    for m in range(micro):
        pl.when(z == 3)(lambda m=m: fill(m, 1))
        pl.when(z == 0)(lambda m=m: fill(m, 3))

    barrier = pltpu.get_barrier_semaphore()
    for n in range(1, 4):
        pl.semaphore_signal(barrier, inc=1, device_id=z_dev(n), device_id_type=MESH)
    for n in range(1, 8):
        pl.semaphore_signal(barrier, inc=1, device_id=any_dev(n), device_id_type=MESH)
    loads = {}
    for i, (name, src, dst) in enumerate(
        (
            ("dx", dx_hbm, dx_ref), ("x", x_hbm, x_ref), ("hs", hs_hbm, hs_ref), ("g", g_hbm, g_ref),
            ("y0", y0_hbm, zy.at[0]), ("y1", y1_hbm.at[0:blk, :], y1r.at[0:blk, :]), ("wo", wo_hbm, wo_ref),
            ("v", v_hbm, v_ref), ("pr", pr_hbm, pr_ref), ("k", k_hbm, k_ref), ("q", q_hbm, q_ref),
            ("tab", tab_hbm, tab_ref), ("wq", wq_hbm, wq_ref), ("wk", wk_hbm, wk_ref), ("wv", wv_hbm, wv_ref),
            ("hot", hot_hbm, hot), ("tok", tok_hbm, tok_ref),
            ("fa", fa_hbm.at[rows:, :], fa.at[rows:, :]), ("fa0", att_hbm.at[:, part(qy, wa)], fa.at[0:rows, :]),
            ("fn", fn_hbm.at[rows:, :], fn.at[rows:, :]), ("fn0", nrm_hbm.at[:, part(qx, wn)], fn.at[0:rows, :]),
        )
    ):
        loads[name] = pltpu.make_async_copy(src, dst, in_sem.at[i])
        loads[name].start()
    saves = []

    def save(src, dst):
        cp = pltpu.make_async_copy(src, dst, out_sem.at[len(saves)])
        cp.start()
        saves.append(cp)

    def need(*names):
        for name in names:
            loads[name].wait()

    pl.semaphore_wait(barrier, 10)

    sent = []
    got_f = {}
    bits = {3: 0, 1: 1}

    def piece(src, i, d):
        bit = flip(qx, d % 2) if bits[i] == 0 else flip(qy, d // 2)
        return part(bit, src.shape[1] // 2)

    def mine(d):
        return pl.ds(pl.multiple_of(d * rows + c * per, per), per)

    def factor(i, src, dst):
        for d in (1, 2):
            if bits[i] == 0:
                view = src.at[pl.ds(pl.multiple_of(c * per, per), per), piece(src, i, d)]
                to = dst.at[mine(d), :]
            else:
                view = src.at[:, piece(src, i, d)]
                to = dst.at[pl.ds(d * rows, rows), :]
            cp = remote(view, to, f_s.at[d * 4 + i], f_r.at[d * 4 + i], p_dev(d))
            cp.start()
            sent.append(cp)
            got_f[(i, d)] = cp

    def to_twin(i, d, dst):
        cp = remote(dst.at[mine(d), :], dst.at[mine(d), :], w_s.at[d * 4 + i], w_r.at[d * 4 + i], twin)
        cp.start()
        sent.append(cp)
        got_f[("twin", i, d)] = cp

    def relay(i, dst):
        via, over = (1, 2) if bits[i] == 0 else (2, 1)
        got_f[(i, via)].wait_recv()
        if bits[i] == 0:
            src, to = dst.at[mine(via), :], dst.at[mine(3), :]
        else:
            src, to = dst.at[pl.ds(via * rows, rows), :], dst.at[pl.ds(3 * rows, rows), :]
        cp = remote(src, to, f_s.at[12 + i], f_r.at[12 + i], p_dev(over))
        cp.start()
        sent.append(cp)
        got_f[(i, 3)] = cp
        if bits[i] == 0:
            to_twin(i, via, dst)
            got_f[(i, over)].wait_recv()
            to_twin(i, over, dst)

    def arrive(i, dst):
        if bits[i]:
            got_f[(i, 1)].wait_recv()
            got_f[(i, 3)].wait_recv()
        else:
            got_f[(i, 3)].wait_recv()
            to_twin(i, 3, dst)
            for d in (1, 2, 3):
                got_f[("twin", i, d)].wait_recv()

    got_v = {}
    def send_y1(j):
        wide = pl.ds(j * (width // 2), width // 2)
        for n in range(1, 8):
            at = pl.ds(n * blk, blk)
            cp = remote(
                y1_hbm.at[at, wide], y1r.at[at, wide], yp_s.at[j * 8 + n], yp_r.at[j * 8 + n], any_back(n)
            )
            cp.start()
            sent.append(cp)
            got_v[(n, j, "row")] = cp

    send_y1(0)

    def z_back(n):
        return (lax.rem(z + 4 - n, 4) * 4 + q, c)

    def send_far(m):
        far = part(jnp.where(z == 0, 1, 3), half)
        cp = remote(zy.at[m, far, :], rel.at[m], rel_s.at[m], rel_r.at[m], beside_dev)
        start_if(edge, cp)
        got_v[("far", m)] = cp
        for n in (1, 3):
            at = pl.ds(n * half, half)
            cp = remote(zy.at[m, at, :], yz.at[m, at, :], yz_s.at[m * 4 + n], yz_r.at[m * 4 + n], z_back(n))
            start_if(not_first if n == 1 else not_last, cp)
            got_v[(m, n)] = cp

    def send_near(m):
        at = pl.ds(2 * half, half)

        @pl.when(inner)
        def _():
            got_v[("far", m)].wait_recv()
            zy[m, at, :] = (zy[m, at, :].astype(f32) + rel[m].astype(f32)).astype(bf)

        cp = remote(zy.at[m, at, :], yz.at[m, at, :], yz_s.at[m * 4 + 2], yz_r.at[m * 4 + 2], z_back(2))
        cp.start()
        sent.append(cp)
        got_v[(m, 2)] = cp

    def layer(m):
        pl.when(not_last)(got_v[(m, 1)].wait_recv)
        pl.when(not_first)(got_v[(m, 3)].wait_recv)
        got_v[(m, 2)].wait_recv()
        total = zy[m, 0:half, :].astype(f32)
        for n in range(1, 4):
            total = total + yz[m, n * half : (n + 1) * half, :].astype(f32)
        lay_ref[m, own_rows, :] = (hs_ref[m, own_rows, :] + total).astype(bf)
        cp = remote(
            lay_ref.at[m, own_rows, :], lay_ref.at[m, own_rows, :], pair_s.at[m], pair_r.at[m], twin
        )
        cp.start()
        sent.append(cp)
        got_v[("pair", m)] = cp

    need("dx", "x", "hs", "g")
    lane = lax.broadcasted_iota(jnp.int32, (1, 128), 1)
    gain_row = jnp.zeros((1, width), f32)
    s_ref[...] = jnp.zeros_like(s_ref)
    router_row = jnp.zeros((128, width), f32)
    for m in range(micro):
        here = slice(m * length, (m + 1) * length)
        tail = dx_ref[m, :, width:]
        grad = tail + pltpu.roll(tail, 128 - EXPERTS, 1)
        tail = x_ref[m, :, width:].astype(f32)
        prob = jnp.where(lane < EXPERTS, tail + pltpu.roll(tail, 128 - EXPERTS, 1), 0.0)
        shared = jnp.sum(prob * grad, axis=1, keepdims=True)
        low = (prob * (grad - shared)).astype(bf)
        router_row = router_row + mm_tn(low, x_ref[m, :, 0:width])
        full = dx_ref[m, :, 0:width] + mm(low[:, 0:EXPERTS], router_ref[...])
        state = hs_ref[m]
        scale = lax.rsqrt(jnp.mean(state * state, axis=1, keepdims=True) + epsilon)
        u = full * gain_f[...].reshape(1, width)
        common = jnp.mean(u * state, axis=1, keepdims=True) * (scale * scale * scale)
        total = g_ref[m].astype(f32) + (scale * u - state * common)
        sg[m] = total
        a_ref[here, :] = total.astype(bf)
        gain_row = gain_row + jnp.sum(full * state * scale, axis=0, keepdims=True)
    s_ref[0:EXPERTS, :] = router_row[0:EXPERTS].astype(bf)
    factor(3, a_ref, fg)
    need("y0", "wo")
    send_far(0)

    def inward(i):
        at = cols(i, tw)
        both = mm_nt(a_ref[...], wo_ref[at, :]).astype(bf)
        for m in range(micro):
            for j in range(tw // head):
                to = pl.ds(pl.multiple_of((i * (tw // head) + j) * length, length), length)
                ag[m, to, :] = both[m * length : (m + 1) * length, j * head : (j + 1) * head]

    tiles(wq // tw, inward)
    relay(3, fg)
    send_near(0)
    need("v", "pr", "k", "q", "tab")

    def unrope(u, m):
        return u * tab_ref[m, 0] - pltpu.roll(u, head // 2, 1) * tab_ref[m, 1]

    for m in range(micro):
        here = slice(m * length, (m + 1) * length)
        prob = pr_ref[m]
        back = mm_nt(ag[m], v_ref[m])
        shared = jnp.sum(prob * back, axis=1, keepdims=True)
        low = (prob * (back - shared)).astype(bf)
        dq = mm(low, k_ref[m]) * (head**-0.5)
        for h in range(heads):
            u = unrope(dq[h * length : (h + 1) * length], m)
            d_ref[here, h * head : (h + 1) * head] = u.astype(bf)
        dk = mm_tn(low, q_ref[m]) * (head**-0.5)
        d_ref[here, wq : wq + head] = unrope(dk, m).astype(bf)
        d_ref[here, wq + head : wq + 2 * head] = mm_tn(prob.astype(bf), ag[m]).astype(bf)
    factor(1, d_ref, fd)
    need("wq", "wk", "wv")
    got_part = []
    for j in range(3):

        def outward(i, j=j):
            at = cols(i + j * (nt // 3), tw)
            own_part[:, at] = (
                mm_nt(d_ref[:, 0:wq], wq_ref[at, :])
                + mm_nt(d_ref[:, wq : wq + head], wk_ref[at, :])
                + mm_nt(d_ref[:, wq + head :], wv_ref[at, :])
            )

        tiles(nt // 3, outward)
        at = pl.ds(j * (width // 3), width // 3)
        cp = remote(
            own_part.at[:, at], other_part.at[:, at], part_s.at[j], part_r.at[j], (e, 1 - c)
        )
        cp.start()
        sent.append(cp)
        got_part.append(cp)
    fd[0:rows, :] = d_ref[:, part(qy, wd)]
    fg[0:rows, :] = a_ref[:, part(qx, wg)]
    need("fa", "fa0")
    arrive(3, fg)

    def two(i):
        at = cols(i, tw)
        pb[:, at] = mm_tn(fa[...], fg[:, at]).astype(bf)

    tiles(wg // tw, two)
    got_y = {}

    def spread(i):
        src, dst, size, rest = ((pa, za, ha, ra), (pb, zb, hb, rb))[i]
        far = lax.rem(z + jnp.where(z == 0, 3, 1), 4)
        cp = remote(src.at[part(far, size), :], rest, l_s.at[i], l_r.at[i], beside_dev)
        start_if(edge, cp)
        got_y[("far", i)] = cp
        for k in (1, 3):
            cp = remote(
                src.at[part(lax.rem(z + k, 4), size), :], dst.at[k],
                y_s.at[k * 3 + i], y_r.at[k * 3 + i], z_dev(k),
            )
            start_if(not_last if k == 1 else not_first, cp)
            got_y[(i, k)] = cp

    def spread_rest(i):
        src, dst, size, rest = ((pa, za, ha, ra), (pb, zb, hb, rb))[i]
        across = part(lax.rem(z + 2, 4), size)

        @pl.when(inner)
        def _():
            got_y[("far", i)].wait_recv()
            src[across, :] = (src[across, :].astype(f32) + rest[...].astype(f32)).astype(bf)

        cp = remote(src.at[across, :], dst.at[2], y_s.at[6 + i], y_r.at[6 + i], z_dev(2))
        cp.start()
        sent.append(cp)
        got_y[(i, 2)] = cp

    spread(1)
    relay(1, fd)
    send_y1(1)
    need("tok")
    for cp in got_part:
        cp.wait_recv()
    last_row = jnp.zeros((1, width), f32)
    for m in range(micro):
        here = slice(m * length, (m + 1) * length)
        full = own_part[here, :] + other_part[here, :]
        state = tok_ref[m].astype(f32)
        scale = lax.rsqrt(jnp.mean(state * state, axis=1, keepdims=True) + epsilon)
        u = full * gain_a[...].reshape(1, width)
        common = jnp.mean(u * state, axis=1, keepdims=True) * (scale * scale * scale)
        tg_ref[m] = sg[m] + (scale * u - state * common)
        save(tg_ref.at[m], tg_hbm.at[m])
        last_row = last_row + jnp.sum(full * state * scale, axis=0, keepdims=True)
    index = lax.broadcasted_iota(jnp.int32, (hs, 1), 0)
    s_ref[2 * hs : 3 * hs, :] = jnp.where(
        index == 0, gain_row, jnp.where(index == 1, last_row, 0.0)
    ).astype(bf)
    got_s = []
    for d in (3, 1, 2):
        to = flip(qy, d // 2) * 2 + flip(qx, d % 2)
        cp = remote(s_ref.at[part(to, hs), :], fs.at[d], c_s.at[d], c_r.at[d], p_dev(d))
        cp.start()
        sent.append(cp)
        got_s.append(cp)
    spread_rest(1)
    need("fn", "fn0")
    arrive(1, fd)

    def one(i):
        at = cols(i, tw)
        pa[:, at] = mm_tn(fn[...], fd[:, at]).astype(bf)

    tiles(wd // tw, one)
    spread(0)
    total = s_ref[part(q, hs), :].astype(jnp.float32)
    for cp in got_s:
        cp.wait_recv()
    for d in range(1, 4):
        total = total + fs[d].astype(jnp.float32)
    fs[0] = total.astype(jnp.bfloat16)
    for k in (2, 1, 3):
        cp = remote(
            fs.at[0, :, part(lax.rem(z + k, 4), ws)], zs.at[k],
            y_s.at[k * 3 + 2], y_r.at[k * 3 + 2], z_dev(k),
        )
        cp.start()
        sent.append(cp)
        got_y[(2, k)] = cp
    spread_rest(0)
    layer(0)
    need("y1", "hot")
    for n in range(1, 8):
        for j in range(2):
            got_v[(n, j, "row")].wait_recv()

    def outputs(i):
        at = cols(i, tw)
        zy[1, :, at] = mm_tn(hot[...], y1r[:, at]).astype(bf)

    tiles(nt, outputs)
    send_far(1)

    def spots(px, py, t):
        return (
            oa.at[part(px * 4 + t, ha), part(py, wd)],
            ob.at[part(py * 4 + t, hb), part(px, wg)],
            os.at[part(py * 2 + px, hs), part(t, ws)],
        )

    home = spots(qx, qy, z)

    def total_of(i):
        first, others = (
            (pa[part(z, ha), :], za), (pb[part(z, hb), :], zb), (fs[0, :, part(z, ws)], zs),
        )[i]
        if i < 2:
            pl.when(not_first)(got_y[(i, 1)].wait_recv)
            pl.when(not_last)(got_y[(i, 3)].wait_recv)
        else:
            got_y[(i, 1)].wait_recv()
            got_y[(i, 3)].wait_recv()
        got_y[(i, 2)].wait_recv()
        acc = first.astype(f32)
        for k in range(1, 4):
            acc = acc + others[k].astype(f32)
        home[i][...] = acc.astype(bf)
        for k in (2, 1, 3):
            cp = remote(home[i], home[i], z_s.at[k * 3 + i], z_r.at[k * 3 + i], z_dev(k))
            if k == 2:
                cp.start()
                sent.append(cp)
            else:
                start_if(not_last if k == 1 else not_first, cp)

    turns = (
        0,
        jnp.where(inner, 2, jnp.where(z == 0, 3, 1)),
        jnp.where(inner, 1, 2),
        jnp.where(inner, 3, jnp.where(z == 0, 1, 3)),
    )
    got_p = {}

    def send(ref, i, n, d, j):
        at = ((n * 3) + i) * 4 + j
        cp = remote(ref, ref, p_s.at[at], p_r.at[at], p_dev(d))
        cp.start()
        sent.append(cp)
        got_p[(n, i, j)] = cp

    def own(n, i):
        k = turns[n]
        here = spots(qx, qy, lax.rem(z + 4 - k, 4))[i]
        if n:
            cp = remote(here, here, z_s.at[k * 3 + i], z_r.at[k * 3 + i], beside_dev)
            cp.wait_recv()
        if n == 1:
            to = jnp.where(z == 1, 1, 3)
            cp = remote(here, here, h_s.at[i], z_r.at[to * 3 + i], beside_dev)
            start_if(inner, cp)
        send(here, i, n, 1, 1)
        send(here, i, n, 2, 2)

    def forward(n, i):
        t = lax.rem(z + 4 - turns[n], 4)
        if i == 1:
            got_p[(n, i, 2)].wait_recv()
            send(spots(qx, flip(qy, 1), t)[i], i, n, 1, 3)
        else:
            got_p[(n, i, 1)].wait_recv()
            send(spots(flip(qx, 1), qy, t)[i], i, n, 2, 3)

    total_of(1)
    own(0, 1)
    total_of(0)
    own(0, 0)
    total_of(2)
    own(0, 2)
    own(1, 1)
    forward(0, 1)
    own(1, 0)
    send_near(1)
    forward(0, 0)
    forward(0, 2)
    own(1, 2)
    for n in (2, 3):
        for i in (1, 0, 2):
            own(n, i)
            forward(n - 1, i)
    for i in (1, 0, 2):
        forward(3, i)
    layer(1)
    for i in (1, 0, 2):
        for n in range(4):
            first = 1 if i == 1 else 2
            got_p[(n, i, first)].wait_recv()
            got_p[(n, i, 3)].wait_recv()
        if i == 1:
            save(ob, ob_hbm)
    for m in range(micro):
        got_v[("pair", m)].wait_recv()
    for cp in saves:
        cp.wait()
    for cp in sent:
        cp.wait_send()
    for cond, cp in sent_if:
        pl.when(cond)(cp.wait_send)


def back_call(
    tokens, cotangent, gain_a, gain_f, wq, wk, wv, wo, router,
    dx, nrm, att, q, k, v, pr, tab, hs, xrows, y0, y1, hot, fn, fa,
):
    bf = jnp.bfloat16
    f32 = jnp.float32
    micro, length, width = tokens.shape
    rows = micro * length
    half = length // 2
    wd = wq.shape[1] + wk.shape[1] + wv.shape[1]
    wa = wq.shape[1]
    heads = wa // HEAD_SIZE
    vmem = pl.BlockSpec(memory_space=pltpu.VMEM)
    hbm = pl.BlockSpec(memory_space=ANY)

    def buf(*shape, dtype=bf):
        return pltpu.VMEM(shape, dtype)

    def like(array):
        return pltpu.VMEM(array.shape, array.dtype)

    sem = pltpu.SemaphoreType.DMA
    small = (64, width)
    hsm, wsm = 16, width // 4
    return pl.pallas_call(
        back_kernel,
        out_shape=(
            jax.ShapeDtypeStruct((micro, length, width), bf),
            jax.ShapeDtypeStruct((micro, length, width), f32),
            jax.ShapeDtypeStruct((width, wd), bf),
            jax.ShapeDtypeStruct((wa, width), bf),
            jax.ShapeDtypeStruct(small, bf),
        ),
        in_specs=[hbm] * 21 + [vmem] * 3,
        out_specs=(vmem, hbm, vmem, hbm, vmem),
        scratch_shapes=[
            like(tokens), like(cotangent), like(wq), like(wk), like(wv), like(wo), like(dx), like(q), like(k),
            like(v), like(pr), like(tab), like(hs), like(xrows), like(hot), like(y1), buf(micro, 4 * half, width),
            buf(micro, 4 * half, width), buf(micro, half, width), buf(micro, length, width, dtype=f32), buf(wa, width),
            buf(rows, wd), buf(rows, width), buf(*small), buf(micro, length, width, dtype=f32),
            buf(micro, heads * length, HEAD_SIZE), buf(rows, width, dtype=f32), buf(rows, width, dtype=f32),
            buf(4 * rows, width // 2), buf(4 * rows, wd // 2), buf(4 * rows, wa // 2), buf(4 * rows, width // 2),
            buf(4, hsm, width),
            buf(width // 2, wd // 2), buf(wa // 2, width // 2),
            buf(4, width // 8, wd // 2), buf(4, wa // 8, width // 2), buf(4, hsm, wsm),
            buf(width // 8, wd // 2), buf(wa // 8, width // 2),
            sem((16,)), sem((16,)), sem((16,)), sem((16,)), sem((4,)), sem((4,)), sem((12,)), sem((12,)),
            sem((2,)), sem((2,)), sem((12,)), sem((12,)), sem((3,)), sem((3,)), sem((48,)), sem((48,)),
            sem((3,)), sem((3,)),
            sem((16,)), sem((16,)), sem((4 * micro,)), sem((4 * micro,)), sem((micro,)), sem((micro,)), sem((micro,)),
            sem((micro,)), sem((21,)), sem((1 + micro,)),
        ],
        compiler_params=pltpu.CompilerParams(
            collective_id=2, has_side_effects=True, vmem_limit_bytes=VMEM_LIMIT
        ),
        cost_estimate=pl.CostEstimate(
            flops=2 * rows * 4 * (width * wd + wa * width) // 4, bytes_accessed=20 * 2**20, transcendentals=0
        ),
        name="back",
    )(
        tokens, cotangent, wq, wk, wv, wo,
        dx, nrm.reshape(rows, width), att.reshape(rows, wa), q, k, v, pr, tab, hs, xrows, y0, y1, hot, fn, fa,
        gain_a, gain_f, router,
    )


def grads_kernel(
    x_ref, h_ref, g_ref, u_ref, e_ref, qkv_ref, o_ref, s_ref,
    gate_out, up_out, down_out, q_out, k_out, v_out, o_out, router_out, ffn_out, att_out,
):
    gate_out[...] = mm_tn(x_ref[0], g_ref[0])
    up_out[...] = mm_tn(x_ref[0], u_ref[0])
    down_out[...] = mm_tn(h_ref[0], e_ref[0])
    wq = q_out.shape[1]
    wk = wq + k_out.shape[1]
    f32 = jnp.float32
    q_out[...] = qkv_ref[:, 0:wq].astype(f32)
    k_out[...] = qkv_ref[:, wq:wk].astype(f32)
    v_out[...] = qkv_ref[:, wk:].astype(f32)
    o_out[...] = o_ref[...].astype(f32)

    @pl.when(pl.program_id(0) == 0)
    def _():
        small = s_ref[...].astype(f32)
        router_out[...] = small[0:EXPERTS]
        width = small.shape[1]
        ffn_out[...] = small[EXPERTS : EXPERTS + 1].reshape(width)
        att_out[...] = small[EXPERTS + 1 : EXPERTS + 2].reshape(width)


def grads_call(rx, rh, rg, ru, re, qkv, o, small, wq, wk):
    _, micro, rows, width = rx.shape
    ff = rh.shape[3]
    n = micro * rows
    tw = 256
    per = ff // tw
    steps = 2 * per
    f32 = jnp.float32
    wide = pl.BlockSpec((1, n, width), lambda i: (i // per, 0, 0))
    thin = pl.BlockSpec((1, n, tw), lambda i: (i // per, 0, i % per))
    down = lambda a, w: pl.BlockSpec((a // steps, w), lambda i: (i, 0))
    whole = lambda *s: pl.BlockSpec(s, lambda i: (0,) * len(s))
    out = lambda *s: jax.ShapeDtypeStruct(s, f32)
    wv = qkv.shape[1] - wq - wk
    return pl.pallas_call(
        grads_kernel,
        grid=(steps,),
        in_specs=[
            wide, thin, thin, thin, wide,
            down(*qkv.shape), down(*o.shape), whole(*small.shape),
        ],
        out_specs=(
            pl.BlockSpec((width, tw), lambda i: (0, i)),
            pl.BlockSpec((width, tw), lambda i: (0, i)),
            pl.BlockSpec((tw, width), lambda i: (i, 0)),
            down(width, wq), down(width, wk), down(width, wv), down(*o.shape),
            whole(EXPERTS, width), whole(width), whole(width),
        ),
        out_shape=(
            out(width, 2 * ff), out(width, 2 * ff), out(2 * ff, width),
            out(width, wq), out(width, wk), out(width, wv), out(*o.shape),
            out(EXPERTS, width), out(width), out(width),
        ),
        compiler_params=pltpu.CompilerParams(vmem_limit_bytes=VMEM_LIMIT),
        cost_estimate=pl.CostEstimate(
            flops=2 * 6 * n * width * ff, bytes_accessed=62 * 2**20, transcendentals=0
        ),
        name="expert_grads",
    )(
        rx.reshape(2, n, width), rh.reshape(2, n, ff), rg.reshape(2, n, ff),
        ru.reshape(2, n, ff), re.reshape(2, n, width), qkv, o, small,
    )


def suits(mesh):
    return mesh.shape["expert"] == 16 and mesh.shape["tensor"] == 2


def local_fast(
    tokens, cotangent, positions, routes, attention_gain, feedforward_gain, query_weight, key_matrix,
    value_matrix, output_weight, router_weight, gate_weight, up_weight, down_weight,
):
    micro_count, length, model_width = tokens.shape
    gain_a, gain_f = attention_gain, feedforward_gain
    router_t = router_weight.T
    dx, *kept, rx, rh, rg, ru, re = front_call(
        tokens, cotangent, positions, routes.transpose(0, 2, 1), gain_a, gain_f, query_weight, key_matrix,
        value_matrix, output_weight, router_t, gate_weight, up_weight, down_weight,
    )
    layer_out, tokens_grad, oa, ob, os = back_call(
        tokens, cotangent, gain_a, gain_f, query_weight, key_matrix, value_matrix, output_weight,
        router_t, dx, *kept,
    )
    gate, up, down, dq, dk, dv, do, router, ffn_gain, att_gain = grads_call(
        rx, rh, rg, ru, re, oa, ob, os, query_weight.shape[1], key_matrix.shape[1]
    )
    return (
        layer_out, tokens_grad, att_gain, ffn_gain, dq, dk, dv, do, router.T, gate, up, down,
    )


def solution(mesh):
    in_specs = (
        P(None, "expert", None),
        P(None, "expert", None),
        P(None, "expert"),
        P(None, "expert", None),
        P(),
        P(),
        P(None, "tensor"),
        P(None, "tensor"),
        P(None, "tensor"),
        P("tensor", None),
        P(),
        P(None, "expert"),
        P(None, "expert"),
        P("expert", None),
    )
    out_specs = (
        P(None, "expert", None),
        P(None, "expert", None),
        P(),
        P(),
        P(None, "tensor"),
        P(None, "tensor"),
        P(None, "tensor"),
        P("tensor", None),
        P(),
        P(None, "expert"),
        P(None, "expert"),
        P("expert", None),
    )
    body = local_fast if suits(mesh) else local
    return jax.shard_map(body, mesh=mesh, in_specs=in_specs, out_specs=out_specs, check_vma=False)
```

```python
import functools

import jax
import jax.numpy as jnp
from jax import lax
from jax.experimental import pallas as pl
from jax.experimental.pallas import tpu as pltpu
from jax.sharding import PartitionSpec as P

HEAD_SIZE = 128
EXPERTS = 32


epsilon = 1e-05
theta_base = 1000000.0
masked_score = -1e30


def rms_norm(value_row_states, gain_vector):
    return (
        value_row_states
        * lax.rsqrt(jnp.mean(value_row_states * value_row_states, axis=-1, keepdims=True) + epsilon)
        * gain_vector
    )


def gelu_exact(value_row_states):
    return jax.nn.gelu(value_row_states, approximate=False)


def rope_tables(positions, head_dim):
    half_dim = head_dim // 2
    inverse = jnp.exp(
        -jnp.log(theta_base) * (2.0 * jnp.arange(half_dim, dtype=jnp.float32) / head_dim)
    )
    angles = positions.astype(jnp.float32)[:, None] * inverse[None, :]
    return (jnp.cos(angles), jnp.sin(angles))


def widen_table(table_part, value_row_states):
    return table_part.reshape(
        (table_part.shape[0],) + (1,) * (value_row_states.ndim - 2) + (table_part.shape[1],)
    )


def rotary_apply(value_row_states, cosine_table, sine_table):
    half_dim = value_row_states.shape[-1] // 2
    first_part = value_row_states[..., :half_dim]
    second = value_row_states[..., half_dim:]
    cos_wide = widen_table(cosine_table, value_row_states)
    sin_wide = widen_table(sine_table, value_row_states)
    return jnp.concatenate(
        [first_part * cos_wide - second * sin_wide, second * cos_wide + first_part * sin_wide],
        axis=-1,
    )


def unrotate(value_row_states, cosine_table, sine_table):
    half_dim = value_row_states.shape[-1] // 2
    first_part = value_row_states[..., :half_dim]
    second = value_row_states[..., half_dim:]
    cos_wide = widen_table(cosine_table, value_row_states)
    sin_wide = widen_table(sine_table, value_row_states)
    return jnp.concatenate(
        [first_part * cos_wide + second * sin_wide, second * cos_wide - first_part * sin_wide],
        axis=-1,
    )


def block_scores(query_block, key_row_states, starts, row_ids, offset, block_rows, score_scale):
    query_ids = offset + jnp.arange(block_rows, dtype=jnp.int32)
    allowed = (row_ids[None, :] <= query_ids[:, None]) & (row_ids[None, :] >= starts[:, None])
    scores = (
        jnp.einsum(
            "qcgd,kcd->cgqk", query_block, key_row_states, preferred_element_type=jnp.float32
        )
        * score_scale
    )
    return jnp.where(allowed, scores, masked_score)


def attention_forward(
    query_rows, key_row_states, value_rows, starts, row_ids, block_rows, score_scale
):

    def one_block(block_index):
        offset = block_index * block_rows
        scores = block_scores(
            query_rows, key_row_states, starts, row_ids, offset, block_rows, score_scale
        )
        row_peak = jnp.max(scores, axis=-1, keepdims=True)
        weights = jnp.exp(scores - row_peak)
        totals = jnp.sum(weights, axis=-1, keepdims=True)
        prob_low = (weights / totals).astype(jnp.bfloat16)
        attention_output = jnp.einsum(
            "cgqk,kcd->qcgd", prob_low, value_rows, preferred_element_type=jnp.float32
        )
        return (attention_output.astype(jnp.bfloat16), row_peak[..., 0] + jnp.log(totals[..., 0]))

    return lax.map(one_block, jnp.arange(query_rows.shape[0] // block_rows, dtype=jnp.int32))


def attention_backward(
    query_rows,
    key_row_states,
    value_rows,
    starts,
    row_ids,
    block_rows,
    score_scale,
    log_totals,
    attended_grad,
):

    def one_block(carried, block_index):
        key_grad, value_grad = carried
        offset = block_index * block_rows
        scores = block_scores(
            query_rows, key_row_states, starts, row_ids, offset, block_rows, score_scale
        )
        probs = jnp.exp(scores - log_totals[block_index][..., None])
        prob_low = probs.astype(jnp.bfloat16)
        prob_grad = jnp.einsum(
            "qcgd,kcd->cgqk", attended_grad, value_rows, preferred_element_type=jnp.float32
        )
        row_dot = jnp.sum(probs * prob_grad, axis=-1, keepdims=True)
        score_grad = (probs * (prob_grad - row_dot)).astype(jnp.bfloat16)
        query_grad = (
            jnp.einsum(
                "cgqk,kcd->qcgd", score_grad, key_row_states, preferred_element_type=jnp.float32
            )
            * score_scale
        )
        key_grad = (
            key_grad
            + jnp.einsum(
                "cgqk,qcgd->kcd", score_grad, query_rows, preferred_element_type=jnp.float32
            )
            * score_scale
        )
        value_grad = value_grad + jnp.einsum(
            "cgqk,qcgd->kcd", prob_low, attended_grad, preferred_element_type=jnp.float32
        )
        return ((key_grad, value_grad), query_grad)

    empty_grad = jnp.zeros(key_row_states.shape, jnp.float32)
    totals_out, query_grad = lax.scan(
        one_block,
        (empty_grad, empty_grad),
        jnp.arange(query_rows.shape[0] // block_rows, dtype=jnp.int32),
    )
    return (query_grad.reshape(query_rows.shape), totals_out[0], totals_out[1])


def spread_rows(base, group, capacity, n_dev, per_dev, width):
    widened = jnp.broadcast_to(
        base.reshape(EXPERTS, 1, capacity, width), (EXPERTS, group, capacity, width)
    )
    return widened.reshape(n_dev, per_dev * capacity, width)


def collect_rows(back, group, capacity, width, slot_index, rows, top_count):
    summed = jnp.sum(back.reshape(EXPERTS, group, capacity, width), axis=1).astype(jnp.bfloat16)
    return (
        summed.reshape(EXPERTS * capacity, width)[slot_index]
        .reshape(rows, top_count, width)
        .astype(jnp.float32)
    )


def local(
    tokens,
    cotangent,
    positions,
    routes,
    attention_gain,
    feedforward_gain,
    query_weight,
    key_matrix,
    value_matrix,
    output_weight,
    router_weight,
    gate_weight,
    up_weight,
    down_weight,
):
    micro_count, length, model_width = tokens.shape
    head_dim = HEAD_SIZE
    kv_local = key_matrix.shape[1] // head_dim
    query_group_count = query_weight.shape[1] // head_dim // kv_local
    top_count = routes.shape[2]
    n_dev = lax.axis_size("expert")
    n_tensor = lax.axis_size("tensor")
    half = length // n_tensor
    offset = lax.axis_index("tensor") * half
    per_dev = max(1, EXPERTS // n_dev)
    group = max(1, n_dev // EXPERTS)
    local_width = gate_weight.shape[1]
    ff_local = local_width // per_dev
    capacity = max(2, 3 * half * top_count // (2 * EXPERTS))
    block_rows = min(512, length)
    score_scale = head_dim ** (-0.5)
    expert_ids = jnp.arange(EXPERTS, dtype=jnp.int32)
    row_ids = jnp.arange(length, dtype=jnp.int32)
    gate_three = gate_weight.reshape(model_width, per_dev, ff_local)
    up_three = up_weight.reshape(model_width, per_dev, ff_local)
    down_three = down_weight.reshape(per_dev, ff_local, model_width)
    query_sum = jnp.zeros(query_weight.shape, jnp.float32)
    key_sum = jnp.zeros(key_matrix.shape, jnp.float32)
    value_sum = jnp.zeros(value_matrix.shape, jnp.float32)
    output_sum = jnp.zeros(output_weight.shape, jnp.float32)
    router_sum = jnp.zeros(router_weight.shape, jnp.float32)
    attn_gain_sum = jnp.zeros(attention_gain.shape, jnp.float32)
    ffn_gain_sum = jnp.zeros(feedforward_gain.shape, jnp.float32)
    gate_sum = jnp.zeros(gate_weight.shape, jnp.float32)
    up_sum = jnp.zeros(up_weight.shape, jnp.float32)
    down_sum = jnp.zeros(down_weight.shape, jnp.float32)
    layer_outputs = []
    input_grads = []
    for micro_index in range(micro_count):
        states = tokens[micro_index].astype(jnp.float32)
        out_grad = cotangent[micro_index].astype(jnp.float32)
        place = positions[micro_index]
        chosen = routes[micro_index]
        starts = row_ids - place
        cosine_table, sine_table = rope_tables(place, head_dim)
        normed_full, attn_norm_pull = jax.vjp(rms_norm, states, attention_gain)
        normalized_input = normed_full.astype(jnp.bfloat16)
        query_pre = jnp.dot(
            normalized_input, query_weight, preferred_element_type=jnp.float32
        ).reshape(length, kv_local, query_group_count, head_dim)
        query_rows = rotary_apply(query_pre, cosine_table, sine_table).astype(jnp.bfloat16)
        key_pre = jnp.dot(normalized_input, key_matrix, preferred_element_type=jnp.float32).reshape(
            length, kv_local, head_dim
        )
        key_row_states = rotary_apply(key_pre, cosine_table, sine_table).astype(jnp.bfloat16)
        value_rows = (
            jnp.dot(normalized_input, value_matrix, preferred_element_type=jnp.float32)
            .astype(jnp.bfloat16)
            .reshape(length, kv_local, head_dim)
        )
        attention_output, log_totals = attention_forward(
            query_rows, key_row_states, value_rows, starts, row_ids, block_rows, score_scale
        )
        attention_output = attention_output.reshape(length, kv_local * query_group_count * head_dim)
        attn_part = jnp.dot(attention_output, output_weight, preferred_element_type=jnp.float32)
        hidden_state = states + lax.psum(attn_part, "tensor")
        normed_ffn_full, ffn_norm_pull = jax.vjp(rms_norm, hidden_state, feedforward_gain)
        normed_ffn = normed_ffn_full.astype(jnp.bfloat16)
        state_half = lax.dynamic_slice_in_dim(normed_ffn, offset, half, 0)
        route_half = lax.dynamic_slice_in_dim(chosen, offset, half, 0)
        grad_half = lax.dynamic_slice_in_dim(out_grad, offset, half, 0)
        route_mask = (route_half[..., None] == expert_ids[None, None, :]).astype(jnp.float32)

        def gate_softmax(logits, route_mask=route_mask):
            return jax.nn.softmax(jnp.sum(logits[:, None, :] * route_mask, axis=-1), axis=-1)

        logits = jnp.dot(state_half, router_weight, preferred_element_type=jnp.float32)
        gate_probs, gate_pull = jax.vjp(gate_softmax, logits)
        flat_routes = route_half.reshape(-1)
        route_onehot = (flat_routes[:, None] == expert_ids[None, :]).astype(jnp.int32)
        ahead = jnp.tril(jnp.ones((half * top_count, half * top_count), jnp.float32), -1)
        ranks = jnp.sum(
            jnp.dot(ahead, route_onehot.astype(jnp.float32)).astype(jnp.int32) * route_onehot, axis=1
        )
        slot_index = flat_routes * capacity + ranks
        copies = jnp.repeat(state_half, top_count, axis=0)
        send_rows = (
            jnp.zeros((EXPERTS * capacity, model_width), jnp.bfloat16).at[slot_index].set(copies)
        )
        received = lax.all_to_all(
            spread_rows(send_rows, group, capacity, n_dev, per_dev, model_width),
            "expert",
            split_axis=0,
            concat_axis=0,
            tiled=True,
        ).reshape(n_dev, per_dev, capacity, model_width)
        gate_pre = jnp.einsum(
            "skcd,dkf->skcf", received, gate_three, preferred_element_type=jnp.float32
        )
        up_pre = jnp.einsum(
            "skcd,dkf->skcf", received, up_three, preferred_element_type=jnp.float32
        )
        activated, gelu_pull = jax.vjp(gelu_exact, gate_pre)
        expert_hidden = (activated * up_pre).astype(jnp.bfloat16)
        partial_out = jnp.einsum(
            "skcf,kfd->skcd", expert_hidden, down_three, preferred_element_type=jnp.float32
        )
        back_rows = lax.all_to_all(
            partial_out.reshape(n_dev, per_dev * capacity, model_width).astype(jnp.bfloat16),
            "expert",
            split_axis=0,
            concat_axis=0,
            tiled=True,
        ).astype(jnp.float32)
        returned_rows = collect_rows(
            back_rows, group, capacity, model_width, slot_index, half, top_count
        )
        mixture_half = jnp.sum(gate_probs[..., None] * returned_rows, axis=1)
        mixture = lax.all_gather(
            mixture_half.astype(jnp.bfloat16), "tensor", axis=0, tiled=True
        ).astype(mixture_half.dtype)
        layer_outputs.append((hidden_state + mixture).astype(jnp.bfloat16))
        gate_grad = jnp.sum(grad_half[:, None, :] * returned_rows, axis=-1)
        row_grad = (
            (gate_probs[..., None] * grad_half[:, None, :])
            .astype(jnp.bfloat16)
            .reshape(-1, model_width)
        )
        send_grad = (
            jnp.zeros((EXPERTS * capacity, model_width), jnp.bfloat16).at[slot_index].set(row_grad)
        )
        grad_received = lax.all_to_all(
            spread_rows(send_grad, group, capacity, n_dev, per_dev, model_width),
            "expert",
            split_axis=0,
            concat_axis=0,
            tiled=True,
        ).reshape(n_dev, per_dev, capacity, model_width)
        hidden_grad = jnp.einsum(
            "skcd,kfd->skcf", grad_received, down_three, preferred_element_type=jnp.float32
        )
        down_part = jnp.einsum(
            "skcf,skcd->kfd", expert_hidden, grad_received, preferred_element_type=jnp.float32
        ).reshape(down_weight.shape)
        gate_pre_grad = gelu_pull(hidden_grad * up_pre)[0].astype(jnp.bfloat16)
        up_pre_grad = (hidden_grad * activated).astype(jnp.bfloat16)
        gate_part = jnp.einsum(
            "skcd,skcf->dkf", received, gate_pre_grad, preferred_element_type=jnp.float32
        ).reshape(gate_weight.shape)
        up_part = jnp.einsum(
            "skcd,skcf->dkf", received, up_pre_grad, preferred_element_type=jnp.float32
        ).reshape(up_weight.shape)
        input_part = jnp.einsum(
            "skcf,dkf->skcd", gate_pre_grad, gate_three, preferred_element_type=jnp.float32
        )
        input_part = input_part + jnp.einsum(
            "skcf,dkf->skcd", up_pre_grad, up_three, preferred_element_type=jnp.float32
        )
        input_back = lax.all_to_all(
            input_part.reshape(n_dev, per_dev * capacity, model_width).astype(jnp.bfloat16),
            "expert",
            split_axis=0,
            concat_axis=0,
            tiled=True,
        ).astype(jnp.float32)
        route_input = collect_rows(
            input_back, group, capacity, model_width, slot_index, half, top_count
        )
        logit_grad = gate_pull(gate_grad)[0].astype(jnp.bfloat16)
        router_part = jnp.dot(state_half.T, logit_grad, preferred_element_type=jnp.float32)
        ffn_half_grad = jnp.sum(route_input, axis=1) + jnp.dot(
            logit_grad, router_weight.T, preferred_element_type=jnp.float32
        )
        gate_sum = gate_sum + gate_part
        up_sum = up_sum + up_part
        down_sum = down_sum + down_part
        router_sum = router_sum + router_part
        normed_ffn_grad = lax.all_gather(ffn_half_grad, "tensor", axis=0, tiled=True)
        state_norm_grad, ffn_gain_grad = ffn_norm_pull(normed_ffn_grad)
        state_grad = out_grad + state_norm_grad
        ffn_gain_sum = ffn_gain_sum + ffn_gain_grad
        attention_grad = state_grad.astype(jnp.bfloat16)
        output_sum = output_sum + jnp.dot(
            attention_output.T, attention_grad, preferred_element_type=jnp.float32
        )
        attended_grad = (
            jnp.dot(attention_grad, output_weight.T, preferred_element_type=jnp.float32)
            .astype(jnp.bfloat16)
            .reshape(length, kv_local, query_group_count, head_dim)
        )
        query_grad, key_grad, value_grad = attention_backward(
            query_rows,
            key_row_states,
            value_rows,
            starts,
            row_ids,
            block_rows,
            score_scale,
            log_totals,
            attended_grad,
        )
        query_grad = (
            unrotate(query_grad, cosine_table, sine_table).astype(jnp.bfloat16).reshape(length, -1)
        )
        key_grad = (
            unrotate(key_grad, cosine_table, sine_table).astype(jnp.bfloat16).reshape(length, -1)
        )
        value_grad = value_grad.astype(jnp.bfloat16).reshape(length, -1)
        query_sum = query_sum + jnp.dot(
            normalized_input.T, query_grad, preferred_element_type=jnp.float32
        )
        key_sum = key_sum + jnp.dot(
            normalized_input.T, key_grad, preferred_element_type=jnp.float32
        )
        value_sum = value_sum + jnp.dot(
            normalized_input.T, value_grad, preferred_element_type=jnp.float32
        )
        normed_part = jnp.dot(query_grad, query_weight.T, preferred_element_type=jnp.float32)
        normed_part = normed_part + jnp.dot(
            key_grad, key_matrix.T, preferred_element_type=jnp.float32
        )
        normed_part = normed_part + jnp.dot(
            value_grad, value_matrix.T, preferred_element_type=jnp.float32
        )
        normed_grad = lax.psum(normed_part, "tensor")
        state_in_grad, attn_gain_grad = attn_norm_pull(normed_grad)
        attn_gain_sum = attn_gain_sum + attn_gain_grad
        input_grads.append(state_grad + state_in_grad)
    gate_sum, up_sum, down_sum, router_sum = lax.psum(
        (gate_sum, up_sum, down_sum, router_sum), "tensor"
    )
    reduced = lax.psum(
        (query_sum, key_sum, value_sum, output_sum, router_sum, attn_gain_sum, ffn_gain_sum),
        "expert",
    )
    return (
        jnp.stack(layer_outputs),
        jnp.stack(input_grads),
        reduced[5],
        reduced[6],
        reduced[0],
        reduced[1],
        reduced[2],
        reduced[3],
        reduced[4],
        gate_sum,
        up_sum,
        down_sum,
    )


MESH = pl.DeviceIdType.MESH
ANY = pl.ANY
VMEM_LIMIT = 60 * 2**20


def mm(a, b):
    return lax.dot_general(a, b, (((1,), (0,)), ((), ())), preferred_element_type=jnp.float32)


def mm_nt(a, b):
    return lax.dot_general(a, b, (((1,), (1,)), ((), ())), preferred_element_type=jnp.float32)


def mm_tn(a, b):
    return lax.dot_general(a, b, (((0,), (0,)), ((), ())), preferred_element_type=jnp.float32)


def remote(src, dst, send_sem, recv_sem, device):
    return pltpu.make_async_remote_copy(
        src_ref=src,
        dst_ref=dst,
        send_sem=send_sem,
        recv_sem=recv_sem,
        device_id=device,
        device_id_type=MESH,
    )


def tiles(count, body):
    def step(i, carry):
        body(i)
        return carry

    lax.fori_loop(0, count, step, 0)


def cols(i, width):
    return pl.ds(pl.multiple_of(i * width, width), width)


def front_kernel(
    tok_hbm, g_hbm, wq_hbm, wk_hbm, wv_hbm, wo_hbm, wg_hbm, wu_hbm, wd_hbm,
    pos_ref, routes_ref, gain_a, gain_f, router_ref,
    dx_hbm, nrm_hbm, att_hbm, q_hbm, k_hbm, v_hbm, pr_hbm, tab_hbm, hs_hbm, x_hbm, y0_hbm, y1_hbm, hot_hbm,
    fn, fa, rx_ref, rh_ref, rg_ref, ru_ref, re_ref,
    tok_ref, wq_ref, wk_ref, wv_ref, wo_ref, nrm_ref, att_ref, q_ref, k_ref, v_ref, pr_ref, tab_ref, hs_ref, x_ref,
    xz, gz, rz, xs, gs, xr, gr, eg, hid, gpg, upg, dx_ref, dr, dz, own_part, other_part, rel,
    onehot, prob, gg, wg, wu, wd,
    r_s, r_r, za_s, za_r, xa_s, xa_r, xb_s, xb_r, zb_s, zb_r, pair_s, pair_r, part_s, part_r, fw_s, rel_s, rel_r,
    f_s, f_r, w_s, w_r, in_sem, out_sem, own_sem,
):
    ys, ds_, zd = gs, xs, xz
    e = lax.axis_index("expert")
    c = lax.axis_index("tensor")
    z = e // 4
    o = lax.rem(e, 4) * 2 + c
    micro, length, width = tok_ref.shape
    half = length // 2
    f32 = jnp.float32
    bf = jnp.bfloat16
    ff = wg.shape[1]
    col = 4 * half
    rows = xs.shape[1]
    blk = rows // 8
    cap = blk // 4
    me = 2 * e + c
    tw = 256
    nt = width // tw

    def z_dev(k):
        return (lax.rem(z + k, 4) * 4 + lax.rem(e, 4), c)

    def z_back(k):
        return (lax.rem(z + 4 - k, 4) * 4 + lax.rem(e, 4), c)

    def p_dev(d):
        t = lax.rem(o + d, 8)
        return (z * 4 + t // 2, lax.rem(t, 2))

    def p_back(d):
        t = lax.rem(o + 8 - d, 8)
        return (z * 4 + t // 2, lax.rem(t, 2))

    inner = (z == 1) | (z == 2)
    edge = (z == 0) | (z == 3)
    not_first = z != 0
    not_last = z != 3
    beside = jnp.where((z == 0) | (z == 3), jnp.where(z == 0, 1, 2), jnp.where(z == 1, 0, 3))
    beside_dev = (beside * 4 + lax.rem(e, 4), c)
    far_slot = jnp.where(z == 1, 1, 3)
    far_back = jnp.where(z == 0, 1, 3)

    @pl.when(z == 3)
    def _():
        for m in range(micro):
            dz[m, half : 2 * half, :] = jnp.zeros((half, width + 128), bf)

    @pl.when(z == 0)
    def _():
        for m in range(micro):
            dz[m, 3 * half : 4 * half, :] = jnp.zeros((half, width + 128), bf)

    barrier = pltpu.get_barrier_semaphore()
    for k in range(1, 4):
        pl.semaphore_signal(barrier, inc=1, device_id=z_dev(k), device_id_type=MESH)
    for d in range(1, 8):
        pl.semaphore_signal(barrier, inc=1, device_id=p_dev(d), device_id_type=MESH)
    loads = {}
    for i, (name, src, dst) in enumerate(
        (
            ("tok", tok_hbm, tok_ref), ("wq", wq_hbm, wq_ref), ("wk", wk_hbm, wk_ref), ("wv", wv_hbm, wv_ref),
            ("wo", wo_hbm, wo_ref), ("wg", wg_hbm.at[:, cols(c, ff)], wg), ("wu", wu_hbm.at[:, cols(c, ff)], wu),
            ("wd", wd_hbm.at[cols(c, ff), :], wd),
        )
    ):
        loads[name] = pltpu.make_async_copy(src, dst, in_sem.at[i])
        loads[name].start()
    saves = []

    def save(src, dst):
        cp = pltpu.make_async_copy(src, dst, out_sem.at[len(saves)])
        cp.start()
        saves.append(cp)

    pl.semaphore_wait(barrier, 10)

    mine = pl.ds(pl.multiple_of(c * half, half), half)
    sent = []
    got_r = []
    for k in range(1, 4):
        cp = remote(routes_ref, rz.at[k], r_s.at[k], r_r.at[k], z_dev(k))
        cp.start()
        sent.append(cp)
        got_r.append(cp)
    got_z = {}

    sent_if = []
    away = {}
    got_f = {}

    def start_if(cond, cp):
        pl.when(cond)(cp.start)
        sent_if.append((cond, cp))

    cut = width // 2
    parts = (((0, width),), ((0, cut), (cut, width + 128 - cut)))

    def sem_of(m, a, j, k, per):
        return ((m * 2 + a) * 2 + j) * per + k

    def z_send(m, a):
        src, dst = ((g_hbm, gz), (x_ref, xz))[a]
        for j, (left, size) in enumerate(parts[a]):
            wide = pl.ds(left, size)
            for k in (2, 1, 3):
                i = sem_of(m, a, j, k, 4)
                cp = remote(
                    src.at[m, mine, wide], dst.at[m, pl.ds(k * half, half), wide],
                    za_s.at[i], za_r.at[i], z_dev(k),
                )
                cond = {1: not_last, 2: True, 3: not_first}[k]
                if k == 2:
                    cp.start()
                else:
                    pl.when(cond)(cp.start)
                got_z[(m, a, j, k)] = cp
                away.setdefault((m, a), []).append((cond, cp))
        if a == 1:
            dst[m, 0:half, :] = src[m, mine, :]
        else:
            cp = pltpu.make_async_copy(src.at[m, mine, :], dst.at[m, 0:half, :], in_sem.at[8 + m])
            cp.start()
            loads[("g", m)] = cp

    def z_sent(m, a):
        for cond, cp in away.pop((m, a)):
            if cond is True:
                cp.wait_send()
            else:
                pl.when(cond)(cp.wait_send)

    def z_forward(m, a):
        dst = (gz, xz)[a]
        for j, (left, size) in enumerate(parts[a]):
            wide = pl.ds(left, size)
            got_z[(m, a, j, 2)].wait_recv()
            cp = remote(
                dst.at[m, pl.ds(2 * half, half), wide],
                dst.at[m, pl.ds(pl.multiple_of(far_slot * half, half), half), wide],
                fw_s.at[sem_of(m, a, j, 0, 1)], za_r.at[sem_of(m, a, j, 0, 4) + far_slot], beside_dev,
            )
            pl.when(inner)(cp.start)
            got_f[(m, a, j)] = cp

    z_send(0, 0)
    rz[0] = routes_ref[...]

    qx = lax.rem(e, 2)
    qy = lax.rem(e, 4) // 2
    every = micro * length
    twin = (e, 1 - c)
    got_a = {}

    def f_dev(d):
        return (z * 4 + lax.rem(qy + d // 2, 2) * 2 + lax.rem(qx + d % 2, 2), c)

    def block(d):
        return pl.ds(pl.multiple_of(d * every + c * length, length), length)

    def factor(i, dst):
        for d in (1, 2):
            if i == 0:
                size = width // 2
                view = nrm_ref.at[c, :, cols(lax.rem(qx + d % 2, 2), size)]
                to = dst.at[block(d), :]
                copies = [(view, to)]
            else:
                size = att_ref.shape[2] // 2
                at = cols(lax.rem(qy + d // 2, 2), size)
                copies = [
                    (att_ref.at[m, :, at], dst.at[pl.ds(d * every + m * length, length), :])
                    for m in range(micro)
                ]
            for m, (view, to) in enumerate(copies):
                n = (d * 2 + i // 2) * 2 + m
                cp = remote(view, to, f_s.at[n], f_r.at[n], f_dev(d))
                cp.start()
                sent.append(cp)
                got_a[(i, d, m)] = cp

    def to_twin(d):
        got_a[(0, d, 0)].wait_recv()
        cp = remote(fn.at[block(d), :], fn.at[block(d), :], w_s.at[d], w_r.at[d], twin)
        cp.start()
        sent.append(cp)
        got_a[("twin", d)] = cp

    def pass_on():
        to_twin(1)
        to_twin(2)
        cp = remote(fn.at[block(1), :], fn.at[block(3), :], f_s.at[12], f_r.at[12], f_dev(2))
        cp.start()
        sent.append(cp)
        got_a[(0, 3, 0)] = cp
        for m in range(micro):
            got_a[(2, 2, m)].wait_recv()
        cp = remote(
            fa.at[pl.ds(2 * every, every), :], fa.at[pl.ds(3 * every, every), :], f_s.at[13], f_r.at[13], f_dev(1)
        )
        cp.start()
        sent.append(cp)
        got_a[(2, 3, 0)] = cp

    head = HEAD_SIZE
    heads = wq_ref.shape[1] // head
    lane = lax.broadcasted_iota(jnp.int32, (1, 128), 1)
    row = lax.broadcasted_iota(jnp.int32, (length, length), 0)
    column = lax.broadcasted_iota(jnp.int32, (length, length), 1)
    turn = jnp.exp(
        (-2.0 / head * jnp.log(jnp.float32(theta_base))) * lax.rem(lane, head // 2).astype(f32)
    )
    allowed = []
    loads["tok"].wait()
    for m in range(micro):
        states = tok_ref[m].astype(f32)
        scale = lax.rsqrt(jnp.mean(states * states, axis=1, keepdims=True) + epsilon)
        nrm_ref[m] = (states * scale * gain_a[...].reshape(1, width)).astype(bf)
        place = pos_ref[m : m + 1, :].astype(f32)
        place = jnp.sum(jnp.where(row == column, place, 0.0), axis=1, keepdims=True)
        angle = place * turn
        tab_ref[m, 0] = jnp.cos(angle)
        tab_ref[m, 1] = jnp.where(lane < head // 2, -1.0, 1.0) * jnp.sin(angle)
        allowed.append((column <= row) & (column >= row - place.astype(jnp.int32)))

    def rope(u, m):
        return u * tab_ref[m, 0] + pltpu.roll(u, head // 2, 1) * tab_ref[m, 1]

    factor(0, fn)
    save(nrm_ref, nrm_hbm)
    save(tab_ref, tab_hbm)
    everything = nrm_ref[...].reshape(micro * length, width)

    def project(i):
        both = mm(everything, wq_ref[:, cols(i, tw)])
        for m in range(micro):
            for j in range(tw // head):
                at = pl.ds(pl.multiple_of((i * (tw // head) + j) * length, length), length)
                u = both[m * length : (m + 1) * length, j * head : (j + 1) * head]
                q_ref[m, at, :] = rope(u, m).astype(bf)

    for name in ("wq", "wk", "wv"):
        loads[name].wait()
    tiles(wq_ref.shape[1] // tw, project)
    key_pre = mm(everything, wk_ref[...])
    value_pre = mm(everything, wv_ref[...])
    for m in range(micro):
        at = slice(m * length, (m + 1) * length)
        k_ref[m] = rope(key_pre[at], m).astype(bf)
        v_ref[m] = value_pre[at].astype(bf)
    for m in range(micro):
        score = mm_nt(q_ref[m], k_ref[m]).reshape(heads, length, length) * (head**-0.5)
        score = jnp.where(allowed[m][None], score, masked_score)
        weight = jnp.exp(score - jnp.max(score, axis=-1, keepdims=True))
        weight = weight / jnp.sum(weight, axis=-1, keepdims=True)
        weight = weight.reshape(heads * length, length)
        pr_ref[m] = weight
        out = mm(weight.astype(bf), v_ref[m]).astype(bf)
        for h in range(heads):
            att_ref[m, :, h * head : (h + 1) * head] = out[h * length : (h + 1) * length]
    for src, dst in ((q_ref, q_hbm), (k_ref, k_hbm), (v_ref, v_hbm), (pr_ref, pr_hbm), (att_ref, att_hbm)):
        save(src, dst)
    factor(2, fa)
    z_forward(0, 0)
    z_sent(0, 0)
    for m in range(1, micro):
        z_send(m, 0)
    loads["wo"].wait()
    att_all = att_ref[...].reshape(micro * length, heads * head)
    got_part = []
    for j in range(3):

        def outward(i, j=j):
            at = cols(i + j * (nt // 3), tw)
            own_part[:, at] = mm(att_all, wo_ref[:, at])

        tiles(nt // 3, outward)
        at = pl.ds(j * (width // 3), width // 3)
        cp = remote(
            own_part.at[:, at], other_part.at[:, at], part_s.at[j], part_r.at[j], (e, 1 - c)
        )
        cp.start()
        sent.append(cp)
        got_part.append(cp)

    for cp in got_r:
        cp.wait_recv()

    before = ((row < column) & (row // half == column // half)).astype(bf)
    expert = 8 * z + lax.rem(o + lax.broadcasted_iota(jnp.int32, (8, length), 0), 8)
    place_row = lax.broadcasted_iota(jnp.int32, (length, col), 0)
    place_col = lax.broadcasted_iota(jnp.int32, (length, col), 1)
    slots = [jnp.zeros((8, col), f32) for _ in range(micro)]
    for k in range(4):
        at = place_col - k * half
        put = ((at >= 0) & (at < half) & (place_row == at + c * half)).astype(bf)
        for m in range(micro):
            named = rz[k, m]
            hit = named[0:1, :] == expert
            for j in range(1, routes_ref.shape[1]):
                hit = hit | (named[j : j + 1, :] == expert)
            mask = jnp.where(hit, 1.0, 0.0)
            rank = mm(mask.astype(bf), before)
            slots[m] = slots[m] + mm((mask * (rank + (cap * k + 1))).astype(bf), put)
    number = lax.broadcasted_iota(jnp.int32, (blk, col), 0) + 1
    for m in range(micro):
        for d in range(8):
            spot = slots[m][d : d + 1, :].astype(jnp.int32)
            onehot[m, d * blk : (d + 1) * blk, :] = jnp.where(spot == number, 1.0, 0.0).astype(
                jnp.bfloat16
            )

    got_p = {}

    def pack(m, a):
        src, out, dst = ((gz, gs, gr), (xz, xs, xr))[a]
        if a == 0:
            loads[("g", m)].wait()
        for j, (left, size) in enumerate(parts[a]):
            for k in (1, 3):
                got_z[(m, a, j, k)].wait_recv()

            def body(i, left=left):
                at = cols(i + left // tw, tw)
                out[m, :, at] = mm(onehot[m], src[m, :, at]).astype(bf)

            tiles(size // tw, body)
            if (left + size) % tw:
                out[m, :, width:] = mm(onehot[m], src[m, :, width:]).astype(bf)
            wide = slice(left, left + size)
            dst[m, 0:blk, wide] = out[m, 0:blk, wide]
            wide = pl.ds(left, size)
            for d in range(1, 8):
                i = sem_of(m, a, j, d, 8)
                at = pl.ds(d * blk, blk)
                cp = remote(
                    out.at[m, at, wide], dst.at[m, at, wide], xa_s.at[i], xa_r.at[i], p_dev(d)
                )
                cp.start()
                sent_p.setdefault((m, a), []).append(cp)
                got_p[(m, a, j, d)] = cp

    sent_p = {}
    pack(0, 0)
    pass_on()
    tall = lax.broadcasted_iota(jnp.int32, (128, EXPERTS), 0)
    double = (lax.rem(tall, EXPERTS) == lax.broadcasted_iota(jnp.int32, (128, EXPERTS), 1)) & (
        tall < 2 * EXPERTS
    )
    router = mm(jnp.where(double, 1.0, 0.0).astype(bf), router_ref[...]).astype(bf)
    for cp in got_part:
        cp.wait_recv()
    for m in range(micro):
        at = slice(m * length, (m + 1) * length)
        state = tok_ref[m].astype(f32) + (own_part[at, :] + other_part[at, :])
        hs_ref[m] = state
        save(hs_ref.at[m], hs_hbm.at[m])
        scale = lax.rsqrt(jnp.mean(state * state, axis=1, keepdims=True) + epsilon)
        low = (state * scale * gain_f[...].reshape(1, width)).astype(bf)
        x_ref[m, :, 0:width] = low
        logits = mm_nt(low, router)
        names = lax.rem(lane, EXPERTS)
        hit = lane < 0
        for j in range(routes_ref.shape[1]):
            named = routes_ref[m, j : j + 1, :].astype(f32)
            named = jnp.sum(jnp.where(row == column, named, 0.0), axis=1, keepdims=True)
            hit = hit | (named.astype(jnp.int32) == names)
        hit = hit & (lane < 2 * EXPERTS)
        best = jnp.max(jnp.where(hit, logits, masked_score), axis=1, keepdims=True)
        weight = jnp.where(hit, jnp.exp(logits - best), 0.0)
        first = jnp.sum(jnp.where(lane < EXPERTS, weight, 0.0), axis=1, keepdims=True)
        weight = weight / first
        top = weight.astype(bf).astype(f32)
        x_ref[m, :, width:] = jnp.where(lane < EXPERTS, top, weight - top).astype(bf)
        if m == 0:
            z_send(m, 1)
        save(x_ref.at[m], x_hbm.at[m])
    for m in range(1, micro):
        z_forward(m, 0)
        pack(m, 0)
    z_forward(0, 1)
    z_sent(0, 1)
    for m in range(1, micro):
        z_send(m, 1)
    pack(0, 1)
    for m in range(1, micro):
        z_forward(m, 1)
        pack(m, 1)
    for name in ("wg", "wu", "wd"):
        loads[name].wait()
    save(onehot, hot_hbm)

    got_b = {}
    def to_pair(m):
        for i, (src, dst) in enumerate(
            ((xr, rx_ref), (hid, rh_ref), (gpg, rg_ref), (upg, ru_ref), (eg, re_ref))
        ):
            src_at = src.at[m, :, 0:width] if i == 0 else src.at[m]
            n = m * 8 + i
            cp = remote(src_at, dst.at[c, m], pair_s.at[n], pair_r.at[n], (e, 1 - c))
            cp.start()
            sent.append(cp)
            got_b[("pair", m, i)] = cp
            cp = pltpu.make_async_copy(src_at, dst.at[c, m], own_sem.at[n])
            cp.start()
            saves.append(cp)

    def send_back(m, a, j):
        src, dst = ((ds_.at[m], dr.at[m]), (ys.at[m], y0_hbm))[a]
        left, size = parts[1 - a][j]
        if a == 0:
            wide = slice(left, left + size)
            dst[0:blk, wide] = src[0:blk, wide]
        else:
            save(src.at[0:blk, :], dst.at[0:blk, :])
        wide = pl.ds(left, size)
        for d in range(1, 8):
            i = sem_of(m, a, j, d, 8)
            at = pl.ds(d * blk, blk)
            cp = remote(src.at[at, wide], dst.at[at, wide], xb_s.at[i], xb_r.at[i], p_back(d))
            cp.start()
            sent.append(cp)
            got_b[(m, a, j, d)] = cp

    def run(m):
        for a in range(2):
            for j in range(len(parts[a])):
                for d in range(1, 8):
                    got_p[(m, a, j, d)].wait_recv()
            for cp in sent_p[(m, a)]:
                cp.wait_send()
        tail = xr[m, :, width:].astype(jnp.float32)
        pick = (lane == me) | (lane == me + 32)
        prob[...] = jnp.broadcast_to(
            jnp.sum(jnp.where(pick, tail, 0.0), axis=1, keepdims=True), (rows, 128)
        )
        gg[...] = jnp.zeros_like(gg)

        def weigh(i):
            at = cols(i, tw)
            eg[m, :, at] = (prob[:, 0:1] * gr[m, :, at].astype(jnp.float32)).astype(jnp.bfloat16)

        tiles(nt, weigh)

        def inner(i):
            at = cols(i, tw)
            xrow = xr[m, :, 0:width]
            gate = mm(xrow, wg[:, at])
            upv = mm(xrow, wu[:, at])
            back = mm_nt(eg[m], wd[at, :])
            cdf = 0.5 * (1.0 + lax.erf(gate * 0.7071067811865476))
            act = gate * cdf
            slope = cdf + gate * (jnp.exp(gate * gate * -0.5) * 0.3989422804014327)
            hid[m, :, at] = (act * upv).astype(jnp.bfloat16)
            gpg[m, :, at] = (back * upv * slope).astype(jnp.bfloat16)
            upg[m, :, at] = (back * act).astype(jnp.bfloat16)

        tiles(ff // tw, inner)

        def outer(i):
            at = cols(i, tw)
            low = mm(hid[m], wd[:, at]).astype(jnp.bfloat16).astype(jnp.float32)
            gg[...] += jnp.broadcast_to(
                jnp.sum(low * gr[m, :, at].astype(jnp.float32), axis=1, keepdims=True),
                (rows, 128),
            )
            ys[m, :, at] = (prob[:, 0:1] * low).astype(jnp.bfloat16)

        tiles(nt, outer)

        def inputs(i):
            at = cols(i, tw)
            ds_[m, :, at] = (mm_nt(gpg[m], wg[at, :]) + mm_nt(upg[m], wu[at, :])).astype(
                jnp.bfloat16
            )

        tiles(cut // tw, inputs)
        send_back(m, 0, 0)
        tiles((width - cut) // tw, lambda i: inputs(i + cut // tw))
        total = gg[...]
        high = total.astype(jnp.bfloat16).astype(jnp.float32)
        ds_[m, :, width:] = jnp.where(
            lane == me, high, jnp.where(lane == me + 32, total - high, 0.0)
        ).astype(jnp.bfloat16)
        send_back(m, 0, 1)
        to_pair(m)

    for m in range(micro):
        run(m)
    send_back(0, 1, 0)
    save(ys.at[1], y1_hbm)

    got_c = {}

    def gather(m, j):
        left, size = parts[1][j]
        for d in range(1, 8):
            got_b[(m, 0, j, d)].wait_recv()
        pl.when(inner)(got_f[(m, 1, j)].wait_send)

        def body(i):
            at = cols(i + left // tw, tw)
            zd[m, :, at] = mm_tn(onehot[m], dr[m, :, at]).astype(bf)

        tiles(size // tw, body)
        if j == 1:
            zd[m, :, width:] = mm_tn(onehot[m], dr[m, :, width:]).astype(bf)
        wide = pl.ds(left, size)
        far = pl.ds(pl.multiple_of(far_back * half, half), half)
        relay = remote(
            zd.at[m, far, wide], rel.at[m, :, wide], rel_s.at[m * 2 + j], rel_r.at[m * 2 + j], beside_dev
        )
        start_if(edge, relay)
        for k in (1, 3, 2):
            i = (m * 2 + j) * 4 + k
            at = pl.ds(k * half, half)
            cp = remote(zd.at[m, at, wide], dz.at[m, at, wide], zb_s.at[i], zb_r.at[i], z_back(k))
            got_c[(m, j, k)] = cp
            if k == 2:

                @pl.when(inner)
                def _():
                    relay.wait_recv()
                    here = slice(left, left + size)
                    zd[m, 2 * half : 3 * half, here] = (
                        zd[m, 2 * half : 3 * half, here].astype(f32) + rel[m, :, here].astype(f32)
                    ).astype(bf)

                cp.start()
                sent.append(cp)
            else:
                start_if(not_first if k == 1 else not_last, cp)

    def finish(m, j):
        left, size = parts[1][j]
        here = slice(left, left + size)
        pl.when(not_last)(got_c[(m, j, 1)].wait_recv)
        pl.when(not_first)(got_c[(m, j, 3)].wait_recv)
        got_c[(m, j, 2)].wait_recv()
        total = zd[m, 0:half, here].astype(f32)
        for k in range(1, 4):
            total = total + dz[m, k * half : (k + 1) * half, here].astype(f32)
        dx_ref[m, mine, here] = total
        n = m * 8 + 5 + j
        wide = pl.ds(left, size)
        cp = remote(
            dx_ref.at[m, mine, wide], dx_ref.at[m, mine, wide], pair_s.at[n], pair_r.at[n], (e, 1 - c)
        )
        cp.start()
        sent.append(cp)
        got_c[("pair", m, j)] = cp

    order = [(m, j) for m in range(micro) for j in range(2)]
    for i, (m, j) in enumerate(order):
        gather(m, j)
        if i >= 1:
            finish(*order[i - 1])
    finish(*order[-1])
    for m in range(micro):
        pl.when(inner)(got_f[(m, 0, 0)].wait_send)
    to_twin(3)
    got_a[(2, 3, 0)].wait_recv()
    for m in range(micro):
        got_a[(2, 1, m)].wait_recv()
    for d in range(1, 4):
        got_a[("twin", d)].wait_recv()
    for m in range(micro):
        for i in range(5):
            got_b[("pair", m, i)].wait_recv()
        for j in range(2):
            got_c[("pair", m, j)].wait_recv()
        save(dx_ref.at[m], dx_hbm.at[m])
    for d in range(1, 8):
        got_b[(0, 1, 0, d)].wait_recv()
    for at in list(away):
        z_sent(*at)
    for cp in saves:
        cp.wait()
    for cp in sent:
        cp.wait_send()
    for cond, cp in sent_if:
        pl.when(cond)(cp.wait_send)


def front_call(
    tokens, cotangent, positions, routes, gain_a, gain_f, wq, wk, wv, wo, router, gate_weight,
    up_weight, down_weight,
):
    micro, length, width = tokens.shape
    wide = width + 128
    half = length // 2
    ff = gate_weight.shape[1] // 2
    cap = 3 * half * routes.shape[1] // (2 * EXPERTS)
    rows = 8 * 4 * cap
    bf = jnp.bfloat16
    f32 = jnp.float32
    vmem = pl.BlockSpec(memory_space=pltpu.VMEM)
    hbm = pl.BlockSpec(memory_space=ANY)
    heads = wq.shape[1] // HEAD_SIZE

    def buf(*shape, dtype=bf):
        return pltpu.VMEM(shape, dtype)

    def out(*shape, dtype=bf):
        return jax.ShapeDtypeStruct(shape, dtype)

    sem = pltpu.SemaphoreType.DMA
    col = 4 * half
    hw = wq.shape[1]
    return pl.pallas_call(
        front_kernel,
        out_shape=(
            out(micro, length, wide, dtype=f32),
            out(micro, length, width),
            out(micro, length, hw),
            out(micro, heads * length, HEAD_SIZE),
            out(micro, length, HEAD_SIZE),
            out(micro, length, HEAD_SIZE),
            out(micro, heads * length, length, dtype=f32),
            out(micro, 2, length, HEAD_SIZE, dtype=f32),
            out(micro, length, width, dtype=f32),
            out(micro, length, wide),
            out(rows, width),
            out(rows, width),
            out(micro, rows, col),
            out(4 * micro * length, width // 2),
            out(4 * micro * length, hw // 2),
            out(2, micro, rows, width),
            out(2, micro, rows, ff),
            out(2, micro, rows, ff),
            out(2, micro, rows, ff),
            out(2, micro, rows, width),
        ),
        in_specs=[hbm] * 9 + [vmem] * 5,
        out_specs=(hbm,) * 20,
        scratch_shapes=[
            buf(micro, length, width), buf(width, hw), buf(width, HEAD_SIZE), buf(width, HEAD_SIZE), buf(hw, width),
            buf(micro, length, width), buf(micro, length, hw), buf(micro, heads * length, HEAD_SIZE),
            buf(micro, length, HEAD_SIZE), buf(micro, length, HEAD_SIZE),
            buf(micro, heads * length, length, dtype=f32), buf(micro, 2, length, HEAD_SIZE, dtype=f32),
            buf(micro, length, width, dtype=f32), buf(micro, length, wide),
            buf(micro, col, wide), buf(micro, col, width), pltpu.VMEM((4, *routes.shape), jnp.int32),
            buf(micro, rows, wide), buf(micro, rows, width), buf(micro, rows, wide), buf(micro, rows, width),
            buf(micro, rows, width), buf(micro, rows, ff), buf(micro, rows, ff), buf(micro, rows, ff),
            buf(micro, length, wide, dtype=f32), buf(micro, rows, wide), buf(micro, col, wide),
            buf(micro * length, width, dtype=f32), buf(micro * length, width, dtype=f32),
            buf(micro, half, wide), buf(micro, rows, col), buf(rows, 128, dtype=f32), buf(rows, 128, dtype=f32),
            buf(width, ff), buf(width, ff), buf(ff, width),
            sem((4,)), sem((4,)), sem((16 * micro,)), sem((16 * micro,)), sem((32 * micro,)), sem((32 * micro,)),
            sem((32 * micro,)), sem((32 * micro,)), sem((8 * micro,)), sem((8 * micro,)), sem((8 * micro,)),
            sem((8 * micro,)), sem((3,)), sem((3,)), sem((4 * micro,)), sem((2 * micro,)), sem((2 * micro,)),
            sem((14,)), sem((14,)), sem((4,)), sem((4,)), sem((8 + micro,)), sem((16 + 5 * micro,)), sem((8 * micro,)),
        ],
        compiler_params=pltpu.CompilerParams(
            collective_id=1, has_side_effects=True, vmem_limit_bytes=VMEM_LIMIT
        ),
        cost_estimate=pl.CostEstimate(
            flops=2 * 6 * micro * rows * width * ff, bytes_accessed=40 * 2**20, transcendentals=0
        ),
        name="front",
    )(
        tokens, cotangent, wq, wk, wv, wo, gate_weight, up_weight, down_weight,
        positions, routes, gain_a, gain_f, router,
    )


def back_kernel(
    tok_hbm, g_hbm, wq_hbm, wk_hbm, wv_hbm, wo_hbm,
    dx_hbm, nrm_hbm, att_hbm, q_hbm, k_hbm, v_hbm, pr_hbm, tab_hbm, hs_hbm, x_hbm, y0_hbm, y1_hbm, hot_hbm,
    fn_hbm, fa_hbm, gain_a, gain_f, router_ref,
    lay_ref, tg_hbm, oa, ob_hbm, os,
    tok_ref, g_ref, wq_ref, wk_ref, wv_ref, wo_ref, dx_ref, q_ref, k_ref, v_ref, pr_ref, tab_ref, hs_ref, x_ref,
    hot, y0r, y1r, zy, yz, rel, tg_ref, ob,
    d_ref, a_ref, s_ref, sg, ag, own_part, other_part,
    fn, fd, fa, fg, fs, pa, pb, za, zb, zs, ra, rb,
    f_s, f_r, w_s, w_r, c_s, c_r, y_s, y_r, l_s, l_r, z_s, z_r, h_s, h_r, p_s, p_r, part_s, part_r,
    yp_s, yp_r, yz_s, yz_r, rel_s, rel_r, pair_s, pair_r, in_sem, out_sem,
):
    micro, length, width = tok_ref.shape
    half = length // 2
    f32 = jnp.float32
    bf = jnp.bfloat16
    head = HEAD_SIZE
    heads = wq_ref.shape[1] // head
    wq = wq_ref.shape[1]
    tw = 256
    nt = width // tw
    e = lax.axis_index("expert")
    c = lax.axis_index("tensor")
    z = e // 4
    q = lax.rem(e, 4)
    qx = lax.rem(q, 2)
    qy = q // 2
    rows = micro * length
    wn = fn.shape[1]
    wd = d_ref.shape[1] // 2
    wa = fa.shape[1]
    per = length
    wg = a_ref.shape[1] // 2
    ws = s_ref.shape[1] // 4
    hs = s_ref.shape[0] // 4
    ha = wn // 4
    hb = wa // 4

    def flip(bit, by):
        return lax.rem(bit + by, 2)

    def p_dev(d):
        return (z * 4 + flip(qy, d // 2) * 2 + flip(qx, d % 2), c)

    def z_dev(k):
        return (lax.rem(z + k, 4) * 4 + q, c)

    def part(i, size):
        return pl.ds(pl.multiple_of(i * size, size), size)

    inner = (z == 1) | (z == 2)
    edge = (z == 0) | (z == 3)
    not_first = z != 0
    not_last = z != 3
    beside = jnp.where(edge, jnp.where(z == 0, 1, 2), jnp.where(z == 1, 0, 3))
    beside_dev = (beside * 4 + q, c)
    twin = (e, 1 - c)
    sent_if = []

    def start_if(cond, cp):
        pl.when(cond)(cp.start)
        sent_if.append((cond, cp))

    o = q * 2 + c
    blk = y1r.shape[0] // 8
    own_rows = pl.ds(pl.multiple_of(c * half, half), half)

    def any_dev(n):
        t = lax.rem(o + n, 8)
        return (z * 4 + t // 2, lax.rem(t, 2))

    def any_back(n):
        t = lax.rem(o + 8 - n, 8)
        return (z * 4 + t // 2, lax.rem(t, 2))

    def fill(m, slot):
        yz[m, slot * half : (slot + 1) * half, :] = jnp.zeros((half, width), bf)

    def clear(slot):
        za[slot] = jnp.zeros((ha, wd), bf)
        zb[slot] = jnp.zeros((hb, wg), bf)

    pl.when(z == 0)(lambda: clear(1))
    pl.when(z == 3)(lambda: clear(3))

    for m in range(micro):
        pl.when(z == 3)(lambda m=m: fill(m, 1))
        pl.when(z == 0)(lambda m=m: fill(m, 3))

    barrier = pltpu.get_barrier_semaphore()
    for n in range(1, 4):
        pl.semaphore_signal(barrier, inc=1, device_id=z_dev(n), device_id_type=MESH)
    for n in range(1, 8):
        pl.semaphore_signal(barrier, inc=1, device_id=any_dev(n), device_id_type=MESH)
    loads = {}
    for i, (name, src, dst) in enumerate(
        (
            ("dx", dx_hbm, dx_ref), ("x", x_hbm, x_ref), ("hs", hs_hbm, hs_ref), ("g", g_hbm, g_ref),
            ("y0", y0_hbm, y0r), ("hot", hot_hbm, hot), ("y1", y1_hbm.at[0:blk, :], y1r.at[0:blk, :]), ("wo", wo_hbm, wo_ref),
            ("v", v_hbm, v_ref), ("pr", pr_hbm, pr_ref), ("k", k_hbm, k_ref), ("q", q_hbm, q_ref),
            ("tab", tab_hbm, tab_ref), ("wq", wq_hbm, wq_ref), ("wk", wk_hbm, wk_ref), ("wv", wv_hbm, wv_ref),
            ("tok", tok_hbm, tok_ref),
            ("fa", fa_hbm.at[rows:, :], fa.at[rows:, :]), ("fa0", att_hbm.at[:, part(qy, wa)], fa.at[0:rows, :]),
            ("fn", fn_hbm.at[rows:, :], fn.at[rows:, :]), ("fn0", nrm_hbm.at[:, part(qx, wn)], fn.at[0:rows, :]),
        )
    ):
        loads[name] = pltpu.make_async_copy(src, dst, in_sem.at[i])
        loads[name].start()
    saves = []

    def save(src, dst):
        cp = pltpu.make_async_copy(src, dst, out_sem.at[len(saves)])
        cp.start()
        saves.append(cp)

    def need(*names):
        for name in names:
            loads[name].wait()

    pl.semaphore_wait(barrier, 10)

    sent = []
    got_f = {}
    bits = {3: 0, 1: 1}

    def piece(src, i, d):
        bit = flip(qx, d % 2) if bits[i] == 0 else flip(qy, d // 2)
        return part(bit, src.shape[1] // 2)

    def mine(d):
        return pl.ds(pl.multiple_of(d * rows + c * per, per), per)

    def factor(i, src, dst):
        for d in (1, 2):
            if bits[i] == 0:
                view = src.at[pl.ds(pl.multiple_of(c * per, per), per), piece(src, i, d)]
                to = dst.at[mine(d), :]
            else:
                view = src.at[:, piece(src, i, d)]
                to = dst.at[pl.ds(d * rows, rows), :]
            cp = remote(view, to, f_s.at[d * 4 + i], f_r.at[d * 4 + i], p_dev(d))
            cp.start()
            sent.append(cp)
            got_f[(i, d)] = cp

    def to_twin(i, d, dst):
        cp = remote(dst.at[mine(d), :], dst.at[mine(d), :], w_s.at[d * 4 + i], w_r.at[d * 4 + i], twin)
        cp.start()
        sent.append(cp)
        got_f[("twin", i, d)] = cp

    def relay(i, dst):
        via, over = (1, 2) if bits[i] == 0 else (2, 1)
        got_f[(i, via)].wait_recv()
        if bits[i] == 0:
            src, to = dst.at[mine(via), :], dst.at[mine(3), :]
        else:
            src, to = dst.at[pl.ds(via * rows, rows), :], dst.at[pl.ds(3 * rows, rows), :]
        cp = remote(src, to, f_s.at[12 + i], f_r.at[12 + i], p_dev(over))
        cp.start()
        sent.append(cp)
        got_f[(i, 3)] = cp
        if bits[i] == 0:
            to_twin(i, via, dst)
            got_f[(i, over)].wait_recv()
            to_twin(i, over, dst)

    def d_rows(d, m):
        return pl.ds(d * rows + m * per, per)

    def factor_d(m):
        for d in (2, 1):
            cp = remote(
                d_ref.at[pl.ds(m * per, per), part(flip(qy, d // 2), wd)], fd.at[d_rows(d, m), :],
                f_s.at[d * 4 + m], f_r.at[d * 4 + m], p_dev(d),
            )
            cp.start()
            sent.append(cp)
            got_f[("d", m, d)] = cp

    def relay_d(m):
        got_f[("d", m, 2)].wait_recv()
        cp = remote(fd.at[d_rows(2, m), :], fd.at[d_rows(3, m), :], f_s.at[12 + m], f_r.at[12 + m], p_dev(1))
        cp.start()
        sent.append(cp)
        got_f[("d", m, 3)] = cp

    def arrive(i, dst):
        if bits[i]:
            got_f[(i, 1)].wait_recv()
            got_f[(i, 3)].wait_recv()
        else:
            got_f[(i, 3)].wait_recv()
            to_twin(i, 3, dst)
            for d in (1, 2, 3):
                got_f[("twin", i, d)].wait_recv()

    got_v = {}
    def send_y1(j):
        wide = pl.ds(j * (width // 2), width // 2)
        for n in range(1, 8):
            at = pl.ds(n * blk, blk)
            cp = remote(
                y1_hbm.at[at, wide], y1r.at[at, wide], yp_s.at[j * 8 + n], yp_r.at[j * 8 + n], any_back(n)
            )
            cp.start()
            sent.append(cp)
            got_v[(n, j, "row")] = cp

    send_y1(0)

    def z_back(n):
        return (lax.rem(z + 4 - n, 4) * 4 + q, c)

    def regroup(m, src):
        def outputs(i):
            at = cols(i, tw)
            zy[m, :, at] = mm_tn(hot[m], src[:, at]).astype(bf)

        tiles(nt, outputs)

    def send_far(m):
        far = part(jnp.where(z == 0, 1, 3), half)
        cp = remote(zy.at[m, far, :], rel.at[m], rel_s.at[m], rel_r.at[m], beside_dev)
        start_if(edge, cp)
        got_v[("far", m)] = cp
        for n in (1, 3):
            at = pl.ds(n * half, half)
            cp = remote(zy.at[m, at, :], yz.at[m, at, :], yz_s.at[m * 4 + n], yz_r.at[m * 4 + n], z_back(n))
            start_if(not_first if n == 1 else not_last, cp)
            got_v[(m, n)] = cp

    def send_near(m):
        at = pl.ds(2 * half, half)

        @pl.when(inner)
        def _():
            got_v[("far", m)].wait_recv()
            zy[m, at, :] = (zy[m, at, :].astype(f32) + rel[m].astype(f32)).astype(bf)

        cp = remote(zy.at[m, at, :], yz.at[m, at, :], yz_s.at[m * 4 + 2], yz_r.at[m * 4 + 2], z_back(2))
        cp.start()
        sent.append(cp)
        got_v[(m, 2)] = cp

    def layer(m):
        pl.when(not_last)(got_v[(m, 1)].wait_recv)
        pl.when(not_first)(got_v[(m, 3)].wait_recv)
        got_v[(m, 2)].wait_recv()
        total = zy[m, 0:half, :].astype(f32)
        for n in range(1, 4):
            total = total + yz[m, n * half : (n + 1) * half, :].astype(f32)
        lay_ref[m, own_rows, :] = (hs_ref[m, own_rows, :] + total).astype(bf)
        cp = remote(
            lay_ref.at[m, own_rows, :], lay_ref.at[m, own_rows, :], pair_s.at[m], pair_r.at[m], twin
        )
        cp.start()
        sent.append(cp)
        got_v[("pair", m)] = cp

    need("dx", "x", "hs", "g")
    lane = lax.broadcasted_iota(jnp.int32, (1, 128), 1)
    gain_row = jnp.zeros((1, width), f32)
    s_ref[...] = jnp.zeros_like(s_ref)
    router_row = jnp.zeros((128, width), f32)
    for m in range(micro):
        here = slice(m * length, (m + 1) * length)
        tail = dx_ref[m, :, width:]
        grad = tail + pltpu.roll(tail, 128 - EXPERTS, 1)
        tail = x_ref[m, :, width:].astype(f32)
        prob = jnp.where(lane < EXPERTS, tail + pltpu.roll(tail, 128 - EXPERTS, 1), 0.0)
        shared = jnp.sum(prob * grad, axis=1, keepdims=True)
        low = (prob * (grad - shared)).astype(bf)
        router_row = router_row + mm_tn(low, x_ref[m, :, 0:width])
        full = dx_ref[m, :, 0:width] + mm(low[:, 0:EXPERTS], router_ref[...])
        state = hs_ref[m]
        scale = lax.rsqrt(jnp.mean(state * state, axis=1, keepdims=True) + epsilon)
        u = full * gain_f[...].reshape(1, width)
        common = jnp.mean(u * state, axis=1, keepdims=True) * (scale * scale * scale)
        total = g_ref[m].astype(f32) + (scale * u - state * common)
        sg[m] = total
        a_ref[here, :] = total.astype(bf)
        gain_row = gain_row + jnp.sum(full * state * scale, axis=0, keepdims=True)
    s_ref[0:EXPERTS, :] = router_row[0:EXPERTS].astype(bf)
    factor(3, a_ref, fg)
    need("y0", "hot", "wo")
    regroup(0, y0r)
    send_far(0)

    def inward(i):
        at = cols(i, tw)
        both = mm_nt(a_ref[...], wo_ref[at, :]).astype(bf)
        for m in range(micro):
            for j in range(tw // head):
                to = pl.ds(pl.multiple_of((i * (tw // head) + j) * length, length), length)
                ag[m, to, :] = both[m * length : (m + 1) * length, j * head : (j + 1) * head]

    tiles(wq // tw, inward)
    relay(3, fg)
    send_near(0)
    need("v", "pr", "k", "q", "tab")

    def unrope(u, m):
        return u * tab_ref[m, 0] - pltpu.roll(u, head // 2, 1) * tab_ref[m, 1]

    for m in range(micro):
        here = slice(m * length, (m + 1) * length)
        prob = pr_ref[m]
        back = mm_nt(ag[m], v_ref[m])
        shared = jnp.sum(prob * back, axis=1, keepdims=True)
        low = (prob * (back - shared)).astype(bf)
        dq = mm(low, k_ref[m]) * (head**-0.5)
        for h in range(heads):
            u = unrope(dq[h * length : (h + 1) * length], m)
            d_ref[here, h * head : (h + 1) * head] = u.astype(bf)
        dk = mm_tn(low, q_ref[m]) * (head**-0.5)
        d_ref[here, wq : wq + head] = unrope(dk, m).astype(bf)
        d_ref[here, wq + head : wq + 2 * head] = mm_tn(prob.astype(bf), ag[m]).astype(bf)
    for m in range(micro):
        factor_d(m)
    need("wq", "wk", "wv")
    got_part = []
    for j in range(3):

        def outward(i, j=j):
            at = cols(i + j * (nt // 3), tw)
            own_part[:, at] = (
                mm_nt(d_ref[:, 0:wq], wq_ref[at, :])
                + mm_nt(d_ref[:, wq : wq + head], wk_ref[at, :])
                + mm_nt(d_ref[:, wq + head :], wv_ref[at, :])
            )

        tiles(nt // 3, outward)
        at = pl.ds(j * (width // 3), width // 3)
        cp = remote(
            own_part.at[:, at], other_part.at[:, at], part_s.at[j], part_r.at[j], (e, 1 - c)
        )
        cp.start()
        sent.append(cp)
        got_part.append(cp)
    fd[0:rows, :] = d_ref[:, part(qy, wd)]
    fg[0:rows, :] = a_ref[:, part(qx, wg)]
    need("fa", "fa0")
    arrive(3, fg)

    def two(i):
        at = cols(i, tw)
        pb[:, at] = mm_tn(fa[...], fg[:, at]).astype(bf)

    tiles(wg // tw, two)
    got_y = {}

    def spread(i):
        src, dst, size, rest = ((pa, za, ha, ra), (pb, zb, hb, rb))[i]
        far = lax.rem(z + jnp.where(z == 0, 3, 1), 4)
        cp = remote(src.at[part(far, size), :], rest, l_s.at[i], l_r.at[i], beside_dev)
        start_if(edge, cp)
        got_y[("far", i)] = cp
        for k in (1, 3):
            cp = remote(
                src.at[part(lax.rem(z + k, 4), size), :], dst.at[k],
                y_s.at[k * 3 + i], y_r.at[k * 3 + i], z_dev(k),
            )
            start_if(not_last if k == 1 else not_first, cp)
            got_y[(i, k)] = cp

    def spread_rest(i):
        src, dst, size, rest = ((pa, za, ha, ra), (pb, zb, hb, rb))[i]
        across = part(lax.rem(z + 2, 4), size)

        @pl.when(inner)
        def _():
            got_y[("far", i)].wait_recv()
            src[across, :] = (src[across, :].astype(f32) + rest[...].astype(f32)).astype(bf)

        cp = remote(src.at[across, :], dst.at[2], y_s.at[6 + i], y_r.at[6 + i], z_dev(2))
        cp.start()
        sent.append(cp)
        got_y[(i, 2)] = cp

    spread(1)
    relay_d(0)
    relay_d(1)
    send_y1(1)
    need("tok")
    for cp in got_part:
        cp.wait_recv()
    last_row = jnp.zeros((1, width), f32)
    for m in range(micro):
        here = slice(m * length, (m + 1) * length)
        full = own_part[here, :] + other_part[here, :]
        state = tok_ref[m].astype(f32)
        scale = lax.rsqrt(jnp.mean(state * state, axis=1, keepdims=True) + epsilon)
        u = full * gain_a[...].reshape(1, width)
        common = jnp.mean(u * state, axis=1, keepdims=True) * (scale * scale * scale)
        tg_ref[m] = sg[m] + (scale * u - state * common)
        save(tg_ref.at[m], tg_hbm.at[m])
        last_row = last_row + jnp.sum(full * state * scale, axis=0, keepdims=True)
    index = lax.broadcasted_iota(jnp.int32, (hs, 1), 0)
    s_ref[2 * hs : 3 * hs, :] = jnp.where(
        index == 0, gain_row, jnp.where(index == 1, last_row, 0.0)
    ).astype(bf)
    got_s = []
    for d in (3, 1, 2):
        to = flip(qy, d // 2) * 2 + flip(qx, d % 2)
        cp = remote(s_ref.at[part(to, hs), :], fs.at[d], c_s.at[d], c_r.at[d], p_dev(d))
        cp.start()
        sent.append(cp)
        got_s.append(cp)
    spread_rest(1)
    need("fn", "fn0")
    for m in range(micro):
        got_f[("d", m, 1)].wait_recv()
        got_f[("d", m, 3)].wait_recv()

    def one(i):
        at = cols(i, tw)
        pa[:, at] = mm_tn(fn[...], fd[:, at]).astype(bf)

    tiles(wd // tw, one)
    spread(0)
    total = s_ref[part(q, hs), :].astype(jnp.float32)
    for cp in got_s:
        cp.wait_recv()
    for d in range(1, 4):
        total = total + fs[d].astype(jnp.float32)
    fs[0] = total.astype(jnp.bfloat16)
    for k in (2, 1, 3):
        cp = remote(
            fs.at[0, :, part(lax.rem(z + k, 4), ws)], zs.at[k],
            y_s.at[k * 3 + 2], y_r.at[k * 3 + 2], z_dev(k),
        )
        cp.start()
        sent.append(cp)
        got_y[(2, k)] = cp
    spread_rest(0)
    layer(0)
    need("y1")
    for n in range(1, 8):
        for j in range(2):
            got_v[(n, j, "row")].wait_recv()

    regroup(1, y1r)
    send_far(1)

    def spots(px, py, t):
        return (
            oa.at[part(px * 4 + t, ha), part(py, wd)],
            ob.at[part(py * 4 + t, hb), part(px, wg)],
            os.at[part(py * 2 + px, hs), part(t, ws)],
        )

    home = spots(qx, qy, z)

    def total_of(i):
        first, others = (
            (pa[part(z, ha), :], za), (pb[part(z, hb), :], zb), (fs[0, :, part(z, ws)], zs),
        )[i]
        if i < 2:
            pl.when(not_first)(got_y[(i, 1)].wait_recv)
            pl.when(not_last)(got_y[(i, 3)].wait_recv)
        else:
            got_y[(i, 1)].wait_recv()
            got_y[(i, 3)].wait_recv()
        got_y[(i, 2)].wait_recv()
        acc = first.astype(f32)
        for k in range(1, 4):
            acc = acc + others[k].astype(f32)
        home[i][...] = acc.astype(bf)
        for k in (2, 1, 3):
            cp = remote(home[i], home[i], z_s.at[k * 3 + i], z_r.at[k * 3 + i], z_dev(k))
            if k == 2:
                cp.start()
                sent.append(cp)
            else:
                start_if(not_last if k == 1 else not_first, cp)

    turns = (
        0,
        jnp.where(inner, 2, jnp.where(z == 0, 3, 1)),
        jnp.where(inner, 1, 2),
        jnp.where(inner, 3, jnp.where(z == 0, 1, 3)),
    )
    got_p = {}

    def send(ref, i, n, d, j):
        at = ((n * 3) + i) * 4 + j
        cp = remote(ref, ref, p_s.at[at], p_r.at[at], p_dev(d))
        cp.start()
        sent.append(cp)
        got_p[(n, i, j)] = cp

    def own(n, i):
        k = turns[n]
        here = spots(qx, qy, lax.rem(z + 4 - k, 4))[i]
        if n:
            cp = remote(here, here, z_s.at[k * 3 + i], z_r.at[k * 3 + i], beside_dev)
            cp.wait_recv()
        if n == 1:
            to = jnp.where(z == 1, 1, 3)
            cp = remote(here, here, h_s.at[i], z_r.at[to * 3 + i], beside_dev)
            start_if(inner, cp)
        send(here, i, n, 1, 1)
        send(here, i, n, 2, 2)

    def forward(n, i):
        t = lax.rem(z + 4 - turns[n], 4)
        if i == 1:
            got_p[(n, i, 2)].wait_recv()
            send(spots(qx, flip(qy, 1), t)[i], i, n, 1, 3)
        else:
            got_p[(n, i, 1)].wait_recv()
            send(spots(flip(qx, 1), qy, t)[i], i, n, 2, 3)

    total_of(1)
    own(0, 1)
    total_of(0)
    own(0, 0)
    total_of(2)
    own(0, 2)
    own(1, 1)
    forward(0, 1)
    own(1, 0)
    send_near(1)
    forward(0, 0)
    forward(0, 2)
    own(1, 2)
    for n in (2, 3):
        for i in (1, 0, 2):
            own(n, i)
            forward(n - 1, i)
    for i in (1, 0, 2):
        forward(3, i)
    layer(1)
    for i in (1, 0, 2):
        for n in range(4):
            first = 1 if i == 1 else 2
            got_p[(n, i, first)].wait_recv()
            got_p[(n, i, 3)].wait_recv()
        if i == 1:
            save(ob, ob_hbm)
    for m in range(micro):
        got_v[("pair", m)].wait_recv()
    for cp in saves:
        cp.wait()
    for cp in sent:
        cp.wait_send()
    for cond, cp in sent_if:
        pl.when(cond)(cp.wait_send)


def back_call(
    tokens, cotangent, gain_a, gain_f, wq, wk, wv, wo, router,
    dx, nrm, att, q, k, v, pr, tab, hs, xrows, y0, y1, hot, fn, fa,
):
    bf = jnp.bfloat16
    f32 = jnp.float32
    micro, length, width = tokens.shape
    rows = micro * length
    half = length // 2
    wd = wq.shape[1] + wk.shape[1] + wv.shape[1]
    wa = wq.shape[1]
    heads = wa // HEAD_SIZE
    vmem = pl.BlockSpec(memory_space=pltpu.VMEM)
    hbm = pl.BlockSpec(memory_space=ANY)

    def buf(*shape, dtype=bf):
        return pltpu.VMEM(shape, dtype)

    def like(array):
        return pltpu.VMEM(array.shape, array.dtype)

    sem = pltpu.SemaphoreType.DMA
    small = (64, width)
    hsm, wsm = 16, width // 4
    return pl.pallas_call(
        back_kernel,
        out_shape=(
            jax.ShapeDtypeStruct((micro, length, width), bf),
            jax.ShapeDtypeStruct((micro, length, width), f32),
            jax.ShapeDtypeStruct((width, wd), bf),
            jax.ShapeDtypeStruct((wa, width), bf),
            jax.ShapeDtypeStruct(small, bf),
        ),
        in_specs=[hbm] * 21 + [vmem] * 3,
        out_specs=(vmem, hbm, vmem, hbm, vmem),
        scratch_shapes=[
            like(tokens), like(cotangent), like(wq), like(wk), like(wv), like(wo), like(dx), like(q), like(k),
            like(v), like(pr), like(tab), like(hs), like(xrows), like(hot), like(y0), like(y1), buf(micro, 4 * half, width),
            buf(micro, 4 * half, width), buf(micro, half, width), buf(micro, length, width, dtype=f32), buf(wa, width),
            buf(rows, wd), buf(rows, width), buf(*small), buf(micro, length, width, dtype=f32),
            buf(micro, heads * length, HEAD_SIZE), buf(rows, width, dtype=f32), buf(rows, width, dtype=f32),
            buf(4 * rows, width // 2), buf(4 * rows, wd // 2), buf(4 * rows, wa // 2), buf(4 * rows, width // 2),
            buf(4, hsm, width),
            buf(width // 2, wd // 2), buf(wa // 2, width // 2),
            buf(4, width // 8, wd // 2), buf(4, wa // 8, width // 2), buf(4, hsm, wsm),
            buf(width // 8, wd // 2), buf(wa // 8, width // 2),
            sem((16,)), sem((16,)), sem((16,)), sem((16,)), sem((4,)), sem((4,)), sem((12,)), sem((12,)),
            sem((2,)), sem((2,)), sem((12,)), sem((12,)), sem((3,)), sem((3,)), sem((48,)), sem((48,)),
            sem((3,)), sem((3,)),
            sem((16,)), sem((16,)), sem((4 * micro,)), sem((4 * micro,)), sem((micro,)), sem((micro,)), sem((micro,)),
            sem((micro,)), sem((21,)), sem((1 + micro,)),
        ],
        compiler_params=pltpu.CompilerParams(
            collective_id=2, has_side_effects=True, vmem_limit_bytes=VMEM_LIMIT
        ),
        cost_estimate=pl.CostEstimate(
            flops=2 * rows * 4 * (width * wd + wa * width) // 4, bytes_accessed=20 * 2**20, transcendentals=0
        ),
        name="back",
    )(
        tokens, cotangent, wq, wk, wv, wo,
        dx, nrm.reshape(rows, width), att.reshape(rows, wa), q, k, v, pr, tab, hs, xrows, y0, y1, hot, fn, fa,
        gain_a, gain_f, router,
    )


def grads_kernel(
    x_ref, h_ref, g_ref, u_ref, e_ref, qkv_ref, o_ref, s_ref, lay_ref, tok_ref,
    gate_out, up_out, down_out, q_out, k_out, v_out, o_out, router_out, ffn_out, att_out, lay_out, tok_out,
):
    gate_out[...] = mm_tn(x_ref[0], g_ref[0])
    up_out[...] = mm_tn(x_ref[0], u_ref[0])
    down_out[...] = mm_tn(h_ref[0], e_ref[0])
    wq = q_out.shape[1]
    wk = wq + k_out.shape[1]
    f32 = jnp.float32
    q_out[...] = qkv_ref[:, 0:wq].astype(f32)
    k_out[...] = qkv_ref[:, wq:wk].astype(f32)
    v_out[...] = qkv_ref[:, wk:].astype(f32)
    o_out[...] = o_ref[...].astype(f32)
    lay_out[...] = lay_ref[...]
    tok_out[...] = tok_ref[...]

    @pl.when(pl.program_id(0) == 0)
    def _():
        small = s_ref[...].astype(f32)
        router_out[...] = small[0:EXPERTS]
        width = small.shape[1]
        ffn_out[...] = small[EXPERTS : EXPERTS + 1].reshape(width)
        att_out[...] = small[EXPERTS + 1 : EXPERTS + 2].reshape(width)


def grads_call(rx, rh, rg, ru, re, qkv, o, small, layer, tokens_grad, wq, wk):
    _, micro, rows, width = rx.shape
    ff = rh.shape[3]
    n = micro * rows
    tw = 256
    per = ff // tw
    steps = 2 * per
    f32 = jnp.float32
    wide = pl.BlockSpec((1, n, width), lambda i: (i // per, 0, 0))
    thin = pl.BlockSpec((1, n, tw), lambda i: (i // per, 0, i % per))
    down = lambda a, w: pl.BlockSpec((a // steps, w), lambda i: (i, 0))
    whole = lambda *s: pl.BlockSpec(s, lambda i: (0,) * len(s))
    tall = layer.shape[0] // 4
    some = pl.BlockSpec((tall, width), lambda i: (jnp.minimum(i, 3), 0))
    out = lambda *s: jax.ShapeDtypeStruct(s, f32)
    wv = qkv.shape[1] - wq - wk
    return pl.pallas_call(
        grads_kernel,
        grid=(steps,),
        in_specs=[
            wide, thin, thin, thin, wide,
            down(*qkv.shape), down(*o.shape), whole(*small.shape), some, some,
        ],
        out_specs=(
            pl.BlockSpec((width, tw), lambda i: (0, i)),
            pl.BlockSpec((width, tw), lambda i: (0, i)),
            pl.BlockSpec((tw, width), lambda i: (i, 0)),
            down(width, wq), down(width, wk), down(width, wv), down(*o.shape),
            whole(EXPERTS, width), whole(width), whole(width), some, some,
        ),
        out_shape=(
            out(width, 2 * ff), out(width, 2 * ff), out(2 * ff, width),
            out(width, wq), out(width, wk), out(width, wv), out(*o.shape),
            out(EXPERTS, width), out(width), out(width),
            jax.ShapeDtypeStruct(layer.shape, layer.dtype), out(*tokens_grad.shape),
        ),
        compiler_params=pltpu.CompilerParams(vmem_limit_bytes=VMEM_LIMIT),
        cost_estimate=pl.CostEstimate(
            flops=2 * 6 * n * width * ff, bytes_accessed=62 * 2**20, transcendentals=0
        ),
        name="expert_grads",
    )(
        rx.reshape(2, n, width), rh.reshape(2, n, ff), rg.reshape(2, n, ff),
        ru.reshape(2, n, ff), re.reshape(2, n, width), qkv, o, small, layer, tokens_grad,
    )


def suits(mesh):
    return mesh.shape["expert"] == 16 and mesh.shape["tensor"] == 2


def local_fast(
    tokens, cotangent, positions, routes, attention_gain, feedforward_gain, query_weight, key_matrix,
    value_matrix, output_weight, router_weight, gate_weight, up_weight, down_weight,
):
    micro_count, length, model_width = tokens.shape
    gain_a, gain_f = attention_gain, feedforward_gain
    router_t = router_weight.T
    dx, *kept, rx, rh, rg, ru, re = front_call(
        tokens, cotangent, positions, routes.transpose(0, 2, 1), gain_a, gain_f, query_weight, key_matrix,
        value_matrix, output_weight, router_t, gate_weight, up_weight, down_weight,
    )
    layer_out, tokens_grad, oa, ob, os = back_call(
        tokens, cotangent, gain_a, gain_f, query_weight, key_matrix, value_matrix, output_weight,
        router_t, dx, *kept,
    )
    shape = layer_out.shape
    flat = (shape[0] * shape[1], shape[2])
    gate, up, down, dq, dk, dv, do, router, ffn_gain, att_gain, layer_out, tokens_grad = grads_call(
        rx, rh, rg, ru, re, oa, ob, os, layer_out.reshape(flat), tokens_grad.reshape(flat),
        query_weight.shape[1], key_matrix.shape[1],
    )
    return (
        layer_out.reshape(shape), tokens_grad.reshape(shape), att_gain, ffn_gain, dq, dk, dv, do, router.T, gate,
        up, down,
    )


def solution(mesh):
    in_specs = (
        P(None, "expert", None),
        P(None, "expert", None),
        P(None, "expert"),
        P(None, "expert", None),
        P(),
        P(),
        P(None, "tensor"),
        P(None, "tensor"),
        P(None, "tensor"),
        P("tensor", None),
        P(),
        P(None, "expert"),
        P(None, "expert"),
        P("expert", None),
    )
    out_specs = (
        P(None, "expert", None),
        P(None, "expert", None),
        P(),
        P(),
        P(None, "tensor"),
        P(None, "tensor"),
        P(None, "tensor"),
        P("tensor", None),
        P(),
        P(None, "expert"),
        P(None, "expert"),
        P("expert", None),
    )
    body = local_fast if suits(mesh) else local
    return jax.shard_map(body, mesh=mesh, in_specs=in_specs, out_specs=out_specs, check_vma=False)
```

```python
import functools

import jax
import jax.numpy as jnp
from jax import lax
from jax.experimental import pallas as pl
from jax.experimental.pallas import tpu as pltpu
from jax.sharding import PartitionSpec as P

HEAD_SIZE = 128
EXPERTS = 32


epsilon = 1e-05
theta_base = 1000000.0
masked_score = -1e30


def rms_norm(value_row_states, gain_vector):
    return (
        value_row_states
        * lax.rsqrt(jnp.mean(value_row_states * value_row_states, axis=-1, keepdims=True) + epsilon)
        * gain_vector
    )


def gelu_exact(value_row_states):
    return jax.nn.gelu(value_row_states, approximate=False)


def rope_tables(positions, head_dim):
    half_dim = head_dim // 2
    inverse = jnp.exp(
        -jnp.log(theta_base) * (2.0 * jnp.arange(half_dim, dtype=jnp.float32) / head_dim)
    )
    angles = positions.astype(jnp.float32)[:, None] * inverse[None, :]
    return (jnp.cos(angles), jnp.sin(angles))


def widen_table(table_part, value_row_states):
    return table_part.reshape(
        (table_part.shape[0],) + (1,) * (value_row_states.ndim - 2) + (table_part.shape[1],)
    )


def rotary_apply(value_row_states, cosine_table, sine_table):
    half_dim = value_row_states.shape[-1] // 2
    first_part = value_row_states[..., :half_dim]
    second = value_row_states[..., half_dim:]
    cos_wide = widen_table(cosine_table, value_row_states)
    sin_wide = widen_table(sine_table, value_row_states)
    return jnp.concatenate(
        [first_part * cos_wide - second * sin_wide, second * cos_wide + first_part * sin_wide],
        axis=-1,
    )


def unrotate(value_row_states, cosine_table, sine_table):
    half_dim = value_row_states.shape[-1] // 2
    first_part = value_row_states[..., :half_dim]
    second = value_row_states[..., half_dim:]
    cos_wide = widen_table(cosine_table, value_row_states)
    sin_wide = widen_table(sine_table, value_row_states)
    return jnp.concatenate(
        [first_part * cos_wide + second * sin_wide, second * cos_wide - first_part * sin_wide],
        axis=-1,
    )


def block_scores(query_block, key_row_states, starts, row_ids, offset, block_rows, score_scale):
    query_ids = offset + jnp.arange(block_rows, dtype=jnp.int32)
    allowed = (row_ids[None, :] <= query_ids[:, None]) & (row_ids[None, :] >= starts[:, None])
    scores = (
        jnp.einsum(
            "qcgd,kcd->cgqk", query_block, key_row_states, preferred_element_type=jnp.float32
        )
        * score_scale
    )
    return jnp.where(allowed, scores, masked_score)


def attention_forward(
    query_rows, key_row_states, value_rows, starts, row_ids, block_rows, score_scale
):

    def one_block(block_index):
        offset = block_index * block_rows
        scores = block_scores(
            query_rows, key_row_states, starts, row_ids, offset, block_rows, score_scale
        )
        row_peak = jnp.max(scores, axis=-1, keepdims=True)
        weights = jnp.exp(scores - row_peak)
        totals = jnp.sum(weights, axis=-1, keepdims=True)
        prob_low = (weights / totals).astype(jnp.bfloat16)
        attention_output = jnp.einsum(
            "cgqk,kcd->qcgd", prob_low, value_rows, preferred_element_type=jnp.float32
        )
        return (attention_output.astype(jnp.bfloat16), row_peak[..., 0] + jnp.log(totals[..., 0]))

    return lax.map(one_block, jnp.arange(query_rows.shape[0] // block_rows, dtype=jnp.int32))


def attention_backward(
    query_rows,
    key_row_states,
    value_rows,
    starts,
    row_ids,
    block_rows,
    score_scale,
    log_totals,
    attended_grad,
):

    def one_block(carried, block_index):
        key_grad, value_grad = carried
        offset = block_index * block_rows
        scores = block_scores(
            query_rows, key_row_states, starts, row_ids, offset, block_rows, score_scale
        )
        probs = jnp.exp(scores - log_totals[block_index][..., None])
        prob_low = probs.astype(jnp.bfloat16)
        prob_grad = jnp.einsum(
            "qcgd,kcd->cgqk", attended_grad, value_rows, preferred_element_type=jnp.float32
        )
        row_dot = jnp.sum(probs * prob_grad, axis=-1, keepdims=True)
        score_grad = (probs * (prob_grad - row_dot)).astype(jnp.bfloat16)
        query_grad = (
            jnp.einsum(
                "cgqk,kcd->qcgd", score_grad, key_row_states, preferred_element_type=jnp.float32
            )
            * score_scale
        )
        key_grad = (
            key_grad
            + jnp.einsum(
                "cgqk,qcgd->kcd", score_grad, query_rows, preferred_element_type=jnp.float32
            )
            * score_scale
        )
        value_grad = value_grad + jnp.einsum(
            "cgqk,qcgd->kcd", prob_low, attended_grad, preferred_element_type=jnp.float32
        )
        return ((key_grad, value_grad), query_grad)

    empty_grad = jnp.zeros(key_row_states.shape, jnp.float32)
    totals_out, query_grad = lax.scan(
        one_block,
        (empty_grad, empty_grad),
        jnp.arange(query_rows.shape[0] // block_rows, dtype=jnp.int32),
    )
    return (query_grad.reshape(query_rows.shape), totals_out[0], totals_out[1])


def spread_rows(base, group, capacity, n_dev, per_dev, width):
    widened = jnp.broadcast_to(
        base.reshape(EXPERTS, 1, capacity, width), (EXPERTS, group, capacity, width)
    )
    return widened.reshape(n_dev, per_dev * capacity, width)


def collect_rows(back, group, capacity, width, slot_index, rows, top_count):
    summed = jnp.sum(back.reshape(EXPERTS, group, capacity, width), axis=1).astype(jnp.bfloat16)
    return (
        summed.reshape(EXPERTS * capacity, width)[slot_index]
        .reshape(rows, top_count, width)
        .astype(jnp.float32)
    )


def local(
    tokens,
    cotangent,
    positions,
    routes,
    attention_gain,
    feedforward_gain,
    query_weight,
    key_matrix,
    value_matrix,
    output_weight,
    router_weight,
    gate_weight,
    up_weight,
    down_weight,
):
    micro_count, length, model_width = tokens.shape
    head_dim = HEAD_SIZE
    kv_local = key_matrix.shape[1] // head_dim
    query_group_count = query_weight.shape[1] // head_dim // kv_local
    top_count = routes.shape[2]
    n_dev = lax.axis_size("expert")
    n_tensor = lax.axis_size("tensor")
    half = length // n_tensor
    offset = lax.axis_index("tensor") * half
    per_dev = max(1, EXPERTS // n_dev)
    group = max(1, n_dev // EXPERTS)
    local_width = gate_weight.shape[1]
    ff_local = local_width // per_dev
    capacity = max(2, 3 * half * top_count // (2 * EXPERTS))
    block_rows = min(512, length)
    score_scale = head_dim ** (-0.5)
    expert_ids = jnp.arange(EXPERTS, dtype=jnp.int32)
    row_ids = jnp.arange(length, dtype=jnp.int32)
    gate_three = gate_weight.reshape(model_width, per_dev, ff_local)
    up_three = up_weight.reshape(model_width, per_dev, ff_local)
    down_three = down_weight.reshape(per_dev, ff_local, model_width)
    query_sum = jnp.zeros(query_weight.shape, jnp.float32)
    key_sum = jnp.zeros(key_matrix.shape, jnp.float32)
    value_sum = jnp.zeros(value_matrix.shape, jnp.float32)
    output_sum = jnp.zeros(output_weight.shape, jnp.float32)
    router_sum = jnp.zeros(router_weight.shape, jnp.float32)
    attn_gain_sum = jnp.zeros(attention_gain.shape, jnp.float32)
    ffn_gain_sum = jnp.zeros(feedforward_gain.shape, jnp.float32)
    gate_sum = jnp.zeros(gate_weight.shape, jnp.float32)
    up_sum = jnp.zeros(up_weight.shape, jnp.float32)
    down_sum = jnp.zeros(down_weight.shape, jnp.float32)
    layer_outputs = []
    input_grads = []
    for micro_index in range(micro_count):
        states = tokens[micro_index].astype(jnp.float32)
        out_grad = cotangent[micro_index].astype(jnp.float32)
        place = positions[micro_index]
        chosen = routes[micro_index]
        starts = row_ids - place
        cosine_table, sine_table = rope_tables(place, head_dim)
        normed_full, attn_norm_pull = jax.vjp(rms_norm, states, attention_gain)
        normalized_input = normed_full.astype(jnp.bfloat16)
        query_pre = jnp.dot(
            normalized_input, query_weight, preferred_element_type=jnp.float32
        ).reshape(length, kv_local, query_group_count, head_dim)
        query_rows = rotary_apply(query_pre, cosine_table, sine_table).astype(jnp.bfloat16)
        key_pre = jnp.dot(normalized_input, key_matrix, preferred_element_type=jnp.float32).reshape(
            length, kv_local, head_dim
        )
        key_row_states = rotary_apply(key_pre, cosine_table, sine_table).astype(jnp.bfloat16)
        value_rows = (
            jnp.dot(normalized_input, value_matrix, preferred_element_type=jnp.float32)
            .astype(jnp.bfloat16)
            .reshape(length, kv_local, head_dim)
        )
        attention_output, log_totals = attention_forward(
            query_rows, key_row_states, value_rows, starts, row_ids, block_rows, score_scale
        )
        attention_output = attention_output.reshape(length, kv_local * query_group_count * head_dim)
        attn_part = jnp.dot(attention_output, output_weight, preferred_element_type=jnp.float32)
        hidden_state = states + lax.psum(attn_part, "tensor")
        normed_ffn_full, ffn_norm_pull = jax.vjp(rms_norm, hidden_state, feedforward_gain)
        normed_ffn = normed_ffn_full.astype(jnp.bfloat16)
        state_half = lax.dynamic_slice_in_dim(normed_ffn, offset, half, 0)
        route_half = lax.dynamic_slice_in_dim(chosen, offset, half, 0)
        grad_half = lax.dynamic_slice_in_dim(out_grad, offset, half, 0)
        route_mask = (route_half[..., None] == expert_ids[None, None, :]).astype(jnp.float32)

        def gate_softmax(logits, route_mask=route_mask):
            return jax.nn.softmax(jnp.sum(logits[:, None, :] * route_mask, axis=-1), axis=-1)

        logits = jnp.dot(state_half, router_weight, preferred_element_type=jnp.float32)
        gate_probs, gate_pull = jax.vjp(gate_softmax, logits)
        flat_routes = route_half.reshape(-1)
        route_onehot = (flat_routes[:, None] == expert_ids[None, :]).astype(jnp.int32)
        ahead = jnp.tril(jnp.ones((half * top_count, half * top_count), jnp.float32), -1)
        ranks = jnp.sum(
            jnp.dot(ahead, route_onehot.astype(jnp.float32)).astype(jnp.int32) * route_onehot, axis=1
        )
        slot_index = flat_routes * capacity + ranks
        copies = jnp.repeat(state_half, top_count, axis=0)
        send_rows = (
            jnp.zeros((EXPERTS * capacity, model_width), jnp.bfloat16).at[slot_index].set(copies)
        )
        received = lax.all_to_all(
            spread_rows(send_rows, group, capacity, n_dev, per_dev, model_width),
            "expert",
            split_axis=0,
            concat_axis=0,
            tiled=True,
        ).reshape(n_dev, per_dev, capacity, model_width)
        gate_pre = jnp.einsum(
            "skcd,dkf->skcf", received, gate_three, preferred_element_type=jnp.float32
        )
        up_pre = jnp.einsum(
            "skcd,dkf->skcf", received, up_three, preferred_element_type=jnp.float32
        )
        activated, gelu_pull = jax.vjp(gelu_exact, gate_pre)
        expert_hidden = (activated * up_pre).astype(jnp.bfloat16)
        partial_out = jnp.einsum(
            "skcf,kfd->skcd", expert_hidden, down_three, preferred_element_type=jnp.float32
        )
        back_rows = lax.all_to_all(
            partial_out.reshape(n_dev, per_dev * capacity, model_width).astype(jnp.bfloat16),
            "expert",
            split_axis=0,
            concat_axis=0,
            tiled=True,
        ).astype(jnp.float32)
        returned_rows = collect_rows(
            back_rows, group, capacity, model_width, slot_index, half, top_count
        )
        mixture_half = jnp.sum(gate_probs[..., None] * returned_rows, axis=1)
        mixture = lax.all_gather(
            mixture_half.astype(jnp.bfloat16), "tensor", axis=0, tiled=True
        ).astype(mixture_half.dtype)
        layer_outputs.append((hidden_state + mixture).astype(jnp.bfloat16))
        gate_grad = jnp.sum(grad_half[:, None, :] * returned_rows, axis=-1)
        row_grad = (
            (gate_probs[..., None] * grad_half[:, None, :])
            .astype(jnp.bfloat16)
            .reshape(-1, model_width)
        )
        send_grad = (
            jnp.zeros((EXPERTS * capacity, model_width), jnp.bfloat16).at[slot_index].set(row_grad)
        )
        grad_received = lax.all_to_all(
            spread_rows(send_grad, group, capacity, n_dev, per_dev, model_width),
            "expert",
            split_axis=0,
            concat_axis=0,
            tiled=True,
        ).reshape(n_dev, per_dev, capacity, model_width)
        hidden_grad = jnp.einsum(
            "skcd,kfd->skcf", grad_received, down_three, preferred_element_type=jnp.float32
        )
        down_part = jnp.einsum(
            "skcf,skcd->kfd", expert_hidden, grad_received, preferred_element_type=jnp.float32
        ).reshape(down_weight.shape)
        gate_pre_grad = gelu_pull(hidden_grad * up_pre)[0].astype(jnp.bfloat16)
        up_pre_grad = (hidden_grad * activated).astype(jnp.bfloat16)
        gate_part = jnp.einsum(
            "skcd,skcf->dkf", received, gate_pre_grad, preferred_element_type=jnp.float32
        ).reshape(gate_weight.shape)
        up_part = jnp.einsum(
            "skcd,skcf->dkf", received, up_pre_grad, preferred_element_type=jnp.float32
        ).reshape(up_weight.shape)
        input_part = jnp.einsum(
            "skcf,dkf->skcd", gate_pre_grad, gate_three, preferred_element_type=jnp.float32
        )
        input_part = input_part + jnp.einsum(
            "skcf,dkf->skcd", up_pre_grad, up_three, preferred_element_type=jnp.float32
        )
        input_back = lax.all_to_all(
            input_part.reshape(n_dev, per_dev * capacity, model_width).astype(jnp.bfloat16),
            "expert",
            split_axis=0,
            concat_axis=0,
            tiled=True,
        ).astype(jnp.float32)
        route_input = collect_rows(
            input_back, group, capacity, model_width, slot_index, half, top_count
        )
        logit_grad = gate_pull(gate_grad)[0].astype(jnp.bfloat16)
        router_part = jnp.dot(state_half.T, logit_grad, preferred_element_type=jnp.float32)
        ffn_half_grad = jnp.sum(route_input, axis=1) + jnp.dot(
            logit_grad, router_weight.T, preferred_element_type=jnp.float32
        )
        gate_sum = gate_sum + gate_part
        up_sum = up_sum + up_part
        down_sum = down_sum + down_part
        router_sum = router_sum + router_part
        normed_ffn_grad = lax.all_gather(ffn_half_grad, "tensor", axis=0, tiled=True)
        state_norm_grad, ffn_gain_grad = ffn_norm_pull(normed_ffn_grad)
        state_grad = out_grad + state_norm_grad
        ffn_gain_sum = ffn_gain_sum + ffn_gain_grad
        attention_grad = state_grad.astype(jnp.bfloat16)
        output_sum = output_sum + jnp.dot(
            attention_output.T, attention_grad, preferred_element_type=jnp.float32
        )
        attended_grad = (
            jnp.dot(attention_grad, output_weight.T, preferred_element_type=jnp.float32)
            .astype(jnp.bfloat16)
            .reshape(length, kv_local, query_group_count, head_dim)
        )
        query_grad, key_grad, value_grad = attention_backward(
            query_rows,
            key_row_states,
            value_rows,
            starts,
            row_ids,
            block_rows,
            score_scale,
            log_totals,
            attended_grad,
        )
        query_grad = (
            unrotate(query_grad, cosine_table, sine_table).astype(jnp.bfloat16).reshape(length, -1)
        )
        key_grad = (
            unrotate(key_grad, cosine_table, sine_table).astype(jnp.bfloat16).reshape(length, -1)
        )
        value_grad = value_grad.astype(jnp.bfloat16).reshape(length, -1)
        query_sum = query_sum + jnp.dot(
            normalized_input.T, query_grad, preferred_element_type=jnp.float32
        )
        key_sum = key_sum + jnp.dot(
            normalized_input.T, key_grad, preferred_element_type=jnp.float32
        )
        value_sum = value_sum + jnp.dot(
            normalized_input.T, value_grad, preferred_element_type=jnp.float32
        )
        normed_part = jnp.dot(query_grad, query_weight.T, preferred_element_type=jnp.float32)
        normed_part = normed_part + jnp.dot(
            key_grad, key_matrix.T, preferred_element_type=jnp.float32
        )
        normed_part = normed_part + jnp.dot(
            value_grad, value_matrix.T, preferred_element_type=jnp.float32
        )
        normed_grad = lax.psum(normed_part, "tensor")
        state_in_grad, attn_gain_grad = attn_norm_pull(normed_grad)
        attn_gain_sum = attn_gain_sum + attn_gain_grad
        input_grads.append(state_grad + state_in_grad)
    gate_sum, up_sum, down_sum, router_sum = lax.psum(
        (gate_sum, up_sum, down_sum, router_sum), "tensor"
    )
    reduced = lax.psum(
        (query_sum, key_sum, value_sum, output_sum, router_sum, attn_gain_sum, ffn_gain_sum),
        "expert",
    )
    return (
        jnp.stack(layer_outputs),
        jnp.stack(input_grads),
        reduced[5],
        reduced[6],
        reduced[0],
        reduced[1],
        reduced[2],
        reduced[3],
        reduced[4],
        gate_sum,
        up_sum,
        down_sum,
    )


MESH = pl.DeviceIdType.MESH
ANY = pl.ANY
VMEM_LIMIT = 60 * 2**20


def mm(a, b):
    return lax.dot_general(a, b, (((1,), (0,)), ((), ())), preferred_element_type=jnp.float32)


def mm_nt(a, b):
    return lax.dot_general(a, b, (((1,), (1,)), ((), ())), preferred_element_type=jnp.float32)


def mm_tn(a, b):
    return lax.dot_general(a, b, (((0,), (0,)), ((), ())), preferred_element_type=jnp.float32)


def remote(src, dst, send_sem, recv_sem, device):
    return pltpu.make_async_remote_copy(
        src_ref=src,
        dst_ref=dst,
        send_sem=send_sem,
        recv_sem=recv_sem,
        device_id=device,
        device_id_type=MESH,
    )


def tiles(count, body):
    def step(i, carry):
        body(i)
        return carry

    lax.fori_loop(0, count, step, 0)


def cols(i, width):
    return pl.ds(pl.multiple_of(i * width, width), width)


def front_kernel(
    tok_hbm, g_hbm, wq_hbm, wk_hbm, wv_hbm, wo_hbm, wg_hbm, wu_hbm, wd_hbm,
    pos_ref, routes_ref, gain_a, gain_f, router_ref,
    dx_hbm, nrm_hbm, att_hbm, q_hbm, k_hbm, v_hbm, pr_hbm, tab_hbm, hs_hbm, x_hbm, y0_hbm, y1_hbm, hot_hbm,
    fn, fa, gate_hbm, up_hbm, down_hbm,
    tok_ref, wq_ref, wk_ref, wv_ref, wo_ref, nrm_ref, att_ref, q_ref, k_ref, v_ref, pr_ref, tab_ref, hs_ref, x_ref,
    xz, gz, rz, xs, gs, xr, gr, eg, hid, gpg, upg, dx_ref, dr, dz, own_part, other_part, rel,
    onehot, prob, gg, wg, wu, wd,
    r_s, r_r, za_s, za_r, xa_s, xa_r, xb_s, xb_r, zb_s, zb_r, pair_s, pair_r, part_s, part_r, fw_s, rel_s, rel_r,
    f_s, f_r, w_s, w_r, in_sem, out_sem,
):
    ys, ds_, zd = gs, xs, xz
    e = lax.axis_index("expert")
    c = lax.axis_index("tensor")
    z = e // 4
    o = lax.rem(e, 4) * 2 + c
    micro, length, width = tok_ref.shape
    half = length // 2
    f32 = jnp.float32
    bf = jnp.bfloat16
    ff = wg.shape[1]
    col = 4 * half
    rows = xs.shape[1]
    blk = rows // 8
    cap = blk // 4
    me = 2 * e + c
    tw = 256
    nt = width // tw

    def z_dev(k):
        return (lax.rem(z + k, 4) * 4 + lax.rem(e, 4), c)

    def z_back(k):
        return (lax.rem(z + 4 - k, 4) * 4 + lax.rem(e, 4), c)

    def p_dev(d):
        t = lax.rem(o + d, 8)
        return (z * 4 + t // 2, lax.rem(t, 2))

    def p_back(d):
        t = lax.rem(o + 8 - d, 8)
        return (z * 4 + t // 2, lax.rem(t, 2))

    inner = (z == 1) | (z == 2)
    edge = (z == 0) | (z == 3)
    not_first = z != 0
    not_last = z != 3
    beside = jnp.where((z == 0) | (z == 3), jnp.where(z == 0, 1, 2), jnp.where(z == 1, 0, 3))
    beside_dev = (beside * 4 + lax.rem(e, 4), c)
    far_slot = jnp.where(z == 1, 1, 3)
    far_back = jnp.where(z == 0, 1, 3)

    @pl.when(z == 3)
    def _():
        for m in range(micro):
            dz[m, half : 2 * half, :] = jnp.zeros((half, width + 128), bf)

    @pl.when(z == 0)
    def _():
        for m in range(micro):
            dz[m, 3 * half : 4 * half, :] = jnp.zeros((half, width + 128), bf)

    barrier = pltpu.get_barrier_semaphore()
    for k in range(1, 4):
        pl.semaphore_signal(barrier, inc=1, device_id=z_dev(k), device_id_type=MESH)
    for d in range(1, 8):
        pl.semaphore_signal(barrier, inc=1, device_id=p_dev(d), device_id_type=MESH)
    loads = {}
    for i, (name, src, dst) in enumerate(
        (
            ("tok", tok_hbm, tok_ref), ("wq", wq_hbm, wq_ref), ("wk", wk_hbm, wk_ref), ("wv", wv_hbm, wv_ref),
            ("wo", wo_hbm, wo_ref), ("wg", wg_hbm.at[:, cols(c, ff)], wg), ("wu", wu_hbm.at[:, cols(c, ff)], wu),
            ("wd", wd_hbm.at[cols(c, ff), :], wd),
        )
    ):
        loads[name] = pltpu.make_async_copy(src, dst, in_sem.at[i])
        loads[name].start()
    saves = []

    def save(src, dst):
        cp = pltpu.make_async_copy(src, dst, out_sem.at[len(saves)])
        cp.start()
        saves.append(cp)

    pl.semaphore_wait(barrier, 10)

    mine = pl.ds(pl.multiple_of(c * half, half), half)
    sent = []
    got_r = []
    for k in range(1, 4):
        cp = remote(routes_ref, rz.at[k], r_s.at[k], r_r.at[k], z_dev(k))
        cp.start()
        sent.append(cp)
        got_r.append(cp)
    got_z = {}

    sent_if = []
    away = {}
    got_f = {}

    def start_if(cond, cp):
        pl.when(cond)(cp.start)
        sent_if.append((cond, cp))

    cut = width // 2
    parts = (((0, width),), ((0, cut), (cut, width + 128 - cut)))

    def sem_of(m, a, j, k, per):
        return ((m * 2 + a) * 2 + j) * per + k

    def z_send(m, a):
        src, dst = ((g_hbm, gz), (x_ref, xz))[a]
        for j, (left, size) in enumerate(parts[a]):
            wide = pl.ds(left, size)
            for k in (2, 1, 3):
                i = sem_of(m, a, j, k, 4)
                cp = remote(
                    src.at[m, mine, wide], dst.at[m, pl.ds(k * half, half), wide],
                    za_s.at[i], za_r.at[i], z_dev(k),
                )
                cond = {1: not_last, 2: True, 3: not_first}[k]
                if k == 2:
                    cp.start()
                else:
                    pl.when(cond)(cp.start)
                got_z[(m, a, j, k)] = cp
                away.setdefault((m, a), []).append((cond, cp))
        if a == 1:
            dst[m, 0:half, :] = src[m, mine, :]
        else:
            cp = pltpu.make_async_copy(src.at[m, mine, :], dst.at[m, 0:half, :], in_sem.at[8 + m])
            cp.start()
            loads[("g", m)] = cp

    def z_sent(m, a):
        for cond, cp in away.pop((m, a)):
            if cond is True:
                cp.wait_send()
            else:
                pl.when(cond)(cp.wait_send)

    def z_forward(m, a):
        dst = (gz, xz)[a]
        for j, (left, size) in enumerate(parts[a]):
            wide = pl.ds(left, size)
            got_z[(m, a, j, 2)].wait_recv()
            cp = remote(
                dst.at[m, pl.ds(2 * half, half), wide],
                dst.at[m, pl.ds(pl.multiple_of(far_slot * half, half), half), wide],
                fw_s.at[sem_of(m, a, j, 0, 1)], za_r.at[sem_of(m, a, j, 0, 4) + far_slot], beside_dev,
            )
            pl.when(inner)(cp.start)
            got_f[(m, a, j)] = cp

    z_send(0, 0)
    rz[0] = routes_ref[...]

    qx = lax.rem(e, 2)
    qy = lax.rem(e, 4) // 2
    every = micro * length
    twin = (e, 1 - c)
    got_a = {}

    def f_dev(d):
        return (z * 4 + lax.rem(qy + d // 2, 2) * 2 + lax.rem(qx + d % 2, 2), c)

    def block(d):
        return pl.ds(pl.multiple_of(d * every + c * length, length), length)

    def factor(i, dst):
        for d in (1, 2):
            if i == 0:
                size = width // 2
                view = nrm_ref.at[c, :, cols(lax.rem(qx + d % 2, 2), size)]
                to = dst.at[block(d), :]
                copies = [(view, to)]
            else:
                size = att_ref.shape[2] // 2
                at = cols(lax.rem(qy + d // 2, 2), size)
                copies = [
                    (att_ref.at[m, :, at], dst.at[pl.ds(d * every + m * length, length), :])
                    for m in range(micro)
                ]
            for m, (view, to) in enumerate(copies):
                n = (d * 2 + i // 2) * 2 + m
                cp = remote(view, to, f_s.at[n], f_r.at[n], f_dev(d))
                cp.start()
                sent.append(cp)
                got_a[(i, d, m)] = cp

    def to_twin(d):
        got_a[(0, d, 0)].wait_recv()
        cp = remote(fn.at[block(d), :], fn.at[block(d), :], w_s.at[d], w_r.at[d], twin)
        cp.start()
        sent.append(cp)
        got_a[("twin", d)] = cp

    def pass_on():
        to_twin(1)
        to_twin(2)
        cp = remote(fn.at[block(1), :], fn.at[block(3), :], f_s.at[12], f_r.at[12], f_dev(2))
        cp.start()
        sent.append(cp)
        got_a[(0, 3, 0)] = cp
        for m in range(micro):
            got_a[(2, 2, m)].wait_recv()
        cp = remote(
            fa.at[pl.ds(2 * every, every), :], fa.at[pl.ds(3 * every, every), :], f_s.at[13], f_r.at[13], f_dev(1)
        )
        cp.start()
        sent.append(cp)
        got_a[(2, 3, 0)] = cp

    head = HEAD_SIZE
    heads = wq_ref.shape[1] // head
    lane = lax.broadcasted_iota(jnp.int32, (1, 128), 1)
    row = lax.broadcasted_iota(jnp.int32, (length, length), 0)
    column = lax.broadcasted_iota(jnp.int32, (length, length), 1)
    turn = jnp.exp(
        (-2.0 / head * jnp.log(jnp.float32(theta_base))) * lax.rem(lane, head // 2).astype(f32)
    )
    allowed = []
    loads["tok"].wait()
    for m in range(micro):
        states = tok_ref[m].astype(f32)
        scale = lax.rsqrt(jnp.mean(states * states, axis=1, keepdims=True) + epsilon)
        nrm_ref[m] = (states * scale * gain_a[...].reshape(1, width)).astype(bf)
        place = pos_ref[m : m + 1, :].astype(f32)
        place = jnp.sum(jnp.where(row == column, place, 0.0), axis=1, keepdims=True)
        angle = place * turn
        tab_ref[m, 0] = jnp.cos(angle)
        tab_ref[m, 1] = jnp.where(lane < head // 2, -1.0, 1.0) * jnp.sin(angle)
        allowed.append((column <= row) & (column >= row - place.astype(jnp.int32)))

    def rope(u, m):
        return u * tab_ref[m, 0] + pltpu.roll(u, head // 2, 1) * tab_ref[m, 1]

    factor(0, fn)
    save(nrm_ref, nrm_hbm)
    save(tab_ref, tab_hbm)
    everything = nrm_ref[...].reshape(micro * length, width)

    def project(i):
        both = mm(everything, wq_ref[:, cols(i, tw)])
        for m in range(micro):
            for j in range(tw // head):
                at = pl.ds(pl.multiple_of((i * (tw // head) + j) * length, length), length)
                u = both[m * length : (m + 1) * length, j * head : (j + 1) * head]
                q_ref[m, at, :] = rope(u, m).astype(bf)

    for name in ("wq", "wk", "wv"):
        loads[name].wait()
    tiles(wq_ref.shape[1] // tw, project)
    key_pre = mm(everything, wk_ref[...])
    value_pre = mm(everything, wv_ref[...])
    for m in range(micro):
        at = slice(m * length, (m + 1) * length)
        k_ref[m] = rope(key_pre[at], m).astype(bf)
        v_ref[m] = value_pre[at].astype(bf)
    for m in range(micro):
        score = mm_nt(q_ref[m], k_ref[m]).reshape(heads, length, length) * (head**-0.5)
        score = jnp.where(allowed[m][None], score, masked_score)
        weight = jnp.exp(score - jnp.max(score, axis=-1, keepdims=True))
        weight = weight / jnp.sum(weight, axis=-1, keepdims=True)
        weight = weight.reshape(heads * length, length)
        pr_ref[m] = weight
        out = mm(weight.astype(bf), v_ref[m]).astype(bf)
        for h in range(heads):
            att_ref[m, :, h * head : (h + 1) * head] = out[h * length : (h + 1) * length]
    for src, dst in ((q_ref, q_hbm), (k_ref, k_hbm), (v_ref, v_hbm), (pr_ref, pr_hbm), (att_ref, att_hbm)):
        save(src, dst)
    factor(2, fa)
    z_forward(0, 0)
    z_sent(0, 0)
    for m in range(1, micro):
        z_send(m, 0)
    loads["wo"].wait()
    att_all = att_ref[...].reshape(micro * length, heads * head)
    got_part = []
    for j in range(3):

        def outward(i, j=j):
            at = cols(i + j * (nt // 3), tw)
            own_part[:, at] = mm(att_all, wo_ref[:, at])

        tiles(nt // 3, outward)
        at = pl.ds(j * (width // 3), width // 3)
        cp = remote(
            own_part.at[:, at], other_part.at[:, at], part_s.at[j], part_r.at[j], (e, 1 - c)
        )
        cp.start()
        sent.append(cp)
        got_part.append(cp)

    for cp in got_r:
        cp.wait_recv()

    before = ((row < column) & (row // half == column // half)).astype(bf)
    expert = 8 * z + lax.rem(o + lax.broadcasted_iota(jnp.int32, (8, length), 0), 8)
    place_row = lax.broadcasted_iota(jnp.int32, (length, col), 0)
    place_col = lax.broadcasted_iota(jnp.int32, (length, col), 1)
    slots = [jnp.zeros((8, col), f32) for _ in range(micro)]
    for k in range(4):
        at = place_col - k * half
        put = ((at >= 0) & (at < half) & (place_row == at + c * half)).astype(bf)
        for m in range(micro):
            named = rz[k, m]
            hit = named[0:1, :] == expert
            for j in range(1, routes_ref.shape[1]):
                hit = hit | (named[j : j + 1, :] == expert)
            mask = jnp.where(hit, 1.0, 0.0)
            rank = mm(mask.astype(bf), before)
            slots[m] = slots[m] + mm((mask * (rank + (cap * k + 1))).astype(bf), put)
    number = lax.broadcasted_iota(jnp.int32, (blk, col), 0) + 1
    for m in range(micro):
        for d in range(8):
            spot = slots[m][d : d + 1, :].astype(jnp.int32)
            onehot[m, d * blk : (d + 1) * blk, :] = jnp.where(spot == number, 1.0, 0.0).astype(
                jnp.bfloat16
            )

    got_p = {}

    def pack(m, a):
        src, out, dst = ((gz, gs, gr), (xz, xs, xr))[a]
        if a == 0:
            loads[("g", m)].wait()
        for j, (left, size) in enumerate(parts[a]):
            for k in (1, 3):
                got_z[(m, a, j, k)].wait_recv()

            def body(i, left=left):
                at = cols(i + left // tw, tw)
                out[m, :, at] = mm(onehot[m], src[m, :, at]).astype(bf)

            tiles(size // tw, body)
            if (left + size) % tw:
                out[m, :, width:] = mm(onehot[m], src[m, :, width:]).astype(bf)
            wide = slice(left, left + size)
            dst[m, 0:blk, wide] = out[m, 0:blk, wide]
            wide = pl.ds(left, size)
            for d in range(1, 8):
                i = sem_of(m, a, j, d, 8)
                at = pl.ds(d * blk, blk)
                cp = remote(
                    out.at[m, at, wide], dst.at[m, at, wide], xa_s.at[i], xa_r.at[i], p_dev(d)
                )
                cp.start()
                sent_p.setdefault((m, a), []).append(cp)
                got_p[(m, a, j, d)] = cp

    sent_p = {}
    pack(0, 0)
    pass_on()
    tall = lax.broadcasted_iota(jnp.int32, (128, EXPERTS), 0)
    double = (lax.rem(tall, EXPERTS) == lax.broadcasted_iota(jnp.int32, (128, EXPERTS), 1)) & (
        tall < 2 * EXPERTS
    )
    router = mm(jnp.where(double, 1.0, 0.0).astype(bf), router_ref[...]).astype(bf)
    for cp in got_part:
        cp.wait_recv()
    for m in range(micro):
        at = slice(m * length, (m + 1) * length)
        state = tok_ref[m].astype(f32) + (own_part[at, :] + other_part[at, :])
        hs_ref[m] = state
        save(hs_ref.at[m], hs_hbm.at[m])
        scale = lax.rsqrt(jnp.mean(state * state, axis=1, keepdims=True) + epsilon)
        low = (state * scale * gain_f[...].reshape(1, width)).astype(bf)
        x_ref[m, :, 0:width] = low
        logits = mm_nt(low, router)
        names = lax.rem(lane, EXPERTS)
        hit = lane < 0
        for j in range(routes_ref.shape[1]):
            named = routes_ref[m, j : j + 1, :].astype(f32)
            named = jnp.sum(jnp.where(row == column, named, 0.0), axis=1, keepdims=True)
            hit = hit | (named.astype(jnp.int32) == names)
        hit = hit & (lane < 2 * EXPERTS)
        best = jnp.max(jnp.where(hit, logits, masked_score), axis=1, keepdims=True)
        weight = jnp.where(hit, jnp.exp(logits - best), 0.0)
        first = jnp.sum(jnp.where(lane < EXPERTS, weight, 0.0), axis=1, keepdims=True)
        weight = weight / first
        top = weight.astype(bf).astype(f32)
        x_ref[m, :, width:] = jnp.where(lane < EXPERTS, top, weight - top).astype(bf)
        if m == 0:
            z_send(m, 1)
        save(x_ref.at[m], x_hbm.at[m])
    for m in range(1, micro):
        z_forward(m, 0)
        pack(m, 0)
    z_forward(0, 1)
    z_sent(0, 1)
    for m in range(1, micro):
        z_send(m, 1)
    pack(0, 1)
    for m in range(1, micro):
        z_forward(m, 1)
        pack(m, 1)
    for name in ("wg", "wu", "wd"):
        loads[name].wait()
    save(onehot, hot_hbm)

    got_b = {}
    def weight_grads():
        def columns(i):
            at = cols(i, tw)
            for out, back in ((wg, gpg), (wu, upg)):
                total = mm_tn(xr[0, :, 0:width], back[0, :, at])
                for m in range(1, micro):
                    total = total + mm_tn(xr[m, :, 0:width], back[m, :, at])
                out[:, at] = total.astype(bf)
            total = mm_tn(hid[0, :, at], eg[0])
            for m in range(1, micro):
                total = total + mm_tn(hid[m, :, at], eg[m])
            wd[at, :] = total.astype(bf)

        tiles(ff // tw, columns)
        for n, (src, dst) in enumerate(((wg, gate_hbm), (wu, up_hbm), (wd, down_hbm))):
            cp = remote(src, dst.at[c], pair_s.at[n], pair_r.at[n], twin)
            cp.start()
            sent.append(cp)
            got_b[("pair", n)] = cp
            save(src, dst.at[c])

    def send_back(m, a, j):
        src, dst = ((ds_.at[m], dr.at[m]), (ys.at[m], y0_hbm))[a]
        left, size = parts[1 - a][j]
        if a == 0:
            wide = slice(left, left + size)
            dst[0:blk, wide] = src[0:blk, wide]
        else:
            save(src.at[0:blk, :], dst.at[0:blk, :])
        wide = pl.ds(left, size)
        for d in range(1, 8):
            i = sem_of(m, a, j, d, 8)
            at = pl.ds(d * blk, blk)
            cp = remote(src.at[at, wide], dst.at[at, wide], xb_s.at[i], xb_r.at[i], p_back(d))
            cp.start()
            sent.append(cp)
            got_b[(m, a, j, d)] = cp

    def run(m):
        for a in range(2):
            for j in range(len(parts[a])):
                for d in range(1, 8):
                    got_p[(m, a, j, d)].wait_recv()
            for cp in sent_p[(m, a)]:
                cp.wait_send()
        tail = xr[m, :, width:].astype(jnp.float32)
        pick = (lane == me) | (lane == me + 32)
        prob[...] = jnp.broadcast_to(
            jnp.sum(jnp.where(pick, tail, 0.0), axis=1, keepdims=True), (rows, 128)
        )
        gg[...] = jnp.zeros_like(gg)

        def weigh(i):
            at = cols(i, tw)
            eg[m, :, at] = (prob[:, 0:1] * gr[m, :, at].astype(jnp.float32)).astype(jnp.bfloat16)

        tiles(nt, weigh)

        def inner(i):
            at = cols(i, tw)
            xrow = xr[m, :, 0:width]
            gate = mm(xrow, wg[:, at])
            upv = mm(xrow, wu[:, at])
            back = mm_nt(eg[m], wd[at, :])
            cdf = 0.5 * (1.0 + lax.erf(gate * 0.7071067811865476))
            act = gate * cdf
            slope = cdf + gate * (jnp.exp(gate * gate * -0.5) * 0.3989422804014327)
            hid[m, :, at] = (act * upv).astype(jnp.bfloat16)
            gpg[m, :, at] = (back * upv * slope).astype(jnp.bfloat16)
            upg[m, :, at] = (back * act).astype(jnp.bfloat16)

        tiles(ff // tw, inner)

        def outer(i):
            at = cols(i, tw)
            low = mm(hid[m], wd[:, at]).astype(jnp.bfloat16).astype(jnp.float32)
            gg[...] += jnp.broadcast_to(
                jnp.sum(low * gr[m, :, at].astype(jnp.float32), axis=1, keepdims=True),
                (rows, 128),
            )
            ys[m, :, at] = (prob[:, 0:1] * low).astype(jnp.bfloat16)

        tiles(nt, outer)

        def inputs(i):
            at = cols(i, tw)
            ds_[m, :, at] = (mm_nt(gpg[m], wg[at, :]) + mm_nt(upg[m], wu[at, :])).astype(
                jnp.bfloat16
            )

        tiles(cut // tw, inputs)
        send_back(m, 0, 0)
        tiles((width - cut) // tw, lambda i: inputs(i + cut // tw))
        total = gg[...]
        high = total.astype(jnp.bfloat16).astype(jnp.float32)
        ds_[m, :, width:] = jnp.where(
            lane == me, high, jnp.where(lane == me + 32, total - high, 0.0)
        ).astype(jnp.bfloat16)
        send_back(m, 0, 1)

    for m in range(micro):
        run(m)
    send_back(0, 1, 0)
    save(ys.at[1], y1_hbm)

    got_c = {}

    def gather(m, j):
        left, size = parts[1][j]
        for d in range(1, 8):
            got_b[(m, 0, j, d)].wait_recv()
        pl.when(inner)(got_f[(m, 1, j)].wait_send)

        def body(i):
            at = cols(i + left // tw, tw)
            zd[m, :, at] = mm_tn(onehot[m], dr[m, :, at]).astype(bf)

        tiles(size // tw, body)
        if j == 1:
            zd[m, :, width:] = mm_tn(onehot[m], dr[m, :, width:]).astype(bf)
        wide = pl.ds(left, size)
        far = pl.ds(pl.multiple_of(far_back * half, half), half)
        relay = remote(
            zd.at[m, far, wide], rel.at[m, :, wide], rel_s.at[m * 2 + j], rel_r.at[m * 2 + j], beside_dev
        )
        start_if(edge, relay)
        for k in (1, 3, 2):
            i = (m * 2 + j) * 4 + k
            at = pl.ds(k * half, half)
            cp = remote(zd.at[m, at, wide], dz.at[m, at, wide], zb_s.at[i], zb_r.at[i], z_back(k))
            got_c[(m, j, k)] = cp
            if k == 2:

                @pl.when(inner)
                def _():
                    relay.wait_recv()
                    here = slice(left, left + size)
                    zd[m, 2 * half : 3 * half, here] = (
                        zd[m, 2 * half : 3 * half, here].astype(f32) + rel[m, :, here].astype(f32)
                    ).astype(bf)

                cp.start()
                sent.append(cp)
            else:
                start_if(not_first if k == 1 else not_last, cp)

    def finish(m, j):
        left, size = parts[1][j]
        here = slice(left, left + size)
        pl.when(not_last)(got_c[(m, j, 1)].wait_recv)
        pl.when(not_first)(got_c[(m, j, 3)].wait_recv)
        got_c[(m, j, 2)].wait_recv()
        total = zd[m, 0:half, here].astype(f32)
        for k in range(1, 4):
            total = total + dz[m, k * half : (k + 1) * half, here].astype(f32)
        dx_ref[m, mine, here] = total
        n = m * 8 + 5 + j
        wide = pl.ds(left, size)
        cp = remote(
            dx_ref.at[m, mine, wide], dx_ref.at[m, mine, wide], pair_s.at[n], pair_r.at[n], (e, 1 - c)
        )
        cp.start()
        sent.append(cp)
        got_c[("pair", m, j)] = cp

    order = [(m, j) for m in range(micro) for j in range(2)]
    for i, (m, j) in enumerate(order):
        gather(m, j)
        if i == 1:
            weight_grads()
        if i >= 1:
            finish(*order[i - 1])
    finish(*order[-1])
    for m in range(micro):
        pl.when(inner)(got_f[(m, 0, 0)].wait_send)
    to_twin(3)
    got_a[(2, 3, 0)].wait_recv()
    for m in range(micro):
        got_a[(2, 1, m)].wait_recv()
    for d in range(1, 4):
        got_a[("twin", d)].wait_recv()
    for m in range(micro):
        for j in range(2):
            got_c[("pair", m, j)].wait_recv()
        save(dx_ref.at[m], dx_hbm.at[m])
    for n in range(3):
        got_b[("pair", n)].wait_recv()
    for d in range(1, 8):
        got_b[(0, 1, 0, d)].wait_recv()
    for at in list(away):
        z_sent(*at)
    for cp in saves:
        cp.wait()
    for cp in sent:
        cp.wait_send()
    for cond, cp in sent_if:
        pl.when(cond)(cp.wait_send)


def front_call(
    tokens, cotangent, positions, routes, gain_a, gain_f, wq, wk, wv, wo, router, gate_weight,
    up_weight, down_weight,
):
    micro, length, width = tokens.shape
    wide = width + 128
    half = length // 2
    ff = gate_weight.shape[1] // 2
    cap = 3 * half * routes.shape[1] // (2 * EXPERTS)
    rows = 8 * 4 * cap
    bf = jnp.bfloat16
    f32 = jnp.float32
    vmem = pl.BlockSpec(memory_space=pltpu.VMEM)
    hbm = pl.BlockSpec(memory_space=ANY)
    heads = wq.shape[1] // HEAD_SIZE

    def buf(*shape, dtype=bf):
        return pltpu.VMEM(shape, dtype)

    def out(*shape, dtype=bf):
        return jax.ShapeDtypeStruct(shape, dtype)

    sem = pltpu.SemaphoreType.DMA
    col = 4 * half
    hw = wq.shape[1]
    return pl.pallas_call(
        front_kernel,
        out_shape=(
            out(micro, length, wide, dtype=f32),
            out(micro, length, width),
            out(micro, length, hw),
            out(micro, heads * length, HEAD_SIZE),
            out(micro, length, HEAD_SIZE),
            out(micro, length, HEAD_SIZE),
            out(micro, heads * length, length, dtype=f32),
            out(micro, 2, length, HEAD_SIZE, dtype=f32),
            out(micro, length, width, dtype=f32),
            out(micro, length, wide),
            out(rows, width),
            out(rows, width),
            out(micro, rows, col),
            out(4 * micro * length, width // 2),
            out(4 * micro * length, hw // 2),
            out(2, width, ff),
            out(2, width, ff),
            out(2, ff, width),
        ),
        in_specs=[hbm] * 9 + [vmem] * 5,
        out_specs=(hbm,) * 18,
        scratch_shapes=[
            buf(micro, length, width), buf(width, hw), buf(width, HEAD_SIZE), buf(width, HEAD_SIZE), buf(hw, width),
            buf(micro, length, width), buf(micro, length, hw), buf(micro, heads * length, HEAD_SIZE),
            buf(micro, length, HEAD_SIZE), buf(micro, length, HEAD_SIZE),
            buf(micro, heads * length, length, dtype=f32), buf(micro, 2, length, HEAD_SIZE, dtype=f32),
            buf(micro, length, width, dtype=f32), buf(micro, length, wide),
            buf(micro, col, wide), buf(micro, col, width), pltpu.VMEM((4, *routes.shape), jnp.int32),
            buf(micro, rows, wide), buf(micro, rows, width), buf(micro, rows, wide), buf(micro, rows, width),
            buf(micro, rows, width), buf(micro, rows, ff), buf(micro, rows, ff), buf(micro, rows, ff),
            buf(micro, length, wide, dtype=f32), buf(micro, rows, wide), buf(micro, col, wide),
            buf(micro * length, width, dtype=f32), buf(micro * length, width, dtype=f32),
            buf(micro, half, wide), buf(micro, rows, col), buf(rows, 128, dtype=f32), buf(rows, 128, dtype=f32),
            buf(width, ff), buf(width, ff), buf(ff, width),
            sem((4,)), sem((4,)), sem((16 * micro,)), sem((16 * micro,)), sem((32 * micro,)), sem((32 * micro,)),
            sem((32 * micro,)), sem((32 * micro,)), sem((8 * micro,)), sem((8 * micro,)), sem((8 * micro,)),
            sem((8 * micro,)), sem((3,)), sem((3,)), sem((4 * micro,)), sem((2 * micro,)), sem((2 * micro,)),
            sem((14,)), sem((14,)), sem((4,)), sem((4,)), sem((8 + micro,)), sem((16 + 5 * micro,)),
        ],
        compiler_params=pltpu.CompilerParams(
            collective_id=1, has_side_effects=True, vmem_limit_bytes=VMEM_LIMIT
        ),
        cost_estimate=pl.CostEstimate(
            flops=2 * 6 * micro * rows * width * ff, bytes_accessed=40 * 2**20, transcendentals=0
        ),
        name="front",
    )(
        tokens, cotangent, wq, wk, wv, wo, gate_weight, up_weight, down_weight,
        positions, routes, gain_a, gain_f, router,
    )


def back_kernel(
    tok_hbm, g_hbm, wq_hbm, wk_hbm, wv_hbm, wo_hbm,
    dx_hbm, nrm_hbm, att_hbm, q_hbm, k_hbm, v_hbm, pr_hbm, tab_hbm, hs_hbm, x_hbm, y0_hbm, y1_hbm, hot_hbm,
    fn_hbm, fa_hbm, gain_a, gain_f, router_ref,
    lay_ref, tg_hbm, oa, ob_hbm, os,
    tok_ref, g_ref, wq_ref, wk_ref, wv_ref, wo_ref, dx_ref, q_ref, k_ref, v_ref, pr_ref, tab_ref, hs_ref, x_ref,
    hot, y0r, y1r, zy, yz, rel, tg_ref, ob,
    d_ref, a_ref, s_ref, sg, ag, own_part, other_part,
    fn, fd, fa, fg, fs, pa, pb, za, zb, zs, ra, rb,
    f_s, f_r, w_s, w_r, c_s, c_r, y_s, y_r, l_s, l_r, z_s, z_r, h_s, h_r, p_s, p_r, part_s, part_r,
    yp_s, yp_r, yz_s, yz_r, rel_s, rel_r, pair_s, pair_r, in_sem, out_sem,
):
    micro, length, width = tok_ref.shape
    half = length // 2
    f32 = jnp.float32
    bf = jnp.bfloat16
    head = HEAD_SIZE
    heads = wq_ref.shape[1] // head
    wq = wq_ref.shape[1]
    tw = 256
    nt = width // tw
    e = lax.axis_index("expert")
    c = lax.axis_index("tensor")
    z = e // 4
    q = lax.rem(e, 4)
    qx = lax.rem(q, 2)
    qy = q // 2
    rows = micro * length
    wn = fn.shape[1]
    wd = d_ref.shape[1] // 2
    wa = fa.shape[1]
    per = length
    wg = a_ref.shape[1] // 2
    ws = s_ref.shape[1] // 4
    hs = s_ref.shape[0] // 4
    ha = wn // 4
    hb = wa // 4

    def flip(bit, by):
        return lax.rem(bit + by, 2)

    def p_dev(d):
        return (z * 4 + flip(qy, d // 2) * 2 + flip(qx, d % 2), c)

    def z_dev(k):
        return (lax.rem(z + k, 4) * 4 + q, c)

    def part(i, size):
        return pl.ds(pl.multiple_of(i * size, size), size)

    inner = (z == 1) | (z == 2)
    edge = (z == 0) | (z == 3)
    not_first = z != 0
    not_last = z != 3
    beside = jnp.where(edge, jnp.where(z == 0, 1, 2), jnp.where(z == 1, 0, 3))
    beside_dev = (beside * 4 + q, c)
    twin = (e, 1 - c)
    sent_if = []

    def start_if(cond, cp):
        pl.when(cond)(cp.start)
        sent_if.append((cond, cp))

    o = q * 2 + c
    blk = y1r.shape[0] // 8
    own_rows = pl.ds(pl.multiple_of(c * half, half), half)

    def any_dev(n):
        t = lax.rem(o + n, 8)
        return (z * 4 + t // 2, lax.rem(t, 2))

    def any_back(n):
        t = lax.rem(o + 8 - n, 8)
        return (z * 4 + t // 2, lax.rem(t, 2))

    def fill(m, slot):
        yz[m, slot * half : (slot + 1) * half, :] = jnp.zeros((half, width), bf)

    def clear(slot):
        za[slot] = jnp.zeros((ha, wd), bf)
        zb[slot] = jnp.zeros((hb, wg), bf)

    pl.when(z == 0)(lambda: clear(1))
    pl.when(z == 3)(lambda: clear(3))

    for m in range(micro):
        pl.when(z == 3)(lambda m=m: fill(m, 1))
        pl.when(z == 0)(lambda m=m: fill(m, 3))

    barrier = pltpu.get_barrier_semaphore()
    for n in range(1, 4):
        pl.semaphore_signal(barrier, inc=1, device_id=z_dev(n), device_id_type=MESH)
    for n in range(1, 8):
        pl.semaphore_signal(barrier, inc=1, device_id=any_dev(n), device_id_type=MESH)
    loads = {}
    for i, (name, src, dst) in enumerate(
        (
            ("dx", dx_hbm, dx_ref), ("x", x_hbm, x_ref), ("hs", hs_hbm, hs_ref), ("g", g_hbm, g_ref),
            ("y0", y0_hbm, y0r), ("hot", hot_hbm, hot), ("y1", y1_hbm.at[0:blk, :], y1r.at[0:blk, :]), ("wo", wo_hbm, wo_ref),
            ("v", v_hbm, v_ref), ("pr", pr_hbm, pr_ref), ("k", k_hbm, k_ref), ("q", q_hbm, q_ref),
            ("tab", tab_hbm, tab_ref), ("wq", wq_hbm, wq_ref), ("wk", wk_hbm, wk_ref), ("wv", wv_hbm, wv_ref),
            ("tok", tok_hbm, tok_ref),
            ("fa", fa_hbm.at[rows:, :], fa.at[rows:, :]), ("fa0", att_hbm.at[:, part(qy, wa)], fa.at[0:rows, :]),
            ("fn", fn_hbm.at[rows:, :], fn.at[rows:, :]), ("fn0", nrm_hbm.at[:, part(qx, wn)], fn.at[0:rows, :]),
        )
    ):
        loads[name] = pltpu.make_async_copy(src, dst, in_sem.at[i])
        loads[name].start()
    saves = []

    def save(src, dst):
        cp = pltpu.make_async_copy(src, dst, out_sem.at[len(saves)])
        cp.start()
        saves.append(cp)

    def need(*names):
        for name in names:
            loads[name].wait()

    pl.semaphore_wait(barrier, 10)

    sent = []
    got_f = {}
    bits = {3: 0, 1: 1}

    def piece(src, i, d):
        bit = flip(qx, d % 2) if bits[i] == 0 else flip(qy, d // 2)
        return part(bit, src.shape[1] // 2)

    def mine(d):
        return pl.ds(pl.multiple_of(d * rows + c * per, per), per)

    def factor(i, src, dst):
        for d in (1, 2):
            if bits[i] == 0:
                view = src.at[pl.ds(pl.multiple_of(c * per, per), per), piece(src, i, d)]
                to = dst.at[mine(d), :]
            else:
                view = src.at[:, piece(src, i, d)]
                to = dst.at[pl.ds(d * rows, rows), :]
            cp = remote(view, to, f_s.at[d * 4 + i], f_r.at[d * 4 + i], p_dev(d))
            cp.start()
            sent.append(cp)
            got_f[(i, d)] = cp

    def to_twin(i, d, dst):
        cp = remote(dst.at[mine(d), :], dst.at[mine(d), :], w_s.at[d * 4 + i], w_r.at[d * 4 + i], twin)
        cp.start()
        sent.append(cp)
        got_f[("twin", i, d)] = cp

    def relay(i, dst):
        via, over = (1, 2) if bits[i] == 0 else (2, 1)
        got_f[(i, via)].wait_recv()
        if bits[i] == 0:
            src, to = dst.at[mine(via), :], dst.at[mine(3), :]
        else:
            src, to = dst.at[pl.ds(via * rows, rows), :], dst.at[pl.ds(3 * rows, rows), :]
        cp = remote(src, to, f_s.at[12 + i], f_r.at[12 + i], p_dev(over))
        cp.start()
        sent.append(cp)
        got_f[(i, 3)] = cp
        if bits[i] == 0:
            to_twin(i, via, dst)
            got_f[(i, over)].wait_recv()
            to_twin(i, over, dst)

    def d_rows(d, m):
        return pl.ds(d * rows + m * per, per)

    def factor_d(m):
        for d in (2, 1):
            cp = remote(
                d_ref.at[pl.ds(m * per, per), part(flip(qy, d // 2), wd)], fd.at[d_rows(d, m), :],
                f_s.at[d * 4 + m], f_r.at[d * 4 + m], p_dev(d),
            )
            cp.start()
            sent.append(cp)
            got_f[("d", m, d)] = cp

    def relay_d(m):
        got_f[("d", m, 2)].wait_recv()
        cp = remote(fd.at[d_rows(2, m), :], fd.at[d_rows(3, m), :], f_s.at[12 + m], f_r.at[12 + m], p_dev(1))
        cp.start()
        sent.append(cp)
        got_f[("d", m, 3)] = cp

    def arrive(i, dst):
        if bits[i]:
            got_f[(i, 1)].wait_recv()
            got_f[(i, 3)].wait_recv()
        else:
            got_f[(i, 3)].wait_recv()
            to_twin(i, 3, dst)
            for d in (1, 2, 3):
                got_f[("twin", i, d)].wait_recv()

    got_v = {}
    def send_y1(j):
        wide = pl.ds(j * (width // 2), width // 2)
        for n in range(1, 8):
            at = pl.ds(n * blk, blk)
            cp = remote(
                y1_hbm.at[at, wide], y1r.at[at, wide], yp_s.at[j * 8 + n], yp_r.at[j * 8 + n], any_back(n)
            )
            cp.start()
            sent.append(cp)
            got_v[(n, j, "row")] = cp

    send_y1(0)

    def z_back(n):
        return (lax.rem(z + 4 - n, 4) * 4 + q, c)

    def regroup(m, src):
        def outputs(i):
            at = cols(i, tw)
            zy[m, :, at] = mm_tn(hot[m], src[:, at]).astype(bf)

        tiles(nt, outputs)

    def send_far(m):
        far = part(jnp.where(z == 0, 1, 3), half)
        cp = remote(zy.at[m, far, :], rel.at[m], rel_s.at[m], rel_r.at[m], beside_dev)
        start_if(edge, cp)
        got_v[("far", m)] = cp
        for n in (1, 3):
            at = pl.ds(n * half, half)
            cp = remote(zy.at[m, at, :], yz.at[m, at, :], yz_s.at[m * 4 + n], yz_r.at[m * 4 + n], z_back(n))
            start_if(not_first if n == 1 else not_last, cp)
            got_v[(m, n)] = cp

    def send_near(m):
        at = pl.ds(2 * half, half)

        @pl.when(inner)
        def _():
            got_v[("far", m)].wait_recv()
            zy[m, at, :] = (zy[m, at, :].astype(f32) + rel[m].astype(f32)).astype(bf)

        cp = remote(zy.at[m, at, :], yz.at[m, at, :], yz_s.at[m * 4 + 2], yz_r.at[m * 4 + 2], z_back(2))
        cp.start()
        sent.append(cp)
        got_v[(m, 2)] = cp

    def layer(m):
        pl.when(not_last)(got_v[(m, 1)].wait_recv)
        pl.when(not_first)(got_v[(m, 3)].wait_recv)
        got_v[(m, 2)].wait_recv()
        total = zy[m, 0:half, :].astype(f32)
        for n in range(1, 4):
            total = total + yz[m, n * half : (n + 1) * half, :].astype(f32)
        lay_ref[m, own_rows, :] = (hs_ref[m, own_rows, :] + total).astype(bf)
        cp = remote(
            lay_ref.at[m, own_rows, :], lay_ref.at[m, own_rows, :], pair_s.at[m], pair_r.at[m], twin
        )
        cp.start()
        sent.append(cp)
        got_v[("pair", m)] = cp

    need("dx", "x", "hs", "g")
    lane = lax.broadcasted_iota(jnp.int32, (1, 128), 1)
    gain_row = jnp.zeros((1, width), f32)
    s_ref[...] = jnp.zeros_like(s_ref)
    router_row = jnp.zeros((128, width), f32)
    for m in range(micro):
        here = slice(m * length, (m + 1) * length)
        tail = dx_ref[m, :, width:]
        grad = tail + pltpu.roll(tail, 128 - EXPERTS, 1)
        tail = x_ref[m, :, width:].astype(f32)
        prob = jnp.where(lane < EXPERTS, tail + pltpu.roll(tail, 128 - EXPERTS, 1), 0.0)
        shared = jnp.sum(prob * grad, axis=1, keepdims=True)
        low = (prob * (grad - shared)).astype(bf)
        router_row = router_row + mm_tn(low, x_ref[m, :, 0:width])
        full = dx_ref[m, :, 0:width] + mm(low[:, 0:EXPERTS], router_ref[...])
        state = hs_ref[m]
        scale = lax.rsqrt(jnp.mean(state * state, axis=1, keepdims=True) + epsilon)
        u = full * gain_f[...].reshape(1, width)
        common = jnp.mean(u * state, axis=1, keepdims=True) * (scale * scale * scale)
        total = g_ref[m].astype(f32) + (scale * u - state * common)
        sg[m] = total
        a_ref[here, :] = total.astype(bf)
        gain_row = gain_row + jnp.sum(full * state * scale, axis=0, keepdims=True)
    s_ref[0:EXPERTS, :] = router_row[0:EXPERTS].astype(bf)
    factor(3, a_ref, fg)
    need("y0", "hot", "wo")
    regroup(0, y0r)
    send_far(0)

    def inward(i):
        at = cols(i, tw)
        both = mm_nt(a_ref[...], wo_ref[at, :]).astype(bf)
        for m in range(micro):
            for j in range(tw // head):
                to = pl.ds(pl.multiple_of((i * (tw // head) + j) * length, length), length)
                ag[m, to, :] = both[m * length : (m + 1) * length, j * head : (j + 1) * head]

    tiles(wq // tw, inward)
    relay(3, fg)
    send_near(0)
    need("v", "pr", "k", "q", "tab")

    def unrope(u, m):
        return u * tab_ref[m, 0] - pltpu.roll(u, head // 2, 1) * tab_ref[m, 1]

    for m in range(micro):
        here = slice(m * length, (m + 1) * length)
        prob = pr_ref[m]
        back = mm_nt(ag[m], v_ref[m])
        shared = jnp.sum(prob * back, axis=1, keepdims=True)
        low = (prob * (back - shared)).astype(bf)
        dq = mm(low, k_ref[m]) * (head**-0.5)
        for h in range(heads):
            u = unrope(dq[h * length : (h + 1) * length], m)
            d_ref[here, h * head : (h + 1) * head] = u.astype(bf)
        dk = mm_tn(low, q_ref[m]) * (head**-0.5)
        d_ref[here, wq : wq + head] = unrope(dk, m).astype(bf)
        d_ref[here, wq + head : wq + 2 * head] = mm_tn(prob.astype(bf), ag[m]).astype(bf)
    for m in range(micro):
        factor_d(m)
    need("wq", "wk", "wv")
    got_part = []
    for j in range(3):

        def outward(i, j=j):
            at = cols(i + j * (nt // 3), tw)
            own_part[:, at] = (
                mm_nt(d_ref[:, 0:wq], wq_ref[at, :])
                + mm_nt(d_ref[:, wq : wq + head], wk_ref[at, :])
                + mm_nt(d_ref[:, wq + head :], wv_ref[at, :])
            )

        tiles(nt // 3, outward)
        at = pl.ds(j * (width // 3), width // 3)
        cp = remote(
            own_part.at[:, at], other_part.at[:, at], part_s.at[j], part_r.at[j], (e, 1 - c)
        )
        cp.start()
        sent.append(cp)
        got_part.append(cp)
    fd[0:rows, :] = d_ref[:, part(qy, wd)]
    fg[0:rows, :] = a_ref[:, part(qx, wg)]
    need("fa", "fa0")
    arrive(3, fg)

    def two(i):
        at = cols(i, tw)
        pb[:, at] = mm_tn(fa[...], fg[:, at]).astype(bf)

    tiles(wg // tw, two)
    got_y = {}

    def spread(i):
        src, dst, size, rest = ((pa, za, ha, ra), (pb, zb, hb, rb))[i]
        far = lax.rem(z + jnp.where(z == 0, 3, 1), 4)
        cp = remote(src.at[part(far, size), :], rest, l_s.at[i], l_r.at[i], beside_dev)
        start_if(edge, cp)
        got_y[("far", i)] = cp
        for k in (1, 3):
            cp = remote(
                src.at[part(lax.rem(z + k, 4), size), :], dst.at[k],
                y_s.at[k * 3 + i], y_r.at[k * 3 + i], z_dev(k),
            )
            start_if(not_last if k == 1 else not_first, cp)
            got_y[(i, k)] = cp

    def spread_rest(i):
        src, dst, size, rest = ((pa, za, ha, ra), (pb, zb, hb, rb))[i]
        across = part(lax.rem(z + 2, 4), size)

        @pl.when(inner)
        def _():
            got_y[("far", i)].wait_recv()
            src[across, :] = (src[across, :].astype(f32) + rest[...].astype(f32)).astype(bf)

        cp = remote(src.at[across, :], dst.at[2], y_s.at[6 + i], y_r.at[6 + i], z_dev(2))
        cp.start()
        sent.append(cp)
        got_y[(i, 2)] = cp

    spread(1)
    relay_d(0)
    relay_d(1)
    send_y1(1)
    need("tok")
    for cp in got_part:
        cp.wait_recv()
    last_row = jnp.zeros((1, width), f32)
    for m in range(micro):
        here = slice(m * length, (m + 1) * length)
        full = own_part[here, :] + other_part[here, :]
        state = tok_ref[m].astype(f32)
        scale = lax.rsqrt(jnp.mean(state * state, axis=1, keepdims=True) + epsilon)
        u = full * gain_a[...].reshape(1, width)
        common = jnp.mean(u * state, axis=1, keepdims=True) * (scale * scale * scale)
        tg_ref[m] = sg[m] + (scale * u - state * common)
        save(tg_ref.at[m], tg_hbm.at[m])
        last_row = last_row + jnp.sum(full * state * scale, axis=0, keepdims=True)
    index = lax.broadcasted_iota(jnp.int32, (hs, 1), 0)
    s_ref[2 * hs : 3 * hs, :] = jnp.where(
        index == 0, gain_row, jnp.where(index == 1, last_row, 0.0)
    ).astype(bf)
    got_s = []
    for d in (3, 1, 2):
        to = flip(qy, d // 2) * 2 + flip(qx, d % 2)
        cp = remote(s_ref.at[part(to, hs), :], fs.at[d], c_s.at[d], c_r.at[d], p_dev(d))
        cp.start()
        sent.append(cp)
        got_s.append(cp)
    spread_rest(1)
    need("fn", "fn0")
    for m in range(micro):
        got_f[("d", m, 1)].wait_recv()
        got_f[("d", m, 3)].wait_recv()

    def one(i):
        at = cols(i, tw)
        pa[:, at] = mm_tn(fn[...], fd[:, at]).astype(bf)

    tiles(wd // tw, one)
    spread(0)
    total = s_ref[part(q, hs), :].astype(jnp.float32)
    for cp in got_s:
        cp.wait_recv()
    for d in range(1, 4):
        total = total + fs[d].astype(jnp.float32)
    fs[0] = total.astype(jnp.bfloat16)
    for k in (2, 1, 3):
        cp = remote(
            fs.at[0, :, part(lax.rem(z + k, 4), ws)], zs.at[k],
            y_s.at[k * 3 + 2], y_r.at[k * 3 + 2], z_dev(k),
        )
        cp.start()
        sent.append(cp)
        got_y[(2, k)] = cp
    spread_rest(0)
    layer(0)
    need("y1")
    for n in range(1, 8):
        for j in range(2):
            got_v[(n, j, "row")].wait_recv()

    regroup(1, y1r)
    send_far(1)

    def spots(px, py, t):
        return (
            oa.at[part(px * 4 + t, ha), part(py, wd)],
            ob.at[part(py * 4 + t, hb), part(px, wg)],
            os.at[part(py * 2 + px, hs), part(t, ws)],
        )

    home = spots(qx, qy, z)

    def total_of(i):
        first, others = (
            (pa[part(z, ha), :], za), (pb[part(z, hb), :], zb), (fs[0, :, part(z, ws)], zs),
        )[i]
        if i < 2:
            pl.when(not_first)(got_y[(i, 1)].wait_recv)
            pl.when(not_last)(got_y[(i, 3)].wait_recv)
        else:
            got_y[(i, 1)].wait_recv()
            got_y[(i, 3)].wait_recv()
        got_y[(i, 2)].wait_recv()
        acc = first.astype(f32)
        for k in range(1, 4):
            acc = acc + others[k].astype(f32)
        home[i][...] = acc.astype(bf)
        for k in (2, 1, 3):
            cp = remote(home[i], home[i], z_s.at[k * 3 + i], z_r.at[k * 3 + i], z_dev(k))
            if k == 2:
                cp.start()
                sent.append(cp)
            else:
                start_if(not_last if k == 1 else not_first, cp)

    turns = (
        0,
        jnp.where(inner, 2, jnp.where(z == 0, 3, 1)),
        jnp.where(inner, 1, 2),
        jnp.where(inner, 3, jnp.where(z == 0, 1, 3)),
    )
    got_p = {}

    def send(ref, i, n, d, j):
        at = ((n * 3) + i) * 4 + j
        cp = remote(ref, ref, p_s.at[at], p_r.at[at], p_dev(d))
        cp.start()
        sent.append(cp)
        got_p[(n, i, j)] = cp

    def own(n, i):
        k = turns[n]
        here = spots(qx, qy, lax.rem(z + 4 - k, 4))[i]
        if n:
            cp = remote(here, here, z_s.at[k * 3 + i], z_r.at[k * 3 + i], beside_dev)
            cp.wait_recv()
        if n == 1:
            to = jnp.where(z == 1, 1, 3)
            cp = remote(here, here, h_s.at[i], z_r.at[to * 3 + i], beside_dev)
            start_if(inner, cp)
        send(here, i, n, 1, 1)
        send(here, i, n, 2, 2)

    def forward(n, i):
        t = lax.rem(z + 4 - turns[n], 4)
        if i == 1:
            got_p[(n, i, 2)].wait_recv()
            send(spots(qx, flip(qy, 1), t)[i], i, n, 1, 3)
        else:
            got_p[(n, i, 1)].wait_recv()
            send(spots(flip(qx, 1), qy, t)[i], i, n, 2, 3)

    total_of(1)
    own(0, 1)
    total_of(0)
    own(0, 0)
    total_of(2)
    own(0, 2)
    own(1, 1)
    forward(0, 1)
    own(1, 0)
    send_near(1)
    forward(0, 0)
    forward(0, 2)
    own(1, 2)
    for n in (2, 3):
        for i in (1, 0, 2):
            own(n, i)
            forward(n - 1, i)
    for i in (1, 0, 2):
        forward(3, i)
    layer(1)
    for i in (1, 0, 2):
        for n in range(4):
            first = 1 if i == 1 else 2
            got_p[(n, i, first)].wait_recv()
            got_p[(n, i, 3)].wait_recv()
        if i == 1:
            save(ob, ob_hbm)
    for m in range(micro):
        got_v[("pair", m)].wait_recv()
    for cp in saves:
        cp.wait()
    for cp in sent:
        cp.wait_send()
    for cond, cp in sent_if:
        pl.when(cond)(cp.wait_send)


def back_call(
    tokens, cotangent, gain_a, gain_f, wq, wk, wv, wo, router,
    dx, nrm, att, q, k, v, pr, tab, hs, xrows, y0, y1, hot, fn, fa,
):
    bf = jnp.bfloat16
    f32 = jnp.float32
    micro, length, width = tokens.shape
    rows = micro * length
    half = length // 2
    wd = wq.shape[1] + wk.shape[1] + wv.shape[1]
    wa = wq.shape[1]
    heads = wa // HEAD_SIZE
    vmem = pl.BlockSpec(memory_space=pltpu.VMEM)
    hbm = pl.BlockSpec(memory_space=ANY)

    def buf(*shape, dtype=bf):
        return pltpu.VMEM(shape, dtype)

    def like(array):
        return pltpu.VMEM(array.shape, array.dtype)

    sem = pltpu.SemaphoreType.DMA
    small = (64, width)
    hsm, wsm = 16, width // 4
    return pl.pallas_call(
        back_kernel,
        out_shape=(
            jax.ShapeDtypeStruct((micro, length, width), bf),
            jax.ShapeDtypeStruct((micro, length, width), f32),
            jax.ShapeDtypeStruct((width, wd), bf),
            jax.ShapeDtypeStruct((wa, width), bf),
            jax.ShapeDtypeStruct(small, bf),
        ),
        in_specs=[hbm] * 21 + [vmem] * 3,
        out_specs=(vmem, hbm, vmem, hbm, vmem),
        scratch_shapes=[
            like(tokens), like(cotangent), like(wq), like(wk), like(wv), like(wo), like(dx), like(q), like(k),
            like(v), like(pr), like(tab), like(hs), like(xrows), like(hot), like(y0), like(y1), buf(micro, 4 * half, width),
            buf(micro, 4 * half, width), buf(micro, half, width), buf(micro, length, width, dtype=f32), buf(wa, width),
            buf(rows, wd), buf(rows, width), buf(*small), buf(micro, length, width, dtype=f32),
            buf(micro, heads * length, HEAD_SIZE), buf(rows, width, dtype=f32), buf(rows, width, dtype=f32),
            buf(4 * rows, width // 2), buf(4 * rows, wd // 2), buf(4 * rows, wa // 2), buf(4 * rows, width // 2),
            buf(4, hsm, width),
            buf(width // 2, wd // 2), buf(wa // 2, width // 2),
            buf(4, width // 8, wd // 2), buf(4, wa // 8, width // 2), buf(4, hsm, wsm),
            buf(width // 8, wd // 2), buf(wa // 8, width // 2),
            sem((16,)), sem((16,)), sem((16,)), sem((16,)), sem((4,)), sem((4,)), sem((12,)), sem((12,)),
            sem((2,)), sem((2,)), sem((12,)), sem((12,)), sem((3,)), sem((3,)), sem((48,)), sem((48,)),
            sem((3,)), sem((3,)),
            sem((16,)), sem((16,)), sem((4 * micro,)), sem((4 * micro,)), sem((micro,)), sem((micro,)), sem((micro,)),
            sem((micro,)), sem((21,)), sem((1 + micro,)),
        ],
        compiler_params=pltpu.CompilerParams(
            collective_id=2, has_side_effects=True, vmem_limit_bytes=VMEM_LIMIT
        ),
        cost_estimate=pl.CostEstimate(
            flops=2 * rows * 4 * (width * wd + wa * width) // 4, bytes_accessed=20 * 2**20, transcendentals=0
        ),
        name="back",
    )(
        tokens, cotangent, wq, wk, wv, wo,
        dx, nrm.reshape(rows, width), att.reshape(rows, wa), q, k, v, pr, tab, hs, xrows, y0, y1, hot, fn, fa,
        gain_a, gain_f, router,
    )


def results_kernel(
    gate_ref, up_ref, down_ref, qkv_ref, o_ref, s_ref, lay_ref, tok_ref,
    gate_out, up_out, down_out, q_out, k_out, v_out, o_out, router_out, ffn_out, att_out, lay_out, tok_out,
):
    wq = q_out.shape[1]
    wk = wq + k_out.shape[1]
    ff = gate_ref.shape[2]
    f32 = jnp.float32
    for i in range(2):
        gate_out[:, i * ff : (i + 1) * ff] = gate_ref[i].astype(f32)
        up_out[:, i * ff : (i + 1) * ff] = up_ref[i].astype(f32)
    down_out[...] = down_ref[...].astype(f32)
    q_out[...] = qkv_ref[:, 0:wq].astype(f32)
    k_out[...] = qkv_ref[:, wq:wk].astype(f32)
    v_out[...] = qkv_ref[:, wk:].astype(f32)
    o_out[...] = o_ref[...].astype(f32)
    lay_out[...] = lay_ref[...]
    tok_out[...] = tok_ref[...]

    @pl.when(pl.program_id(0) == 0)
    def _():
        small = s_ref[...].astype(f32)
        router_out[...] = small[0:EXPERTS]
        width = small.shape[1]
        ffn_out[...] = small[EXPERTS : EXPERTS + 1].reshape(width)
        att_out[...] = small[EXPERTS + 1 : EXPERTS + 2].reshape(width)


def results_call(gate, up, down, qkv, o, small, layer, tokens_grad, wq, wk):
    _, width, ff = gate.shape
    steps = 6
    f32 = jnp.float32
    down_rows = lambda a, w: pl.BlockSpec((a // steps, w), lambda i: (i, 0))
    pair = pl.BlockSpec((2, width // steps, ff), lambda i: (0, i, 0))
    whole = lambda *s: pl.BlockSpec(s, lambda i: (0,) * len(s))
    out = lambda *s: jax.ShapeDtypeStruct(s, f32)
    wv = qkv.shape[1] - wq - wk
    few = 4
    some = pl.BlockSpec((layer.shape[0] // few, width), lambda i: (jnp.minimum(i, few - 1), 0))
    return pl.pallas_call(
        results_kernel,
        grid=(steps,),
        in_specs=[
            pair, pair, down_rows(2 * ff, width), down_rows(*qkv.shape), down_rows(*o.shape), whole(*small.shape),
            some, some,
        ],
        out_specs=(
            down_rows(width, 2 * ff), down_rows(width, 2 * ff), down_rows(2 * ff, width),
            down_rows(width, wq), down_rows(width, wk), down_rows(width, wv), down_rows(*o.shape),
            whole(EXPERTS, width), whole(width), whole(width), some, some,
        ),
        out_shape=(
            out(width, 2 * ff), out(width, 2 * ff), out(2 * ff, width),
            out(width, wq), out(width, wk), out(width, wv), out(*o.shape),
            out(EXPERTS, width), out(width), out(width),
            jax.ShapeDtypeStruct(layer.shape, layer.dtype), out(*tokens_grad.shape),
        ),
        compiler_params=pltpu.CompilerParams(vmem_limit_bytes=VMEM_LIMIT),
        cost_estimate=pl.CostEstimate(flops=0, bytes_accessed=64 * 2**20, transcendentals=0),
        name="results",
    )(gate, up, down.reshape(2 * ff, width), qkv, o, small, layer, tokens_grad)


def suits(mesh):
    return mesh.shape["expert"] == 16 and mesh.shape["tensor"] == 2


def local_fast(
    tokens, cotangent, positions, routes, attention_gain, feedforward_gain, query_weight, key_matrix,
    value_matrix, output_weight, router_weight, gate_weight, up_weight, down_weight,
):
    micro_count, length, model_width = tokens.shape
    gain_a, gain_f = attention_gain, feedforward_gain
    router_t = router_weight.T
    dx, *kept, gate_low, up_low, down_low = front_call(
        tokens, cotangent, positions, routes.transpose(0, 2, 1), gain_a, gain_f, query_weight, key_matrix,
        value_matrix, output_weight, router_t, gate_weight, up_weight, down_weight,
    )
    layer_out, tokens_grad, oa, ob, os = back_call(
        tokens, cotangent, gain_a, gain_f, query_weight, key_matrix, value_matrix, output_weight,
        router_t, dx, *kept,
    )
    shape = layer_out.shape
    flat = (shape[0] * shape[1], shape[2])
    gate, up, down, dq, dk, dv, do, router, ffn_gain, att_gain, layer_out, tokens_grad = results_call(
        gate_low, up_low, down_low, oa, ob, os, layer_out.reshape(flat), tokens_grad.reshape(flat),
        query_weight.shape[1], key_matrix.shape[1],
    )
    return (
        layer_out.reshape(shape), tokens_grad.reshape(shape), att_gain, ffn_gain, dq, dk, dv, do, router.T, gate,
        up, down,
    )


def solution(mesh):
    in_specs = (
        P(None, "expert", None),
        P(None, "expert", None),
        P(None, "expert"),
        P(None, "expert", None),
        P(),
        P(),
        P(None, "tensor"),
        P(None, "tensor"),
        P(None, "tensor"),
        P("tensor", None),
        P(),
        P(None, "expert"),
        P(None, "expert"),
        P("expert", None),
    )
    out_specs = (
        P(None, "expert", None),
        P(None, "expert", None),
        P(),
        P(),
        P(None, "tensor"),
        P(None, "tensor"),
        P(None, "tensor"),
        P("tensor", None),
        P(),
        P(None, "expert"),
        P(None, "expert"),
        P("expert", None),
    )
    body = local_fast if suits(mesh) else local
    return jax.shard_map(body, mesh=mesh, in_specs=in_specs, out_specs=out_specs, check_vma=False)
```

```python
import functools

import jax
import jax.numpy as jnp
from jax import lax
from jax.experimental import pallas as pl
from jax.experimental.pallas import tpu as pltpu
from jax.sharding import PartitionSpec as P

HEAD_SIZE = 128
EXPERTS = 32


epsilon = 1e-05
theta_base = 1000000.0
masked_score = -1e30


def rms_norm(value_row_states, gain_vector):
    return (
        value_row_states
        * lax.rsqrt(jnp.mean(value_row_states * value_row_states, axis=-1, keepdims=True) + epsilon)
        * gain_vector
    )


def gelu_exact(value_row_states):
    return jax.nn.gelu(value_row_states, approximate=False)


def rope_tables(positions, head_dim):
    half_dim = head_dim // 2
    inverse = jnp.exp(
        -jnp.log(theta_base) * (2.0 * jnp.arange(half_dim, dtype=jnp.float32) / head_dim)
    )
    angles = positions.astype(jnp.float32)[:, None] * inverse[None, :]
    return (jnp.cos(angles), jnp.sin(angles))


def widen_table(table_part, value_row_states):
    return table_part.reshape(
        (table_part.shape[0],) + (1,) * (value_row_states.ndim - 2) + (table_part.shape[1],)
    )


def rotary_apply(value_row_states, cosine_table, sine_table):
    half_dim = value_row_states.shape[-1] // 2
    first_part = value_row_states[..., :half_dim]
    second = value_row_states[..., half_dim:]
    cos_wide = widen_table(cosine_table, value_row_states)
    sin_wide = widen_table(sine_table, value_row_states)
    return jnp.concatenate(
        [first_part * cos_wide - second * sin_wide, second * cos_wide + first_part * sin_wide],
        axis=-1,
    )


def unrotate(value_row_states, cosine_table, sine_table):
    half_dim = value_row_states.shape[-1] // 2
    first_part = value_row_states[..., :half_dim]
    second = value_row_states[..., half_dim:]
    cos_wide = widen_table(cosine_table, value_row_states)
    sin_wide = widen_table(sine_table, value_row_states)
    return jnp.concatenate(
        [first_part * cos_wide + second * sin_wide, second * cos_wide - first_part * sin_wide],
        axis=-1,
    )


def block_scores(query_block, key_row_states, starts, row_ids, offset, block_rows, score_scale):
    query_ids = offset + jnp.arange(block_rows, dtype=jnp.int32)
    allowed = (row_ids[None, :] <= query_ids[:, None]) & (row_ids[None, :] >= starts[:, None])
    scores = (
        jnp.einsum(
            "qcgd,kcd->cgqk", query_block, key_row_states, preferred_element_type=jnp.float32
        )
        * score_scale
    )
    return jnp.where(allowed, scores, masked_score)


def attention_forward(
    query_rows, key_row_states, value_rows, starts, row_ids, block_rows, score_scale
):

    def one_block(block_index):
        offset = block_index * block_rows
        scores = block_scores(
            query_rows, key_row_states, starts, row_ids, offset, block_rows, score_scale
        )
        row_peak = jnp.max(scores, axis=-1, keepdims=True)
        weights = jnp.exp(scores - row_peak)
        totals = jnp.sum(weights, axis=-1, keepdims=True)
        prob_low = (weights / totals).astype(jnp.bfloat16)
        attention_output = jnp.einsum(
            "cgqk,kcd->qcgd", prob_low, value_rows, preferred_element_type=jnp.float32
        )
        return (attention_output.astype(jnp.bfloat16), row_peak[..., 0] + jnp.log(totals[..., 0]))

    return lax.map(one_block, jnp.arange(query_rows.shape[0] // block_rows, dtype=jnp.int32))


def attention_backward(
    query_rows,
    key_row_states,
    value_rows,
    starts,
    row_ids,
    block_rows,
    score_scale,
    log_totals,
    attended_grad,
):

    def one_block(carried, block_index):
        key_grad, value_grad = carried
        offset = block_index * block_rows
        scores = block_scores(
            query_rows, key_row_states, starts, row_ids, offset, block_rows, score_scale
        )
        probs = jnp.exp(scores - log_totals[block_index][..., None])
        prob_low = probs.astype(jnp.bfloat16)
        prob_grad = jnp.einsum(
            "qcgd,kcd->cgqk", attended_grad, value_rows, preferred_element_type=jnp.float32
        )
        row_dot = jnp.sum(probs * prob_grad, axis=-1, keepdims=True)
        score_grad = (probs * (prob_grad - row_dot)).astype(jnp.bfloat16)
        query_grad = (
            jnp.einsum(
                "cgqk,kcd->qcgd", score_grad, key_row_states, preferred_element_type=jnp.float32
            )
            * score_scale
        )
        key_grad = (
            key_grad
            + jnp.einsum(
                "cgqk,qcgd->kcd", score_grad, query_rows, preferred_element_type=jnp.float32
            )
            * score_scale
        )
        value_grad = value_grad + jnp.einsum(
            "cgqk,qcgd->kcd", prob_low, attended_grad, preferred_element_type=jnp.float32
        )
        return ((key_grad, value_grad), query_grad)

    empty_grad = jnp.zeros(key_row_states.shape, jnp.float32)
    totals_out, query_grad = lax.scan(
        one_block,
        (empty_grad, empty_grad),
        jnp.arange(query_rows.shape[0] // block_rows, dtype=jnp.int32),
    )
    return (query_grad.reshape(query_rows.shape), totals_out[0], totals_out[1])


def spread_rows(base, group, capacity, n_dev, per_dev, width):
    widened = jnp.broadcast_to(
        base.reshape(EXPERTS, 1, capacity, width), (EXPERTS, group, capacity, width)
    )
    return widened.reshape(n_dev, per_dev * capacity, width)


def collect_rows(back, group, capacity, width, slot_index, rows, top_count):
    summed = jnp.sum(back.reshape(EXPERTS, group, capacity, width), axis=1).astype(jnp.bfloat16)
    return (
        summed.reshape(EXPERTS * capacity, width)[slot_index]
        .reshape(rows, top_count, width)
        .astype(jnp.float32)
    )


def local(
    tokens,
    cotangent,
    positions,
    routes,
    attention_gain,
    feedforward_gain,
    query_weight,
    key_matrix,
    value_matrix,
    output_weight,
    router_weight,
    gate_weight,
    up_weight,
    down_weight,
):
    micro_count, length, model_width = tokens.shape
    head_dim = HEAD_SIZE
    kv_local = key_matrix.shape[1] // head_dim
    query_group_count = query_weight.shape[1] // head_dim // kv_local
    top_count = routes.shape[2]
    n_dev = lax.axis_size("expert")
    n_tensor = lax.axis_size("tensor")
    half = length // n_tensor
    offset = lax.axis_index("tensor") * half
    per_dev = max(1, EXPERTS // n_dev)
    group = max(1, n_dev // EXPERTS)
    local_width = gate_weight.shape[1]
    ff_local = local_width // per_dev
    capacity = max(2, 3 * half * top_count // (2 * EXPERTS))
    block_rows = min(512, length)
    score_scale = head_dim ** (-0.5)
    expert_ids = jnp.arange(EXPERTS, dtype=jnp.int32)
    row_ids = jnp.arange(length, dtype=jnp.int32)
    gate_three = gate_weight.reshape(model_width, per_dev, ff_local)
    up_three = up_weight.reshape(model_width, per_dev, ff_local)
    down_three = down_weight.reshape(per_dev, ff_local, model_width)
    query_sum = jnp.zeros(query_weight.shape, jnp.float32)
    key_sum = jnp.zeros(key_matrix.shape, jnp.float32)
    value_sum = jnp.zeros(value_matrix.shape, jnp.float32)
    output_sum = jnp.zeros(output_weight.shape, jnp.float32)
    router_sum = jnp.zeros(router_weight.shape, jnp.float32)
    attn_gain_sum = jnp.zeros(attention_gain.shape, jnp.float32)
    ffn_gain_sum = jnp.zeros(feedforward_gain.shape, jnp.float32)
    gate_sum = jnp.zeros(gate_weight.shape, jnp.float32)
    up_sum = jnp.zeros(up_weight.shape, jnp.float32)
    down_sum = jnp.zeros(down_weight.shape, jnp.float32)
    layer_outputs = []
    input_grads = []
    for micro_index in range(micro_count):
        states = tokens[micro_index].astype(jnp.float32)
        out_grad = cotangent[micro_index].astype(jnp.float32)
        place = positions[micro_index]
        chosen = routes[micro_index]
        starts = row_ids - place
        cosine_table, sine_table = rope_tables(place, head_dim)
        normed_full, attn_norm_pull = jax.vjp(rms_norm, states, attention_gain)
        normalized_input = normed_full.astype(jnp.bfloat16)
        query_pre = jnp.dot(
            normalized_input, query_weight, preferred_element_type=jnp.float32
        ).reshape(length, kv_local, query_group_count, head_dim)
        query_rows = rotary_apply(query_pre, cosine_table, sine_table).astype(jnp.bfloat16)
        key_pre = jnp.dot(normalized_input, key_matrix, preferred_element_type=jnp.float32).reshape(
            length, kv_local, head_dim
        )
        key_row_states = rotary_apply(key_pre, cosine_table, sine_table).astype(jnp.bfloat16)
        value_rows = (
            jnp.dot(normalized_input, value_matrix, preferred_element_type=jnp.float32)
            .astype(jnp.bfloat16)
            .reshape(length, kv_local, head_dim)
        )
        attention_output, log_totals = attention_forward(
            query_rows, key_row_states, value_rows, starts, row_ids, block_rows, score_scale
        )
        attention_output = attention_output.reshape(length, kv_local * query_group_count * head_dim)
        attn_part = jnp.dot(attention_output, output_weight, preferred_element_type=jnp.float32)
        hidden_state = states + lax.psum(attn_part, "tensor")
        normed_ffn_full, ffn_norm_pull = jax.vjp(rms_norm, hidden_state, feedforward_gain)
        normed_ffn = normed_ffn_full.astype(jnp.bfloat16)
        state_half = lax.dynamic_slice_in_dim(normed_ffn, offset, half, 0)
        route_half = lax.dynamic_slice_in_dim(chosen, offset, half, 0)
        grad_half = lax.dynamic_slice_in_dim(out_grad, offset, half, 0)
        route_mask = (route_half[..., None] == expert_ids[None, None, :]).astype(jnp.float32)

        def gate_softmax(logits, route_mask=route_mask):
            return jax.nn.softmax(jnp.sum(logits[:, None, :] * route_mask, axis=-1), axis=-1)

        logits = jnp.dot(state_half, router_weight, preferred_element_type=jnp.float32)
        gate_probs, gate_pull = jax.vjp(gate_softmax, logits)
        flat_routes = route_half.reshape(-1)
        route_onehot = (flat_routes[:, None] == expert_ids[None, :]).astype(jnp.int32)
        ahead = jnp.tril(jnp.ones((half * top_count, half * top_count), jnp.float32), -1)
        ranks = jnp.sum(
            jnp.dot(ahead, route_onehot.astype(jnp.float32)).astype(jnp.int32) * route_onehot, axis=1
        )
        slot_index = flat_routes * capacity + ranks
        copies = jnp.repeat(state_half, top_count, axis=0)
        send_rows = (
            jnp.zeros((EXPERTS * capacity, model_width), jnp.bfloat16).at[slot_index].set(copies)
        )
        received = lax.all_to_all(
            spread_rows(send_rows, group, capacity, n_dev, per_dev, model_width),
            "expert",
            split_axis=0,
            concat_axis=0,
            tiled=True,
        ).reshape(n_dev, per_dev, capacity, model_width)
        gate_pre = jnp.einsum(
            "skcd,dkf->skcf", received, gate_three, preferred_element_type=jnp.float32
        )
        up_pre = jnp.einsum(
            "skcd,dkf->skcf", received, up_three, preferred_element_type=jnp.float32
        )
        activated, gelu_pull = jax.vjp(gelu_exact, gate_pre)
        expert_hidden = (activated * up_pre).astype(jnp.bfloat16)
        partial_out = jnp.einsum(
            "skcf,kfd->skcd", expert_hidden, down_three, preferred_element_type=jnp.float32
        )
        back_rows = lax.all_to_all(
            partial_out.reshape(n_dev, per_dev * capacity, model_width).astype(jnp.bfloat16),
            "expert",
            split_axis=0,
            concat_axis=0,
            tiled=True,
        ).astype(jnp.float32)
        returned_rows = collect_rows(
            back_rows, group, capacity, model_width, slot_index, half, top_count
        )
        mixture_half = jnp.sum(gate_probs[..., None] * returned_rows, axis=1)
        mixture = lax.all_gather(
            mixture_half.astype(jnp.bfloat16), "tensor", axis=0, tiled=True
        ).astype(mixture_half.dtype)
        layer_outputs.append((hidden_state + mixture).astype(jnp.bfloat16))
        gate_grad = jnp.sum(grad_half[:, None, :] * returned_rows, axis=-1)
        row_grad = (
            (gate_probs[..., None] * grad_half[:, None, :])
            .astype(jnp.bfloat16)
            .reshape(-1, model_width)
        )
        send_grad = (
            jnp.zeros((EXPERTS * capacity, model_width), jnp.bfloat16).at[slot_index].set(row_grad)
        )
        grad_received = lax.all_to_all(
            spread_rows(send_grad, group, capacity, n_dev, per_dev, model_width),
            "expert",
            split_axis=0,
            concat_axis=0,
            tiled=True,
        ).reshape(n_dev, per_dev, capacity, model_width)
        hidden_grad = jnp.einsum(
            "skcd,kfd->skcf", grad_received, down_three, preferred_element_type=jnp.float32
        )
        down_part = jnp.einsum(
            "skcf,skcd->kfd", expert_hidden, grad_received, preferred_element_type=jnp.float32
        ).reshape(down_weight.shape)
        gate_pre_grad = gelu_pull(hidden_grad * up_pre)[0].astype(jnp.bfloat16)
        up_pre_grad = (hidden_grad * activated).astype(jnp.bfloat16)
        gate_part = jnp.einsum(
            "skcd,skcf->dkf", received, gate_pre_grad, preferred_element_type=jnp.float32
        ).reshape(gate_weight.shape)
        up_part = jnp.einsum(
            "skcd,skcf->dkf", received, up_pre_grad, preferred_element_type=jnp.float32
        ).reshape(up_weight.shape)
        input_part = jnp.einsum(
            "skcf,dkf->skcd", gate_pre_grad, gate_three, preferred_element_type=jnp.float32
        )
        input_part = input_part + jnp.einsum(
            "skcf,dkf->skcd", up_pre_grad, up_three, preferred_element_type=jnp.float32
        )
        input_back = lax.all_to_all(
            input_part.reshape(n_dev, per_dev * capacity, model_width).astype(jnp.bfloat16),
            "expert",
            split_axis=0,
            concat_axis=0,
            tiled=True,
        ).astype(jnp.float32)
        route_input = collect_rows(
            input_back, group, capacity, model_width, slot_index, half, top_count
        )
        logit_grad = gate_pull(gate_grad)[0].astype(jnp.bfloat16)
        router_part = jnp.dot(state_half.T, logit_grad, preferred_element_type=jnp.float32)
        ffn_half_grad = jnp.sum(route_input, axis=1) + jnp.dot(
            logit_grad, router_weight.T, preferred_element_type=jnp.float32
        )
        gate_sum = gate_sum + gate_part
        up_sum = up_sum + up_part
        down_sum = down_sum + down_part
        router_sum = router_sum + router_part
        normed_ffn_grad = lax.all_gather(ffn_half_grad, "tensor", axis=0, tiled=True)
        state_norm_grad, ffn_gain_grad = ffn_norm_pull(normed_ffn_grad)
        state_grad = out_grad + state_norm_grad
        ffn_gain_sum = ffn_gain_sum + ffn_gain_grad
        attention_grad = state_grad.astype(jnp.bfloat16)
        output_sum = output_sum + jnp.dot(
            attention_output.T, attention_grad, preferred_element_type=jnp.float32
        )
        attended_grad = (
            jnp.dot(attention_grad, output_weight.T, preferred_element_type=jnp.float32)
            .astype(jnp.bfloat16)
            .reshape(length, kv_local, query_group_count, head_dim)
        )
        query_grad, key_grad, value_grad = attention_backward(
            query_rows,
            key_row_states,
            value_rows,
            starts,
            row_ids,
            block_rows,
            score_scale,
            log_totals,
            attended_grad,
        )
        query_grad = (
            unrotate(query_grad, cosine_table, sine_table).astype(jnp.bfloat16).reshape(length, -1)
        )
        key_grad = (
            unrotate(key_grad, cosine_table, sine_table).astype(jnp.bfloat16).reshape(length, -1)
        )
        value_grad = value_grad.astype(jnp.bfloat16).reshape(length, -1)
        query_sum = query_sum + jnp.dot(
            normalized_input.T, query_grad, preferred_element_type=jnp.float32
        )
        key_sum = key_sum + jnp.dot(
            normalized_input.T, key_grad, preferred_element_type=jnp.float32
        )
        value_sum = value_sum + jnp.dot(
            normalized_input.T, value_grad, preferred_element_type=jnp.float32
        )
        normed_part = jnp.dot(query_grad, query_weight.T, preferred_element_type=jnp.float32)
        normed_part = normed_part + jnp.dot(
            key_grad, key_matrix.T, preferred_element_type=jnp.float32
        )
        normed_part = normed_part + jnp.dot(
            value_grad, value_matrix.T, preferred_element_type=jnp.float32
        )
        normed_grad = lax.psum(normed_part, "tensor")
        state_in_grad, attn_gain_grad = attn_norm_pull(normed_grad)
        attn_gain_sum = attn_gain_sum + attn_gain_grad
        input_grads.append(state_grad + state_in_grad)
    gate_sum, up_sum, down_sum, router_sum = lax.psum(
        (gate_sum, up_sum, down_sum, router_sum), "tensor"
    )
    reduced = lax.psum(
        (query_sum, key_sum, value_sum, output_sum, router_sum, attn_gain_sum, ffn_gain_sum),
        "expert",
    )
    return (
        jnp.stack(layer_outputs),
        jnp.stack(input_grads),
        reduced[5],
        reduced[6],
        reduced[0],
        reduced[1],
        reduced[2],
        reduced[3],
        reduced[4],
        gate_sum,
        up_sum,
        down_sum,
    )


MESH = pl.DeviceIdType.MESH
ANY = pl.ANY
VMEM_LIMIT = 60 * 2**20


def mm(a, b):
    return lax.dot_general(a, b, (((1,), (0,)), ((), ())), preferred_element_type=jnp.float32)


def mm_nt(a, b):
    return lax.dot_general(a, b, (((1,), (1,)), ((), ())), preferred_element_type=jnp.float32)


def mm_tn(a, b):
    return lax.dot_general(a, b, (((0,), (0,)), ((), ())), preferred_element_type=jnp.float32)


def remote(src, dst, send_sem, recv_sem, device):
    return pltpu.make_async_remote_copy(
        src_ref=src,
        dst_ref=dst,
        send_sem=send_sem,
        recv_sem=recv_sem,
        device_id=device,
        device_id_type=MESH,
    )


def tiles(count, body):
    def step(i, carry):
        body(i)
        return carry

    lax.fori_loop(0, count, step, 0)


def cols(i, width):
    return pl.ds(pl.multiple_of(i * width, width), width)


def front_kernel(
    tok_hbm, g_hbm, wq_hbm, wk_hbm, wv_hbm, wo_hbm, wg_hbm, wu_hbm, wd_hbm,
    pos_ref, routes_ref, gain_a, gain_f, router_ref,
    dx_hbm, nrm_hbm, att_hbm, q_hbm, k_hbm, v_hbm, pr_hbm, tab_hbm, hs_hbm, x_hbm, y0_hbm, y1_hbm, hot_hbm,
    fn, fa, gate_hbm, up_hbm, down_hbm,
    tok_ref, wq_ref, wk_ref, wv_ref, wo_ref, nrm_ref, att_ref, q_ref, k_ref, v_ref, pr_ref, tab_ref, hs_ref, x_ref,
    xz, gz, rz, xs, gs, xr, gr, eg, hid, gpg, upg, dx_ref, dr, dz, own_part, other_part, rel,
    onehot, prob, gg, wg, wu, wd,
    r_s, r_r, za_s, za_r, xa_s, xa_r, xb_s, xb_r, zb_s, zb_r, pair_s, pair_r, part_s, part_r, fw_s, rel_s, rel_r,
    f_s, f_r, w_s, w_r, in_sem, out_sem,
):
    ys, ds_, zd = gs, xs, xz
    e = lax.axis_index("expert")
    c = lax.axis_index("tensor")
    z = e // 4
    o = lax.rem(e, 4) * 2 + c
    micro, length, width = tok_ref.shape
    half = length // 2
    f32 = jnp.float32
    bf = jnp.bfloat16
    ff = wg.shape[1]
    col = 4 * half
    rows = xs.shape[1]
    blk = rows // 8
    cap = blk // 4
    me = 2 * e + c
    tw = 256
    nt = width // tw

    def z_dev(k):
        return (lax.rem(z + k, 4) * 4 + lax.rem(e, 4), c)

    def z_back(k):
        return (lax.rem(z + 4 - k, 4) * 4 + lax.rem(e, 4), c)

    def p_dev(d):
        t = lax.rem(o + d, 8)
        return (z * 4 + t // 2, lax.rem(t, 2))

    def p_back(d):
        t = lax.rem(o + 8 - d, 8)
        return (z * 4 + t // 2, lax.rem(t, 2))

    inner = (z == 1) | (z == 2)
    edge = (z == 0) | (z == 3)
    not_first = z != 0
    not_last = z != 3
    beside = jnp.where((z == 0) | (z == 3), jnp.where(z == 0, 1, 2), jnp.where(z == 1, 0, 3))
    beside_dev = (beside * 4 + lax.rem(e, 4), c)
    far_slot = jnp.where(z == 1, 1, 3)
    far_back = jnp.where(z == 0, 1, 3)

    @pl.when(z == 3)
    def _():
        for m in range(micro):
            dz[m, half : 2 * half, :] = jnp.zeros((half, width + 128), bf)

    @pl.when(z == 0)
    def _():
        for m in range(micro):
            dz[m, 3 * half : 4 * half, :] = jnp.zeros((half, width + 128), bf)

    barrier = pltpu.get_barrier_semaphore()
    for k in range(1, 4):
        pl.semaphore_signal(barrier, inc=1, device_id=z_dev(k), device_id_type=MESH)
    for d in range(1, 8):
        pl.semaphore_signal(barrier, inc=1, device_id=p_dev(d), device_id_type=MESH)
    loads = {}
    for i, (name, src, dst) in enumerate(
        (
            ("tok", tok_hbm, tok_ref), ("wq", wq_hbm, wq_ref), ("wk", wk_hbm, wk_ref), ("wv", wv_hbm, wv_ref),
            ("wo", wo_hbm, wo_ref), ("wg", wg_hbm.at[:, cols(c, ff)], wg), ("wu", wu_hbm.at[:, cols(c, ff)], wu),
            ("wd", wd_hbm.at[cols(c, ff), :], wd),
        )
    ):
        loads[name] = pltpu.make_async_copy(src, dst, in_sem.at[i])
        if name not in ("wg", "wu", "wd"):
            loads[name].start()
    saves = []

    def save(src, dst):
        cp = pltpu.make_async_copy(src, dst, out_sem.at[len(saves)])
        cp.start()
        saves.append(cp)

    pl.semaphore_wait(barrier, 10)

    mine = pl.ds(pl.multiple_of(c * half, half), half)
    sent = []
    got_r = []
    for k in range(1, 4):
        cp = remote(routes_ref, rz.at[k], r_s.at[k], r_r.at[k], z_dev(k))
        cp.start()
        sent.append(cp)
        got_r.append(cp)
    got_z = {}

    sent_if = []
    away = {}
    got_f = {}

    def start_if(cond, cp):
        pl.when(cond)(cp.start)
        sent_if.append((cond, cp))

    cut = width // 2
    parts = (((0, width),), ((0, cut), (cut, width + 128 - cut)))

    def sem_of(m, a, j, k, per):
        return ((m * 2 + a) * 2 + j) * per + k

    def z_send(m, a):
        src, dst = ((g_hbm, gz), (x_ref, xz))[a]
        for j, (left, size) in enumerate(parts[a]):
            wide = pl.ds(left, size)
            for k in (2, 1, 3):
                i = sem_of(m, a, j, k, 4)
                cp = remote(
                    src.at[m, mine, wide], dst.at[m, pl.ds(k * half, half), wide],
                    za_s.at[i], za_r.at[i], z_dev(k),
                )
                cond = {1: not_last, 2: True, 3: not_first}[k]
                if k == 2:
                    cp.start()
                else:
                    pl.when(cond)(cp.start)
                got_z[(m, a, j, k)] = cp
                away.setdefault((m, a), []).append((cond, cp))
        if a == 1:
            dst[m, 0:half, :] = src[m, mine, :]
        else:
            cp = pltpu.make_async_copy(src.at[m, mine, :], dst.at[m, 0:half, :], in_sem.at[8 + m])
            cp.start()
            loads[("g", m)] = cp

    def z_sent(m, a):
        for cond, cp in away.pop((m, a)):
            if cond is True:
                cp.wait_send()
            else:
                pl.when(cond)(cp.wait_send)

    def z_forward(m, a):
        dst = (gz, xz)[a]
        for j, (left, size) in enumerate(parts[a]):
            wide = pl.ds(left, size)
            got_z[(m, a, j, 2)].wait_recv()
            cp = remote(
                dst.at[m, pl.ds(2 * half, half), wide],
                dst.at[m, pl.ds(pl.multiple_of(far_slot * half, half), half), wide],
                fw_s.at[sem_of(m, a, j, 0, 1)], za_r.at[sem_of(m, a, j, 0, 4) + far_slot], beside_dev,
            )
            pl.when(inner)(cp.start)
            got_f[(m, a, j)] = cp

    z_send(0, 0)
    rz[0] = routes_ref[...]

    qx = lax.rem(e, 2)
    qy = lax.rem(e, 4) // 2
    every = micro * length
    twin = (e, 1 - c)
    got_a = {}

    def f_dev(d):
        return (z * 4 + lax.rem(qy + d // 2, 2) * 2 + lax.rem(qx + d % 2, 2), c)

    def block(d):
        return pl.ds(pl.multiple_of(d * every + c * length, length), length)

    def factor(i, dst):
        for d in (1, 2):
            if i == 0:
                size = width // 2
                view = nrm_ref.at[c, :, cols(lax.rem(qx + d % 2, 2), size)]
                to = dst.at[block(d), :]
                copies = [(view, to)]
            else:
                size = att_ref.shape[2] // 2
                at = cols(lax.rem(qy + d // 2, 2), size)
                copies = [
                    (att_ref.at[m, :, at], dst.at[pl.ds(d * every + m * length, length), :])
                    for m in range(micro)
                ]
            for m, (view, to) in enumerate(copies):
                n = (d * 2 + i // 2) * 2 + m
                cp = remote(view, to, f_s.at[n], f_r.at[n], f_dev(d))
                cp.start()
                sent.append(cp)
                got_a[(i, d, m)] = cp

    def to_twin(d):
        got_a[(0, d, 0)].wait_recv()
        cp = remote(fn.at[block(d), :], fn.at[block(d), :], w_s.at[d], w_r.at[d], twin)
        cp.start()
        sent.append(cp)
        got_a[("twin", d)] = cp

    def pass_on():
        to_twin(1)
        to_twin(2)
        cp = remote(fn.at[block(1), :], fn.at[block(3), :], f_s.at[12], f_r.at[12], f_dev(2))
        cp.start()
        sent.append(cp)
        got_a[(0, 3, 0)] = cp
        for m in range(micro):
            got_a[(2, 2, m)].wait_recv()
        cp = remote(
            fa.at[pl.ds(2 * every, every), :], fa.at[pl.ds(3 * every, every), :], f_s.at[13], f_r.at[13], f_dev(1)
        )
        cp.start()
        sent.append(cp)
        got_a[(2, 3, 0)] = cp

    head = HEAD_SIZE
    heads = wq_ref.shape[1] // head
    lane = lax.broadcasted_iota(jnp.int32, (1, 128), 1)
    row = lax.broadcasted_iota(jnp.int32, (length, length), 0)
    column = lax.broadcasted_iota(jnp.int32, (length, length), 1)
    turn = jnp.exp(
        (-2.0 / head * jnp.log(jnp.float32(theta_base))) * lax.rem(lane, head // 2).astype(f32)
    )
    allowed = []
    loads["tok"].wait()
    for m in range(micro):
        states = tok_ref[m].astype(f32)
        scale = lax.rsqrt(jnp.mean(states * states, axis=1, keepdims=True) + epsilon)
        nrm_ref[m] = (states * scale * gain_a[...].reshape(1, width)).astype(bf)
        place = pos_ref[m : m + 1, :].astype(f32)
        place = jnp.sum(jnp.where(row == column, place, 0.0), axis=1, keepdims=True)
        angle = place * turn
        tab_ref[m, 0] = jnp.cos(angle)
        tab_ref[m, 1] = jnp.where(lane < head // 2, -1.0, 1.0) * jnp.sin(angle)
        allowed.append((column <= row) & (column >= row - place.astype(jnp.int32)))

    def rope(u, m):
        return u * tab_ref[m, 0] + pltpu.roll(u, head // 2, 1) * tab_ref[m, 1]

    factor(0, fn)
    save(nrm_ref, nrm_hbm)
    save(tab_ref, tab_hbm)
    everything = nrm_ref[...].reshape(micro * length, width)

    def project(i):
        both = mm(everything, wq_ref[:, cols(i, tw)])
        for m in range(micro):
            for j in range(tw // head):
                at = pl.ds(pl.multiple_of((i * (tw // head) + j) * length, length), length)
                u = both[m * length : (m + 1) * length, j * head : (j + 1) * head]
                q_ref[m, at, :] = rope(u, m).astype(bf)

    for name in ("wq", "wk", "wv"):
        loads[name].wait()
    for name in ("wg", "wu", "wd"):
        loads[name].start()
    tiles(wq_ref.shape[1] // tw, project)
    z_forward(0, 0)
    z_sent(0, 0)
    for m in range(1, micro):
        z_send(m, 0)
    key_pre = mm(everything, wk_ref[...])
    value_pre = mm(everything, wv_ref[...])
    for m in range(micro):
        at = slice(m * length, (m + 1) * length)
        k_ref[m] = rope(key_pre[at], m).astype(bf)
        v_ref[m] = value_pre[at].astype(bf)
    for m in range(micro):
        score = mm_nt(q_ref[m], k_ref[m]).reshape(heads, length, length) * (head**-0.5)
        score = jnp.where(allowed[m][None], score, masked_score)
        weight = jnp.exp(score - jnp.max(score, axis=-1, keepdims=True))
        weight = weight / jnp.sum(weight, axis=-1, keepdims=True)
        weight = weight.reshape(heads * length, length)
        pr_ref[m] = weight
        out = mm(weight.astype(bf), v_ref[m]).astype(bf)
        for h in range(heads):
            att_ref[m, :, h * head : (h + 1) * head] = out[h * length : (h + 1) * length]
    for src, dst in ((q_ref, q_hbm), (k_ref, k_hbm), (v_ref, v_hbm), (pr_ref, pr_hbm), (att_ref, att_hbm)):
        save(src, dst)
    factor(2, fa)
    loads["wo"].wait()
    att_all = att_ref[...].reshape(micro * length, heads * head)
    got_part = []
    for j in range(3):

        def outward(i, j=j):
            at = cols(i + j * (nt // 3), tw)
            own_part[:, at] = mm(att_all, wo_ref[:, at])

        tiles(nt // 3, outward)
        at = pl.ds(j * (width // 3), width // 3)
        cp = remote(
            own_part.at[:, at], other_part.at[:, at], part_s.at[j], part_r.at[j], (e, 1 - c)
        )
        cp.start()
        sent.append(cp)
        got_part.append(cp)

    for cp in got_r:
        cp.wait_recv()

    before = ((row < column) & (row // half == column // half)).astype(bf)
    expert = 8 * z + lax.rem(o + lax.broadcasted_iota(jnp.int32, (8, length), 0), 8)
    place_row = lax.broadcasted_iota(jnp.int32, (length, col), 0)
    place_col = lax.broadcasted_iota(jnp.int32, (length, col), 1)
    slots = [jnp.zeros((8, col), f32) for _ in range(micro)]
    for k in range(4):
        at = place_col - k * half
        put = ((at >= 0) & (at < half) & (place_row == at + c * half)).astype(bf)
        for m in range(micro):
            named = rz[k, m]
            hit = named[0:1, :] == expert
            for j in range(1, routes_ref.shape[1]):
                hit = hit | (named[j : j + 1, :] == expert)
            mask = jnp.where(hit, 1.0, 0.0)
            rank = mm(mask.astype(bf), before)
            slots[m] = slots[m] + mm((mask * (rank + (cap * k + 1))).astype(bf), put)
    number = lax.broadcasted_iota(jnp.int32, (blk, col), 0) + 1
    for m in range(micro):
        for d in range(8):
            spot = slots[m][d : d + 1, :].astype(jnp.int32)
            onehot[m, d * blk : (d + 1) * blk, :] = jnp.where(spot == number, 1.0, 0.0).astype(
                jnp.bfloat16
            )

    got_p = {}

    def pack(m, a):
        src, out, dst = ((gz, gs, gr), (xz, xs, xr))[a]
        if a == 0:
            loads[("g", m)].wait()
        for j, (left, size) in enumerate(parts[a]):
            for k in (1, 3):
                got_z[(m, a, j, k)].wait_recv()

            def body(i, left=left):
                at = cols(i + left // tw, tw)
                out[m, :, at] = mm(onehot[m], src[m, :, at]).astype(bf)

            tiles(size // tw, body)
            if (left + size) % tw:
                out[m, :, width:] = mm(onehot[m], src[m, :, width:]).astype(bf)
            wide = slice(left, left + size)
            dst[m, 0:blk, wide] = out[m, 0:blk, wide]
            wide = pl.ds(left, size)
            for d in range(1, 8):
                i = sem_of(m, a, j, d, 8)
                at = pl.ds(d * blk, blk)
                cp = remote(
                    out.at[m, at, wide], dst.at[m, at, wide], xa_s.at[i], xa_r.at[i], p_dev(d)
                )
                cp.start()
                sent_p.setdefault((m, a), []).append(cp)
                got_p[(m, a, j, d)] = cp

    sent_p = {}
    pass_on()
    pack(0, 0)
    tall = lax.broadcasted_iota(jnp.int32, (128, EXPERTS), 0)
    double = (lax.rem(tall, EXPERTS) == lax.broadcasted_iota(jnp.int32, (128, EXPERTS), 1)) & (
        tall < 2 * EXPERTS
    )
    router = mm(jnp.where(double, 1.0, 0.0).astype(bf), router_ref[...]).astype(bf)
    for cp in got_part:
        cp.wait_recv()
    for m in range(micro):
        at = slice(m * length, (m + 1) * length)
        state = tok_ref[m].astype(f32) + (own_part[at, :] + other_part[at, :])
        hs_ref[m] = state
        save(hs_ref.at[m], hs_hbm.at[m])
        scale = lax.rsqrt(jnp.mean(state * state, axis=1, keepdims=True) + epsilon)
        low = (state * scale * gain_f[...].reshape(1, width)).astype(bf)
        x_ref[m, :, 0:width] = low
        logits = mm_nt(low, router)
        names = lax.rem(lane, EXPERTS)
        hit = lane < 0
        for j in range(routes_ref.shape[1]):
            named = routes_ref[m, j : j + 1, :].astype(f32)
            named = jnp.sum(jnp.where(row == column, named, 0.0), axis=1, keepdims=True)
            hit = hit | (named.astype(jnp.int32) == names)
        hit = hit & (lane < 2 * EXPERTS)
        best = jnp.max(jnp.where(hit, logits, masked_score), axis=1, keepdims=True)
        weight = jnp.where(hit, jnp.exp(logits - best), 0.0)
        first = jnp.sum(jnp.where(lane < EXPERTS, weight, 0.0), axis=1, keepdims=True)
        weight = weight / first
        top = weight.astype(bf).astype(f32)
        x_ref[m, :, width:] = jnp.where(lane < EXPERTS, top, weight - top).astype(bf)
        if m == 0:
            z_send(m, 1)
        save(x_ref.at[m], x_hbm.at[m])
    for m in range(1, micro):
        z_forward(m, 0)
        pack(m, 0)
    z_forward(0, 1)
    z_sent(0, 1)
    for m in range(1, micro):
        z_send(m, 1)
    pack(0, 1)
    for m in range(1, micro):
        z_forward(m, 1)
        pack(m, 1)
    for name in ("wg", "wu", "wd"):
        loads[name].wait()
    save(onehot, hot_hbm)

    got_b = {}
    def weight_grads():
        def columns(i):
            at = cols(i, tw)
            for out, back in ((wg, gpg), (wu, upg)):
                total = mm_tn(xr[0, :, 0:width], back[0, :, at])
                for m in range(1, micro):
                    total = total + mm_tn(xr[m, :, 0:width], back[m, :, at])
                out[:, at] = total.astype(bf)
            total = mm_tn(hid[0, :, at], eg[0])
            for m in range(1, micro):
                total = total + mm_tn(hid[m, :, at], eg[m])
            wd[at, :] = total.astype(bf)

        tiles(ff // tw, columns)
        for n, (src, dst) in enumerate(((wg, gate_hbm), (wu, up_hbm), (wd, down_hbm))):
            cp = remote(src, dst.at[c], pair_s.at[n], pair_r.at[n], twin)
            cp.start()
            sent.append(cp)
            got_b[("pair", n)] = cp
            save(src, dst.at[c])

    def send_back(m, a, j):
        src, dst = ((ds_.at[m], dr.at[m]), (ys.at[m], y0_hbm))[a]
        left, size = parts[1 - a][j]
        if a == 0:
            wide = slice(left, left + size)
            dst[0:blk, wide] = src[0:blk, wide]
        else:
            save(src.at[0:blk, :], dst.at[0:blk, :])
        wide = pl.ds(left, size)
        for d in range(1, 8):
            i = sem_of(m, a, j, d, 8)
            at = pl.ds(d * blk, blk)
            cp = remote(src.at[at, wide], dst.at[at, wide], xb_s.at[i], xb_r.at[i], p_back(d))
            cp.start()
            sent.append(cp)
            got_b[(m, a, j, d)] = cp

    def run(m):
        for a in range(2):
            for j in range(len(parts[a])):
                for d in range(1, 8):
                    got_p[(m, a, j, d)].wait_recv()
            for cp in sent_p[(m, a)]:
                cp.wait_send()
        tail = xr[m, :, width:].astype(jnp.float32)
        pick = (lane == me) | (lane == me + 32)
        prob[...] = jnp.broadcast_to(
            jnp.sum(jnp.where(pick, tail, 0.0), axis=1, keepdims=True), (rows, 128)
        )
        gg[...] = jnp.zeros_like(gg)

        def weigh(i):
            at = cols(i, tw)
            eg[m, :, at] = (prob[:, 0:1] * gr[m, :, at].astype(jnp.float32)).astype(jnp.bfloat16)

        tiles(nt, weigh)

        def inner(i):
            at = cols(i, tw)
            xrow = xr[m, :, 0:width]
            gate = mm(xrow, wg[:, at])
            upv = mm(xrow, wu[:, at])
            back = mm_nt(eg[m], wd[at, :])
            cdf = 0.5 * (1.0 + lax.erf(gate * 0.7071067811865476))
            act = gate * cdf
            slope = cdf + gate * (jnp.exp(gate * gate * -0.5) * 0.3989422804014327)
            hid[m, :, at] = (act * upv).astype(jnp.bfloat16)
            gpg[m, :, at] = (back * upv * slope).astype(jnp.bfloat16)
            upg[m, :, at] = (back * act).astype(jnp.bfloat16)

        tiles(ff // tw, inner)

        def outer(i):
            at = cols(i, tw)
            low = mm(hid[m], wd[:, at]).astype(jnp.bfloat16).astype(jnp.float32)
            gg[...] += jnp.broadcast_to(
                jnp.sum(low * gr[m, :, at].astype(jnp.float32), axis=1, keepdims=True),
                (rows, 128),
            )
            ys[m, :, at] = (prob[:, 0:1] * low).astype(jnp.bfloat16)

        tiles(nt, outer)

        def inputs(i):
            at = cols(i, tw)
            ds_[m, :, at] = (mm_nt(gpg[m], wg[at, :]) + mm_nt(upg[m], wu[at, :])).astype(
                jnp.bfloat16
            )

        tiles(cut // tw, inputs)
        send_back(m, 0, 0)
        tiles((width - cut) // tw, lambda i: inputs(i + cut // tw))
        total = gg[...]
        high = total.astype(jnp.bfloat16).astype(jnp.float32)
        ds_[m, :, width:] = jnp.where(
            lane == me, high, jnp.where(lane == me + 32, total - high, 0.0)
        ).astype(jnp.bfloat16)
        send_back(m, 0, 1)

    for m in range(micro):
        run(m)
    send_back(0, 1, 0)
    save(ys.at[1], y1_hbm)

    got_c = {}

    def gather(m, j):
        left, size = parts[1][j]
        for d in range(1, 8):
            got_b[(m, 0, j, d)].wait_recv()
        pl.when(inner)(got_f[(m, 1, j)].wait_send)

        def body(i):
            at = cols(i + left // tw, tw)
            zd[m, :, at] = mm_tn(onehot[m], dr[m, :, at]).astype(bf)

        tiles(size // tw, body)
        if j == 1:
            zd[m, :, width:] = mm_tn(onehot[m], dr[m, :, width:]).astype(bf)
        wide = pl.ds(left, size)
        far = pl.ds(pl.multiple_of(far_back * half, half), half)
        relay = remote(
            zd.at[m, far, wide], rel.at[m, :, wide], rel_s.at[m * 2 + j], rel_r.at[m * 2 + j], beside_dev
        )
        start_if(edge, relay)
        for k in (1, 3, 2):
            i = (m * 2 + j) * 4 + k
            at = pl.ds(k * half, half)
            cp = remote(zd.at[m, at, wide], dz.at[m, at, wide], zb_s.at[i], zb_r.at[i], z_back(k))
            got_c[(m, j, k)] = cp
            if k == 2:

                @pl.when(inner)
                def _():
                    relay.wait_recv()
                    here = slice(left, left + size)
                    zd[m, 2 * half : 3 * half, here] = (
                        zd[m, 2 * half : 3 * half, here].astype(f32) + rel[m, :, here].astype(f32)
                    ).astype(bf)

                cp.start()
                sent.append(cp)
            else:
                start_if(not_first if k == 1 else not_last, cp)

    def finish(m, j):
        left, size = parts[1][j]
        here = slice(left, left + size)
        pl.when(not_last)(got_c[(m, j, 1)].wait_recv)
        pl.when(not_first)(got_c[(m, j, 3)].wait_recv)
        got_c[(m, j, 2)].wait_recv()
        total = zd[m, 0:half, here].astype(f32)
        for k in range(1, 4):
            total = total + dz[m, k * half : (k + 1) * half, here].astype(f32)
        dx_ref[m, mine, here] = total
        n = m * 8 + 5 + j
        wide = pl.ds(left, size)
        cp = remote(
            dx_ref.at[m, mine, wide], dx_ref.at[m, mine, wide], pair_s.at[n], pair_r.at[n], (e, 1 - c)
        )
        cp.start()
        sent.append(cp)
        got_c[("pair", m, j)] = cp

    order = [(m, j) for m in range(micro) for j in range(2)]
    for i, (m, j) in enumerate(order):
        gather(m, j)
        if i == 1:
            weight_grads()
        if i >= 1:
            finish(*order[i - 1])
    finish(*order[-1])
    for m in range(micro):
        pl.when(inner)(got_f[(m, 0, 0)].wait_send)
    to_twin(3)
    got_a[(2, 3, 0)].wait_recv()
    for m in range(micro):
        got_a[(2, 1, m)].wait_recv()
    for d in range(1, 4):
        got_a[("twin", d)].wait_recv()
    for m in range(micro):
        for j in range(2):
            got_c[("pair", m, j)].wait_recv()
        save(dx_ref.at[m], dx_hbm.at[m])
    for n in range(3):
        got_b[("pair", n)].wait_recv()
    for d in range(1, 8):
        got_b[(0, 1, 0, d)].wait_recv()
    for at in list(away):
        z_sent(*at)
    for cp in saves:
        cp.wait()
    for cp in sent:
        cp.wait_send()
    for cond, cp in sent_if:
        pl.when(cond)(cp.wait_send)


def front_call(
    tokens, cotangent, positions, routes, gain_a, gain_f, wq, wk, wv, wo, router, gate_weight,
    up_weight, down_weight,
):
    micro, length, width = tokens.shape
    wide = width + 128
    half = length // 2
    ff = gate_weight.shape[1] // 2
    cap = 3 * half * routes.shape[1] // (2 * EXPERTS)
    rows = 8 * 4 * cap
    bf = jnp.bfloat16
    f32 = jnp.float32
    vmem = pl.BlockSpec(memory_space=pltpu.VMEM)
    hbm = pl.BlockSpec(memory_space=ANY)
    heads = wq.shape[1] // HEAD_SIZE

    def buf(*shape, dtype=bf):
        return pltpu.VMEM(shape, dtype)

    def out(*shape, dtype=bf):
        return jax.ShapeDtypeStruct(shape, dtype)

    sem = pltpu.SemaphoreType.DMA
    col = 4 * half
    hw = wq.shape[1]
    return pl.pallas_call(
        front_kernel,
        out_shape=(
            out(micro, length, wide, dtype=f32),
            out(micro, length, width),
            out(micro, length, hw),
            out(micro, heads * length, HEAD_SIZE),
            out(micro, length, HEAD_SIZE),
            out(micro, length, HEAD_SIZE),
            out(micro, heads * length, length, dtype=f32),
            out(micro, 2, length, HEAD_SIZE, dtype=f32),
            out(micro, length, width, dtype=f32),
            out(micro, length, wide),
            out(rows, width),
            out(rows, width),
            out(micro, rows, col),
            out(4 * micro * length, width // 2),
            out(4 * micro * length, hw // 2),
            out(2, width, ff),
            out(2, width, ff),
            out(2, ff, width),
        ),
        in_specs=[hbm] * 9 + [vmem] * 5,
        out_specs=(hbm,) * 18,
        scratch_shapes=[
            buf(micro, length, width), buf(width, hw), buf(width, HEAD_SIZE), buf(width, HEAD_SIZE), buf(hw, width),
            buf(micro, length, width), buf(micro, length, hw), buf(micro, heads * length, HEAD_SIZE),
            buf(micro, length, HEAD_SIZE), buf(micro, length, HEAD_SIZE),
            buf(micro, heads * length, length, dtype=f32), buf(micro, 2, length, HEAD_SIZE, dtype=f32),
            buf(micro, length, width, dtype=f32), buf(micro, length, wide),
            buf(micro, col, wide), buf(micro, col, width), pltpu.VMEM((4, *routes.shape), jnp.int32),
            buf(micro, rows, wide), buf(micro, rows, width), buf(micro, rows, wide), buf(micro, rows, width),
            buf(micro, rows, width), buf(micro, rows, ff), buf(micro, rows, ff), buf(micro, rows, ff),
            buf(micro, length, wide, dtype=f32), buf(micro, rows, wide), buf(micro, col, wide),
            buf(micro * length, width, dtype=f32), buf(micro * length, width, dtype=f32),
            buf(micro, half, wide), buf(micro, rows, col), buf(rows, 128, dtype=f32), buf(rows, 128, dtype=f32),
            buf(width, ff), buf(width, ff), buf(ff, width),
            sem((4,)), sem((4,)), sem((16 * micro,)), sem((16 * micro,)), sem((32 * micro,)), sem((32 * micro,)),
            sem((32 * micro,)), sem((32 * micro,)), sem((8 * micro,)), sem((8 * micro,)), sem((8 * micro,)),
            sem((8 * micro,)), sem((3,)), sem((3,)), sem((4 * micro,)), sem((2 * micro,)), sem((2 * micro,)),
            sem((14,)), sem((14,)), sem((4,)), sem((4,)), sem((8 + micro,)), sem((16 + 5 * micro,)),
        ],
        compiler_params=pltpu.CompilerParams(
            collective_id=1, has_side_effects=True, vmem_limit_bytes=VMEM_LIMIT
        ),
        cost_estimate=pl.CostEstimate(
            flops=2 * 6 * micro * rows * width * ff, bytes_accessed=40 * 2**20, transcendentals=0
        ),
        name="front",
    )(
        tokens, cotangent, wq, wk, wv, wo, gate_weight, up_weight, down_weight,
        positions, routes, gain_a, gain_f, router,
    )


def back_kernel(
    tok_hbm, g_hbm, wq_hbm, wk_hbm, wv_hbm, wo_hbm,
    dx_hbm, nrm_hbm, att_hbm, q_hbm, k_hbm, v_hbm, pr_hbm, tab_hbm, hs_hbm, x_hbm, y0_hbm, y1_hbm, hot_hbm,
    fn_hbm, fa_hbm, gain_a, gain_f, router_ref,
    lay_ref, tg_hbm, oa, ob_hbm, os,
    tok_ref, g_ref, wq_ref, wk_ref, wv_ref, wo_ref, dx_ref, q_ref, k_ref, v_ref, pr_ref, tab_ref, hs_ref, x_ref,
    hot, y0r, y1r, zy, yz, rel, tg_ref, ob,
    d_ref, a_ref, s_ref, sg, ag, own_part, other_part,
    fn, fd, fa, fg, fs, pa, pb, za, zb, zs, ra, rb,
    f_s, f_r, w_s, w_r, c_s, c_r, y_s, y_r, l_s, l_r, z_s, z_r, h_s, h_r, p_s, p_r, part_s, part_r,
    yp_s, yp_r, yz_s, yz_r, rel_s, rel_r, pair_s, pair_r, in_sem, out_sem,
):
    micro, length, width = tok_ref.shape
    half = length // 2
    f32 = jnp.float32
    bf = jnp.bfloat16
    head = HEAD_SIZE
    heads = wq_ref.shape[1] // head
    wq = wq_ref.shape[1]
    tw = 256
    nt = width // tw
    e = lax.axis_index("expert")
    c = lax.axis_index("tensor")
    z = e // 4
    q = lax.rem(e, 4)
    qx = lax.rem(q, 2)
    qy = q // 2
    rows = micro * length
    wn = fn.shape[1]
    wd = d_ref.shape[1] // 2
    wa = fa.shape[1]
    per = length
    wg = a_ref.shape[1] // 2
    ws = s_ref.shape[1] // 4
    hs = s_ref.shape[0] // 4
    ha = wn // 4
    hb = wa // 4

    def flip(bit, by):
        return lax.rem(bit + by, 2)

    def p_dev(d):
        return (z * 4 + flip(qy, d // 2) * 2 + flip(qx, d % 2), c)

    def z_dev(k):
        return (lax.rem(z + k, 4) * 4 + q, c)

    def part(i, size):
        return pl.ds(pl.multiple_of(i * size, size), size)

    inner = (z == 1) | (z == 2)
    edge = (z == 0) | (z == 3)
    not_first = z != 0
    not_last = z != 3
    beside = jnp.where(edge, jnp.where(z == 0, 1, 2), jnp.where(z == 1, 0, 3))
    beside_dev = (beside * 4 + q, c)
    twin = (e, 1 - c)
    sent_if = []

    def start_if(cond, cp):
        pl.when(cond)(cp.start)
        sent_if.append((cond, cp))

    o = q * 2 + c
    blk = y1r.shape[0] // 8
    own_rows = pl.ds(pl.multiple_of(c * half, half), half)

    def any_dev(n):
        t = lax.rem(o + n, 8)
        return (z * 4 + t // 2, lax.rem(t, 2))

    def any_back(n):
        t = lax.rem(o + 8 - n, 8)
        return (z * 4 + t // 2, lax.rem(t, 2))

    def fill(m, slot):
        yz[m, slot * half : (slot + 1) * half, :] = jnp.zeros((half, width), bf)

    def clear(slot):
        za[slot] = jnp.zeros((ha, wd), bf)
        zb[slot] = jnp.zeros((hb, wg), bf)

    pl.when(z == 0)(lambda: clear(1))
    pl.when(z == 3)(lambda: clear(3))

    for m in range(micro):
        pl.when(z == 3)(lambda m=m: fill(m, 1))
        pl.when(z == 0)(lambda m=m: fill(m, 3))

    barrier = pltpu.get_barrier_semaphore()
    for n in range(1, 4):
        pl.semaphore_signal(barrier, inc=1, device_id=z_dev(n), device_id_type=MESH)
    for n in range(1, 8):
        pl.semaphore_signal(barrier, inc=1, device_id=any_dev(n), device_id_type=MESH)
    loads = {}
    for i, (name, src, dst) in enumerate(
        (
            ("dx", dx_hbm, dx_ref), ("x", x_hbm, x_ref), ("hs", hs_hbm, hs_ref), ("g", g_hbm, g_ref),
            ("y0", y0_hbm, y0r), ("hot", hot_hbm, hot), ("y1", y1_hbm.at[0:blk, :], y1r.at[0:blk, :]), ("wo", wo_hbm, wo_ref),
            ("v", v_hbm, v_ref), ("pr", pr_hbm, pr_ref), ("k", k_hbm, k_ref), ("q", q_hbm, q_ref),
            ("tab", tab_hbm, tab_ref), ("wq", wq_hbm, wq_ref), ("wk", wk_hbm, wk_ref), ("wv", wv_hbm, wv_ref),
            ("tok", tok_hbm, tok_ref),
            ("fa", fa_hbm.at[rows:, :], fa.at[rows:, :]), ("fa0", att_hbm.at[:, part(qy, wa)], fa.at[0:rows, :]),
            ("fn", fn_hbm.at[rows:, :], fn.at[rows:, :]), ("fn0", nrm_hbm.at[:, part(qx, wn)], fn.at[0:rows, :]),
        )
    ):
        loads[name] = pltpu.make_async_copy(src, dst, in_sem.at[i])
        loads[name].start()
    saves = []

    def save(src, dst):
        cp = pltpu.make_async_copy(src, dst, out_sem.at[len(saves)])
        cp.start()
        saves.append(cp)

    def need(*names):
        for name in names:
            loads[name].wait()

    pl.semaphore_wait(barrier, 10)

    sent = []
    got_f = {}
    bits = {3: 0, 1: 1}

    def piece(src, i, d):
        bit = flip(qx, d % 2) if bits[i] == 0 else flip(qy, d // 2)
        return part(bit, src.shape[1] // 2)

    def mine(d):
        return pl.ds(pl.multiple_of(d * rows + c * per, per), per)

    def factor(i, src, dst):
        for d in (1, 2):
            if bits[i] == 0:
                view = src.at[pl.ds(pl.multiple_of(c * per, per), per), piece(src, i, d)]
                to = dst.at[mine(d), :]
            else:
                view = src.at[:, piece(src, i, d)]
                to = dst.at[pl.ds(d * rows, rows), :]
            cp = remote(view, to, f_s.at[d * 4 + i], f_r.at[d * 4 + i], p_dev(d))
            cp.start()
            sent.append(cp)
            got_f[(i, d)] = cp

    def to_twin(i, d, dst):
        cp = remote(dst.at[mine(d), :], dst.at[mine(d), :], w_s.at[d * 4 + i], w_r.at[d * 4 + i], twin)
        cp.start()
        sent.append(cp)
        got_f[("twin", i, d)] = cp

    def relay(i, dst):
        via, over = (1, 2) if bits[i] == 0 else (2, 1)
        got_f[(i, via)].wait_recv()
        if bits[i] == 0:
            src, to = dst.at[mine(via), :], dst.at[mine(3), :]
        else:
            src, to = dst.at[pl.ds(via * rows, rows), :], dst.at[pl.ds(3 * rows, rows), :]
        cp = remote(src, to, f_s.at[12 + i], f_r.at[12 + i], p_dev(over))
        cp.start()
        sent.append(cp)
        got_f[(i, 3)] = cp
        if bits[i] == 0:
            to_twin(i, via, dst)
            got_f[(i, over)].wait_recv()
            to_twin(i, over, dst)

    def d_rows(d, m):
        return pl.ds(d * rows + m * per, per)

    def factor_d(m):
        for d in (2, 1):
            cp = remote(
                d_ref.at[pl.ds(m * per, per), part(flip(qy, d // 2), wd)], fd.at[d_rows(d, m), :],
                f_s.at[d * 4 + m], f_r.at[d * 4 + m], p_dev(d),
            )
            cp.start()
            sent.append(cp)
            got_f[("d", m, d)] = cp

    def relay_d(m):
        got_f[("d", m, 2)].wait_recv()
        cp = remote(fd.at[d_rows(2, m), :], fd.at[d_rows(3, m), :], f_s.at[12 + m], f_r.at[12 + m], p_dev(1))
        cp.start()
        sent.append(cp)
        got_f[("d", m, 3)] = cp

    def arrive(i, dst):
        if bits[i]:
            got_f[(i, 1)].wait_recv()
            got_f[(i, 3)].wait_recv()
        else:
            got_f[(i, 3)].wait_recv()
            to_twin(i, 3, dst)
            for d in (1, 2, 3):
                got_f[("twin", i, d)].wait_recv()

    got_v = {}
    def send_y1(j):
        wide = pl.ds(j * (width // 2), width // 2)
        for n in range(1, 8):
            at = pl.ds(n * blk, blk)
            cp = remote(
                y1_hbm.at[at, wide], y1r.at[at, wide], yp_s.at[j * 8 + n], yp_r.at[j * 8 + n], any_back(n)
            )
            cp.start()
            sent.append(cp)
            got_v[(n, j, "row")] = cp

    send_y1(0)

    def z_back(n):
        return (lax.rem(z + 4 - n, 4) * 4 + q, c)

    def regroup(m, src):
        def outputs(i):
            at = cols(i, tw)
            zy[m, :, at] = mm_tn(hot[m], src[:, at]).astype(bf)

        tiles(nt, outputs)

    def send_far(m):
        far = part(jnp.where(z == 0, 1, 3), half)
        cp = remote(zy.at[m, far, :], rel.at[m], rel_s.at[m], rel_r.at[m], beside_dev)
        start_if(edge, cp)
        got_v[("far", m)] = cp
        for n in (1, 3):
            at = pl.ds(n * half, half)
            cp = remote(zy.at[m, at, :], yz.at[m, at, :], yz_s.at[m * 4 + n], yz_r.at[m * 4 + n], z_back(n))
            start_if(not_first if n == 1 else not_last, cp)
            got_v[(m, n)] = cp

    def send_near(m):
        at = pl.ds(2 * half, half)

        @pl.when(inner)
        def _():
            got_v[("far", m)].wait_recv()
            zy[m, at, :] = (zy[m, at, :].astype(f32) + rel[m].astype(f32)).astype(bf)

        cp = remote(zy.at[m, at, :], yz.at[m, at, :], yz_s.at[m * 4 + 2], yz_r.at[m * 4 + 2], z_back(2))
        cp.start()
        sent.append(cp)
        got_v[(m, 2)] = cp

    def layer(m):
        pl.when(not_last)(got_v[(m, 1)].wait_recv)
        pl.when(not_first)(got_v[(m, 3)].wait_recv)
        got_v[(m, 2)].wait_recv()
        total = zy[m, 0:half, :].astype(f32)
        for n in range(1, 4):
            total = total + yz[m, n * half : (n + 1) * half, :].astype(f32)
        lay_ref[m, own_rows, :] = (hs_ref[m, own_rows, :] + total).astype(bf)
        cp = remote(
            lay_ref.at[m, own_rows, :], lay_ref.at[m, own_rows, :], pair_s.at[m], pair_r.at[m], twin
        )
        cp.start()
        sent.append(cp)
        got_v[("pair", m)] = cp

    need("dx", "x", "hs", "g")
    lane = lax.broadcasted_iota(jnp.int32, (1, 128), 1)
    gain_row = jnp.zeros((1, width), f32)
    s_ref[...] = jnp.zeros_like(s_ref)
    router_row = jnp.zeros((128, width), f32)
    for m in range(micro):
        here = slice(m * length, (m + 1) * length)
        tail = dx_ref[m, :, width:]
        grad = tail + pltpu.roll(tail, 128 - EXPERTS, 1)
        tail = x_ref[m, :, width:].astype(f32)
        prob = jnp.where(lane < EXPERTS, tail + pltpu.roll(tail, 128 - EXPERTS, 1), 0.0)
        shared = jnp.sum(prob * grad, axis=1, keepdims=True)
        low = (prob * (grad - shared)).astype(bf)
        router_row = router_row + mm_tn(low, x_ref[m, :, 0:width])
        full = dx_ref[m, :, 0:width] + mm(low[:, 0:EXPERTS], router_ref[...])
        state = hs_ref[m]
        scale = lax.rsqrt(jnp.mean(state * state, axis=1, keepdims=True) + epsilon)
        u = full * gain_f[...].reshape(1, width)
        common = jnp.mean(u * state, axis=1, keepdims=True) * (scale * scale * scale)
        total = g_ref[m].astype(f32) + (scale * u - state * common)
        sg[m] = total
        a_ref[here, :] = total.astype(bf)
        gain_row = gain_row + jnp.sum(full * state * scale, axis=0, keepdims=True)
    s_ref[0:EXPERTS, :] = router_row[0:EXPERTS].astype(bf)
    factor(3, a_ref, fg)
    need("y0", "hot", "wo")
    regroup(0, y0r)
    send_far(0)

    def inward(i):
        at = cols(i, tw)
        both = mm_nt(a_ref[...], wo_ref[at, :]).astype(bf)
        for m in range(micro):
            for j in range(tw // head):
                to = pl.ds(pl.multiple_of((i * (tw // head) + j) * length, length), length)
                ag[m, to, :] = both[m * length : (m + 1) * length, j * head : (j + 1) * head]

    tiles(wq // tw, inward)
    relay(3, fg)
    send_near(0)
    need("v", "pr", "k", "q", "tab")

    def unrope(u, m):
        return u * tab_ref[m, 0] - pltpu.roll(u, head // 2, 1) * tab_ref[m, 1]

    for m in range(micro):
        here = slice(m * length, (m + 1) * length)
        prob = pr_ref[m]
        back = mm_nt(ag[m], v_ref[m])
        shared = jnp.sum(prob * back, axis=1, keepdims=True)
        low = (prob * (back - shared)).astype(bf)
        dq = mm(low, k_ref[m]) * (head**-0.5)
        for h in range(heads):
            u = unrope(dq[h * length : (h + 1) * length], m)
            d_ref[here, h * head : (h + 1) * head] = u.astype(bf)
        dk = mm_tn(low, q_ref[m]) * (head**-0.5)
        d_ref[here, wq : wq + head] = unrope(dk, m).astype(bf)
        d_ref[here, wq + head : wq + 2 * head] = mm_tn(prob.astype(bf), ag[m]).astype(bf)
    for m in range(micro):
        factor_d(m)
    need("wq", "wk", "wv")
    got_part = []
    for j in range(3):

        def outward(i, j=j):
            at = cols(i + j * (nt // 3), tw)
            own_part[:, at] = (
                mm_nt(d_ref[:, 0:wq], wq_ref[at, :])
                + mm_nt(d_ref[:, wq : wq + head], wk_ref[at, :])
                + mm_nt(d_ref[:, wq + head :], wv_ref[at, :])
            )

        tiles(nt // 3, outward)
        at = pl.ds(j * (width // 3), width // 3)
        cp = remote(
            own_part.at[:, at], other_part.at[:, at], part_s.at[j], part_r.at[j], (e, 1 - c)
        )
        cp.start()
        sent.append(cp)
        got_part.append(cp)
    fd[0:rows, :] = d_ref[:, part(qy, wd)]
    fg[0:rows, :] = a_ref[:, part(qx, wg)]
    need("fa", "fa0")
    arrive(3, fg)

    def two(i):
        at = cols(i, tw)
        pb[:, at] = mm_tn(fa[...], fg[:, at]).astype(bf)

    tiles(wg // tw, two)
    got_y = {}

    def spread(i):
        src, dst, size, rest = ((pa, za, ha, ra), (pb, zb, hb, rb))[i]
        far = lax.rem(z + jnp.where(z == 0, 3, 1), 4)
        cp = remote(src.at[part(far, size), :], rest, l_s.at[i], l_r.at[i], beside_dev)
        start_if(edge, cp)
        got_y[("far", i)] = cp
        for k in (1, 3):
            cp = remote(
                src.at[part(lax.rem(z + k, 4), size), :], dst.at[k],
                y_s.at[k * 3 + i], y_r.at[k * 3 + i], z_dev(k),
            )
            start_if(not_last if k == 1 else not_first, cp)
            got_y[(i, k)] = cp

    def spread_rest(i):
        src, dst, size, rest = ((pa, za, ha, ra), (pb, zb, hb, rb))[i]
        across = part(lax.rem(z + 2, 4), size)

        @pl.when(inner)
        def _():
            got_y[("far", i)].wait_recv()
            src[across, :] = (src[across, :].astype(f32) + rest[...].astype(f32)).astype(bf)

        cp = remote(src.at[across, :], dst.at[2], y_s.at[6 + i], y_r.at[6 + i], z_dev(2))
        cp.start()
        sent.append(cp)
        got_y[(i, 2)] = cp

    spread(1)
    relay_d(0)
    relay_d(1)
    send_y1(1)
    need("tok")
    for cp in got_part:
        cp.wait_recv()
    last_row = jnp.zeros((1, width), f32)
    for m in range(micro):
        here = slice(m * length, (m + 1) * length)
        full = own_part[here, :] + other_part[here, :]
        state = tok_ref[m].astype(f32)
        scale = lax.rsqrt(jnp.mean(state * state, axis=1, keepdims=True) + epsilon)
        u = full * gain_a[...].reshape(1, width)
        common = jnp.mean(u * state, axis=1, keepdims=True) * (scale * scale * scale)
        tg_ref[m] = sg[m] + (scale * u - state * common)
        save(tg_ref.at[m], tg_hbm.at[m])
        last_row = last_row + jnp.sum(full * state * scale, axis=0, keepdims=True)
    index = lax.broadcasted_iota(jnp.int32, (hs, 1), 0)
    s_ref[2 * hs : 3 * hs, :] = jnp.where(
        index == 0, gain_row, jnp.where(index == 1, last_row, 0.0)
    ).astype(bf)
    got_s = []
    for d in (3, 1, 2):
        to = flip(qy, d // 2) * 2 + flip(qx, d % 2)
        cp = remote(s_ref.at[part(to, hs), :], fs.at[d], c_s.at[d], c_r.at[d], p_dev(d))
        cp.start()
        sent.append(cp)
        got_s.append(cp)
    spread_rest(1)
    need("fn", "fn0")
    for m in range(micro):
        got_f[("d", m, 1)].wait_recv()
        got_f[("d", m, 3)].wait_recv()

    def one(i):
        at = cols(i, tw)
        pa[:, at] = mm_tn(fn[...], fd[:, at]).astype(bf)

    tiles(wd // tw, one)
    spread(0)
    total = s_ref[part(q, hs), :].astype(jnp.float32)
    for cp in got_s:
        cp.wait_recv()
    for d in range(1, 4):
        total = total + fs[d].astype(jnp.float32)
    fs[0] = total.astype(jnp.bfloat16)
    for k in (2, 1, 3):
        cp = remote(
            fs.at[0, :, part(lax.rem(z + k, 4), ws)], zs.at[k],
            y_s.at[k * 3 + 2], y_r.at[k * 3 + 2], z_dev(k),
        )
        cp.start()
        sent.append(cp)
        got_y[(2, k)] = cp
    spread_rest(0)
    layer(0)

    def spots(px, py, t):
        return (
            oa.at[part(px * 4 + t, ha), part(py, wd)],
            ob.at[part(py * 4 + t, hb), part(px, wg)],
            os.at[part(py * 2 + px, hs), part(t, ws)],
        )

    home = spots(qx, qy, z)

    def total_of(i):
        first, others = (
            (pa[part(z, ha), :], za), (pb[part(z, hb), :], zb), (fs[0, :, part(z, ws)], zs),
        )[i]
        if i < 2:
            pl.when(not_first)(got_y[(i, 1)].wait_recv)
            pl.when(not_last)(got_y[(i, 3)].wait_recv)
        else:
            got_y[(i, 1)].wait_recv()
            got_y[(i, 3)].wait_recv()
        got_y[(i, 2)].wait_recv()
        acc = first.astype(f32)
        for k in range(1, 4):
            acc = acc + others[k].astype(f32)
        home[i][...] = acc.astype(bf)
        for k in (2, 1, 3):
            cp = remote(home[i], home[i], z_s.at[k * 3 + i], z_r.at[k * 3 + i], z_dev(k))
            if k == 2:
                cp.start()
                sent.append(cp)
            else:
                start_if(not_last if k == 1 else not_first, cp)

    turns = (
        0,
        jnp.where(inner, 2, jnp.where(z == 0, 3, 1)),
        jnp.where(inner, 1, 2),
        jnp.where(inner, 3, jnp.where(z == 0, 1, 3)),
    )
    got_p = {}

    def send(ref, i, n, d, j):
        at = ((n * 3) + i) * 4 + j
        cp = remote(ref, ref, p_s.at[at], p_r.at[at], p_dev(d))
        cp.start()
        sent.append(cp)
        got_p[(n, i, j)] = cp

    def own(n, i):
        k = turns[n]
        here = spots(qx, qy, lax.rem(z + 4 - k, 4))[i]
        if n:
            cp = remote(here, here, z_s.at[k * 3 + i], z_r.at[k * 3 + i], beside_dev)
            cp.wait_recv()
        if n == 1:
            to = jnp.where(z == 1, 1, 3)
            cp = remote(here, here, h_s.at[i], z_r.at[to * 3 + i], beside_dev)
            start_if(inner, cp)
        send(here, i, n, 1, 1)
        send(here, i, n, 2, 2)

    def forward(n, i):
        t = lax.rem(z + 4 - turns[n], 4)
        if i == 1:
            got_p[(n, i, 2)].wait_recv()
            send(spots(qx, flip(qy, 1), t)[i], i, n, 1, 3)
        else:
            got_p[(n, i, 1)].wait_recv()
            send(spots(flip(qx, 1), qy, t)[i], i, n, 2, 3)

    total_of(1)
    own(0, 1)
    total_of(0)
    own(0, 0)
    need("y1")
    for n in range(1, 8):
        for j in range(2):
            got_v[(n, j, "row")].wait_recv()

    regroup(1, y1r)
    send_far(1)
    total_of(2)
    own(0, 2)
    own(1, 1)
    forward(0, 1)
    own(1, 0)
    send_near(1)
    forward(0, 0)
    forward(0, 2)
    own(1, 2)
    for n in (2, 3):
        for i in (1, 0, 2):
            own(n, i)
            forward(n - 1, i)
    for i in (1, 0, 2):
        forward(3, i)
    layer(1)
    for i in (1, 0, 2):
        for n in range(4):
            first = 1 if i == 1 else 2
            got_p[(n, i, first)].wait_recv()
            got_p[(n, i, 3)].wait_recv()
        if i == 1:
            save(ob, ob_hbm)
    for m in range(micro):
        got_v[("pair", m)].wait_recv()
    for cp in saves:
        cp.wait()
    for cp in sent:
        cp.wait_send()
    for cond, cp in sent_if:
        pl.when(cond)(cp.wait_send)


def back_call(
    tokens, cotangent, gain_a, gain_f, wq, wk, wv, wo, router,
    dx, nrm, att, q, k, v, pr, tab, hs, xrows, y0, y1, hot, fn, fa,
):
    bf = jnp.bfloat16
    f32 = jnp.float32
    micro, length, width = tokens.shape
    rows = micro * length
    half = length // 2
    wd = wq.shape[1] + wk.shape[1] + wv.shape[1]
    wa = wq.shape[1]
    heads = wa // HEAD_SIZE
    vmem = pl.BlockSpec(memory_space=pltpu.VMEM)
    hbm = pl.BlockSpec(memory_space=ANY)

    def buf(*shape, dtype=bf):
        return pltpu.VMEM(shape, dtype)

    def like(array):
        return pltpu.VMEM(array.shape, array.dtype)

    sem = pltpu.SemaphoreType.DMA
    small = (64, width)
    hsm, wsm = 16, width // 4
    return pl.pallas_call(
        back_kernel,
        out_shape=(
            jax.ShapeDtypeStruct((micro, length, width), bf),
            jax.ShapeDtypeStruct((micro, length, width), f32),
            jax.ShapeDtypeStruct((width, wd), bf),
            jax.ShapeDtypeStruct((wa, width), bf),
            jax.ShapeDtypeStruct(small, bf),
        ),
        in_specs=[hbm] * 21 + [vmem] * 3,
        out_specs=(vmem, hbm, vmem, hbm, vmem),
        scratch_shapes=[
            like(tokens), like(cotangent), like(wq), like(wk), like(wv), like(wo), like(dx), like(q), like(k),
            like(v), like(pr), like(tab), like(hs), like(xrows), like(hot), like(y0), like(y1), buf(micro, 4 * half, width),
            buf(micro, 4 * half, width), buf(micro, half, width), buf(micro, length, width, dtype=f32), buf(wa, width),
            buf(rows, wd), buf(rows, width), buf(*small), buf(micro, length, width, dtype=f32),
            buf(micro, heads * length, HEAD_SIZE), buf(rows, width, dtype=f32), buf(rows, width, dtype=f32),
            buf(4 * rows, width // 2), buf(4 * rows, wd // 2), buf(4 * rows, wa // 2), buf(4 * rows, width // 2),
            buf(4, hsm, width),
            buf(width // 2, wd // 2), buf(wa // 2, width // 2),
            buf(4, width // 8, wd // 2), buf(4, wa // 8, width // 2), buf(4, hsm, wsm),
            buf(width // 8, wd // 2), buf(wa // 8, width // 2),
            sem((16,)), sem((16,)), sem((16,)), sem((16,)), sem((4,)), sem((4,)), sem((12,)), sem((12,)),
            sem((2,)), sem((2,)), sem((12,)), sem((12,)), sem((3,)), sem((3,)), sem((48,)), sem((48,)),
            sem((3,)), sem((3,)),
            sem((16,)), sem((16,)), sem((4 * micro,)), sem((4 * micro,)), sem((micro,)), sem((micro,)), sem((micro,)),
            sem((micro,)), sem((21,)), sem((1 + micro,)),
        ],
        compiler_params=pltpu.CompilerParams(
            collective_id=2, has_side_effects=True, vmem_limit_bytes=VMEM_LIMIT
        ),
        cost_estimate=pl.CostEstimate(
            flops=2 * rows * 4 * (width * wd + wa * width) // 4, bytes_accessed=20 * 2**20, transcendentals=0
        ),
        name="back",
    )(
        tokens, cotangent, wq, wk, wv, wo,
        dx, nrm.reshape(rows, width), att.reshape(rows, wa), q, k, v, pr, tab, hs, xrows, y0, y1, hot, fn, fa,
        gain_a, gain_f, router,
    )


def results_kernel(
    gate_ref, up_ref, down_ref, qkv_ref, o_ref, s_ref, lay_ref, tok_ref,
    gate_out, up_out, down_out, q_out, k_out, v_out, o_out, router_out, ffn_out, att_out, lay_out, tok_out,
):
    wq = q_out.shape[1]
    wk = wq + k_out.shape[1]
    ff = gate_ref.shape[2]
    f32 = jnp.float32
    for i in range(2):
        gate_out[:, i * ff : (i + 1) * ff] = gate_ref[i].astype(f32)
        up_out[:, i * ff : (i + 1) * ff] = up_ref[i].astype(f32)
    down_out[...] = down_ref[...].astype(f32)
    q_out[...] = qkv_ref[:, 0:wq].astype(f32)
    k_out[...] = qkv_ref[:, wq:wk].astype(f32)
    v_out[...] = qkv_ref[:, wk:].astype(f32)
    o_out[...] = o_ref[...].astype(f32)
    lay_out[...] = lay_ref[...]
    tok_out[...] = tok_ref[...]

    @pl.when(pl.program_id(0) == 0)
    def _():
        small = s_ref[...].astype(f32)
        router_out[...] = small[0:EXPERTS]
        width = small.shape[1]
        ffn_out[...] = small[EXPERTS : EXPERTS + 1].reshape(width)
        att_out[...] = small[EXPERTS + 1 : EXPERTS + 2].reshape(width)


def results_call(gate, up, down, qkv, o, small, layer, tokens_grad, wq, wk):
    _, width, ff = gate.shape
    steps = 6
    f32 = jnp.float32
    down_rows = lambda a, w: pl.BlockSpec((a // steps, w), lambda i: (i, 0))
    pair = pl.BlockSpec((2, width // steps, ff), lambda i: (0, i, 0))
    whole = lambda *s: pl.BlockSpec(s, lambda i: (0,) * len(s))
    out = lambda *s: jax.ShapeDtypeStruct(s, f32)
    wv = qkv.shape[1] - wq - wk
    few = 4
    some = pl.BlockSpec((layer.shape[0] // few, width), lambda i: (jnp.minimum(i, few - 1), 0))
    return pl.pallas_call(
        results_kernel,
        grid=(steps,),
        in_specs=[
            pair, pair, down_rows(2 * ff, width), down_rows(*qkv.shape), down_rows(*o.shape), whole(*small.shape),
            some, some,
        ],
        out_specs=(
            down_rows(width, 2 * ff), down_rows(width, 2 * ff), down_rows(2 * ff, width),
            down_rows(width, wq), down_rows(width, wk), down_rows(width, wv), down_rows(*o.shape),
            whole(EXPERTS, width), whole(width), whole(width), some, some,
        ),
        out_shape=(
            out(width, 2 * ff), out(width, 2 * ff), out(2 * ff, width),
            out(width, wq), out(width, wk), out(width, wv), out(*o.shape),
            out(EXPERTS, width), out(width), out(width),
            jax.ShapeDtypeStruct(layer.shape, layer.dtype), out(*tokens_grad.shape),
        ),
        compiler_params=pltpu.CompilerParams(vmem_limit_bytes=VMEM_LIMIT),
        cost_estimate=pl.CostEstimate(flops=0, bytes_accessed=64 * 2**20, transcendentals=0),
        name="results",
    )(gate, up, down.reshape(2 * ff, width), qkv, o, small, layer, tokens_grad)


def suits(mesh):
    return mesh.shape["expert"] == 16 and mesh.shape["tensor"] == 2


def local_fast(
    tokens, cotangent, positions, routes, attention_gain, feedforward_gain, query_weight, key_matrix,
    value_matrix, output_weight, router_weight, gate_weight, up_weight, down_weight,
):
    micro_count, length, model_width = tokens.shape
    gain_a, gain_f = attention_gain, feedforward_gain
    router_t = router_weight.T
    dx, *kept, gate_low, up_low, down_low = front_call(
        tokens, cotangent, positions, routes.transpose(0, 2, 1), gain_a, gain_f, query_weight, key_matrix,
        value_matrix, output_weight, router_t, gate_weight, up_weight, down_weight,
    )
    layer_out, tokens_grad, oa, ob, os = back_call(
        tokens, cotangent, gain_a, gain_f, query_weight, key_matrix, value_matrix, output_weight,
        router_t, dx, *kept,
    )
    shape = layer_out.shape
    flat = (shape[0] * shape[1], shape[2])
    gate, up, down, dq, dk, dv, do, router, ffn_gain, att_gain, layer_out, tokens_grad = results_call(
        gate_low, up_low, down_low, oa, ob, os, layer_out.reshape(flat), tokens_grad.reshape(flat),
        query_weight.shape[1], key_matrix.shape[1],
    )
    return (
        layer_out.reshape(shape), tokens_grad.reshape(shape), att_gain, ffn_gain, dq, dk, dv, do, router.T, gate,
        up, down,
    )


def solution(mesh):
    in_specs = (
        P(None, "expert", None),
        P(None, "expert", None),
        P(None, "expert"),
        P(None, "expert", None),
        P(),
        P(),
        P(None, "tensor"),
        P(None, "tensor"),
        P(None, "tensor"),
        P("tensor", None),
        P(),
        P(None, "expert"),
        P(None, "expert"),
        P("expert", None),
    )
    out_specs = (
        P(None, "expert", None),
        P(None, "expert", None),
        P(),
        P(),
        P(None, "tensor"),
        P(None, "tensor"),
        P(None, "tensor"),
        P("tensor", None),
        P(),
        P(None, "expert"),
        P(None, "expert"),
        P("expert", None),
    )
    body = local_fast if suits(mesh) else local
    return jax.shard_map(body, mesh=mesh, in_specs=in_specs, out_specs=out_specs, check_vma=False)
```
